32 devices in a mesh: seq: 4 (over y, core), exp: 8 (over z, x).
Axes of the slice: x: 2, y: 2, z: 4, core: 2. Of those that a mesh axis runs over, the one named last changes fastest.
Arguments:
- tokens: bfloat16 [8, 512, 1536], P('exp', 'seq'), may hold values from -6 to 6
- routes: int32 [8, 512, 6], P('exp', 'seq'), may hold values from 0 to 15, all different within a row; in each aligned block of 128 rows (0 to 127, 128 to 255, ..., all dimensions but the last counted through in order) at most 56 rows name the same one
- out_grad: bfloat16 [8, 512, 1536], P('exp', 'seq'), may hold values from -6 to 6
- norm_mix: bfloat16 [1536], P(('seq', 'exp')), may hold values from 0.5 to 1.5
- in_weight: bfloat16 [1536, 6400], P(('seq', 'exp')), may hold values from -0.15625 to 0.15625
- step_weight: bfloat16 [1536, 48], P(('seq', 'exp')), may hold values from -0.15625 to 0.15625
- conv_weight: bfloat16 [4, 3328], P(None, ('seq', 'exp')), may hold values from -3 to 3
- conv_bias: bfloat16 [3328], P(('seq', 'exp')), may hold values from -3 to 3
- step_bias: float32 [48], replicated, may hold values from -4 to -1
- decay_log: float32 [48], replicated, may hold values from -11 to 0
- skip_gain: float32 [48], replicated, may hold values from 0.5 to 1.5
- norm_gate: bfloat16 [3072], P(('seq', 'exp')), may hold values from 0.5 to 1.5
- out_weight: bfloat16 [3072, 1536], P(('seq', 'exp')), may hold values from -0.109375 to 0.109375
- norm_ffn: bfloat16 [1536], P(('seq', 'exp')), may hold values from 0.5 to 1.5
- router_weight: bfloat16 [1536, 16], P(('seq', 'exp')), may hold values from -0.078125 to 0.078125
- shared_gate: bfloat16 [1536, 1024], P(('seq', 'exp')), may hold values from -0.15625 to 0.15625
- shared_up: bfloat16 [1536, 1024], P(('seq', 'exp')), may hold values from -0.15625 to 0.15625
- shared_down: bfloat16 [1024, 1536], P(('seq', 'exp')), may hold values from -0.1875 to 0.1875
- expert_gate: bfloat16 [16, 1536, 512], P('exp'), may hold values from -0.15625 to 0.15625
- expert_up: bfloat16 [16, 1536, 512], P('exp'), may hold values from -0.15625 to 0.15625
- expert_down: bfloat16 [16, 512, 1536], P('exp'), may hold values from -0.25 to 0.25
Outputs:
- result: bfloat16 [8, 512, 1536], P('exp', 'seq')
- tokens_grad: bfloat16 [8, 512, 1536], P('exp', 'seq')
- grad_norm_mix: float32 [1536], P(('seq', 'exp'))
- grad_in_weight: float32 [1536, 6400], P(('seq', 'exp'))
- grad_step_weight: float32 [1536, 48], P(('seq', 'exp'))
- grad_conv_weight: float32 [4, 3328], P(None, ('seq', 'exp'))
- grad_conv_bias: float32 [3328], P(('seq', 'exp'))
- grad_step_bias: float32 [48], replicated
- grad_decay_log: float32 [48], replicated
- grad_skip_gain: float32 [48], replicated
- grad_norm_gate: float32 [3072], P(('seq', 'exp'))
- grad_out_weight: float32 [3072, 1536], P(('seq', 'exp'))
- grad_norm_ffn: float32 [1536], P(('seq', 'exp'))
- grad_router_weight: float32 [1536, 16], P(('seq', 'exp'))
- grad_shared_gate: float32 [1536, 1024], P(('seq', 'exp'))
- grad_shared_up: float32 [1536, 1024], P(('seq', 'exp'))
- grad_shared_down: float32 [1024, 1536], P(('seq', 'exp'))
- grad_expert_gate: float32 [16, 1536, 512], P('exp', 'seq')
- grad_expert_up: float32 [16, 1536, 512], P('exp', 'seq')
- grad_expert_down: float32 [16, 512, 1536], P('exp', None, 'seq')
- stats: float32 [3], replicated
The draws below stay inside these ranges and needn't reach their ends.
Inputs may be any that keep to these rules, and one draw needn't show every extreme that they name: `routes`: each row names 6 different experts. Among the 128 tokens of one device (aligned blocks along a sequence) no expert is named by more than 56 rows, a bound that some block reaches.
All inputs are finite; a program needn't handle non-finite values.
Results may differ from the reference program's by a relative error of at most 0.022.
Values may be sent and summed in bfloat16 or wider, within the bound.
A program may use at most 256 MiB of HBM per device.

```python
import math
import jax
import jax.numpy as jnp
import numpy as np
from jax import lax

D = 1536
HEADS = 48
CONV = 4
FF_E = 512
SHARED = 1024
TOPK = 6
GROUP = 128
TOK_DEV = 128
DIN = 3072
XBC = 3328
EXPERTS = 16
CAP = 56
LENGTH = 512
SEQS = 8
N_SEQ = 4


def draw_decay_log(key, part):
    key = jax.random.fold_in(key, 11)
    unit = jax.random.uniform(key, (HEADS,), jnp.float32)
    lower_end = math.log(2.0 / LENGTH)
    upper_end = math.log(0.4)
    return lower_end + unit * (upper_end - lower_end)


def steps_of(own_key, shape, cuts, smallest, high):
    level = 1.0
    for axis_at, shards_of in cuts:
        heights = jax.random.uniform(jax.random.fold_in(jax.random.fold_in(own_key, 6), axis_at), (shards_of,), jnp.float32, smallest / len(cuts), high / len(cuts))
        level = level * jnp.repeat(jnp.exp(heights), shape[axis_at] // shards_of).reshape((-1,) + (1,) * (len(shape) - 1 - axis_at))
    return level


def deal_out(key, own, number, rows, count, top, limit, slope):
    order = jax.random.permutation(key, count)
    packed, common = load_shares(count, rows * top, limit, slope, True), load_shares(count, rows * top, limit, slope, False)
    places = jnp.arange(count)

    def named(lengths, turn):
        used = int((lengths > 0).sum())
        fixed = max(1, used // 4)
        passed = fixed + (places - fixed + turn * (used - fixed)) % max(1, count - fixed)
        return jnp.zeros((count,), jnp.int32).at[order[jnp.where(places < fixed, places, passed)]].set(jnp.asarray(lengths, jnp.int32))

    lengths = jnp.where(number % 4 == 0, named(packed, number // 4), named(common, number - number // 4 - 1))
    mixed = jax.random.permutation(jax.random.fold_in(own, 3), count)
    giver, sink = mixed[0:count // 2 * 2:2], mixed[1:count // 2 * 2:2]
    slack = jnp.minimum(lengths[giver] - 1, limit - lengths[sink]) // 2
    slack = jnp.where((giver == order[0]) | (sink == order[0]) | (lengths[sink] == 0), 0, jnp.maximum(slack, 0))
    passed = jax.random.randint(jax.random.fold_in(own, 4), (count // 2,), 0, 1 << 20) % (slack + 1)
    lengths = lengths.at[giver].add(-passed).at[sink].add(passed)
    labels = jnp.searchsorted(jnp.cumsum(lengths), jnp.arange(rows * top), side="right").astype(jnp.int32)
    grid = labels.reshape(top, rows).T
    grid = grid[jax.random.permutation(jax.random.fold_in(own, 1), rows)]
    turn = jax.random.randint(jax.random.fold_in(own, 2), (rows, 1), 0, top)
    return jnp.take_along_axis(grid, (jnp.arange(top)[None, :] + turn) % top, axis=1)


def load_shares(count, total, limit, lean, full):
    loads = [(1 << 20) // math.isqrt(rank ** lean) + 1 for rank in range(1, count + 1)]
    largest = limit if full else min(limit, max(-(-total // count), total * loads[0] // sum(loads)))
    least = 1 if total - largest >= count - 1 else 0
    holding, rest = [largest] + [least] * (count - 1), total - largest - least * (count - 1)
    while rest > 0:
        candidates = [i for i in range(1, count) if holding[i] < largest] or [i for i in range(1, count) if holding[i] < limit]
        mass, remaining = sum([loads[i] for i in candidates]), rest
        for i in candidates:
            addition = min(limit - holding[i], max(1, remaining * loads[i] // mass), rest)
            holding[i] = holding[i] + addition
            rest = rest - addition
    return np.array(holding)


def centred(rng, shape, scale, most, split=(), held_as=jnp.bfloat16):
    entries = jax.random.normal(rng, shape, jnp.float32) * scale
    if len(split) > 0:
        entries = steps_of(rng, shape, split, -0.22, 0.18) * entries
    return jnp.clip(entries, min=-most, max=most).astype(held_as)


def setup_inputs(seed: int = 0) -> dict:
    arg_keys = jax.random.split(jax.random.key(seed), 22)
    tokens = centred(arg_keys[0], (SEQS, LENGTH, D), 1.0, 6.0, ((0, 8), (1, 4)))
    routes_keys = jax.random.split(jax.random.fold_in(arg_keys[1], 1), SEQS * LENGTH // TOK_DEV)
    routes_turns = jax.random.permutation(jax.random.fold_in(arg_keys[1], 3), SEQS * LENGTH // TOK_DEV)
    routes = jax.vmap(lambda own, number: deal_out(jax.random.fold_in(arg_keys[1], 2), own, number, TOK_DEV, EXPERTS, TOPK, CAP, 1))(routes_keys, routes_turns).reshape((SEQS, LENGTH, TOPK))
    out_grad = centred(arg_keys[2], (SEQS, LENGTH, D), 1.0, 6.0, ((0, 8), (1, 4)))
    norm_mix = jnp.clip(1.0 + 0.1 * jax.random.normal(arg_keys[3], (D,), jnp.float32), 0.5, 1.5).astype(jnp.bfloat16)
    in_weight = centred(arg_keys[4], (D, DIN + XBC), D ** -0.5, 0.15625, ((0, 32),))
    step_weight = centred(arg_keys[5], (D, HEADS), D ** -0.5, 0.15625, ((0, 32),))
    conv_weight = centred(arg_keys[6], (CONV, XBC), CONV ** -0.5, 3.0, ((1, 32),))
    conv_bias = centred(arg_keys[7], (XBC,), 0.5, 3.0, ((0, 32),))
    step_bias = jnp.clip(jax.random.uniform(arg_keys[8], (HEADS,), jnp.float32, -4.0, -1.0), -4.0, -1.0)
    decay_log = draw_decay_log(jax.random.fold_in(arg_keys[21], 71), 0)
    skip_gain = jnp.clip(jax.random.uniform(arg_keys[10], (HEADS,), jnp.float32, 0.5, 1.5), 0.5, 1.5)
    norm_gate = jnp.clip(1.0 + 0.1 * jax.random.normal(arg_keys[11], (DIN,), jnp.float32), 0.5, 1.5).astype(jnp.bfloat16)
    out_weight = centred(arg_keys[12], (DIN, D), DIN ** -0.5, 0.109375, ((0, 32),))
    norm_ffn = jnp.clip(1.0 + 0.1 * jax.random.normal(arg_keys[13], (D,), jnp.float32), 0.5, 1.5).astype(jnp.bfloat16)
    router_weight = centred(arg_keys[14], (D, EXPERTS), (4 * D) ** -0.5, 0.078125, ((0, 32),))
    shared_gate = centred(arg_keys[15], (D, SHARED), D ** -0.5, 0.15625, ((0, 32),))
    shared_up = centred(arg_keys[16], (D, SHARED), D ** -0.5, 0.15625, ((0, 32),))
    shared_down = centred(arg_keys[17], (SHARED, D), SHARED ** -0.5, 0.1875, ((0, 32),))
    expert_gate = centred(arg_keys[18], (EXPERTS, D, FF_E), D ** -0.5, 0.15625, ((0, 8),))
    expert_up = centred(arg_keys[19], (EXPERTS, D, FF_E), D ** -0.5, 0.15625, ((0, 8),))
    expert_down = centred(arg_keys[20], (EXPERTS, FF_E, D), FF_E ** -0.5, 0.25, ((0, 8),))
    return dict(tokens=tokens, routes=routes, out_grad=out_grad, norm_mix=norm_mix, in_weight=in_weight, step_weight=step_weight, conv_weight=conv_weight, conv_bias=conv_bias, step_bias=step_bias, decay_log=decay_log, skip_gain=skip_gain, norm_gate=norm_gate, out_weight=out_weight, norm_ffn=norm_ffn, router_weight=router_weight, shared_gate=shared_gate, shared_up=shared_up, shared_down=shared_down, expert_gate=expert_gate, expert_up=expert_up, expert_down=expert_down)


EPSILON = 1e-05
PRECISE = lax.Precision.HIGHEST

@jax.custom_vjp
def low(v):
    return lax.optimization_barrier(v.astype(jnp.bfloat16)).astype(jnp.float32)

@jax.custom_vjp
def low_back(v):
    return v

def low_keep(v):
    return (low(v), None)

def low_pass(kept, grad):
    return (grad,)

def back_keep(v):
    return (v, None)

def back_low(kept, grad):
    return (low(grad),)
low.defvjp(low_keep, low_pass)
low_back.defvjp(back_keep, back_low)

def rms_scale(value, gain):
    return value * lax.rsqrt(lax.optimization_barrier(jnp.mean(value * value, -1, keepdims=True)) + EPSILON) * gain

def matmul_exact(left, right):
    return jnp.dot(left, right, precision=PRECISE, preferred_element_type=jnp.float32)

def group_step(carried, pieces, rate):
    values, steps, input_b, input_c = pieces
    length = values.shape[0]
    logs = jnp.cumsum(steps * rate[None, :], axis=0)
    spread = logs[:, None, :] - logs[None, :, :]
    causal = (jnp.arange(length)[:, None] >= jnp.arange(length)[None, :])[:, :, None]
    kernel = jnp.where(causal, jnp.exp(jnp.where(causal, spread, 0.0)), 0.0)
    intersection = jnp.dot(input_c, input_b.T, precision=PRECISE)
    weights = intersection[:, :, None] * kernel * steps[None, :, :]
    inner_part = jnp.einsum('tsh,shp->thp', weights, values, precision=PRECISE)
    carried_part = jnp.einsum('tn,hpn->thp', input_c, carried, precision=PRECISE) * jnp.exp(logs)[:, :, None]
    tail = jnp.exp(logs[-1][None, :] - logs) * steps
    fresh = jnp.einsum('sh,shp,sn->hpn', tail, values, input_b, precision=PRECISE)
    updated = jnp.exp(logs[-1])[:, None, None] * carried + fresh
    return (updated, inner_part + carried_part)

def sequence_forward(params, tokens, routes):
    norm_mix, in_weight, step_weight, conv_weight, conv_bias, step_bias, decay_log, skip_gain, norm_gate, out_weight, norm_ffn, router_weight, shared_gate, shared_up, shared_down, expert_gate, expert_up, expert_down = params
    length = tokens.shape[0]
    inner = norm_gate.shape[0]
    heads = step_bias.shape[0]
    head_dim = inner // heads
    state_dim = (conv_weight.shape[1] - inner) // 2
    width = conv_weight.shape[0]
    lowered_one = low(rms_scale(tokens, norm_mix))
    projected = low_back(matmul_exact(lowered_one, in_weight))
    step_raw = low_back(matmul_exact(lowered_one, step_weight))
    gate_z = projected[:, :inner]
    conv_in = projected[:, inner:]
    padded = jnp.concatenate([jnp.zeros((width - 1, conv_in.shape[1]), jnp.float32), conv_in], 0)
    mixed = conv_bias + sum((conv_weight[offset] * padded[offset:offset + length] for offset in range(width)))
    conv_out = jax.nn.silu(mixed)
    values = conv_out[:, :inner].reshape(length, heads, head_dim)
    input_b = conv_out[:, inner:inner + state_dim]
    input_c = conv_out[:, inner + state_dim:]
    steps = jax.nn.softplus(step_raw + step_bias)
    rate = -jnp.exp(decay_log)
    groups = length // GROUP
    blocks = (values.reshape(groups, GROUP, heads, head_dim), steps.reshape(groups, GROUP, heads), input_b.reshape(groups, GROUP, state_dim), input_c.reshape(groups, GROUP, state_dim))
    start = jnp.zeros((heads, head_dim, state_dim), jnp.float32)
    stepper = jax.checkpoint(lambda carried, pieces: group_step(carried, pieces, rate))
    outputs = lax.scan(stepper, start, blocks)[1]
    scanned = outputs.reshape(length, heads, head_dim) + skip_gain[None, :, None] * values
    gated = scanned.reshape(length, inner) * jax.nn.silu(gate_z)
    normed_mix = low(rms_scale(gated, norm_gate))
    mixer_out = low_back(matmul_exact(normed_mix, out_weight))
    resid = tokens + mixer_out
    ffn_in = low(rms_scale(resid, norm_ffn))
    logits = low_back(matmul_exact(ffn_in, router_weight))
    picked = jnp.take_along_axis(logits, routes, axis=1)
    gates = jax.nn.softmax(picked, axis=-1)
    shared_a = low_back(matmul_exact(ffn_in, shared_gate))
    shared_b = low_back(matmul_exact(ffn_in, shared_up))
    shared_out = matmul_exact(low(jax.nn.silu(shared_a) * shared_b), shared_down)
    experts = expert_gate.shape[0]
    model = tokens.shape[1]
    topk = routes.shape[1]
    room = N_SEQ * CAP
    flat_ids = routes.reshape(-1)
    hits = (flat_ids[:, None] == jnp.arange(experts, dtype=jnp.int32)[None, :]).astype(jnp.int32)
    ranks = lax.optimization_barrier(jnp.sum((jnp.cumsum(hits, 0) - 1) * hits, 1))
    places = (flat_ids * room + ranks).astype(jnp.int32)
    slot_rows = low_back(jnp.broadcast_to(ffn_in[:, None, :], (length, topk, model)).reshape(length * topk, model))
    buffer = jnp.zeros((experts * room, model), jnp.float32).at[places].set(slot_rows).reshape(experts, room, model)
    expert_a = low_back(jnp.einsum('erd,edf->erf', buffer, expert_gate, precision=PRECISE))
    expert_b = low_back(jnp.einsum('erd,edf->erf', buffer, expert_up, precision=PRECISE))
    expert_hidden = low(jax.nn.silu(expert_a) * expert_b)
    expert_out = jnp.einsum('erf,efd->erd', expert_hidden, expert_down, precision=PRECISE)
    slot_out = low_back(low(expert_out.reshape(experts * room, model)[places])).reshape(length, topk, model)
    ffn_out = lax.optimization_barrier(jnp.sum(gates[:, :, None] * slot_out, 1)) + shared_out
    result = resid + ffn_out
    stats = jnp.stack([jnp.sum(resid * resid), jnp.sum(mixer_out * mixer_out), jnp.sum(ffn_out * ffn_out)])
    return (result, stats)

def reference(tokens, routes, out_grad, norm_mix, in_weight, step_weight, conv_weight, conv_bias, step_bias, decay_log, skip_gain, norm_gate, out_weight, norm_ffn, router_weight, shared_gate, shared_up, shared_down, expert_gate, expert_up, expert_down):
    params = tuple((array.astype(jnp.float32) for array in (norm_mix, in_weight, step_weight, conv_weight, conv_bias, step_bias, decay_log, skip_gain, norm_gate, out_weight, norm_ffn, router_weight, shared_gate, shared_up, shared_down, expert_gate, expert_up, expert_down)))

    def one_sequence(totals, pieces):
        seq_tokens, seq_routes, seq_grad = pieces

        def forward(weights, inputs):
            return sequence_forward(weights, inputs, seq_routes)
        result, pullback, stats = jax.vjp(forward, params, seq_tokens.astype(jnp.float32), has_aux=True)
        grad_params, grad_tokens = pullback(seq_grad.astype(jnp.float32))
        summed = jax.tree.map(jnp.add, totals[0], grad_params)
        return ((summed, totals[1] + stats), (result.astype(jnp.bfloat16), grad_tokens.astype(jnp.bfloat16)))
    start = (jax.tree.map(jnp.zeros_like, params), jnp.zeros((3,), jnp.float32))
    (grads, stat_sums), (results, token_grads) = lax.scan(one_sequence, start, (tokens, routes, out_grad))
    stats = stat_sums / (SEQS * LENGTH * D)
    return (results, token_grads, grads[0], grads[1], grads[2], grads[3], grads[4], grads[5], grads[6], grads[7], grads[8], grads[9], grads[10], grads[11], grads[12], grads[13], grads[14], grads[15], grads[16], grads[17], stats)
```

```python
import functools

import jax
import jax.numpy as jnp
from jax import lax
from jax.experimental import pallas as pl
from jax.experimental.pallas import tpu as pltpu
from jax.sharding import PartitionSpec as P

GROUP = 128
EPSILON = 1e-05
PRECISE = lax.Precision.HIGHEST
MESH = pl.DeviceIdType.MESH
BF = jnp.bfloat16
F32 = jnp.float32
ANY = pl.BlockSpec(memory_space=pl.ANY)
VMEM = pl.BlockSpec(memory_space=pltpu.VMEM)
DMA = pltpu.SemaphoreType.DMA


def ring_place(e, n):
    odd = e % 2
    return (1 - odd) * (e // 2) + odd * (n - 1 - e // 2)


def ring_index(p, n):
    back = p // (n // 2)
    return (1 - back) * (2 * p) + back * (2 * (n - 1 - p) + 1)


def ring_sides(e, n):
    p = ring_place(e, n)
    return p, ring_index((p + 1) % n, n), ring_index((p + n - 1) % n, n)


def greet(partners):
    barrier = pltpu.get_barrier_semaphore()
    for partner in partners:
        pl.semaphore_signal(barrier, inc=1, device_id=partner, device_id_type=MESH)
    pl.semaphore_wait(barrier, len(partners))


def remote(src, dst, send, recv, device):
    copy = pltpu.make_async_remote_copy(
        src_ref=src,
        dst_ref=dst,
        send_sem=send,
        recv_sem=recv,
        device_id=device,
        device_id_type=MESH,
    )
    copy.start()
    return copy


def params(cid):
    return pltpu.CompilerParams(
        collective_id=cid, has_side_effects=True, vmem_limit_bytes=56 << 20
    )


def tile_rows(rows, most=16):
    return most if rows % most == 0 else rows


def gather_in_kernel(
    ns, ne, hw, inner, in_ref, pack_ref, tok_ref, w_ref, x_ref, lsem, ssem0, rsem0, ssem, rsem
):
    s, e = lax.axis_index("seq"), lax.axis_index("exp")
    p, right, left = ring_sides(e, ne)
    width = in_ref.shape[1] - 2 * inner
    parts = (
        (lambda to: in_ref.at[:, pl.ds(pl.multiple_of(to * hw, 128), hw)], 0, hw),
        (lambda to: in_ref.at[:, pl.ds(pl.multiple_of(inner + to * hw, 128), hw)], hw, hw),
        (lambda to: in_ref.at[:, pl.ds(2 * inner, width)], 2 * hw, width),
        (lambda to: pack_ref, 2 * hw + width, pack_ref.shape[1]),
    )
    greet([((s + t) % ns, e) for t in range(1, ns)] + [(s, right), (s, left)])
    own = []
    for i, (piece, start, size) in enumerate(parts):
        own.append(
            pltpu.make_async_copy(piece(s), w_ref.at[s, e, :, pl.ds(start, size)], lsem.at[i])
        )
    own.append(pltpu.make_async_copy(tok_ref, x_ref.at[s], lsem.at[len(parts)]))
    for copy in own:
        copy.start()
    first = {}
    for t in range(1, ns):
        to = (s + t) % ns
        for i, (piece, start, size) in enumerate(parts):
            first[t, i] = remote(
                piece(to),
                w_ref.at[s, e, :, pl.ds(start, size)],
                ssem0.at[t - 1, i],
                rsem0.at[t - 1, i],
                (to, e),
            )
    for t in range(1, ns):
        first[t, len(parts)] = remote(
            tok_ref,
            x_ref.at[s],
            ssem0.at[t - 1, len(parts)],
            rsem0.at[t - 1, len(parts)],
            ((s + t) % ns, e),
        )
    for copy in own:
        copy.wait()
    sent = {}
    for k in range(ne - 1):
        for t in range(ns):
            way = t % 2
            place = (p - k + ne) % ne if way == 0 else (p + k) % ne
            slot = ring_index(place, ne)
            if k > 0:
                sent[k - 1, t].wait_recv()
            elif t > 0:
                for i in range(len(parts)):
                    first[t, i].wait_recv()
            block = w_ref.at[(s + ns - t) % ns, slot]
            sent[k, t] = remote(
                block, block, ssem.at[k, t], rsem.at[k, t], (s, right if way == 0 else left)
            )
    for t in range(ns):
        sent[ne - 2, t].wait_recv()
    for t in range(1, ns):
        first[t, len(parts)].wait_recv()
    for copy in list(first.values()) + list(sent.values()):
        copy.wait_send()


def gather_in(in_weight, pack, tokens, ns, ne, inner, cid):
    rows, columns = in_weight.shape
    hw = inner // ns
    wide = 2 * hw + columns - 2 * inner + pack.shape[1]
    return pl.pallas_call(
        functools.partial(gather_in_kernel, ns, ne, hw, inner),
        out_shape=(
            jax.ShapeDtypeStruct((ns, ne, rows, wide), BF),
            jax.ShapeDtypeStruct((ns,) + tokens.shape, BF),
        ),
        in_specs=[ANY, ANY, ANY],
        out_specs=(ANY, ANY),
        scratch_shapes=[
            DMA((5,)),
            DMA((ns - 1, 5)),
            DMA((ns - 1, 5)),
            DMA((ne - 1, ns)),
            DMA((ne - 1, ns)),
        ],
        compiler_params=params(cid),
        name="gather_in",
    )(in_weight, pack, tokens)


def sum_seq_kernel(ns, subs, *refs):
    (part, aux, out, aux_out, one, two, aux_in, s1, r1, s2, r2, sa, ra) = refs
    s, e = lax.axis_index("seq"), lax.axis_index("exp")
    ny = ns // 2
    y, c = s // 2, s % 2
    mate = (2 * y + 1 - c, e)
    rows = part.shape[1]
    step = rows // subs
    tile = tile_rows(step)
    greet([((s + t) % ns, e) for t in range(1, ns)])
    aux_copies = []
    for t in range(1, ns):
        to = (s + t) % ns
        aux_copies.append(
            remote(aux.at[to], aux_in.at[t - 1], sa.at[t - 1], ra.at[t - 1], (to, e))
        )
    first = {}
    for j in list(range(1, ny)) + [0]:
        for u in range(subs):
            block = part.at[2 * ((y + j) % ny) + 1 - c, pl.ds(u * step, step)]
            first[j, u] = remote(
                block, one.at[j, pl.ds(u * step, step)], s1.at[j, u], r1.at[j, u], mate
            )
    second = {}
    for j in range(1, ny):
        to = 2 * ((y + j) % ny) + c
        for u in range(subs):
            first[j, u].wait_recv()

            def join(i, carry):
                r = pl.ds(pl.multiple_of(u * step + i * tile, tile), tile)
                total = one[j, r, :].astype(F32) + part[to, r, :].astype(F32)
                one[j, r, :] = total.astype(BF)
                return carry

            lax.fori_loop(0, step // tile, join, 0)
            second[j, u] = remote(
                one.at[j, pl.ds(u * step, step)],
                two.at[j - 1, pl.ds(u * step, step)],
                s2.at[j - 1, u],
                r2.at[j - 1, u],
                (to, e),
            )
    for u in range(subs):
        first[0, u].wait_recv()
        for j in range(1, ny):
            second[j, u].wait_recv()

        def close(i, carry):
            r = pl.ds(pl.multiple_of(u * step + i * tile, tile), tile)
            total = one[0, r, :].astype(F32) + part[s, r, :].astype(F32)
            for j in range(1, ny):
                total = total + two[j - 1, r, :].astype(F32)
            out[r, :] = total
            return carry

        lax.fori_loop(0, step // tile, close, 0)
    aux_total = aux[s]
    for t in range(1, ns):
        aux_copies[t - 1].wait_recv()
        aux_total = aux_total + aux_in[t - 1]
    aux_out[...] = aux_total
    for copy in list(first.values()) + list(second.values()) + aux_copies:
        copy.wait_send()


def sum_seq(part, aux, ns, cid, subs=2):
    rows, width = part.shape[1:]
    ny = ns // 2
    return pl.pallas_call(
        functools.partial(sum_seq_kernel, ns, subs),
        out_shape=(
            jax.ShapeDtypeStruct((rows, width), F32),
            jax.ShapeDtypeStruct(aux.shape[1:], F32),
        ),
        in_specs=[VMEM, VMEM],
        out_specs=(VMEM, VMEM),
        scratch_shapes=[
            pltpu.VMEM((ny, rows, width), BF),
            pltpu.VMEM((max(ny - 1, 1), rows, width), BF),
            pltpu.VMEM((ns - 1,) + aux.shape[1:], F32),
            DMA((ny, subs)),
            DMA((ny, subs)),
            DMA((max(ny - 1, 1), subs)),
            DMA((max(ny - 1, 1), subs)),
            DMA((ns - 1,)),
            DMA((ns - 1,)),
        ],
        compiler_params=params(cid),
        name="sum_seq",
    )(part, aux)


def gather_seq_kernel(ns, v, aux, out, aux_out, lsem, s1, r1, s2, r2, sa, ra):
    s, e = lax.axis_index("seq"), lax.axis_index("exp")
    ny = ns // 2
    y, c = s // 2, s % 2
    mate = (2 * y + 1 - c, e)
    greet([((s + t) % ns, e) for t in range(1, ns)])
    own = pltpu.make_async_copy(v, out.at[s], lsem.at[0])
    own_aux = pltpu.make_async_copy(aux, aux_out.at[s], lsem.at[1])
    first = {}
    for j in range(1, ny):
        to = (2 * ((y + j) % ny) + c, e)
        first[j] = remote(v, out.at[s], s1.at[j], r1.at[j], to)
    first[0] = remote(v, out.at[s], s1.at[0], r1.at[0], mate)
    extra = []
    for t in range(1, ns):
        extra.append(
            remote(aux, aux_out.at[s], sa.at[t - 1], ra.at[t - 1], ((s + t) % ns, e))
        )
    own.start()
    own_aux.start()
    second = []
    for j in range(1, ny):
        first[j].wait_recv()
        block = out.at[2 * ((y + ny - j) % ny) + c]
        second.append(remote(block, block, s2.at[j - 1], r2.at[j - 1], mate))
    first[0].wait_recv()
    for copy in second + extra:
        copy.wait_recv()
    for copy in list(first.values()) + second + extra:
        copy.wait_send()
    own.wait()
    own_aux.wait()


def gather_seq(v, aux, ns, cid):
    ny = ns // 2
    return pl.pallas_call(
        functools.partial(gather_seq_kernel, ns),
        out_shape=(
            jax.ShapeDtypeStruct((ns,) + v.shape, v.dtype),
            jax.ShapeDtypeStruct((ns,) + aux.shape, aux.dtype),
        ),
        in_specs=[VMEM, VMEM],
        out_specs=(VMEM, VMEM),
        scratch_shapes=[
            DMA((2,)),
            DMA((ny,)),
            DMA((ny,)),
            DMA((max(ny - 1, 1),)),
            DMA((max(ny - 1, 1),)),
            DMA((ns - 1,)),
            DMA((ns - 1,)),
        ],
        compiler_params=params(cid),
        name="gather_seq",
    )(v, aux)


def gather_exp_kernel(ne, subs, v, aux, out, aux_out, lsem, ssem, rsem, sa, ra):
    s, e = lax.axis_index("seq"), lax.axis_index("exp")
    p, right, left = ring_sides(e, ne)
    greet([(s, right), (s, left)])
    own = pltpu.make_async_copy(v, out.at[e], lsem.at[0])
    own_aux = pltpu.make_async_copy(aux, aux_out.at[e], lsem.at[1])
    own.start()
    own_aux.start()
    step = v.shape[0] // (2 * subs)
    sent = {}
    for k in range(ne - 1):
        for u in range(subs):
            for way, to in ((0, right), (1, left)):
                place = (p - k + ne) % ne if way == 0 else (p + k) % ne
                slot = ring_index(place, ne)
                rows = pl.ds((way * subs + u) * step, step)
                if k > 0:
                    sent[k - 1, way, u].wait_recv()
                src = v.at[rows] if k == 0 else out.at[slot, rows]
                sent[k, way, u] = remote(
                    src, out.at[slot, rows], ssem.at[k, way, u], rsem.at[k, way, u], (s, to)
                )
        slot = ring_index((p - k + ne) % ne, ne)
        if k > 0:
            sent[k - 1, 2, 0].wait_recv()
        src = aux if k == 0 else aux_out.at[slot]
        sent[k, 2, 0] = remote(src, aux_out.at[slot], sa.at[k], ra.at[k], (s, right))
    for u in range(subs):
        for way in range(2):
            sent[ne - 2, way, u].wait_recv()
    sent[ne - 2, 2, 0].wait_recv()
    for copy in sent.values():
        copy.wait_send()
    own.wait()
    own_aux.wait()


def gather_exp(v, aux, ne, cid, subs=2):
    return pl.pallas_call(
        functools.partial(gather_exp_kernel, ne, subs),
        out_shape=(
            jax.ShapeDtypeStruct((ne,) + v.shape, v.dtype),
            jax.ShapeDtypeStruct((ne,) + aux.shape, aux.dtype),
        ),
        in_specs=[VMEM, VMEM],
        out_specs=(VMEM, VMEM),
        scratch_shapes=[
            DMA((2,)),
            DMA((ne - 1, 2, subs)),
            DMA((ne - 1, 2, subs)),
            DMA((ne - 1,)),
            DMA((ne - 1,)),
        ],
        compiler_params=params(cid),
        name="gather_exp",
    )(v, aux)


def sum_exp_kernel(ne, subs, count, *refs):
    parts = refs[:count]
    aux = refs[count]
    outs = refs[count + 1 : 2 * count + 1]
    aux_out = refs[2 * count + 1]
    accs = refs[2 * count + 2 : 3 * count + 2]
    lsem, ssem, rsem, sa, ra = refs[3 * count + 2 :]
    s, e = lax.axis_index("seq"), lax.axis_index("exp")
    p, right, left = ring_sides(e, ne)
    greet([(s, (e + t) % ne) for t in range(1, ne)])
    own = pltpu.make_async_copy(aux.at[e], aux_out.at[e], lsem)
    own.start()
    extra = []
    for t in range(1, ne):
        to = (e + t) % ne
        extra.append(remote(aux.at[to], aux_out.at[e], sa.at[t - 1], ra.at[t - 1], (s, to)))
    sent = {}
    for k in range(ne):
        for m in range(count):
            part, out, acc = parts[m], outs[m], accs[m]
            step = part.shape[1] // (2 * subs)
            tile = tile_rows(step)
            for u in range(subs):
                for way, to in ((0, right), (1, left)):
                    place = (p - 1 - k + 2 * ne) % ne if way == 0 else (p + 1 + k) % ne
                    slot = ring_index(place, ne)
                    base = (way * subs + u) * step
                    rows = pl.ds(base, step)
                    if k > 0:
                        sent[k - 1, m, way, u].wait_recv()

                        def join(i, carry):
                            r = pl.ds(pl.multiple_of(base + i * tile, tile), tile)
                            total = acc[k - 1, r, :].astype(F32) + part[slot, r, :].astype(F32)
                            if k < ne - 1:
                                acc[k - 1, r, :] = total.astype(BF)
                            else:
                                out[r, :] = total
                            return carry

                        lax.fori_loop(0, step // tile, join, 0)
                    if k < ne - 1:
                        src = part.at[slot, rows] if k == 0 else acc.at[k - 1, rows]
                        sent[k, m, way, u] = remote(
                            src,
                            acc.at[k, rows],
                            ssem.at[k, m, way, u],
                            rsem.at[k, m, way, u],
                            (s, to),
                        )
    for copy in extra:
        copy.wait_recv()
    for copy in list(sent.values()) + extra:
        copy.wait_send()
    own.wait()


def sum_exp(parts, aux, ne, cid, subs=2):
    count = len(parts)
    return pl.pallas_call(
        functools.partial(sum_exp_kernel, ne, subs, count),
        out_shape=tuple(jax.ShapeDtypeStruct(v.shape[1:], F32) for v in parts)
        + (jax.ShapeDtypeStruct(aux.shape, F32),),
        in_specs=[VMEM] * (count + 1),
        out_specs=(VMEM,) * (count + 1),
        scratch_shapes=[pltpu.VMEM((ne - 1,) + v.shape[1:], BF) for v in parts]
        + [
            DMA,
            DMA((ne - 1, count, 2, subs)),
            DMA((ne - 1, count, 2, subs)),
            DMA((ne - 1,)),
            DMA((ne - 1,)),
        ],
        compiler_params=params(cid),
        name="sum_exp",
    )(*parts, aux)


def sum_weights_kernel(
    ns, ne, gin, gout, out, out_rows, acc, acc_out, fin, ssem, rsem, so, ro, sx, rx
):
    s, e = lax.axis_index("seq"), lax.axis_index("exp")
    p, right, left = ring_sides(e, ne)
    greet([((s + t) % ns, e) for t in range(1, ns)] + [(s, right), (s, left)])
    rows = gin.shape[2]
    tile = tile_rows(rows)
    half = gout.shape[2] // 2
    tile_out = tile_rows(gout.shape[1])
    sent = {}
    last = {}
    for k in range(ne):
        for t in range(ns + 2):
            way = t % 2
            to = right if way == 0 else left
            place = (p - 1 - k + 2 * ne) % ne if way == 0 else (p + 1 + k) % ne
            slot = ring_index(place, ne)
            if t < ns:
                piece = (s + t) % ns
                if k > 0:
                    sent[k - 1, t].wait_recv()

                    def join(i, carry):
                        r = pl.ds(pl.multiple_of(i * tile, tile), tile)
                        total = acc[k - 1, t, r, :].astype(F32) + gin[piece, slot, r, :].astype(
                            F32
                        )
                        if k < ne - 1:
                            acc[k - 1, t, r, :] = total.astype(BF)
                        elif t == 0:
                            out[s, r, :] = total.astype(BF)
                        else:
                            fin[t - 1, r, :] = total.astype(BF)
                        return carry

                    lax.fori_loop(0, rows // tile, join, 0)
                if k < ne - 1:
                    src = gin.at[piece, slot] if k == 0 else acc.at[k - 1, t]
                    sent[k, t] = remote(
                        src, acc.at[k, t], ssem.at[k, t], rsem.at[k, t], (s, to)
                    )
                elif t > 0:
                    last[t] = remote(
                        fin.at[t - 1], out.at[s], sx.at[t - 1], rx.at[t - 1], (piece, e)
                    )
            else:
                part_columns = pl.ds(way * half, half)
                if k > 0:
                    sent[k - 1, t].wait_recv()

                    def join_out(i, carry):
                        r = pl.ds(pl.multiple_of(i * tile_out, tile_out), tile_out)
                        total = acc_out[k - 1, r, part_columns].astype(F32)
                        total = total + gout[slot, r, part_columns].astype(F32)
                        if k < ne - 1:
                            acc_out[k - 1, r, part_columns] = total.astype(BF)
                        else:
                            out_rows[r, part_columns] = total
                        return carry

                    lax.fori_loop(0, gout.shape[1] // tile_out, join_out, 0)
                if k < ne - 1:
                    src = (
                        gout.at[slot, :, part_columns]
                        if k == 0
                        else acc_out.at[k - 1, :, part_columns]
                    )
                    sent[k, t] = remote(
                        src,
                        acc_out.at[k, :, part_columns],
                        so.at[k, way],
                        ro.at[k, way],
                        (s, to),
                    )
    for copy in last.values():
        copy.wait_recv()
    for copy in list(sent.values()) + list(last.values()):
        copy.wait_send()


def sum_weights(gin, gout, ns, ne, cid):
    rows, wide = gin.shape[2:]
    return pl.pallas_call(
        functools.partial(sum_weights_kernel, ns, ne),
        out_shape=(
            jax.ShapeDtypeStruct((ns, rows, wide), BF),
            jax.ShapeDtypeStruct(gout.shape[1:], F32),
        ),
        in_specs=[VMEM, VMEM],
        out_specs=(VMEM, VMEM),
        scratch_shapes=[
            pltpu.VMEM((ne - 1, ns, rows, wide), BF),
            pltpu.VMEM((ne - 1,) + gout.shape[1:], BF),
            pltpu.VMEM((ns - 1, rows, wide), BF),
            DMA((ne - 1, ns)),
            DMA((ne - 1, ns)),
            DMA((ne - 1, 2)),
            DMA((ne - 1, 2)),
            DMA((ns - 1,)),
            DMA((ns - 1,)),
        ],
        compiler_params=params(cid),
        name="sum_weights",
    )(gin, gout)


def matmul_plain(left, right):
    return jnp.dot(left, right, preferred_element_type=F32)


def matmul_rows(left, right):
    return lax.dot_general(left, right, (((0,), (0,)), ((), ())), preferred_element_type=F32)


def matmul_cols(left, right):
    return lax.dot_general(left, right, (((1,), (1,)), ((), ())), preferred_element_type=F32)


def chain_step(carried, pieces):
    decay_end, fresh_one = pieces
    return (decay_end[:, None, None] * carried + fresh_one, carried)


def mixer(
    conv_in, step_raw, gate_z, conv_weight, conv_bias, step_bias, decay_log, skip_gain, group
):
    length, inner = gate_z.shape
    width = conv_weight.shape[0]
    heads = step_bias.shape[0]
    state_dim = (conv_in.shape[1] - inner) // 2
    blocks = length // group
    padded = jnp.concatenate([jnp.zeros((width - 1, conv_in.shape[1]), F32), conv_in], 0)
    mixed = conv_bias + sum(
        (conv_weight[offset] * padded[offset : offset + length] for offset in range(width))
    )
    conv_out = jax.nn.silu(mixed)
    values = conv_out[:, :inner].reshape(blocks, group, heads, inner // heads)
    input_b = conv_out[:, inner : inner + state_dim].reshape(blocks, group, state_dim)
    input_c = conv_out[:, inner + state_dim :].reshape(blocks, group, state_dim)
    steps = jax.nn.softplus(step_raw + step_bias).reshape(blocks, group, heads)
    logs = jnp.cumsum(steps * -jnp.exp(decay_log), axis=1)
    tail = jnp.exp(logs[:, -1:, :] - logs) * steps
    fresh = jnp.einsum("csh,cshp,csn->chpn", tail, values, input_b, precision=PRECISE)
    ends = jnp.exp(logs[:, -1, :])
    _, entries = lax.scan(chain_step, jnp.zeros(fresh.shape[1:], F32), (ends, fresh))
    positions = jnp.arange(group)
    causal = (positions[:, None] >= positions[None, :])[None, None]
    rows = jnp.swapaxes(logs, 1, 2)
    spread = rows[:, :, :, None] - rows[:, :, None, :]
    kernel = jnp.where(causal, jnp.exp(jnp.where(causal, spread, 0.0)), 0.0)
    intersection = jnp.einsum("ctn,csn->cts", input_c, input_b, precision=PRECISE)
    weights = intersection[:, None] * kernel * jnp.swapaxes(steps, 1, 2)[:, :, None, :]
    inner_part = jnp.einsum("chts,cshp->cthp", weights, values, precision=PRECISE)
    carried = (
        jnp.einsum("ctn,chpn->cthp", input_c, entries, precision=PRECISE) * jnp.exp(logs)[..., None]
    )
    scanned = inner_part + carried + skip_gain[None, None, :, None] * values
    return scanned.reshape(length, inner) * jax.nn.silu(gate_z)


def rms_back(value, gain, grad):
    scale = lax.rsqrt(jnp.mean(value * value, -1, keepdims=True) + EPSILON)
    inside = gain * grad
    back = scale * inside - value * scale**3 * jnp.mean(value * inside, -1, keepdims=True)
    return back, jnp.sum(value * scale * grad, 0)


def swiglu_back(a, b, grad):
    sig = jax.nn.sigmoid(a)
    return grad * b * sig * (1 + a * (1 - sig)), grad * a * sig


def on_device(
    tokens,
    routes,
    out_grad,
    norm_mix,
    in_weight,
    step_weight,
    conv_weight,
    conv_bias,
    step_bias,
    decay_log,
    skip_gain,
    norm_gate,
    out_weight,
    norm_ffn,
    router_weight,
    shared_gate,
    shared_up,
    shared_down,
    expert_gate,
    expert_up,
    expert_down,
):
    ns, ne = lax.axis_size("seq"), lax.axis_size("exp")
    s, e = lax.axis_index("seq"), lax.axis_index("exp")
    total = ns * ne
    rows, columns = in_weight.shape
    model = tokens.shape[2]
    length = tokens.shape[1]
    whole = length * ns
    width, channels = conv_weight.shape
    gains = norm_gate.shape[0]
    inner = gains * total
    hw = inner // ns
    heads = step_bias.shape[0]
    local_heads = heads // ns
    state2 = columns - 2 * inner
    experts = router_weight.shape[1]
    local_experts = expert_gate.shape[0]
    place = s * ne + e

    small = jnp.concatenate([conv_weight.reshape(-1), conv_bias, norm_gate])
    small = jnp.pad(small, (0, 16 * rows - small.shape[0])).reshape(rows, 16)
    pack = jnp.concatenate(
        [step_weight, router_weight, norm_mix[:, None], norm_ffn[:, None], small], 1
    )
    at_small = heads + experts + 2
    pack = jnp.pad(pack, ((0, 0), (0, 128 - pack.shape[1])))
    in_blocks, token_blocks = gather_in(in_weight, pack, tokens[0], ns, ne, inner, 0)
    in_local = in_blocks.reshape(model, -1)
    full_pack = in_local[:, 2 * hw + state2 :]
    full_router = full_pack[:, heads : heads + experts]
    full_norm_mix = full_pack[:, heads + experts].astype(F32)
    full_norm_ffn = full_pack[:, heads + experts + 1].astype(F32)
    full_small = full_pack[:, at_small : at_small + 16].reshape(total, 16 * rows).astype(F32)
    full_conv = full_small[:, : (width + 1) * channels].reshape(total, width + 1, channels)
    full_conv = jnp.swapaxes(full_conv, 0, 1).reshape(width + 1, total * channels)
    at_gain = (width + 1) * channels
    full_norm_gate = full_small[:, at_gain : at_gain + gains].reshape(inner)
    local_conv = jnp.concatenate(
        [lax.dynamic_slice_in_dim(full_conv, s * hw, hw, 1), full_conv[:, inner:]], 1
    )
    local_gain = lax.dynamic_slice_in_dim(full_norm_gate, s * hw, hw)
    at_head = s * local_heads
    local_bias = lax.dynamic_slice_in_dim(step_bias, at_head, local_heads)
    local_decay = lax.dynamic_slice_in_dim(decay_log, at_head, local_heads)
    local_skip = lax.dynamic_slice_in_dim(skip_gain, at_head, local_heads)

    out_local = lax.all_gather(out_weight, "exp", axis=0, tiled=True)
    grad_low = out_grad[0]
    grad_all = lax.all_gather(grad_low, "exp", axis=0, tiled=True)
    hidden_rows = shared_down.shape[0]

    def by_owner(weight):
        split = weight.reshape(rows, ns, ne, hidden_rows)
        return jnp.transpose(split, (2, 0, 1, 3)).reshape(ne, rows, ns * hidden_rows)

    shared_two = jnp.concatenate([by_owner(shared_gate), by_owner(shared_up)], -1)
    shared_two = lax.all_to_all(shared_two, "exp", split_axis=0, concat_axis=0, tiled=True)
    shared_two = lax.all_gather(shared_two, "seq", axis=0, tiled=True)
    shared_two = shared_two.reshape(model, 2 * ns * hidden_rows)
    local_gate, local_up = shared_two[:, : ns * hidden_rows], shared_two[:, ns * hidden_rows :]
    local_down = lax.all_gather(shared_down, "seq", axis=0, tiled=True)

    token_rows = tokens[0].astype(F32)
    sequence = token_blocks.reshape(whole, model).astype(F32)
    scale_one = lax.rsqrt(jnp.mean(sequence * sequence, -1, keepdims=True) + EPSILON)
    lowered = (sequence * scale_one * full_norm_mix).astype(BF)
    projected = matmul_plain(lowered, in_local)
    gate_z = projected[:, :hw]
    conv_in = projected[:, hw : 2 * hw + state2]
    step_all = projected[:, 2 * hw + state2 : 2 * hw + state2 + heads]
    step_raw = lax.dynamic_slice_in_dim(step_all, at_head, local_heads, 1)
    gated, mixer_pull = jax.vjp(
        functools.partial(mixer, group=GROUP),
        conv_in,
        step_raw,
        gate_z,
        local_conv[:width],
        local_conv[width],
        local_bias,
        local_decay,
        local_skip,
    )
    out_part = matmul_plain((gated * local_gain).astype(BF), out_local).astype(BF)
    squares = jnp.sum(gated * gated, -1).reshape(ns, 1, length)
    mixed_raw, squares = sum_seq(
        out_part.reshape(ns, length, model), jnp.broadcast_to(squares, (ns, 8, length)), ns, 1
    )
    scale_gate = lax.rsqrt(squares[0] / inner + EPSILON)
    mixer_out = mixed_raw * scale_gate[:, None]
    resid = token_rows + mixer_out
    scale_two = lax.rsqrt(jnp.mean(resid * resid, -1, keepdims=True) + EPSILON)
    ffn_in = (resid * scale_two * full_norm_ffn).astype(BF)

    logits = matmul_plain(ffn_in, full_router)
    named = jnp.any(
        routes[0][:, :, None] == jnp.arange(experts, dtype=jnp.int32)[None, None, :], 1
    )
    top = jnp.max(jnp.where(named, logits, -jnp.inf), -1, keepdims=True)
    raised = jnp.where(named, jnp.exp(jnp.where(named, logits - top, 0.0)), 0.0)
    gates = (raised / jnp.sum(raised, -1, keepdims=True)).T

    ffn_all, gates_all = gather_exp(ffn_in, gates, ne, 2)
    ffn_all = ffn_all.reshape(ne * length, model)
    local_gates = lax.dynamic_slice_in_dim(gates_all, e * local_experts, local_experts, 1)
    out_total, back_total = 0.0, 0.0
    gate_grads, expert_sums = [], []
    for j in range(local_experts + 1):
        if j < local_experts:
            weight_gate, weight_up, weight_down = expert_gate[j], expert_up[j], expert_down[j]
            gate = local_gates[:, j].reshape(ne * length, 1)
        else:
            weight_gate, weight_up, weight_down = local_gate, local_up, local_down
            gate = 1.0
        part_a = matmul_plain(ffn_all, weight_gate)
        part_b = matmul_plain(ffn_all, weight_up)
        hidden_grad = matmul_cols(grad_all, weight_down)
        act = jax.nn.silu(part_a) * part_b
        hidden = (gate * act).astype(BF)
        gate_grads.append(jnp.sum(act * hidden_grad, -1))
        grad_a, grad_b = swiglu_back(part_a, part_b, gate * hidden_grad)
        grad_a, grad_b = grad_a.astype(BF), grad_b.astype(BF)
        out_total = out_total + matmul_plain(hidden, weight_down)
        back_total = (
            back_total + matmul_cols(grad_a, weight_gate) + matmul_cols(grad_b, weight_up)
        )
        expert_sums.append(
            (
                matmul_rows(ffn_all, grad_a).astype(BF),
                matmul_rows(ffn_all, grad_b).astype(BF),
                matmul_rows(hidden, grad_all).astype(BF),
            )
        )
    gate_grads = jnp.stack(gate_grads[:local_experts]).reshape(local_experts, ne, length)
    gate_grads = jnp.pad(
        jnp.swapaxes(gate_grads, 0, 1), ((0, 0), (0, 8 - local_experts), (0, 0))
    )
    back_sum, ffn_out, gate_grads = sum_exp(
        [
            back_total.astype(BF).reshape(ne, length, model),
            out_total.astype(BF).reshape(ne, length, model),
        ],
        gate_grads,
        ne,
        3,
    )
    gate_grads = gate_grads[:, :local_experts].reshape(experts, length)
    result = (resid + ffn_out).astype(BF)
    stat_terms = jnp.stack(
        [jnp.sum(resid * resid), jnp.sum(mixer_out * mixer_out), jnp.sum(ffn_out * ffn_out)]
    )
    expert_parts = []
    for which in range(3):
        both = jnp.stack([expert_sums[j][which] for j in range(local_experts)])
        if which < 2:
            both = both.reshape(local_experts, ns, model // ns, -1)
            both = jnp.swapaxes(both, 0, 1)
        else:
            both = both.reshape(local_experts, -1, ns, model // ns)
            both = jnp.transpose(both, (2, 0, 1, 3))
        expert_parts.append(
            lax.psum_scatter(both, "seq", scatter_dimension=0, tiled=False).astype(F32)
        )
    shared_parts = jnp.concatenate(
        [expert_sums[local_experts][0], expert_sums[local_experts][1]], 1
    )
    shared_parts = lax.psum_scatter(shared_parts, "seq", scatter_dimension=0, tiled=True)
    shared_parts = lax.all_to_all(
        shared_parts.reshape(ne, rows, -1), "exp", split_axis=0, concat_axis=0, tiled=True
    ).astype(F32)

    def to_rows(piece):
        piece = piece.reshape(ne, rows, ns, hidden_rows)
        return jnp.transpose(piece, (1, 2, 0, 3)).reshape(rows, total * hidden_rows)

    grad_shared_gate = to_rows(shared_parts[:, :, : ns * hidden_rows])
    grad_shared_up = to_rows(shared_parts[:, :, ns * hidden_rows :])
    grad_shared_down = lax.psum_scatter(
        expert_sums[local_experts][2], "seq", scatter_dimension=0, tiled=True
    ).astype(F32)

    picked_grad = gates * (gate_grads - jnp.sum(gates * gate_grads, 0, keepdims=True))
    logit_grad = picked_grad.T.astype(BF)
    grad_router = matmul_rows(ffn_in, logit_grad)
    ffn_in_grad = matmul_cols(logit_grad, full_router) + back_sum
    resid_norm_grad, grad_norm_ffn = rms_back(resid, full_norm_ffn, ffn_in_grad)
    resid_grad = grad_low.astype(F32) + resid_norm_grad
    resid_low = resid_grad.astype(BF)
    inside = jnp.sum(resid_low.astype(F32) * mixer_out, -1) / (scale_gate * inner)
    scales = jnp.concatenate(
        [scale_gate[None], inside[None], jnp.zeros((6, length), F32)], 0
    )

    resid_all, scales = gather_seq(resid_low, scales, ns, 4)
    resid_all = resid_all.reshape(whole, model)
    scale_all = scales[:, 0].reshape(whole, 1)
    inside_all = scales[:, 1].reshape(whole, 1)
    grad_out = matmul_rows((gated * local_gain * scale_all).astype(BF), resid_all).astype(BF)
    normed_grad = matmul_cols(resid_all, out_local)
    gated_grad = scale_all * (local_gain * normed_grad) - gated * scale_all**3 * inside_all
    grad_gain = jnp.sum(gated * scale_all * normed_grad, 0)
    (
        conv_in_grad,
        step_raw_grad,
        gate_z_grad,
        grad_conv,
        grad_conv_bias,
        grad_step_bias,
        grad_decay,
        grad_skip,
    ) = mixer_pull(gated_grad)
    step_wide = lax.dynamic_update_slice(
        jnp.zeros((whole, 128), BF), step_raw_grad.astype(BF), (0, at_head)
    )
    projected_grad = jnp.concatenate(
        [gate_z_grad.astype(BF), conv_in_grad.astype(BF), step_wide], 1
    )
    lowered_part = matmul_cols(projected_grad, in_local).astype(BF)
    lowered_grad, _ = sum_seq(
        lowered_part.reshape(ns, length, model), jnp.zeros((ns, 8, length), F32), ns, 5
    )
    tokens_norm_grad, grad_norm_mix = rms_back(token_rows, full_norm_mix, lowered_grad)
    tokens_grad = (resid_grad + tokens_norm_grad).astype(BF)

    conv_grads = jnp.concatenate([grad_conv, grad_conv_bias[None]], 0)
    wide = jnp.zeros((width + 1, total * channels), F32)
    wide = lax.dynamic_update_slice(wide, conv_grads[:, :hw], (0, s * hw))
    wide = lax.dynamic_update_slice(wide, conv_grads[:, hw:], (0, inner))
    wide_gain = lax.dynamic_update_slice(jnp.zeros((inner,), F32), grad_gain, (s * hw,))
    wide_heads = lax.dynamic_update_slice(
        jnp.zeros((3, heads), F32),
        jnp.stack([grad_step_bias, grad_decay, grad_skip]),
        (0, at_head),
    )
    sums = lax.psum(
        (wide, wide_gain, wide_heads, grad_router, grad_norm_mix, grad_norm_ffn, stat_terms),
        ("seq", "exp"),
    )
    wide, wide_gain, wide_heads, grad_router, grad_norm_mix, grad_norm_ffn, stat_terms = sums
    conv_grads = lax.dynamic_slice_in_dim(wide, place * channels, channels, 1)

    grad_in = matmul_rows(lowered, projected_grad).astype(BF)
    pieces, grad_out = sum_weights(
        grad_in.reshape(ns, ne, rows, -1),
        grad_out.reshape(ne, hw // ne, model),
        ns,
        ne,
        6,
    )
    pieces = pieces.astype(F32)
    grad_in = jnp.concatenate(
        [
            jnp.swapaxes(pieces[:, :, :hw], 0, 1).reshape(rows, inner),
            jnp.swapaxes(pieces[:, :, hw : 2 * hw], 0, 1).reshape(rows, inner),
            jnp.sum(pieces[:, :, 2 * hw : 2 * hw + state2], 0),
        ],
        1,
    )
    grad_step = jnp.sum(pieces[:, :, 2 * hw + state2 : 2 * hw + state2 + heads], 0)
    return (
        result[None],
        tokens_grad[None],
        lax.dynamic_slice_in_dim(grad_norm_mix, place * rows, rows),
        grad_in,
        grad_step,
        conv_grads[:width],
        conv_grads[width],
        wide_heads[0],
        wide_heads[1],
        wide_heads[2],
        lax.dynamic_slice_in_dim(wide_gain, place * gains, gains),
        grad_out,
        lax.dynamic_slice_in_dim(grad_norm_ffn, place * rows, rows),
        lax.dynamic_slice_in_dim(grad_router, place * rows, rows),
        grad_shared_gate,
        grad_shared_up,
        grad_shared_down,
        expert_parts[0],
        expert_parts[1],
        expert_parts[2],
        stat_terms / (total * length * model),
    )


def solution(mesh):
    both = ("seq", "exp")
    return jax.shard_map(
        on_device,
        mesh=mesh,
        in_specs=(
            P("exp", "seq", None),
            P("exp", "seq", None),
            P("exp", "seq", None),
            P(both),
            P(both, None),
            P(both, None),
            P(None, both),
            P(both),
            P(),
            P(),
            P(),
            P(both),
            P(both, None),
            P(both),
            P(both, None),
            P(both, None),
            P(both, None),
            P(both, None),
            P("exp", None, None),
            P("exp", None, None),
            P("exp", None, None),
        ),
        out_specs=(
            P("exp", "seq", None),
            P("exp", "seq", None),
            P(both),
            P(both, None),
            P(both, None),
            P(None, both),
            P(both),
            P(),
            P(),
            P(),
            P(both),
            P(both, None),
            P(both),
            P(both, None),
            P(both, None),
            P(both, None),
            P(both, None),
            P("exp", "seq", None),
            P("exp", "seq", None),
            P("exp", None, "seq"),
            P(),
        ),
        check_vma=False,
    )
```

```python
import functools

import jax
import jax.numpy as jnp
from jax import lax
from jax.experimental import pallas as pl
from jax.experimental.pallas import tpu as pltpu
from jax.sharding import PartitionSpec as P

GROUP = 128
EPSILON = 1e-05
PRECISE = lax.Precision.HIGHEST
MESH = pl.DeviceIdType.MESH
BF = jnp.bfloat16
F32 = jnp.float32
ANY = pl.BlockSpec(memory_space=pl.ANY)
VMEM = pl.BlockSpec(memory_space=pltpu.VMEM)
DMA = pltpu.SemaphoreType.DMA


def ring_place(e, n):
    odd = e % 2
    return (1 - odd) * (e // 2) + odd * (n - 1 - e // 2)


def ring_index(p, n):
    back = p // (n // 2)
    return (1 - back) * (2 * p) + back * (2 * (n - 1 - p) + 1)


def ring_sides(e, n):
    p = ring_place(e, n)
    return p, ring_index((p + 1) % n, n), ring_index((p + n - 1) % n, n)


def greet(partners):
    barrier = pltpu.get_barrier_semaphore()
    for partner in partners:
        pl.semaphore_signal(barrier, inc=1, device_id=partner, device_id_type=MESH)
    pl.semaphore_wait(barrier, len(partners))


def remote(src, dst, send, recv, device):
    copy = pltpu.make_async_remote_copy(
        src_ref=src,
        dst_ref=dst,
        send_sem=send,
        recv_sem=recv,
        device_id=device,
        device_id_type=MESH,
    )
    copy.start()
    return copy


def params(cid, mib=48):
    return pltpu.CompilerParams(
        collective_id=cid, has_side_effects=True, vmem_limit_bytes=mib << 20
    )


def tile_rows(rows, most=16):
    return most if rows % most == 0 else rows


def gather_in_kernel(
    ns,
    ne,
    hw,
    inner,
    in_ref,
    pack_ref,
    tok_ref,
    out_ref,
    two_ref,
    down_ref,
    w_ref,
    x_ref,
    o_ref,
    shared_ref,
    sd_ref,
    lsem,
    ssem0,
    rsem0,
    ssem,
    rsem,
    sa,
    ra,
    sb,
    rb,
):
    s, e = lax.axis_index("seq"), lax.axis_index("exp")
    p, right, left = ring_sides(e, ne)
    width = in_ref.shape[1] - 2 * inner
    half = out_ref.shape[1] // 2
    parts = (
        (lambda to: in_ref.at[:, pl.ds(pl.multiple_of(to * hw, 128), hw)], 0, hw),
        (lambda to: in_ref.at[:, pl.ds(pl.multiple_of(inner + to * hw, 128), hw)], hw, hw),
        (lambda to: in_ref.at[:, pl.ds(2 * inner, width)], 2 * hw, width),
        (lambda to: pack_ref, 2 * hw + width, pack_ref.shape[1]),
    )
    greet([((s + t) % ns, e) for t in range(1, ns)] + [(s, (e + t) % ne) for t in range(1, ne)])
    own = []
    for i, (piece, start, size) in enumerate(parts):
        own.append(
            pltpu.make_async_copy(piece(s), w_ref.at[s, e, :, pl.ds(start, size)], lsem.at[i])
        )
    own.append(pltpu.make_async_copy(out_ref, o_ref.at[e], lsem.at[4]))
    own.append(pltpu.make_async_copy(two_ref.at[e], shared_ref.at[s, e], lsem.at[5]))
    own.append(pltpu.make_async_copy(tok_ref, x_ref.at[s], lsem.at[6]))
    own.append(pltpu.make_async_copy(down_ref, sd_ref.at[s], lsem.at[7]))
    for copy in own:
        copy.start()
    first = {}
    for t in range(1, ns):
        to = (s + t) % ns
        for i, (piece, start, size) in enumerate(parts):
            first[t, i] = remote(
                piece(to),
                w_ref.at[s, e, :, pl.ds(start, size)],
                ssem0.at[t - 1, i],
                rsem0.at[t - 1, i],
                (to, e),
            )
    for copy in own:
        copy.wait()
    sent = {}
    across = {}
    along = {}
    for k in range(ne - 1):
        for t in range(ns + 2):
            way = t % 2
            to = (s, right if way == 0 else left)
            place = (p - k + ne) % ne if way == 0 else (p + k) % ne
            slot = ring_index(place, ne)
            if k > 0:
                sent[k - 1, t].wait_recv()
            elif 0 < t < ns:
                for i in range(len(parts)):
                    first[t, i].wait_recv()
            if t < ns:
                block = w_ref.at[(s + ns - t) % ns, slot]
            else:
                block = o_ref.at[slot, :, pl.ds(way * half, half)]
            sent[k, t] = remote(block, block, ssem.at[k, t], rsem.at[k, t], to)
        if k == 0:
            for t in range(1, ns):
                to = ((s + t) % ns, e)
                first[t, 4] = remote(
                    tok_ref, x_ref.at[s], ssem0.at[t - 1, 4], rsem0.at[t - 1, 4], to
                )
                first[t, 5] = remote(
                    down_ref, sd_ref.at[s], ssem0.at[t - 1, 5], rsem0.at[t - 1, 5], to
                )
            for t in range(1, ne):
                to = (e + t) % ne
                across[t] = remote(
                    two_ref.at[to], shared_ref.at[s, e], sa.at[t - 1], ra.at[t - 1], (s, to)
                )
        if k == 2:
            for t in range(1, ne):
                across[t].wait_recv()
            for t in range(1, ns):
                along[t] = remote(
                    shared_ref.at[s], shared_ref.at[s], sb.at[t - 1], rb.at[t - 1], ((s + t) % ns, e)
                )
    for t in range(ns + 2):
        sent[ne - 2, t].wait_recv()
    for t in range(1, ns):
        first[t, 4].wait_recv()
        first[t, 5].wait_recv()
        along[t].wait_recv()
    for group in (first, sent, across, along):
        for copy in group.values():
            copy.wait_send()


def gather_in(in_weight, pack, tokens, out_weight, shared_two, shared_down, ns, ne, inner, cid):
    rows, columns = in_weight.shape
    hw = inner // ns
    wide = 2 * hw + columns - 2 * inner + pack.shape[1]
    return pl.pallas_call(
        functools.partial(gather_in_kernel, ns, ne, hw, inner),
        out_shape=(
            jax.ShapeDtypeStruct((ns, ne, rows, wide), BF),
            jax.ShapeDtypeStruct((ns,) + tokens.shape, BF),
            jax.ShapeDtypeStruct((ne,) + out_weight.shape, BF),
            jax.ShapeDtypeStruct((ns,) + shared_two.shape, BF),
            jax.ShapeDtypeStruct((ns,) + shared_down.shape, BF),
        ),
        in_specs=[ANY] * 6,
        out_specs=(ANY,) * 5,
        scratch_shapes=[
            DMA((8,)),
            DMA((ns - 1, 6)),
            DMA((ns - 1, 6)),
            DMA((ne - 1, ns + 2)),
            DMA((ne - 1, ns + 2)),
            DMA((ne - 1,)),
            DMA((ne - 1,)),
            DMA((ns - 1,)),
            DMA((ns - 1,)),
        ],
        compiler_params=params(cid, 8),
        name="gather_in",
    )(in_weight, pack, tokens, out_weight, shared_two, shared_down)


class SeqSum:
    def __init__(self, ns, subs, part, aux, one, two, aux_in, s1, r1, s2, r2, sa, ra):
        self.s, self.e = lax.axis_index("seq"), lax.axis_index("exp")
        self.ns, self.ny, self.subs = ns, ns // 2, subs
        self.y, self.c = self.s // 2, self.s % 2
        self.part, self.aux, self.one, self.two, self.aux_in = part, aux, one, two, aux_in
        self.sems = (s1, r1, s2, r2, sa, ra)
        self.step = part.shape[1] // subs
        self.tile = tile_rows(self.step)
        self.first, self.second, self.extra = {}, {}, []

    @staticmethod
    def scratch(ns, subs, rows, width, aux_shape):
        ny = ns // 2
        return [
            pltpu.VMEM((ny, rows, width), BF),
            pltpu.VMEM((max(ny - 1, 1), rows, width), BF),
            pltpu.VMEM((ns - 1,) + aux_shape, F32),
            DMA((ny, subs)),
            DMA((ny, subs)),
            DMA((max(ny - 1, 1), subs)),
            DMA((max(ny - 1, 1), subs)),
            DMA((ns - 1,)),
            DMA((ns - 1,)),
        ]

    def rows(self, u):
        return pl.ds(u * self.step, self.step)

    def begin(self, fill=None):
        s1, r1, s2, r2, sa, ra = self.sems
        mate = (2 * self.y + 1 - self.c, self.e)
        for t in range(1, self.ns):
            to = (self.s + t) % self.ns
            self.extra.append(
                remote(
                    self.aux.at[to], self.aux_in.at[t - 1], sa.at[t - 1], ra.at[t - 1], (to, self.e)
                )
            )
        for j in list(range(1, self.ny)) + [0]:
            block = 2 * ((self.y + j) % self.ny) + 1 - self.c
            if fill is not None:
                fill(block)
            for u in range(self.subs):
                self.first[j, u] = remote(
                    self.part.at[block, self.rows(u)],
                    self.one.at[j, self.rows(u)],
                    s1.at[j, u],
                    r1.at[j, u],
                    mate,
                )
        if fill is not None:
            for j in list(range(1, self.ny)) + [0]:
                fill(2 * ((self.y + j) % self.ny) + self.c)

    def middle(self):
        s1, r1, s2, r2, sa, ra = self.sems
        for j in range(1, self.ny):
            to = 2 * ((self.y + j) % self.ny) + self.c
            for u in range(self.subs):
                self.first[j, u].wait_recv()

                def join(i, carry):
                    r = pl.ds(pl.multiple_of(u * self.step + i * self.tile, self.tile), self.tile)
                    total = self.one[j, r, :].astype(F32) + self.part[to, r, :].astype(F32)
                    self.one[j, r, :] = total.astype(BF)
                    return carry

                lax.fori_loop(0, self.step // self.tile, join, 0)
                self.second[j, u] = remote(
                    self.one.at[j, self.rows(u)],
                    self.two.at[j - 1, self.rows(u)],
                    s2.at[j - 1, u],
                    r2.at[j - 1, u],
                    (to, self.e),
                )

    def finish(self, out, aux_out):
        for u in range(self.subs):
            self.first[0, u].wait_recv()
            for j in range(1, self.ny):
                self.second[j, u].wait_recv()

            def close(i, carry):
                r = pl.ds(pl.multiple_of(u * self.step + i * self.tile, self.tile), self.tile)
                total = self.one[0, r, :].astype(F32) + self.part[self.s, r, :].astype(F32)
                for j in range(1, self.ny):
                    total = total + self.two[j - 1, r, :].astype(F32)
                out[r, :] = total
                return carry

            lax.fori_loop(0, self.step // self.tile, close, 0)
        total = self.aux[self.s]
        for t in range(1, self.ns):
            self.extra[t - 1].wait_recv()
            total = total + self.aux_in[t - 1]
        aux_out[...] = total

    def drain(self):
        for copy in list(self.first.values()) + list(self.second.values()) + self.extra:
            copy.wait_send()


def sum_seq_kernel(ns, subs, part, aux, out, aux_out, *scratch):
    s, e = lax.axis_index("seq"), lax.axis_index("exp")
    greet([((s + t) % ns, e) for t in range(1, ns)])
    job = SeqSum(ns, subs, part, aux, *scratch)
    job.begin()
    job.middle()
    job.finish(out, aux_out)
    job.drain()


def sum_seq(part, aux, ns, cid, subs=2):
    rows, width = part.shape[1:]
    return pl.pallas_call(
        functools.partial(sum_seq_kernel, ns, subs),
        out_shape=(
            jax.ShapeDtypeStruct((rows, width), F32),
            jax.ShapeDtypeStruct(aux.shape[1:], F32),
        ),
        in_specs=[VMEM, VMEM],
        out_specs=(VMEM, VMEM),
        scratch_shapes=SeqSum.scratch(ns, subs, rows, width, aux.shape[1:]),
        compiler_params=params(cid),
        name="sum_seq",
    )(part, aux)


class RingGather:
    def __init__(self, ne, v, out, lsem, ssem, rsem):
        self.s, self.e = lax.axis_index("seq"), lax.axis_index("exp")
        self.ne, self.v, self.out = ne, v, out
        self.p, self.right, self.left = ring_sides(self.e, ne)
        self.ssem, self.rsem = ssem, rsem
        self.subs = ssem.shape[2]
        self.step_rows = v.shape[0] // (2 * self.subs)
        self.own = pltpu.make_async_copy(v, out.at[self.e], lsem)

    @staticmethod
    def scratch(ne, subs):
        return [DMA, DMA((ne - 1, 2, subs)), DMA((ne - 1, 2, subs))]

    def copy(self, k, way, u, src=None):
        place = (self.p - k + self.ne) % self.ne if way == 0 else (self.p + k) % self.ne
        slot = ring_index(place, self.ne)
        rows = pl.ds((way * self.subs + u) * self.step_rows, self.step_rows)
        block = self.out.at[slot, rows]
        return pltpu.make_async_remote_copy(
            src_ref=block if src is None else src.at[rows],
            dst_ref=block,
            send_sem=self.ssem.at[k, way, u],
            recv_sem=self.rsem.at[k, way, u],
            device_id=(self.s, self.right if way == 0 else self.left),
            device_id_type=MESH,
        )

    def begin(self):
        self.own.start()
        for u in range(self.subs):
            for way in range(2):
                self.copy(0, way, u, self.v).start()

    def step(self, k):
        for u in range(self.subs):
            for way in range(2):
                self.copy(k - 1, way, u).wait_recv()
                self.copy(k, way, u).start()

    def finish(self):
        for u in range(self.subs):
            for way in range(2):
                self.copy(self.ne - 2, way, u).wait_recv()
        for k in range(self.ne - 1):
            for u in range(self.subs):
                for way in range(2):
                    self.copy(k, way, u).wait_send()
        self.own.wait()


def gather_seq_kernel(ns, v, aux, out, aux_out, lsem, s1, r1, s2, r2, sa, ra):
    s, e = lax.axis_index("seq"), lax.axis_index("exp")
    ny = ns // 2
    y, c = s // 2, s % 2
    mate = (2 * y + 1 - c, e)
    greet([((s + t) % ns, e) for t in range(1, ns)])
    own = pltpu.make_async_copy(v, out.at[s], lsem.at[0])
    own_aux = pltpu.make_async_copy(aux, aux_out.at[s], lsem.at[1])
    first = {}
    for j in range(1, ny):
        to = (2 * ((y + j) % ny) + c, e)
        first[j] = remote(v, out.at[s], s1.at[j], r1.at[j], to)
    first[0] = remote(v, out.at[s], s1.at[0], r1.at[0], mate)
    extra = []
    for t in range(1, ns):
        extra.append(
            remote(aux, aux_out.at[s], sa.at[t - 1], ra.at[t - 1], ((s + t) % ns, e))
        )
    own.start()
    own_aux.start()
    second = []
    for j in range(1, ny):
        first[j].wait_recv()
        block = out.at[2 * ((y + ny - j) % ny) + c]
        second.append(remote(block, block, s2.at[j - 1], r2.at[j - 1], mate))
    first[0].wait_recv()
    for copy in second + extra:
        copy.wait_recv()
    for copy in list(first.values()) + second + extra:
        copy.wait_send()
    own.wait()
    own_aux.wait()


def gather_seq(v, aux, ns, cid):
    ny = ns // 2
    return pl.pallas_call(
        functools.partial(gather_seq_kernel, ns),
        out_shape=(
            jax.ShapeDtypeStruct((ns,) + v.shape, v.dtype),
            jax.ShapeDtypeStruct((ns,) + aux.shape, aux.dtype),
        ),
        in_specs=[VMEM, VMEM],
        out_specs=(VMEM, VMEM),
        scratch_shapes=[
            DMA((2,)),
            DMA((ny,)),
            DMA((ny,)),
            DMA((max(ny - 1, 1),)),
            DMA((max(ny - 1, 1),)),
            DMA((ns - 1,)),
            DMA((ns - 1,)),
        ],
        compiler_params=params(cid),
        name="gather_seq",
    )(v, aux)


def gather_exp_kernel(ne, subs, v, aux, out, aux_out, lsem, ssem, rsem, sa, ra):
    s, e = lax.axis_index("seq"), lax.axis_index("exp")
    p, right, left = ring_sides(e, ne)
    greet([(s, right), (s, left)])
    own = pltpu.make_async_copy(v, out.at[e], lsem.at[0])
    own_aux = pltpu.make_async_copy(aux, aux_out.at[e], lsem.at[1])
    own.start()
    own_aux.start()
    step = v.shape[0] // (2 * subs)
    sent = {}
    for k in range(ne - 1):
        for u in range(subs):
            for way, to in ((0, right), (1, left)):
                place = (p - k + ne) % ne if way == 0 else (p + k) % ne
                slot = ring_index(place, ne)
                rows = pl.ds((way * subs + u) * step, step)
                if k > 0:
                    sent[k - 1, way, u].wait_recv()
                src = v.at[rows] if k == 0 else out.at[slot, rows]
                sent[k, way, u] = remote(
                    src, out.at[slot, rows], ssem.at[k, way, u], rsem.at[k, way, u], (s, to)
                )
        slot = ring_index((p - k + ne) % ne, ne)
        if k > 0:
            sent[k - 1, 2, 0].wait_recv()
        src = aux if k == 0 else aux_out.at[slot]
        sent[k, 2, 0] = remote(src, aux_out.at[slot], sa.at[k], ra.at[k], (s, right))
    for u in range(subs):
        for way in range(2):
            sent[ne - 2, way, u].wait_recv()
    sent[ne - 2, 2, 0].wait_recv()
    for copy in sent.values():
        copy.wait_send()
    own.wait()
    own_aux.wait()


def gather_exp(v, aux, ne, cid, subs=2):
    return pl.pallas_call(
        functools.partial(gather_exp_kernel, ne, subs),
        out_shape=(
            jax.ShapeDtypeStruct((ne,) + v.shape, v.dtype),
            jax.ShapeDtypeStruct((ne,) + aux.shape, aux.dtype),
        ),
        in_specs=[VMEM, VMEM],
        out_specs=(VMEM, VMEM),
        scratch_shapes=[
            DMA((2,)),
            DMA((ne - 1, 2, subs)),
            DMA((ne - 1, 2, subs)),
            DMA((ne - 1,)),
            DMA((ne - 1,)),
        ],
        compiler_params=params(cid),
        name="gather_exp",
    )(v, aux)


def sum_exp_kernel(ne, subs, count, *refs):
    parts = refs[:count]
    aux = refs[count]
    outs = refs[count + 1 : 2 * count + 1]
    aux_out = refs[2 * count + 1]
    accs = refs[2 * count + 2 : 3 * count + 2]
    lsem, ssem, rsem, sa, ra = refs[3 * count + 2 :]
    s, e = lax.axis_index("seq"), lax.axis_index("exp")
    p, right, left = ring_sides(e, ne)
    greet([(s, (e + t) % ne) for t in range(1, ne)])
    own = pltpu.make_async_copy(aux.at[e], aux_out.at[e], lsem)
    own.start()
    extra = []
    for t in range(1, ne):
        to = (e + t) % ne
        extra.append(remote(aux.at[to], aux_out.at[e], sa.at[t - 1], ra.at[t - 1], (s, to)))
    sent = {}
    for k in range(ne):
        for m in range(count):
            part, out, acc = parts[m], outs[m], accs[m]
            step = part.shape[1] // (2 * subs)
            tile = tile_rows(step)
            for u in range(subs):
                for way, to in ((0, right), (1, left)):
                    place = (p - 1 - k + 2 * ne) % ne if way == 0 else (p + 1 + k) % ne
                    slot = ring_index(place, ne)
                    base = (way * subs + u) * step
                    rows = pl.ds(base, step)
                    if k > 0:
                        sent[k - 1, m, way, u].wait_recv()

                        def join(i, carry):
                            r = pl.ds(pl.multiple_of(base + i * tile, tile), tile)
                            total = acc[k - 1, r, :].astype(F32) + part[slot, r, :].astype(F32)
                            if k < ne - 1:
                                acc[k - 1, r, :] = total.astype(BF)
                            else:
                                out[r, :] = total
                            return carry

                        lax.fori_loop(0, step // tile, join, 0)
                    if k < ne - 1:
                        src = part.at[slot, rows] if k == 0 else acc.at[k - 1, rows]
                        sent[k, m, way, u] = remote(
                            src,
                            acc.at[k, rows],
                            ssem.at[k, m, way, u],
                            rsem.at[k, m, way, u],
                            (s, to),
                        )
    for copy in extra:
        copy.wait_recv()
    for copy in list(sent.values()) + extra:
        copy.wait_send()
    own.wait()


def sum_exp(parts, aux, ne, cid, subs=2):
    count = len(parts)
    return pl.pallas_call(
        functools.partial(sum_exp_kernel, ne, subs, count),
        out_shape=tuple(jax.ShapeDtypeStruct(v.shape[1:], F32) for v in parts)
        + (jax.ShapeDtypeStruct(aux.shape, F32),),
        in_specs=[VMEM] * (count + 1),
        out_specs=(VMEM,) * (count + 1),
        scratch_shapes=[pltpu.VMEM((ne - 1,) + v.shape[1:], BF) for v in parts]
        + [
            DMA,
            DMA((ne - 1, count, 2, subs)),
            DMA((ne - 1, count, 2, subs)),
            DMA((ne - 1,)),
            DMA((ne - 1,)),
        ],
        compiler_params=params(cid),
        name="sum_exp",
    )(*parts, aux)


def sum_weights_kernel(
    ns, ne, gin, gout, out, out_rows, acc, acc_out, fin, ssem, rsem, so, ro, sx, rx
):
    s, e = lax.axis_index("seq"), lax.axis_index("exp")
    p, right, left = ring_sides(e, ne)
    greet([((s + t) % ns, e) for t in range(1, ns)] + [(s, right), (s, left)])
    rows = gin.shape[2]
    tile = tile_rows(rows)
    half = gout.shape[2] // 2
    tile_out = tile_rows(gout.shape[1])
    sent = {}
    last = {}
    for k in range(ne):
        for t in range(ns + 2):
            way = t % 2
            to = right if way == 0 else left
            place = (p - 1 - k + 2 * ne) % ne if way == 0 else (p + 1 + k) % ne
            slot = ring_index(place, ne)
            if t < ns:
                piece = (s + t) % ns
                if k > 0:
                    sent[k - 1, t].wait_recv()

                    def join(i, carry):
                        r = pl.ds(pl.multiple_of(i * tile, tile), tile)
                        total = acc[k - 1, t, r, :].astype(F32) + gin[piece, slot, r, :].astype(
                            F32
                        )
                        if k < ne - 1:
                            acc[k - 1, t, r, :] = total.astype(BF)
                        elif t == 0:
                            out[s, r, :] = total.astype(BF)
                        else:
                            fin[t - 1, r, :] = total.astype(BF)
                        return carry

                    lax.fori_loop(0, rows // tile, join, 0)
                if k < ne - 1:
                    src = gin.at[piece, slot] if k == 0 else acc.at[k - 1, t]
                    sent[k, t] = remote(
                        src, acc.at[k, t], ssem.at[k, t], rsem.at[k, t], (s, to)
                    )
                elif t > 0:
                    last[t] = remote(
                        fin.at[t - 1], out.at[s], sx.at[t - 1], rx.at[t - 1], (piece, e)
                    )
            else:
                part_columns = pl.ds(way * half, half)
                if k > 0:
                    sent[k - 1, t].wait_recv()

                    def join_out(i, carry):
                        r = pl.ds(pl.multiple_of(i * tile_out, tile_out), tile_out)
                        total = acc_out[k - 1, r, part_columns].astype(F32)
                        total = total + gout[slot, r, part_columns].astype(F32)
                        if k < ne - 1:
                            acc_out[k - 1, r, part_columns] = total.astype(BF)
                        else:
                            out_rows[r, part_columns] = total
                        return carry

                    lax.fori_loop(0, gout.shape[1] // tile_out, join_out, 0)
                if k < ne - 1:
                    src = (
                        gout.at[slot, :, part_columns]
                        if k == 0
                        else acc_out.at[k - 1, :, part_columns]
                    )
                    sent[k, t] = remote(
                        src,
                        acc_out.at[k, :, part_columns],
                        so.at[k, way],
                        ro.at[k, way],
                        (s, to),
                    )
    for copy in last.values():
        copy.wait_recv()
    for copy in list(sent.values()) + list(last.values()):
        copy.wait_send()


def sum_weights(gin, gout, ns, ne, cid):
    rows, wide = gin.shape[2:]
    return pl.pallas_call(
        functools.partial(sum_weights_kernel, ns, ne),
        out_shape=(
            jax.ShapeDtypeStruct((ns, rows, wide), BF),
            jax.ShapeDtypeStruct(gout.shape[1:], F32),
        ),
        in_specs=[VMEM, VMEM],
        out_specs=(VMEM, VMEM),
        scratch_shapes=[
            pltpu.VMEM((ne - 1, ns, rows, wide), BF),
            pltpu.VMEM((ne - 1,) + gout.shape[1:], BF),
            pltpu.VMEM((ns - 1, rows, wide), BF),
            DMA((ne - 1, ns)),
            DMA((ne - 1, ns)),
            DMA((ne - 1, 2)),
            DMA((ne - 1, 2)),
            DMA((ns - 1,)),
            DMA((ns - 1,)),
        ],
        compiler_params=params(cid),
        name="sum_weights",
    )(gin, gout)


def matmul_plain(left, right):
    return jnp.dot(left, right, preferred_element_type=F32)


def matmul_rows(left, right):
    return lax.dot_general(left, right, (((0,), (0,)), ((), ())), preferred_element_type=F32)


def matmul_cols(left, right):
    return lax.dot_general(left, right, (((1,), (1,)), ((), ())), preferred_element_type=F32)


def mm(left, right):
    return jnp.dot(left, right, preferred_element_type=F32)


def mm_t(left, right):
    return lax.dot_general(left, right, (((1,), (1,)), ((), ())), preferred_element_type=F32)


def t_mm(left, right):
    return lax.dot_general(left, right, (((0,), (0,)), ((), ())), preferred_element_type=F32)


def exact(left, right):
    return jnp.dot(left, right, precision=PRECISE, preferred_element_type=F32)


def spread_heads(table, heads, head_dim):
    rows = table.shape[0]
    per = 128 // head_dim
    lane = lax.broadcasted_iota(jnp.int32, (rows, 128), 1)
    tiles = []
    for h in range(0, heads, per):
        tile = jnp.broadcast_to(table[:, h : h + 1], (rows, 128))
        for i in range(1, per):
            other = jnp.broadcast_to(table[:, h + i : h + i + 1], (rows, 128))
            tile = jnp.where(lane >= i * head_dim, other, tile)
        tiles.append(tile)
    return jnp.concatenate(tiles, 1)


def sigmoid(v):
    return 1.0 / (1.0 + jnp.exp(-v))


def softplus(v):
    return jnp.maximum(v, 0.0) + jnp.log1p(jnp.exp(-jnp.abs(v)))


def triangle(flip=False):
    t = lax.broadcasted_iota(jnp.int32, (GROUP, GROUP), 0)
    u = lax.broadcasted_iota(jnp.int32, (GROUP, GROUP), 1)
    return u >= t if flip else t >= u


def step_table(pack, bias, heads, s):
    turned = pltpu.roll(pack, (128 - heads * s) % 128, 1)
    lane = lax.broadcasted_iota(jnp.int32, turned.shape, 1)
    raw = jnp.where(lane < heads, turned + bias, 0.0)
    return raw, jnp.where(lane < heads, softplus(raw), 0.0)


def convolved(ext, table, width):
    mixed = table[width : width + 1]
    for j in range(width):
        mixed = mixed + table[j : j + 1] * ext[8 - width + 1 + j : 8 - width + 1 + j + GROUP]
    return mixed


def with_before(proj_ref, at, columns, first):
    before = proj_ref[pl.ds(pl.multiple_of(jnp.maximum(at - 8, 0), 8), 8), columns]
    before = jnp.where(first, 0.0, before)
    return jnp.concatenate([before, proj_ref[pl.ds(at, GROUP), columns]], 0)


def mix_forward_kernel(
    ns,
    ne,
    hw,
    state2,
    heads,
    width,
    proj_ref,
    table_ref,
    head_ref,
    out_ref,
    grad_ref,
    scan_ref,
    mix_ref,
    entry_ref,
    sum_ref,
    square_out,
    grad_all,
    state,
    low_ref,
    square_ref,
    part_ref,
    *sems,
):
    s, e = lax.axis_index("seq"), lax.axis_index("exp")
    p, right, left = ring_sides(e, ne)
    greet([((s + t) % ns, e) for t in range(1, ns)] + [(s, right), (s, left)])
    ring = RingGather(ne, grad_ref, grad_all, *sems[:3])
    job = SeqSum(ns, 2, part_ref, square_ref, *sems[3:])
    ring.begin()
    blocks = proj_ref.shape[0] // GROUP
    head_dim = hw // heads
    n = state2 // 2
    state[...] = jnp.zeros_like(state)
    lane = lax.broadcasted_iota(jnp.int32, (GROUP, 128), 1)
    table = table_ref[...]
    skip = table[width + 2 : width + 3, :hw]
    gain = table[width + 1 : width + 2, :hw]
    bias, rate = head_ref[0:1, :], head_ref[1:2, :]

    def chunk(c, carry):
        at = pl.multiple_of(c * GROUP, GROUP)
        rows = pl.ds(at, GROUP)
        causal = triangle()
        ext = with_before(proj_ref, at, slice(hw, 2 * hw + state2), c == 0)
        mixed = convolved(ext, table, width)
        mix_ref[rows, :] = mixed
        conv = mixed * sigmoid(mixed)
        values = conv[:, :hw]
        b = conv[:, hw : hw + n].astype(BF)
        ct = conv[:, hw + n :].astype(BF)
        _, steps = step_table(proj_ref[rows, 2 * hw + state2 :], bias, heads, s)
        logs = exact(causal.astype(F32), steps * rate)
        logs_t, steps_t = logs.T, steps.T
        end = logs[GROUP - 1 : GROUP, :]
        before = state[...]
        entry_ref[c] = before
        carried = mm(ct, before.astype(BF)) * spread_heads(jnp.exp(logs), heads, head_dim)
        tails = spread_heads(jnp.exp(end - logs) * steps, heads, head_dim)
        fresh = t_mm(b, (values * tails).astype(BF))
        state[...] = spread_heads(jnp.exp(end), heads, head_dim) * before + fresh
        cross = mm_t(ct, b)
        low = values.astype(BF)
        tiles = []
        per = 128 // head_dim
        for h in range(0, heads, per):
            tile = None
            part = low[:, h * head_dim : h * head_dim + 128]
            for i in range(per):
                gap = logs[:, h + i : h + i + 1] - logs_t[h + i : h + i + 1, :]
                kernel = jnp.exp(jnp.where(causal, gap, -1e30))
                weights = cross * kernel * steps_t[h + i : h + i + 1, :]
                one = mm(weights.astype(BF), part)
                tile = one if i == 0 else jnp.where(lane >= i * head_dim, one, tile)
            tiles.append(tile)
        scanned = jnp.concatenate(tiles, 1) + carried + skip * values
        scan_ref[rows, :] = scanned
        gate = proj_ref[rows, :hw]
        gated = scanned * (gate * sigmoid(gate))
        low_ref[rows, :] = (gated * gain).astype(BF)
        square_ref[c] = lax.dot_general(
            jnp.ones((8, hw), F32),
            gated * gated,
            (((1,), (1,)), ((), ())),
            precision=PRECISE,
            preferred_element_type=F32,
        )
        ring.step(c + 1)
        return carry

    lax.fori_loop(0, blocks, chunk, 0)

    def fill(block):
        rows = pl.ds(pl.multiple_of(block * GROUP, GROUP), GROUP)
        part_ref[block] = mm(low_ref[rows, :], out_ref[...]).astype(BF)

    k = blocks + 1
    job.begin(fill)
    if k < ne - 1:
        ring.step(k)
        k += 1
    job.middle()
    if k < ne - 1:
        ring.step(k)
        k += 1
    job.finish(sum_ref, square_out)
    while k < ne - 1:
        ring.step(k)
        k += 1
    ring.finish()
    job.drain()


def mix_forward(proj, table, head_table, out_local, grad_low, ns, ne, hw, state2, heads, width, cid):
    whole = proj.shape[0]
    blocks = whole // GROUP
    n = state2 // 2
    rows, model = grad_low.shape
    return pl.pallas_call(
        functools.partial(mix_forward_kernel, ns, ne, hw, state2, heads, width),
        out_shape=(
            jax.ShapeDtypeStruct((whole, hw), F32),
            jax.ShapeDtypeStruct((whole, hw + state2), F32),
            jax.ShapeDtypeStruct((blocks, n, hw), F32),
            jax.ShapeDtypeStruct((rows, model), F32),
            jax.ShapeDtypeStruct((8, rows), F32),
            jax.ShapeDtypeStruct((ne, rows, model), BF),
        ),
        in_specs=[VMEM] * 5,
        out_specs=(VMEM,) * 6,
        scratch_shapes=[
            pltpu.VMEM((n, hw), F32),
            pltpu.VMEM((whole, hw), BF),
            pltpu.VMEM((blocks, 8, GROUP), F32),
            pltpu.VMEM((ns, rows, model), BF),
        ]
        + RingGather.scratch(ne, 2)
        + SeqSum.scratch(ns, 2, rows, model, (8, rows)),
        compiler_params=params(cid),
        name="mix_forward",
    )(proj, table, head_table, out_local, grad_low)


def mix_backward_kernel(
    hw, state2, heads, width,
    proj_ref, table_ref, head_ref, scan_ref, mix_ref, entry_ref, q_ref, scale_ref,
    dproj_ref, low_ref, dtable_ref, dhead_ref, adjoint, after,
):
    s = lax.axis_index("seq")
    blocks = proj_ref.shape[0] // GROUP
    head_dim = hw // heads
    n = state2 // 2
    per = 128 // head_dim
    adjoint[...] = jnp.zeros_like(adjoint)
    after[...] = jnp.zeros_like(after)
    dtable_ref[...] = jnp.zeros_like(dtable_ref)
    dhead_ref[...] = jnp.zeros_like(dhead_ref)
    lane = lax.broadcasted_iota(jnp.int32, (GROUP, 128), 1)
    row = lax.broadcasted_iota(jnp.int32, (GROUP, 128), 0)
    table = table_ref[...]
    skip = table[width + 2 : width + 3, :hw]
    gain = table[width + 1 : width + 2, :hw]
    bias, rate = head_ref[0:1, :], head_ref[1:2, :]

    def chunk(lap, carry):
        c = blocks - 1 - lap
        at = pl.multiple_of(c * GROUP, GROUP)
        rows = pl.ds(at, GROUP)
        causal = triangle()
        head_of = lax.broadcasted_iota(jnp.int32, (hw, 128), 0) // head_dim
        pick = (head_of == lax.broadcasted_iota(jnp.int32, (hw, 128), 1)).astype(F32)
        gate = proj_ref[rows, :hw]
        gate_sig = sigmoid(gate)
        gate_silu = gate * gate_sig
        scanned = scan_ref[rows, :]
        gated = scanned * gate_silu
        scales = scale_ref[c].T
        r, inside = scales[:, 0:1], scales[:, 1:2]
        q = q_ref[rows, :]
        dgated = r * (gain * q) - gated * (r * r * r * inside)
        low_ref[rows, :] = (gated * gain * r).astype(BF)
        dtable_ref[width + 1 : width + 2, :hw] += jnp.sum(gated * r * q, 0, keepdims=True)
        dy = dgated * gate_silu
        dproj_ref[rows, :hw] = (dgated * scanned * (gate_sig + gate_silu * (1 - gate_sig))).astype(BF)

        mixed = mix_ref[rows, :]
        sig = sigmoid(mixed)
        conv = mixed * sig
        values = conv[:, :hw]
        b = conv[:, hw : hw + n].astype(BF)
        ct = conv[:, hw + n :].astype(BF)
        dtable_ref[width + 2 : width + 3, :hw] += jnp.sum(dy * values, 0, keepdims=True)
        raw, steps = step_table(proj_ref[rows, 2 * hw + state2 :], bias, heads, s)
        logs = exact(causal.astype(F32), steps * rate)
        logs_t, steps_t = logs.T, steps.T
        end = logs[GROUP - 1 : GROUP, :]
        rest = jnp.exp(end - logs)
        tail = rest * steps
        ends = jnp.exp(end)
        before = entry_ref[c]
        before_low = before.astype(BF)
        later = adjoint[...]
        later_low = later.astype(BF)
        tails = spread_heads(tail, heads, head_dim)
        dy_carried = dy * spread_heads(jnp.exp(logs), heads, head_dim)
        dy_carried_low = dy_carried.astype(BF)
        carried = mm(ct, before_low)
        back = mm(b, later_low)
        dvalues = tails * back + skip * dy
        dc = mm_t(dy_carried_low, before_low)
        db = mm_t((values * tails).astype(BF), later_low)
        kept = jnp.sum(later * before, 0, keepdims=True)
        adjoint[...] = spread_heads(ends, heads, head_dim) * later + t_mm(ct, dy_carried_low)
        sums = exact(jnp.concatenate([dy_carried * carried, values * back, jnp.broadcast_to(kept, (8, hw))], 0), pick)
        from_carried, dtail, kept = sums[:GROUP], sums[GROUP : 2 * GROUP], sums[2 * GROUP : 2 * GROUP + 1]
        cross = mm_t(ct, b)
        low = values.astype(BF)
        dy_low = dy.astype(BF)
        dcross = jnp.zeros((GROUP, GROUP), F32)
        dlogs = from_carried - dtail * tail
        columns = []
        tiles = []
        for h in range(0, heads, per):
            part = low[:, h * head_dim : h * head_dim + 128]
            dy_part = dy_low[:, h * head_dim : h * head_dim + 128]
            tile = None
            for i in range(per):
                gap = logs[:, h + i : h + i + 1] - logs_t[h + i : h + i + 1, :]
                kernel = jnp.exp(jnp.where(causal, gap, -1e30))
                scaled = kernel * steps_t[h + i : h + i + 1, :]
                weights = cross * scaled
                inside_head = (lane >= i * head_dim) & (lane < (i + 1) * head_dim)
                one = t_mm(weights.astype(BF), dy_part)
                tile = one if i == 0 else jnp.where(lane >= i * head_dim, one, tile)
                dweights = mm_t(jnp.where(inside_head, dy_part, jnp.zeros_like(dy_part)), part)
                dcross = dcross + dweights * scaled
                unscaled = dweights * (cross * kernel)
                total = jnp.sum(dweights * weights, 1, keepdims=True)
                dlogs = dlogs + jnp.where(lane == h + i, total, 0.0)
                columns.append(jnp.sum(unscaled, 0, keepdims=True))
            tiles.append(tile)
        dvalues = dvalues + jnp.concatenate(tiles, 1)
        columns = jnp.concatenate(columns + [jnp.zeros((128 - heads, GROUP), F32)], 0).T
        dlogs = dlogs - columns * steps
        at_end = jnp.sum(dtail * tail, 0, keepdims=True) + ends * kept
        dlogs = dlogs + jnp.where(row == GROUP - 1, at_end, 0.0)
        da = exact(triangle(True).astype(F32), dlogs)
        dsteps = columns + dtail * rest + da * rate
        dhead_ref[1:2, :] += jnp.sum(da * steps, 0, keepdims=True)
        draw = jnp.where(lane < heads, dsteps * sigmoid(raw), 0.0)
        dhead_ref[0:1, :] += jnp.sum(draw, 0, keepdims=True)
        dproj_ref[rows, 2 * hw + state2 :] = pltpu.roll(draw, heads * s, 1).astype(BF)
        dcross_low = dcross.astype(BF)
        dc = dc + mm(dcross_low, b)
        db = db + t_mm(dcross_low, ct)
        dmix = jnp.concatenate([dvalues, db, dc], 1) * (sig + conv * (1 - sig))
        dtable_ref[width : width + 1, :] += jnp.sum(dmix, 0, keepdims=True)
        ext = with_before(proj_ref, at, slice(hw, 2 * hw + state2), c == 0)
        dext = jnp.concatenate([dmix, after[...]], 0)
        dconv = 0.0
        for j in range(width):
            first = 8 - width + 1 + j
            dtable_ref[j : j + 1, :] += jnp.sum(dmix * ext[first : first + GROUP], 0, keepdims=True)
            dconv = dconv + table[j : j + 1] * dext[width - 1 - j : width - 1 - j + GROUP]
        after[...] = dmix[:8]
        dproj_ref[rows, hw : 2 * hw + state2] = dconv.astype(BF)
        return carry

    lax.fori_loop(0, blocks, chunk, 0)


def mix_backward(proj, table, head_table, scanned, mixed, entries, q, scales, hw, state2, heads, width):
    whole = proj.shape[0]
    n = state2 // 2
    return pl.pallas_call(
        functools.partial(mix_backward_kernel, hw, state2, heads, width),
        out_shape=(
            jax.ShapeDtypeStruct(proj.shape, BF),
            jax.ShapeDtypeStruct((whole, hw), BF),
            jax.ShapeDtypeStruct((8, hw + state2), F32),
            jax.ShapeDtypeStruct((8, 128), F32),
        ),
        in_specs=[VMEM] * 8,
        out_specs=(VMEM,) * 4,
        scratch_shapes=[pltpu.VMEM((n, hw), F32), pltpu.VMEM((8, hw + state2), F32)],
        compiler_params=pltpu.CompilerParams(vmem_limit_bytes=48 << 20),
        name="mix_backward",
    )(proj, table, head_table, scanned, mixed, entries, q, scales)


def rms_back(value, gain, grad):
    scale = lax.rsqrt(jnp.mean(value * value, -1, keepdims=True) + EPSILON)
    inside = gain * grad
    back = scale * inside - value * scale**3 * jnp.mean(value * inside, -1, keepdims=True)
    return back, jnp.sum(value * scale * grad, 0)


def swiglu_back(a, b, grad):
    sig = jax.nn.sigmoid(a)
    return grad * b * sig * (1 + a * (1 - sig)), grad * a * sig


def on_device(
    tokens,
    routes,
    out_grad,
    norm_mix,
    in_weight,
    step_weight,
    conv_weight,
    conv_bias,
    step_bias,
    decay_log,
    skip_gain,
    norm_gate,
    out_weight,
    norm_ffn,
    router_weight,
    shared_gate,
    shared_up,
    shared_down,
    expert_gate,
    expert_up,
    expert_down,
):
    ns, ne = lax.axis_size("seq"), lax.axis_size("exp")
    s, e = lax.axis_index("seq"), lax.axis_index("exp")
    total = ns * ne
    rows, columns = in_weight.shape
    model = tokens.shape[2]
    length = tokens.shape[1]
    whole = length * ns
    width, channels = conv_weight.shape
    gains = norm_gate.shape[0]
    inner = gains * total
    hw = inner // ns
    heads = step_bias.shape[0]
    local_heads = heads // ns
    state2 = columns - 2 * inner
    experts = router_weight.shape[1]
    local_experts = expert_gate.shape[0]
    place = s * ne + e

    small = jnp.concatenate([conv_weight.reshape(-1), conv_bias, norm_gate])
    small = jnp.pad(small, (0, 16 * rows - small.shape[0])).reshape(rows, 16)
    pack = jnp.concatenate(
        [step_weight, router_weight, norm_mix[:, None], norm_ffn[:, None], small], 1
    )
    at_small = heads + experts + 2
    pack = jnp.pad(pack, ((0, 0), (0, 128 - pack.shape[1])))
    hidden_rows = shared_down.shape[0]

    def by_owner(weight):
        split = weight.reshape(rows, ns, ne, hidden_rows)
        return jnp.transpose(split, (2, 0, 1, 3)).reshape(ne, rows, ns * hidden_rows)

    shared_two = jnp.concatenate([by_owner(shared_gate), by_owner(shared_up)], -1)
    in_blocks, token_blocks, out_local, shared_two, local_down = gather_in(
        in_weight, pack, tokens[0], out_weight, shared_two, shared_down, ns, ne, inner, 0
    )
    out_local = out_local.reshape(hw, model)
    shared_two = shared_two.reshape(model, 2 * ns * hidden_rows)
    local_gate, local_up = shared_two[:, : ns * hidden_rows], shared_two[:, ns * hidden_rows :]
    local_down = local_down.reshape(ns * hidden_rows, model)
    grad_low = out_grad[0]
    in_local = in_blocks.reshape(model, -1)
    full_pack = in_local[:, 2 * hw + state2 :]
    full_router = full_pack[:, heads : heads + experts]
    full_norm_mix = full_pack[:, heads + experts].astype(F32)
    full_norm_ffn = full_pack[:, heads + experts + 1].astype(F32)
    full_small = full_pack[:, at_small : at_small + 16].reshape(total, 16 * rows).astype(F32)
    full_conv = full_small[:, : (width + 1) * channels].reshape(total, width + 1, channels)
    full_conv = jnp.swapaxes(full_conv, 0, 1).reshape(width + 1, total * channels)
    at_gain = (width + 1) * channels
    full_norm_gate = full_small[:, at_gain : at_gain + gains].reshape(inner)
    local_conv = jnp.concatenate(
        [lax.dynamic_slice_in_dim(full_conv, s * hw, hw, 1), full_conv[:, inner:]], 1
    )
    local_gain = lax.dynamic_slice_in_dim(full_norm_gate, s * hw, hw)
    at_head = s * local_heads
    local_bias = lax.dynamic_slice_in_dim(step_bias, at_head, local_heads)
    local_decay = lax.dynamic_slice_in_dim(decay_log, at_head, local_heads)
    local_skip = lax.dynamic_slice_in_dim(skip_gain, at_head, local_heads)

    table = jnp.concatenate(
        [
            local_conv,
            jnp.pad(
                jnp.stack([local_gain, jnp.repeat(local_skip, hw // local_heads)]),
                ((0, 6 - width - 1), (0, state2)),
            ),
        ],
        0,
    )
    head_table = jnp.pad(
        jnp.stack([local_bias, -jnp.exp(local_decay)]), ((0, 6), (0, 128 - local_heads))
    )

    token_rows = tokens[0].astype(F32)
    sequence = token_blocks.reshape(whole, model).astype(F32)
    scale_one = lax.rsqrt(jnp.mean(sequence * sequence, -1, keepdims=True) + EPSILON)
    lowered = (sequence * scale_one * full_norm_mix).astype(BF)
    projected = matmul_plain(lowered, in_local)
    scanned, mixed, entries, mixed_raw, squares, grad_all = mix_forward(
        projected, table, head_table, out_local, grad_low, ns, ne, hw, state2, local_heads, width, 1
    )
    grad_all = grad_all.reshape(ne * length, model)
    scale_gate = lax.rsqrt(squares[0] / inner + EPSILON)
    mixer_out = mixed_raw * scale_gate[:, None]
    resid = token_rows + mixer_out
    scale_two = lax.rsqrt(jnp.mean(resid * resid, -1, keepdims=True) + EPSILON)
    ffn_in = (resid * scale_two * full_norm_ffn).astype(BF)

    logits = matmul_plain(ffn_in, full_router)
    named = jnp.any(
        routes[0][:, :, None] == jnp.arange(experts, dtype=jnp.int32)[None, None, :], 1
    )
    top = jnp.max(jnp.where(named, logits, -jnp.inf), -1, keepdims=True)
    raised = jnp.where(named, jnp.exp(jnp.where(named, logits - top, 0.0)), 0.0)
    gates = (raised / jnp.sum(raised, -1, keepdims=True)).T

    ffn_all, gates_all = gather_exp(ffn_in, gates, ne, 2)
    ffn_all = ffn_all.reshape(ne * length, model)
    local_gates = lax.dynamic_slice_in_dim(gates_all, e * local_experts, local_experts, 1)
    out_total, back_total = 0.0, 0.0
    gate_grads, expert_sums = [], []
    for j in range(local_experts + 1):
        if j < local_experts:
            weight_gate, weight_up, weight_down = expert_gate[j], expert_up[j], expert_down[j]
            gate = local_gates[:, j].reshape(ne * length, 1)
        else:
            weight_gate, weight_up, weight_down = local_gate, local_up, local_down
            gate = 1.0
        part_a = matmul_plain(ffn_all, weight_gate)
        part_b = matmul_plain(ffn_all, weight_up)
        hidden_grad = matmul_cols(grad_all, weight_down)
        act = jax.nn.silu(part_a) * part_b
        hidden = (gate * act).astype(BF)
        gate_grads.append(jnp.sum(act * hidden_grad, -1))
        grad_a, grad_b = swiglu_back(part_a, part_b, gate * hidden_grad)
        grad_a, grad_b = grad_a.astype(BF), grad_b.astype(BF)
        out_total = out_total + matmul_plain(hidden, weight_down)
        back_total = (
            back_total + matmul_cols(grad_a, weight_gate) + matmul_cols(grad_b, weight_up)
        )
        expert_sums.append(
            (
                matmul_rows(ffn_all, grad_a).astype(BF),
                matmul_rows(ffn_all, grad_b).astype(BF),
                matmul_rows(hidden, grad_all).astype(BF),
            )
        )
    gate_grads = jnp.stack(gate_grads[:local_experts]).reshape(local_experts, ne, length)
    gate_grads = jnp.pad(
        jnp.swapaxes(gate_grads, 0, 1), ((0, 0), (0, 8 - local_experts), (0, 0))
    )
    back_sum, ffn_out, gate_grads = sum_exp(
        [
            back_total.astype(BF).reshape(ne, length, model),
            out_total.astype(BF).reshape(ne, length, model),
        ],
        gate_grads,
        ne,
        3,
    )
    gate_grads = gate_grads[:, :local_experts].reshape(experts, length)
    result = (resid + ffn_out).astype(BF)
    stat_terms = jnp.stack(
        [jnp.sum(resid * resid), jnp.sum(mixer_out * mixer_out), jnp.sum(ffn_out * ffn_out)]
    )
    expert_parts = []
    for which in range(3):
        both = jnp.stack([expert_sums[j][which] for j in range(local_experts)])
        if which < 2:
            both = both.reshape(local_experts, ns, model // ns, -1)
            both = jnp.swapaxes(both, 0, 1)
        else:
            both = both.reshape(local_experts, -1, ns, model // ns)
            both = jnp.transpose(both, (2, 0, 1, 3))
        expert_parts.append(
            lax.psum_scatter(both, "seq", scatter_dimension=0, tiled=False).astype(F32)
        )
    shared_parts = jnp.concatenate(
        [expert_sums[local_experts][0], expert_sums[local_experts][1]], 1
    )
    shared_parts = lax.psum_scatter(shared_parts, "seq", scatter_dimension=0, tiled=True)
    shared_parts = lax.all_to_all(
        shared_parts.reshape(ne, rows, -1), "exp", split_axis=0, concat_axis=0, tiled=True
    ).astype(F32)

    def to_rows(piece):
        piece = piece.reshape(ne, rows, ns, hidden_rows)
        return jnp.transpose(piece, (1, 2, 0, 3)).reshape(rows, total * hidden_rows)

    grad_shared_gate = to_rows(shared_parts[:, :, : ns * hidden_rows])
    grad_shared_up = to_rows(shared_parts[:, :, ns * hidden_rows :])
    grad_shared_down = lax.psum_scatter(
        expert_sums[local_experts][2], "seq", scatter_dimension=0, tiled=True
    ).astype(F32)

    picked_grad = gates * (gate_grads - jnp.sum(gates * gate_grads, 0, keepdims=True))
    logit_grad = picked_grad.T.astype(BF)
    grad_router = matmul_rows(ffn_in, logit_grad)
    ffn_in_grad = matmul_cols(logit_grad, full_router) + back_sum
    resid_norm_grad, grad_norm_ffn = rms_back(resid, full_norm_ffn, ffn_in_grad)
    resid_grad = grad_low.astype(F32) + resid_norm_grad
    resid_low = resid_grad.astype(BF)
    inside = jnp.sum(resid_low.astype(F32) * mixer_out, -1) / (scale_gate * inner)
    scales = jnp.concatenate(
        [scale_gate[None], inside[None], jnp.zeros((6, length), F32)], 0
    )

    resid_all, scales = gather_seq(resid_low, scales, ns, 4)
    resid_all = resid_all.reshape(whole, model)
    normed_grad = matmul_cols(resid_all, out_local)
    projected_grad, normed_low, table_grad, head_grad = mix_backward(
        projected,
        table,
        head_table,
        scanned,
        mixed,
        entries,
        normed_grad,
        scales,
        hw,
        state2,
        local_heads,
        width,
    )
    grad_out = matmul_rows(normed_low, resid_all).astype(BF)
    grad_gain = table_grad[width + 1, :hw]
    grad_skip = jnp.sum(table_grad[width + 2, :hw].reshape(local_heads, -1), -1)
    grad_step_bias = head_grad[0, :local_heads]
    grad_decay = head_grad[1, :local_heads] * head_table[1, :local_heads]
    lowered_part = matmul_cols(projected_grad, in_local).astype(BF)
    lowered_grad, _ = sum_seq(
        lowered_part.reshape(ns, length, model), jnp.zeros((ns, 8, length), F32), ns, 5
    )
    tokens_norm_grad, grad_norm_mix = rms_back(token_rows, full_norm_mix, lowered_grad)
    tokens_grad = (resid_grad + tokens_norm_grad).astype(BF)

    conv_grads = table_grad[: width + 1]
    wide = jnp.zeros((width + 1, total * channels), F32)
    wide = lax.dynamic_update_slice(wide, conv_grads[:, :hw], (0, s * hw))
    wide = lax.dynamic_update_slice(wide, conv_grads[:, hw:], (0, inner))
    wide_gain = lax.dynamic_update_slice(jnp.zeros((inner,), F32), grad_gain, (s * hw,))
    wide_heads = lax.dynamic_update_slice(
        jnp.zeros((3, heads), F32),
        jnp.stack([grad_step_bias, grad_decay, grad_skip]),
        (0, at_head),
    )
    sums = lax.psum(
        (wide, wide_gain, wide_heads, grad_router, grad_norm_mix, grad_norm_ffn, stat_terms),
        ("seq", "exp"),
    )
    wide, wide_gain, wide_heads, grad_router, grad_norm_mix, grad_norm_ffn, stat_terms = sums
    conv_grads = lax.dynamic_slice_in_dim(wide, place * channels, channels, 1)

    grad_in = matmul_rows(lowered, projected_grad).astype(BF)
    pieces, grad_out = sum_weights(
        grad_in.reshape(ns, ne, rows, -1),
        grad_out.reshape(ne, hw // ne, model),
        ns,
        ne,
        6,
    )
    pieces = pieces.astype(F32)
    grad_in = jnp.concatenate(
        [
            jnp.swapaxes(pieces[:, :, :hw], 0, 1).reshape(rows, inner),
            jnp.swapaxes(pieces[:, :, hw : 2 * hw], 0, 1).reshape(rows, inner),
            jnp.sum(pieces[:, :, 2 * hw : 2 * hw + state2], 0),
        ],
        1,
    )
    grad_step = jnp.sum(pieces[:, :, 2 * hw + state2 : 2 * hw + state2 + heads], 0)
    return (
        result[None],
        tokens_grad[None],
        lax.dynamic_slice_in_dim(grad_norm_mix, place * rows, rows),
        grad_in,
        grad_step,
        conv_grads[:width],
        conv_grads[width],
        wide_heads[0],
        wide_heads[1],
        wide_heads[2],
        lax.dynamic_slice_in_dim(wide_gain, place * gains, gains),
        grad_out,
        lax.dynamic_slice_in_dim(grad_norm_ffn, place * rows, rows),
        lax.dynamic_slice_in_dim(grad_router, place * rows, rows),
        grad_shared_gate,
        grad_shared_up,
        grad_shared_down,
        expert_parts[0],
        expert_parts[1],
        expert_parts[2],
        stat_terms / (total * length * model),
    )


def solution(mesh):
    both = ("seq", "exp")
    return jax.shard_map(
        on_device,
        mesh=mesh,
        in_specs=(
            P("exp", "seq", None),
            P("exp", "seq", None),
            P("exp", "seq", None),
            P(both),
            P(both, None),
            P(both, None),
            P(None, both),
            P(both),
            P(),
            P(),
            P(),
            P(both),
            P(both, None),
            P(both),
            P(both, None),
            P(both, None),
            P(both, None),
            P(both, None),
            P("exp", None, None),
            P("exp", None, None),
            P("exp", None, None),
        ),
        out_specs=(
            P("exp", "seq", None),
            P("exp", "seq", None),
            P(both),
            P(both, None),
            P(both, None),
            P(None, both),
            P(both),
            P(),
            P(),
            P(),
            P(both),
            P(both, None),
            P(both),
            P(both, None),
            P(both, None),
            P(both, None),
            P(both, None),
            P("exp", "seq", None),
            P("exp", "seq", None),
            P("exp", None, "seq"),
            P(),
        ),
        check_vma=False,
    )
```

```python
import functools

import jax
import jax.numpy as jnp
from jax import lax
from jax.experimental import pallas as pl
from jax.experimental.pallas import tpu as pltpu
from jax.sharding import PartitionSpec as P

GROUP = 128
EPSILON = 1e-05
PRECISE = lax.Precision.HIGHEST
MESH = pl.DeviceIdType.MESH
BF = jnp.bfloat16
F32 = jnp.float32
ANY = pl.BlockSpec(memory_space=pl.ANY)
VMEM = pl.BlockSpec(memory_space=pltpu.VMEM)
DMA = pltpu.SemaphoreType.DMA


def ring_place(e, n):
    odd = e % 2
    return (1 - odd) * (e // 2) + odd * (n - 1 - e // 2)


def ring_index(p, n):
    back = p // (n // 2)
    return (1 - back) * (2 * p) + back * (2 * (n - 1 - p) + 1)


def ring_sides(e, n):
    p = ring_place(e, n)
    return p, ring_index((p + 1) % n, n), ring_index((p + n - 1) % n, n)


def greet(partners):
    barrier = pltpu.get_barrier_semaphore()
    for partner in partners:
        pl.semaphore_signal(barrier, inc=1, device_id=partner, device_id_type=MESH)
    pl.semaphore_wait(barrier, len(partners))


def remote(src, dst, send, recv, device):
    copy = pltpu.make_async_remote_copy(
        src_ref=src,
        dst_ref=dst,
        send_sem=send,
        recv_sem=recv,
        device_id=device,
        device_id_type=MESH,
    )
    copy.start()
    return copy


def params(cid, mib=48):
    return pltpu.CompilerParams(
        collective_id=cid, has_side_effects=True, vmem_limit_bytes=mib << 20
    )


def tile_rows(rows, most=16):
    return most if rows % most == 0 else rows


def gather_in_kernel(
    ns,
    ne,
    hw,
    inner,
    in_ref,
    pack_ref,
    tok_ref,
    out_ref,
    two_ref,
    down_ref,
    w_ref,
    x_ref,
    o_ref,
    shared_ref,
    sd_ref,
    lsem,
    ssem0,
    rsem0,
    ssem,
    rsem,
    sa,
    ra,
    sb,
    rb,
):
    s, e = lax.axis_index("seq"), lax.axis_index("exp")
    p, right, left = ring_sides(e, ne)
    width = in_ref.shape[1] - 2 * inner
    half = out_ref.shape[1] // 2
    parts = (
        (lambda to: in_ref.at[:, pl.ds(pl.multiple_of(to * hw, 128), hw)], 0, hw),
        (lambda to: in_ref.at[:, pl.ds(pl.multiple_of(inner + to * hw, 128), hw)], hw, hw),
        (lambda to: in_ref.at[:, pl.ds(2 * inner, width)], 2 * hw, width),
        (lambda to: pack_ref, 2 * hw + width, pack_ref.shape[1]),
    )
    greet([((s + t) % ns, e) for t in range(1, ns)] + [(s, (e + t) % ne) for t in range(1, ne)])
    own = []
    for i, (piece, start, size) in enumerate(parts):
        own.append(
            pltpu.make_async_copy(piece(s), w_ref.at[s, e, :, pl.ds(start, size)], lsem.at[i])
        )
    own.append(pltpu.make_async_copy(out_ref, o_ref.at[e], lsem.at[4]))
    own.append(pltpu.make_async_copy(two_ref.at[e], shared_ref.at[s, e], lsem.at[5]))
    own.append(pltpu.make_async_copy(tok_ref, x_ref.at[s], lsem.at[6]))
    own.append(pltpu.make_async_copy(down_ref, sd_ref.at[s], lsem.at[7]))
    for copy in own:
        copy.start()
    first = {}
    for t in range(1, ns):
        to = (s + t) % ns
        for i, (piece, start, size) in enumerate(parts):
            first[t, i] = remote(
                piece(to),
                w_ref.at[s, e, :, pl.ds(start, size)],
                ssem0.at[t - 1, i],
                rsem0.at[t - 1, i],
                (to, e),
            )
    for copy in own:
        copy.wait()
    sent = {}
    across = {}
    along = {}
    for k in range(ne - 1):
        for t in range(ns + 2):
            way = t % 2
            to = (s, right if way == 0 else left)
            place = (p - k + ne) % ne if way == 0 else (p + k) % ne
            slot = ring_index(place, ne)
            if k > 0:
                sent[k - 1, t].wait_recv()
            elif 0 < t < ns:
                for i in range(len(parts)):
                    first[t, i].wait_recv()
            if t < ns:
                block = w_ref.at[(s + ns - t) % ns, slot]
            else:
                block = o_ref.at[slot, :, pl.ds(way * half, half)]
            sent[k, t] = remote(block, block, ssem.at[k, t], rsem.at[k, t], to)
        if k == 0:
            for t in range(1, ns):
                to = ((s + t) % ns, e)
                first[t, 4] = remote(
                    tok_ref, x_ref.at[s], ssem0.at[t - 1, 4], rsem0.at[t - 1, 4], to
                )
                first[t, 5] = remote(
                    down_ref, sd_ref.at[s], ssem0.at[t - 1, 5], rsem0.at[t - 1, 5], to
                )
            for t in range(1, ne):
                to = (e + t) % ne
                across[t] = remote(
                    two_ref.at[to], shared_ref.at[s, e], sa.at[t - 1], ra.at[t - 1], (s, to)
                )
        if k == 2:
            for t in range(1, ne):
                across[t].wait_recv()
            for t in range(1, ns):
                along[t] = remote(
                    shared_ref.at[s], shared_ref.at[s], sb.at[t - 1], rb.at[t - 1], ((s + t) % ns, e)
                )
    for t in range(ns + 2):
        sent[ne - 2, t].wait_recv()
    for t in range(1, ns):
        first[t, 4].wait_recv()
        first[t, 5].wait_recv()
        along[t].wait_recv()
    for group in (first, sent, across, along):
        for copy in group.values():
            copy.wait_send()


def gather_in(in_weight, pack, tokens, out_weight, shared_two, shared_down, ns, ne, inner, cid):
    rows, columns = in_weight.shape
    hw = inner // ns
    wide = 2 * hw + columns - 2 * inner + pack.shape[1]
    return pl.pallas_call(
        functools.partial(gather_in_kernel, ns, ne, hw, inner),
        out_shape=(
            jax.ShapeDtypeStruct((ns, ne, rows, wide), BF),
            jax.ShapeDtypeStruct((ns,) + tokens.shape, BF),
            jax.ShapeDtypeStruct((ne,) + out_weight.shape, BF),
            jax.ShapeDtypeStruct((ns,) + shared_two.shape, BF),
            jax.ShapeDtypeStruct((ns,) + shared_down.shape, BF),
        ),
        in_specs=[ANY] * 6,
        out_specs=(ANY,) * 5,
        scratch_shapes=[
            DMA((8,)),
            DMA((ns - 1, 6)),
            DMA((ns - 1, 6)),
            DMA((ne - 1, ns + 2)),
            DMA((ne - 1, ns + 2)),
            DMA((ne - 1,)),
            DMA((ne - 1,)),
            DMA((ns - 1,)),
            DMA((ns - 1,)),
        ],
        compiler_params=params(cid, 8),
        name="gather_in",
    )(in_weight, pack, tokens, out_weight, shared_two, shared_down)


class SeqSum:
    def __init__(self, ns, subs, part, aux, one, two, aux_in, s1, r1, s2, r2, sa, ra):
        self.s, self.e = lax.axis_index("seq"), lax.axis_index("exp")
        self.ns, self.ny, self.subs = ns, ns // 2, subs
        self.y, self.c = self.s // 2, self.s % 2
        self.part, self.aux, self.one, self.two, self.aux_in = part, aux, one, two, aux_in
        self.sems = (s1, r1, s2, r2, sa, ra)
        self.step = part.shape[1] // subs
        self.tile = tile_rows(self.step)
        self.first, self.second, self.extra = {}, {}, []

    @staticmethod
    def scratch(ns, subs, rows, width, aux_shape):
        ny = ns // 2
        return [
            pltpu.VMEM((ny, rows, width), BF),
            pltpu.VMEM((max(ny - 1, 1), rows, width), BF),
            pltpu.VMEM((ns - 1,) + aux_shape, F32),
            DMA((ny, subs)),
            DMA((ny, subs)),
            DMA((max(ny - 1, 1), subs)),
            DMA((max(ny - 1, 1), subs)),
            DMA((ns - 1,)),
            DMA((ns - 1,)),
        ]

    def rows(self, u):
        return pl.ds(u * self.step, self.step)

    def begin(self, fill=None):
        s1, r1, s2, r2, sa, ra = self.sems
        mate = (2 * self.y + 1 - self.c, self.e)
        for t in range(1, self.ns):
            to = (self.s + t) % self.ns
            self.extra.append(
                remote(
                    self.aux.at[to], self.aux_in.at[t - 1], sa.at[t - 1], ra.at[t - 1], (to, self.e)
                )
            )
        for j in list(range(1, self.ny)) + [0]:
            block = 2 * ((self.y + j) % self.ny) + 1 - self.c
            if fill is not None:
                fill(block)
            for u in range(self.subs):
                self.first[j, u] = remote(
                    self.part.at[block, self.rows(u)],
                    self.one.at[j, self.rows(u)],
                    s1.at[j, u],
                    r1.at[j, u],
                    mate,
                )
        if fill is not None:
            for j in list(range(1, self.ny)) + [0]:
                fill(2 * ((self.y + j) % self.ny) + self.c)

    def middle(self):
        s1, r1, s2, r2, sa, ra = self.sems
        for j in range(1, self.ny):
            to = 2 * ((self.y + j) % self.ny) + self.c
            for u in range(self.subs):
                self.first[j, u].wait_recv()

                def join(i, carry):
                    r = pl.ds(pl.multiple_of(u * self.step + i * self.tile, self.tile), self.tile)
                    total = self.one[j, r, :].astype(F32) + self.part[to, r, :].astype(F32)
                    self.one[j, r, :] = total.astype(BF)
                    return carry

                lax.fori_loop(0, self.step // self.tile, join, 0)
                self.second[j, u] = remote(
                    self.one.at[j, self.rows(u)],
                    self.two.at[j - 1, self.rows(u)],
                    s2.at[j - 1, u],
                    r2.at[j - 1, u],
                    (to, self.e),
                )

    def finish(self, out, aux_out):
        for u in range(self.subs):
            self.first[0, u].wait_recv()
            for j in range(1, self.ny):
                self.second[j, u].wait_recv()

            def close(i, carry):
                r = pl.ds(pl.multiple_of(u * self.step + i * self.tile, self.tile), self.tile)
                total = self.one[0, r, :].astype(F32) + self.part[self.s, r, :].astype(F32)
                for j in range(1, self.ny):
                    total = total + self.two[j - 1, r, :].astype(F32)
                out[r, :] = total
                return carry

            lax.fori_loop(0, self.step // self.tile, close, 0)
        total = self.aux[self.s]
        for t in range(1, self.ns):
            self.extra[t - 1].wait_recv()
            total = total + self.aux_in[t - 1]
        aux_out[...] = total

    def drain(self):
        for copy in list(self.first.values()) + list(self.second.values()) + self.extra:
            copy.wait_send()


def sum_seq_kernel(ns, subs, part, aux, out, aux_out, *scratch):
    s, e = lax.axis_index("seq"), lax.axis_index("exp")
    greet([((s + t) % ns, e) for t in range(1, ns)])
    job = SeqSum(ns, subs, part, aux, *scratch)
    job.begin()
    job.middle()
    job.finish(out, aux_out)
    job.drain()


def sum_seq(part, aux, ns, cid, subs=2):
    rows, width = part.shape[1:]
    return pl.pallas_call(
        functools.partial(sum_seq_kernel, ns, subs),
        out_shape=(
            jax.ShapeDtypeStruct((rows, width), F32),
            jax.ShapeDtypeStruct(aux.shape[1:], F32),
        ),
        in_specs=[VMEM, VMEM],
        out_specs=(VMEM, VMEM),
        scratch_shapes=SeqSum.scratch(ns, subs, rows, width, aux.shape[1:]),
        compiler_params=params(cid),
        name="sum_seq",
    )(part, aux)


class RingGather:
    def __init__(self, ne, v, out, lsem, ssem, rsem):
        self.s, self.e = lax.axis_index("seq"), lax.axis_index("exp")
        self.ne, self.v, self.out = ne, v, out
        self.p, self.right, self.left = ring_sides(self.e, ne)
        self.ssem, self.rsem = ssem, rsem
        self.subs = ssem.shape[2]
        self.step_rows = v.shape[0] // (2 * self.subs)
        self.own = pltpu.make_async_copy(v, out.at[self.e], lsem)

    @staticmethod
    def scratch(ne, subs):
        return [DMA, DMA((ne - 1, 2, subs)), DMA((ne - 1, 2, subs))]

    def copy(self, k, way, u, src=None):
        place = (self.p - k + self.ne) % self.ne if way == 0 else (self.p + k) % self.ne
        slot = ring_index(place, self.ne)
        rows = pl.ds((way * self.subs + u) * self.step_rows, self.step_rows)
        block = self.out.at[slot, rows]
        return pltpu.make_async_remote_copy(
            src_ref=block if src is None else src.at[rows],
            dst_ref=block,
            send_sem=self.ssem.at[k, way, u],
            recv_sem=self.rsem.at[k, way, u],
            device_id=(self.s, self.right if way == 0 else self.left),
            device_id_type=MESH,
        )

    def begin(self):
        self.own.start()
        for u in range(self.subs):
            for way in range(2):
                self.copy(0, way, u, self.v).start()

    def step(self, k):
        for u in range(self.subs):
            for way in range(2):
                self.copy(k - 1, way, u).wait_recv()
                self.copy(k, way, u).start()

    def forward(self, k):
        for u in range(self.subs):
            for way in range(2):
                self.copy(k, way, u).start()

    def arrived(self, k):
        for u in range(self.subs):
            for way in range(2):
                self.copy(k, way, u).wait_recv()

    def drain(self):
        for k in range(self.ne - 1):
            for u in range(self.subs):
                for way in range(2):
                    self.copy(k, way, u).wait_send()

    def finish(self):
        self.arrived(self.ne - 2)
        self.drain()
        self.own.wait()


class RingSum:
    def __init__(self, ne, part, acc, ssem, rsem):
        self.s, self.e = lax.axis_index("seq"), lax.axis_index("exp")
        self.ne, self.part, self.acc = ne, part, acc
        self.p, self.right, self.left = ring_sides(self.e, ne)
        self.ssem, self.rsem = ssem, rsem
        self.subs = ssem.shape[2]
        self.size = part.shape[1] // (2 * self.subs)
        self.tile = tile_rows(self.size)

    @staticmethod
    def scratch(ne, subs, rows, width):
        return [
            pltpu.VMEM((ne - 1, rows, width), BF),
            DMA((ne - 1, 2, subs)),
            DMA((ne - 1, 2, subs)),
        ]

    def slot(self, k, way):
        place = (self.p - 1 - k + 2 * self.ne) % self.ne if way == 0 else (self.p + 1 + k) % self.ne
        return ring_index(place, self.ne)

    def copy(self, k, way, u, src=None):
        rows = pl.ds((way * self.subs + u) * self.size, self.size)
        return pltpu.make_async_remote_copy(
            src_ref=self.acc.at[k, rows] if src is None else src.at[rows],
            dst_ref=self.acc.at[k, rows],
            send_sem=self.ssem.at[k, way, u],
            recv_sem=self.rsem.at[k, way, u],
            device_id=(self.s, self.right if way == 0 else self.left),
            device_id_type=MESH,
        )

    def add(self, k, way, u, out):
        base = (way * self.subs + u) * self.size
        slot = self.slot(k, way)

        def join(i, carry):
            r = pl.ds(pl.multiple_of(base + i * self.tile, self.tile), self.tile)
            total = self.acc[k - 1, r, :].astype(F32) + self.part[slot, r, :].astype(F32)
            if out is None:
                self.acc[k - 1, r, :] = total.astype(BF)
            else:
                out[r, :] = total
            return carry

        lax.fori_loop(0, self.size // self.tile, join, 0)

    def begin(self):
        for u in range(self.subs):
            for way in range(2):
                self.copy(0, way, u, self.part.at[self.slot(0, way)]).start()

    def step(self, k):
        for u in range(self.subs):
            for way in range(2):
                self.copy(k - 1, way, u).wait_recv()
                self.add(k, way, u, None)
                rows = pl.ds((way * self.subs + u) * self.size, self.size)
                pltpu.make_async_remote_copy(
                    src_ref=self.acc.at[k - 1, rows],
                    dst_ref=self.acc.at[k, rows],
                    send_sem=self.ssem.at[k, way, u],
                    recv_sem=self.rsem.at[k, way, u],
                    device_id=(self.s, self.right if way == 0 else self.left),
                    device_id_type=MESH,
                ).start()

    def finish(self, out):
        k = self.ne - 1
        for u in range(self.subs):
            for way in range(2):
                self.copy(k - 1, way, u).wait_recv()
                self.add(k, way, u, out)
        for k in range(self.ne - 1):
            for u in range(self.subs):
                for way in range(2):
                    self.copy(k, way, u).wait_send()


class Exchange:
    def __init__(self, ne, src, dst, lsem, ssem, rsem):
        s, e = lax.axis_index("seq"), lax.axis_index("exp")
        self.own = pltpu.make_async_copy(src.at[e], dst.at[e], lsem)
        self.copies = []
        for t in range(1, ne):
            to = (e + t) % ne
            self.copies.append(
                pltpu.make_async_remote_copy(
                    src_ref=src.at[to],
                    dst_ref=dst.at[e],
                    send_sem=ssem.at[t - 1],
                    recv_sem=rsem.at[t - 1],
                    device_id=(s, to),
                    device_id_type=MESH,
                )
            )

    @staticmethod
    def scratch(ne):
        return [DMA, DMA((ne - 1,)), DMA((ne - 1,))]

    def begin(self):
        self.own.start()
        for copy in self.copies:
            copy.start()

    def arrived(self):
        self.own.wait()
        for copy in self.copies:
            copy.wait_recv()

    def drain(self):
        for copy in self.copies:
            copy.wait_send()


def experts_kernel(
    ne,
    count,
    ffn_ref,
    gate_ref,
    grad_ref,
    eg_ref,
    eu_ref,
    ed_ref,
    two_ref,
    sd_ref,
    back_ref,
    gate_back,
    out_ref,
    dw_ref,
    dsd_ref,
    x_ref,
    gates,
    hid_ref,
    da_ref,
    db_ref,
    part_ref,
    gate_part,
    stage,
    stage_sem,
    *scratch,
):
    s, e = lax.axis_index("seq"), lax.axis_index("exp")
    length, model = ffn_ref.shape
    half = length // 2
    width = eg_ref.shape[2]
    narrow = sd_ref.shape[0]
    tile_width = min(width, 256)
    greet([(s, (e + t) % ne) for t in range(1, ne)])
    ring = RingGather(ne, ffn_ref, x_ref, *scratch[:3])
    there = Exchange(ne, gate_ref, gates, *scratch[3:6])
    back = Exchange(ne, gate_part, gate_back, *scratch[6:9])
    total = RingSum(ne, part_ref, *scratch[9:12])
    ring.begin()
    there.begin()
    gate_part[...] = jnp.zeros_like(gate_part)
    ring.own.wait()
    there.arrived()
    lane = lax.broadcasted_iota(jnp.int32, (8, length), 1)
    wide_lane = lax.broadcasted_iota(jnp.int32, (length, 128), 1)

    def compute(one, two):
        x = jnp.concatenate([x_ref[one, :half, :], x_ref[two, half:, :]], 0)
        g = jnp.concatenate([grad_ref[one, :half, :], grad_ref[two, half:, :]], 0)
        table = jnp.where(lane < half, gates[one], gates[two]).T
        slots = jnp.zeros((length, 128), F32)

        def store(ref, at, size, value):
            ref[one, :half, at : at + size] = value[:half]
            ref[two, half:, at : at + size] = value[half:]

        for j in range(count + 1):
            size = width if j < count else narrow
            column = table[:, j : j + 1] if j < count else None
            for f in range(0, size, tile_width):
                wide = min(tile_width, size - f)
                if j < count:
                    a = mm(x, eg_ref[j, :, f : f + wide])
                    b = mm(x, eu_ref[j, :, f : f + wide])
                    h = mm_t(g, ed_ref[j, f : f + wide, :])
                else:
                    both = mm(x, two_ref[...])
                    a, b = both[:, :narrow], both[:, narrow:]
                    h = mm_t(g, sd_ref[...])
                sig = sigmoid(a)
                silu = a * sig
                act = silu * b
                if j < count:
                    found = jnp.sum(act * h, 1, keepdims=True)
                    slots = slots + jnp.where(wide_lane == j, found, 0.0)
                    act = act * column
                    h = h * column
                at = j * width + f
                store(hid_ref, at, wide, act.astype(BF))
                store(da_ref, at, wide, (h * b * (sig + silu * (1 - sig))).astype(BF))
                store(db_ref, at, wide, (h * silu).astype(BF))
        found = slots.T[:8]
        gate_part[one] = jnp.where(lane < half, found, gate_part[one])
        gate_part[two] = jnp.where(lane >= half, found, gate_part[two])

        def rows_of(ref, at, size):
            return jnp.concatenate(
                [ref[one, :half, at : at + size], ref[two, half:, at : at + size]], 0
            )

        at = count * width
        for d in range(0, model, 512):
            cols = slice(d, d + 512)
            out = mm(rows_of(hid_ref, at, narrow), sd_ref[:, cols])
            row = mm_t(rows_of(da_ref, at, narrow), two_ref[cols, :narrow])
            row = row + mm_t(rows_of(db_ref, at, narrow), two_ref[cols, narrow:])
            for j in range(count):
                out = out + mm(rows_of(hid_ref, j * width, width), ed_ref[j, :, cols])
                row = row + mm_t(rows_of(da_ref, j * width, width), eg_ref[j, cols, :])
                row = row + mm_t(rows_of(db_ref, j * width, width), eu_ref[j, cols, :])
            out_ref[one, :half, cols] = out[:half].astype(BF)
            out_ref[two, half:, cols] = out[half:].astype(BF)
            part_ref[one, :half, cols] = row[:half].astype(BF)
            part_ref[two, half:, cols] = row[half:].astype(BF)

    def arrive(k, carry):
        @pl.when(k > 0)
        def _():
            ring.arrived(k - 1)

        @pl.when((k > 0) & (k < ne - 1))
        def _():
            ring.forward(k)

        compute(ring_index((ring.p - k + ne) % ne, ne), ring_index((ring.p + k) % ne, ne))
        return carry

    lax.fori_loop(0, ne, arrive, 0)
    ring.drain()
    back.begin()
    total.begin()
    tiles = model // 256
    every = ne * length

    def stage_copy(i):
        return pltpu.make_async_copy(
            stage.at[i % 2], dw_ref.at[pl.ds(pl.multiple_of(i * 256, 256), 256)], stage_sem.at[i % 2]
        )

    def weights(i):
        @pl.when(i >= 2)
        def _():
            stage_copy(i - 2).wait()

        cols = pl.ds(pl.multiple_of(i * 256, 256), 256)
        slot = i % 2
        x_t = x_ref[:, :, cols].reshape(every, 256).T
        g_t = grad_ref[:, :, cols].reshape(every, 256).T
        for j in range(count):
            at = slice(j * width, (j + 1) * width)
            base = 3 * j * width
            stage[slot, :, base : base + width] = mm(x_t, da_ref[:, :, at].reshape(every, width)).astype(BF)
            stage[slot, :, base + width : base + 2 * width] = mm(
                x_t, db_ref[:, :, at].reshape(every, width)
            ).astype(BF)
            stage[slot, :, base + 2 * width : base + 3 * width] = mm(
                g_t, hid_ref[:, :, at].reshape(every, width)
            ).astype(BF)
        at = slice(count * width, count * width + narrow)
        base = 3 * count * width
        both = jnp.concatenate(
            [da_ref[:, :, at].reshape(every, narrow), db_ref[:, :, at].reshape(every, narrow)], 1
        )
        stage[slot, :, base : base + 2 * narrow] = mm(x_t, both).astype(BF)
        stage_copy(i).start()

    def back_step(k, carry):
        @pl.when(k > 0)
        def _():
            total.step(k)

        @pl.when(k < tiles)
        def _():
            weights(k)

        return carry

    lax.fori_loop(0, ne - 1, back_step, 0)
    at = slice(count * width, count * width + narrow)
    hid_t = hid_ref[:, :, at].reshape(every, narrow).T
    for d in range(0, model, 512):
        dsd_ref[:, d : d + 512] = mm(hid_t, grad_ref[:, :, d : d + 512].reshape(every, 512)).astype(BF)
    for i in range(ne - 1, tiles):
        weights(i)
    for i in range(max(tiles - 2, 0), tiles):
        stage_copy(i).wait()
    total.finish(back_ref)
    back.arrived()
    back.drain()
    there.drain()


def experts_both_ways(ffn_in, gates, grad_all, expert_gate, expert_up, expert_down, shared_two, shared_down, ne, cid):
    length, model = ffn_in.shape
    count, _, width = expert_gate.shape
    narrow = shared_down.shape[0]
    hidden = count * width + narrow
    columns = 3 * count * width + 2 * narrow
    return pl.pallas_call(
        functools.partial(experts_kernel, ne, count),
        out_shape=(
            jax.ShapeDtypeStruct((length, model), F32),
            jax.ShapeDtypeStruct((ne, 8, length), F32),
            jax.ShapeDtypeStruct((ne, length, model), BF),
            jax.ShapeDtypeStruct((model, columns), BF),
            jax.ShapeDtypeStruct((narrow, model), BF),
        ),
        in_specs=[VMEM] * 8,
        out_specs=(VMEM, VMEM, VMEM, ANY, VMEM),
        scratch_shapes=[
            pltpu.VMEM((ne, length, model), BF),
            pltpu.VMEM((ne, 8, length), F32),
            pltpu.VMEM((ne, length, hidden), BF),
            pltpu.VMEM((ne, length, hidden), BF),
            pltpu.VMEM((ne, length, hidden), BF),
            pltpu.VMEM((ne, length, model), BF),
            pltpu.VMEM((ne, 8, length), F32),
            pltpu.VMEM((2, 256, columns), BF),
            DMA((2,)),
        ]
        + RingGather.scratch(ne, 2)
        + Exchange.scratch(ne)
        + Exchange.scratch(ne)
        + RingSum.scratch(ne, 2, length, model),
        compiler_params=params(cid, 60),
        name="experts",
    )(ffn_in, gates, grad_all, expert_gate, expert_up, expert_down, shared_two, shared_down)


class SeqGather:
    def __init__(self, ns, v, aux, out, aux_out, lsem, s1, r1, s2, r2, sa, ra):
        s, e = lax.axis_index("seq"), lax.axis_index("exp")
        ny = ns // 2
        y, c = s // 2, s % 2
        mate = (2 * y + 1 - c, e)

        def make(src, dst, send, recv, device):
            return pltpu.make_async_remote_copy(
                src_ref=src,
                dst_ref=dst,
                send_sem=send,
                recv_sem=recv,
                device_id=device,
                device_id_type=MESH,
            )

        self.own = [
            pltpu.make_async_copy(v, out.at[s], lsem.at[0]),
            pltpu.make_async_copy(aux, aux_out.at[s], lsem.at[1]),
        ]
        self.first = [
            make(v, out.at[s], s1.at[j], r1.at[j], (2 * ((y + j) % ny) + c, e))
            for j in range(1, ny)
        ]
        self.first.append(make(v, out.at[s], s1.at[0], r1.at[0], mate))
        self.extra = [
            make(aux, aux_out.at[s], sa.at[t - 1], ra.at[t - 1], ((s + t) % ns, e))
            for t in range(1, ns)
        ]
        self.second = []
        for j in range(1, ny):
            block = out.at[2 * ((y + ny - j) % ny) + c]
            self.second.append(make(block, block, s2.at[j - 1], r2.at[j - 1], mate))

    @staticmethod
    def scratch(ns):
        ny = ns // 2
        return [
            DMA((2,)),
            DMA((ny,)),
            DMA((ny,)),
            DMA((max(ny - 1, 1),)),
            DMA((max(ny - 1, 1),)),
            DMA((ns - 1,)),
            DMA((ns - 1,)),
        ]

    def begin(self):
        for copy in self.first + self.extra + self.own:
            copy.start()

    def middle(self):
        for arrived, onward in zip(self.first[:-1], self.second):
            arrived.wait_recv()
            onward.start()

    def finish(self):
        for copy in [self.first[-1]] + self.second + self.extra:
            copy.wait_recv()
        for copy in self.own:
            copy.wait()

    def drain(self):
        for copy in self.first + self.second + self.extra:
            copy.wait_send()


def sum_weights_kernel(
    ns, ne, gin, gout, out, out_rows, acc, acc_out, fin, ssem, rsem, so, ro, sx, rx
):
    s, e = lax.axis_index("seq"), lax.axis_index("exp")
    p, right, left = ring_sides(e, ne)
    greet([((s + t) % ns, e) for t in range(1, ns)] + [(s, right), (s, left)])
    rows = gin.shape[2]
    tile = tile_rows(rows)
    half = gout.shape[2] // 2
    tile_out = tile_rows(gout.shape[1])
    sent = {}
    last = {}
    for k in range(ne):
        for t in range(ns + 2):
            way = t % 2
            to = right if way == 0 else left
            place = (p - 1 - k + 2 * ne) % ne if way == 0 else (p + 1 + k) % ne
            slot = ring_index(place, ne)
            if t < ns:
                piece = (s + t) % ns
                if k > 0:
                    sent[k - 1, t].wait_recv()

                    def join(i, carry):
                        r = pl.ds(pl.multiple_of(i * tile, tile), tile)
                        total = acc[k - 1, t, r, :].astype(F32) + gin[piece, slot, r, :].astype(
                            F32
                        )
                        if k < ne - 1:
                            acc[k - 1, t, r, :] = total.astype(BF)
                        elif t == 0:
                            out[s, r, :] = total.astype(BF)
                        else:
                            fin[t - 1, r, :] = total.astype(BF)
                        return carry

                    lax.fori_loop(0, rows // tile, join, 0)
                if k < ne - 1:
                    src = gin.at[piece, slot] if k == 0 else acc.at[k - 1, t]
                    sent[k, t] = remote(
                        src, acc.at[k, t], ssem.at[k, t], rsem.at[k, t], (s, to)
                    )
                elif t > 0:
                    last[t] = remote(
                        fin.at[t - 1], out.at[s], sx.at[t - 1], rx.at[t - 1], (piece, e)
                    )
            else:
                part_columns = pl.ds(way * half, half)
                if k > 0:
                    sent[k - 1, t].wait_recv()

                    def join_out(i, carry):
                        r = pl.ds(pl.multiple_of(i * tile_out, tile_out), tile_out)
                        total = acc_out[k - 1, r, part_columns].astype(F32)
                        total = total + gout[slot, r, part_columns].astype(F32)
                        if k < ne - 1:
                            acc_out[k - 1, r, part_columns] = total.astype(BF)
                        else:
                            out_rows[r, part_columns] = total
                        return carry

                    lax.fori_loop(0, gout.shape[1] // tile_out, join_out, 0)
                if k < ne - 1:
                    src = (
                        gout.at[slot, :, part_columns]
                        if k == 0
                        else acc_out.at[k - 1, :, part_columns]
                    )
                    sent[k, t] = remote(
                        src,
                        acc_out.at[k, :, part_columns],
                        so.at[k, way],
                        ro.at[k, way],
                        (s, to),
                    )
    for copy in last.values():
        copy.wait_recv()
    for copy in list(sent.values()) + list(last.values()):
        copy.wait_send()


def sum_weights(gin, gout, ns, ne, cid):
    rows, wide = gin.shape[2:]
    return pl.pallas_call(
        functools.partial(sum_weights_kernel, ns, ne),
        out_shape=(
            jax.ShapeDtypeStruct((ns, rows, wide), BF),
            jax.ShapeDtypeStruct(gout.shape[1:], F32),
        ),
        in_specs=[VMEM, VMEM],
        out_specs=(VMEM, VMEM),
        scratch_shapes=[
            pltpu.VMEM((ne - 1, ns, rows, wide), BF),
            pltpu.VMEM((ne - 1,) + gout.shape[1:], BF),
            pltpu.VMEM((ns - 1, rows, wide), BF),
            DMA((ne - 1, ns)),
            DMA((ne - 1, ns)),
            DMA((ne - 1, 2)),
            DMA((ne - 1, 2)),
            DMA((ns - 1,)),
            DMA((ns - 1,)),
        ],
        compiler_params=params(cid),
        name="sum_weights",
    )(gin, gout)


def matmul_plain(left, right):
    return jnp.dot(left, right, preferred_element_type=F32)


def matmul_rows(left, right):
    return lax.dot_general(left, right, (((0,), (0,)), ((), ())), preferred_element_type=F32)


def matmul_cols(left, right):
    return lax.dot_general(left, right, (((1,), (1,)), ((), ())), preferred_element_type=F32)


def mm(left, right):
    return jnp.dot(left, right, preferred_element_type=F32)


def mm_t(left, right):
    return lax.dot_general(left, right, (((1,), (1,)), ((), ())), preferred_element_type=F32)


def t_mm(left, right):
    return lax.dot_general(left, right, (((0,), (0,)), ((), ())), preferred_element_type=F32)


def exact(left, right):
    return jnp.dot(left, right, precision=PRECISE, preferred_element_type=F32)


def spread_heads(table, heads, head_dim):
    rows = table.shape[0]
    per = 128 // head_dim
    lane = lax.broadcasted_iota(jnp.int32, (rows, 128), 1)
    tiles = []
    for h in range(0, heads, per):
        tile = jnp.broadcast_to(table[:, h : h + 1], (rows, 128))
        for i in range(1, per):
            other = jnp.broadcast_to(table[:, h + i : h + i + 1], (rows, 128))
            tile = jnp.where(lane >= i * head_dim, other, tile)
        tiles.append(tile)
    return jnp.concatenate(tiles, 1)


def sigmoid(v):
    return 1.0 / (1.0 + jnp.exp(-v))


def softplus(v):
    return jnp.maximum(v, 0.0) + jnp.log1p(jnp.exp(-jnp.abs(v)))


def triangle(flip=False):
    t = lax.broadcasted_iota(jnp.int32, (GROUP, GROUP), 0)
    u = lax.broadcasted_iota(jnp.int32, (GROUP, GROUP), 1)
    return u >= t if flip else t >= u


def step_table(pack, bias, heads, s):
    turned = pltpu.roll(pack, (128 - heads * s) % 128, 1)
    lane = lax.broadcasted_iota(jnp.int32, turned.shape, 1)
    raw = jnp.where(lane < heads, turned + bias, 0.0)
    return raw, jnp.where(lane < heads, softplus(raw), 0.0)


def convolved(ext, table, width):
    mixed = table[width : width + 1]
    for j in range(width):
        mixed = mixed + table[j : j + 1] * ext[8 - width + 1 + j : 8 - width + 1 + j + GROUP]
    return mixed


def with_before(proj_ref, at, columns, first):
    before = proj_ref[pl.ds(pl.multiple_of(jnp.maximum(at - 8, 0), 8), 8), columns]
    before = jnp.where(first, 0.0, before)
    return jnp.concatenate([before, proj_ref[pl.ds(at, GROUP), columns]], 0)


def mix_forward_kernel(
    ns,
    ne,
    hw,
    state2,
    heads,
    width,
    proj_ref,
    table_ref,
    head_ref,
    out_ref,
    grad_ref,
    scan_ref,
    mix_ref,
    entry_ref,
    sum_ref,
    square_out,
    grad_all,
    state,
    low_ref,
    square_ref,
    part_ref,
    *sems,
):
    s, e = lax.axis_index("seq"), lax.axis_index("exp")
    p, right, left = ring_sides(e, ne)
    greet([((s + t) % ns, e) for t in range(1, ns)] + [(s, right), (s, left)])
    ring = RingGather(ne, grad_ref, grad_all, *sems[:3])
    job = SeqSum(ns, 2, part_ref, square_ref, *sems[3:])
    ring.begin()
    blocks = proj_ref.shape[0] // GROUP
    head_dim = hw // heads
    n = state2 // 2
    state[...] = jnp.zeros_like(state)
    lane = lax.broadcasted_iota(jnp.int32, (GROUP, 128), 1)
    table = table_ref[...]
    skip = table[width + 2 : width + 3, :hw]
    gain = table[width + 1 : width + 2, :hw]
    bias, rate = head_ref[0:1, :], head_ref[1:2, :]

    def chunk(c, carry):
        at = pl.multiple_of(c * GROUP, GROUP)
        rows = pl.ds(at, GROUP)
        causal = triangle()
        ext = with_before(proj_ref, at, slice(hw, 2 * hw + state2), c == 0)
        mixed = convolved(ext, table, width)
        mix_ref[rows, :] = mixed
        conv = mixed * sigmoid(mixed)
        values = conv[:, :hw]
        b = conv[:, hw : hw + n].astype(BF)
        ct = conv[:, hw + n :].astype(BF)
        _, steps = step_table(proj_ref[rows, 2 * hw + state2 :], bias, heads, s)
        logs = exact(causal.astype(F32), steps * rate)
        logs_t, steps_t = logs.T, steps.T
        end = logs[GROUP - 1 : GROUP, :]
        before = state[...]
        entry_ref[c] = before
        carried = mm(ct, before.astype(BF)) * spread_heads(jnp.exp(logs), heads, head_dim)
        tails = spread_heads(jnp.exp(end - logs) * steps, heads, head_dim)
        fresh = t_mm(b, (values * tails).astype(BF))
        state[...] = spread_heads(jnp.exp(end), heads, head_dim) * before + fresh
        cross = mm_t(ct, b)
        low = values.astype(BF)
        tiles = []
        per = 128 // head_dim
        for h in range(0, heads, per):
            tile = None
            part = low[:, h * head_dim : h * head_dim + 128]
            for i in range(per):
                gap = logs[:, h + i : h + i + 1] - logs_t[h + i : h + i + 1, :]
                kernel = jnp.exp(jnp.where(causal, gap, -1e30))
                weights = cross * kernel * steps_t[h + i : h + i + 1, :]
                one = mm(weights.astype(BF), part)
                tile = one if i == 0 else jnp.where(lane >= i * head_dim, one, tile)
            tiles.append(tile)
        scanned = jnp.concatenate(tiles, 1) + carried + skip * values
        scan_ref[rows, :] = scanned
        gate = proj_ref[rows, :hw]
        gated = scanned * (gate * sigmoid(gate))
        low_ref[rows, :] = (gated * gain).astype(BF)
        square_ref[c] = lax.dot_general(
            jnp.ones((8, hw), F32),
            gated * gated,
            (((1,), (1,)), ((), ())),
            precision=PRECISE,
            preferred_element_type=F32,
        )
        ring.step(c + 1)
        return carry

    lax.fori_loop(0, blocks, chunk, 0)

    def fill(block):
        rows = pl.ds(pl.multiple_of(block * GROUP, GROUP), GROUP)
        part_ref[block] = mm(low_ref[rows, :], out_ref[...]).astype(BF)

    k = blocks + 1
    job.begin(fill)
    if k < ne - 1:
        ring.step(k)
        k += 1
    job.middle()
    if k < ne - 1:
        ring.step(k)
        k += 1
    job.finish(sum_ref, square_out)
    while k < ne - 1:
        ring.step(k)
        k += 1
    ring.finish()
    job.drain()


def mix_forward(proj, table, head_table, out_local, grad_low, ns, ne, hw, state2, heads, width, cid):
    whole = proj.shape[0]
    blocks = whole // GROUP
    n = state2 // 2
    rows, model = grad_low.shape
    return pl.pallas_call(
        functools.partial(mix_forward_kernel, ns, ne, hw, state2, heads, width),
        out_shape=(
            jax.ShapeDtypeStruct((whole, hw), F32),
            jax.ShapeDtypeStruct((whole, hw + state2), F32),
            jax.ShapeDtypeStruct((blocks, n, hw), F32),
            jax.ShapeDtypeStruct((rows, model), F32),
            jax.ShapeDtypeStruct((8, rows), F32),
            jax.ShapeDtypeStruct((ne, rows, model), BF),
        ),
        in_specs=[VMEM] * 5,
        out_specs=(VMEM,) * 6,
        scratch_shapes=[
            pltpu.VMEM((n, hw), F32),
            pltpu.VMEM((whole, hw), BF),
            pltpu.VMEM((blocks, 8, GROUP), F32),
            pltpu.VMEM((ns, rows, model), BF),
        ]
        + RingGather.scratch(ne, 2)
        + SeqSum.scratch(ns, 2, rows, model, (8, rows)),
        compiler_params=params(cid),
        name="mix_forward",
    )(proj, table, head_table, out_local, grad_low)


def mix_backward_kernel(
    ns,
    ne,
    hw,
    state2,
    heads,
    width,
    proj_ref,
    table_ref,
    head_ref,
    scan_ref,
    mix_ref,
    entry_ref,
    out_ref,
    resid_ref,
    rows_ref,
    part_ref,
    sum_ref,
    dproj_ref,
    grad_out_ref,
    dtable_ref,
    dhead_ref,
    adjoint,
    after,
    low_ref,
    resid_all,
    scale_ref,
    *scratch,
):
    s, e = lax.axis_index("seq"), lax.axis_index("exp")
    p, right, left = ring_sides(e, ne)
    greet([((s + t) % ns, e) for t in range(1, ns)] + [(s, right), (s, left)])
    ring = RingSum(ne, part_ref, *scratch[:3])
    rows_in = SeqGather(ns, resid_ref, rows_ref, resid_all, scale_ref, *scratch[3:])
    rows_in.begin()
    ring.begin()
    rows_in.middle()
    ring.step(1)
    rows_in.finish()
    blocks = proj_ref.shape[0] // GROUP
    head_dim = hw // heads
    n = state2 // 2
    per = 128 // head_dim
    adjoint[...] = jnp.zeros_like(adjoint)
    after[...] = jnp.zeros_like(after)
    dtable_ref[...] = jnp.zeros_like(dtable_ref)
    dhead_ref[...] = jnp.zeros_like(dhead_ref)
    lane = lax.broadcasted_iota(jnp.int32, (GROUP, 128), 1)
    row = lax.broadcasted_iota(jnp.int32, (GROUP, 128), 0)
    table = table_ref[...]
    skip = table[width + 2 : width + 3, :hw]
    gain = table[width + 1 : width + 2, :hw]
    bias, rate = head_ref[0:1, :], head_ref[1:2, :]

    def chunk(lap, carry):
        c = blocks - 1 - lap
        at = pl.multiple_of(c * GROUP, GROUP)
        rows = pl.ds(at, GROUP)
        causal = triangle()
        head_of = lax.broadcasted_iota(jnp.int32, (hw, 128), 0) // head_dim
        pick = (head_of == lax.broadcasted_iota(jnp.int32, (hw, 128), 1)).astype(F32)
        gate = proj_ref[rows, :hw]
        gate_sig = sigmoid(gate)
        gate_silu = gate * gate_sig
        scanned = scan_ref[rows, :]
        gated = scanned * gate_silu
        scales = scale_ref[c].T
        r, inside = scales[:, 0:1], scales[:, 1:2]
        q = mm_t(resid_all[c], out_ref[...])
        dgated = r * (gain * q) - gated * (r * r * r * inside)
        low_ref[rows, :] = (gated * gain * r).astype(BF)
        dtable_ref[width + 1 : width + 2, :hw] += jnp.sum(gated * r * q, 0, keepdims=True)
        dy = dgated * gate_silu
        dproj_ref[rows, :hw] = (dgated * scanned * (gate_sig + gate_silu * (1 - gate_sig))).astype(BF)

        mixed = mix_ref[rows, :]
        sig = sigmoid(mixed)
        conv = mixed * sig
        values = conv[:, :hw]
        b = conv[:, hw : hw + n].astype(BF)
        ct = conv[:, hw + n :].astype(BF)
        dtable_ref[width + 2 : width + 3, :hw] += jnp.sum(dy * values, 0, keepdims=True)
        raw, steps = step_table(proj_ref[rows, 2 * hw + state2 :], bias, heads, s)
        logs = exact(causal.astype(F32), steps * rate)
        logs_t, steps_t = logs.T, steps.T
        end = logs[GROUP - 1 : GROUP, :]
        rest = jnp.exp(end - logs)
        tail = rest * steps
        ends = jnp.exp(end)
        before = entry_ref[c]
        before_low = before.astype(BF)
        later = adjoint[...]
        later_low = later.astype(BF)
        tails = spread_heads(tail, heads, head_dim)
        dy_carried = dy * spread_heads(jnp.exp(logs), heads, head_dim)
        dy_carried_low = dy_carried.astype(BF)
        carried = mm(ct, before_low)
        back = mm(b, later_low)
        dvalues = tails * back + skip * dy
        dc = mm_t(dy_carried_low, before_low)
        db = mm_t((values * tails).astype(BF), later_low)
        kept = jnp.sum(later * before, 0, keepdims=True)
        adjoint[...] = spread_heads(ends, heads, head_dim) * later + t_mm(ct, dy_carried_low)
        sums = exact(jnp.concatenate([dy_carried * carried, values * back, jnp.broadcast_to(kept, (8, hw))], 0), pick)
        from_carried, dtail, kept = sums[:GROUP], sums[GROUP : 2 * GROUP], sums[2 * GROUP : 2 * GROUP + 1]
        cross = mm_t(ct, b)
        low = values.astype(BF)
        dy_low = dy.astype(BF)
        dcross = jnp.zeros((GROUP, GROUP), F32)
        dlogs = from_carried - dtail * tail
        columns = []
        tiles = []
        for h in range(0, heads, per):
            part = low[:, h * head_dim : h * head_dim + 128]
            dy_part = dy_low[:, h * head_dim : h * head_dim + 128]
            tile = None
            for i in range(per):
                gap = logs[:, h + i : h + i + 1] - logs_t[h + i : h + i + 1, :]
                kernel = jnp.exp(jnp.where(causal, gap, -1e30))
                scaled = kernel * steps_t[h + i : h + i + 1, :]
                weights = cross * scaled
                inside_head = (lane >= i * head_dim) & (lane < (i + 1) * head_dim)
                one = t_mm(weights.astype(BF), dy_part)
                tile = one if i == 0 else jnp.where(lane >= i * head_dim, one, tile)
                dweights = mm_t(jnp.where(inside_head, dy_part, jnp.zeros_like(dy_part)), part)
                dcross = dcross + dweights * scaled
                unscaled = dweights * (cross * kernel)
                total = jnp.sum(dweights * weights, 1, keepdims=True)
                dlogs = dlogs + jnp.where(lane == h + i, total, 0.0)
                columns.append(jnp.sum(unscaled, 0, keepdims=True))
            tiles.append(tile)
        dvalues = dvalues + jnp.concatenate(tiles, 1)
        columns = jnp.concatenate(columns + [jnp.zeros((128 - heads, GROUP), F32)], 0).T
        dlogs = dlogs - columns * steps
        at_end = jnp.sum(dtail * tail, 0, keepdims=True) + ends * kept
        dlogs = dlogs + jnp.where(row == GROUP - 1, at_end, 0.0)
        da = exact(triangle(True).astype(F32), dlogs)
        dsteps = columns + dtail * rest + da * rate
        dhead_ref[1:2, :] += jnp.sum(da * steps, 0, keepdims=True)
        draw = jnp.where(lane < heads, dsteps * sigmoid(raw), 0.0)
        dhead_ref[0:1, :] += jnp.sum(draw, 0, keepdims=True)
        dproj_ref[rows, 2 * hw + state2 :] = pltpu.roll(draw, heads * s, 1).astype(BF)
        dcross_low = dcross.astype(BF)
        dc = dc + mm(dcross_low, b)
        db = db + t_mm(dcross_low, ct)
        dmix = jnp.concatenate([dvalues, db, dc], 1) * (sig + conv * (1 - sig))
        dtable_ref[width : width + 1, :] += jnp.sum(dmix, 0, keepdims=True)
        ext = with_before(proj_ref, at, slice(hw, 2 * hw + state2), c == 0)
        dext = jnp.concatenate([dmix, after[...]], 0)
        dconv = 0.0
        for j in range(width):
            first = 8 - width + 1 + j
            dtable_ref[j : j + 1, :] += jnp.sum(dmix * ext[first : first + GROUP], 0, keepdims=True)
            dconv = dconv + table[j : j + 1] * dext[width - 1 - j : width - 1 - j + GROUP]
        after[...] = dmix[:8]
        dproj_ref[rows, hw : 2 * hw + state2] = dconv.astype(BF)
        ring.step(lap + 2)
        return carry

    lax.fori_loop(0, blocks, chunk, 0)
    model = resid_all.shape[2]
    every = resid_all[...].reshape(blocks * GROUP, model)
    for d in range(0, hw, 128):
        low_t = low_ref[:, d : d + 128].T
        grad_out_ref[d : d + 128, :] = mm(low_t, every).astype(BF)
    for k in range(blocks + 2, ne - 1):
        ring.step(k)
    ring.finish(sum_ref)
    rows_in.drain()


def mix_backward(
    proj,
    table,
    head_table,
    scanned,
    mixed,
    entries,
    out_local,
    resid_low,
    scales,
    out_part,
    ns,
    ne,
    hw,
    state2,
    heads,
    width,
    cid,
):
    whole = proj.shape[0]
    n = state2 // 2
    rows, model = resid_low.shape
    return pl.pallas_call(
        functools.partial(mix_backward_kernel, ns, ne, hw, state2, heads, width),
        out_shape=(
            jax.ShapeDtypeStruct((rows, model), F32),
            jax.ShapeDtypeStruct(proj.shape, BF),
            jax.ShapeDtypeStruct((hw, model), BF),
            jax.ShapeDtypeStruct((8, hw + state2), F32),
            jax.ShapeDtypeStruct((8, 128), F32),
        ),
        in_specs=[VMEM] * 10,
        out_specs=(VMEM,) * 5,
        scratch_shapes=[
            pltpu.VMEM((n, hw), F32),
            pltpu.VMEM((8, hw + state2), F32),
            pltpu.VMEM((whole, hw), BF),
            pltpu.VMEM((ns, rows, model), BF),
            pltpu.VMEM((ns, 8, rows), F32),
        ]
        + RingSum.scratch(ne, 2, rows, model)
        + SeqGather.scratch(ns),
        compiler_params=params(cid),
        name="mix_backward",
    )(proj, table, head_table, scanned, mixed, entries, out_local, resid_low, scales, out_part)


def rms_back(value, gain, grad):
    scale = lax.rsqrt(jnp.mean(value * value, -1, keepdims=True) + EPSILON)
    inside = gain * grad
    back = scale * inside - value * scale**3 * jnp.mean(value * inside, -1, keepdims=True)
    return back, jnp.sum(value * scale * grad, 0)


def swiglu_back(a, b, grad):
    sig = jax.nn.sigmoid(a)
    return grad * b * sig * (1 + a * (1 - sig)), grad * a * sig


def on_device(
    tokens,
    routes,
    out_grad,
    norm_mix,
    in_weight,
    step_weight,
    conv_weight,
    conv_bias,
    step_bias,
    decay_log,
    skip_gain,
    norm_gate,
    out_weight,
    norm_ffn,
    router_weight,
    shared_gate,
    shared_up,
    shared_down,
    expert_gate,
    expert_up,
    expert_down,
):
    ns, ne = lax.axis_size("seq"), lax.axis_size("exp")
    s, e = lax.axis_index("seq"), lax.axis_index("exp")
    total = ns * ne
    rows, columns = in_weight.shape
    model = tokens.shape[2]
    length = tokens.shape[1]
    whole = length * ns
    width, channels = conv_weight.shape
    gains = norm_gate.shape[0]
    inner = gains * total
    hw = inner // ns
    heads = step_bias.shape[0]
    local_heads = heads // ns
    state2 = columns - 2 * inner
    experts = router_weight.shape[1]
    local_experts = expert_gate.shape[0]
    place = s * ne + e

    small = jnp.concatenate([conv_weight.reshape(-1), conv_bias, norm_gate])
    small = jnp.pad(small, (0, 16 * rows - small.shape[0])).reshape(rows, 16)
    pack = jnp.concatenate(
        [step_weight, router_weight, norm_mix[:, None], norm_ffn[:, None], small], 1
    )
    at_small = heads + experts + 2
    pack = jnp.pad(pack, ((0, 0), (0, 128 - pack.shape[1])))
    hidden_rows = shared_down.shape[0]

    def by_owner(weight):
        split = weight.reshape(rows, ns, ne, hidden_rows)
        return jnp.transpose(split, (2, 0, 1, 3)).reshape(ne, rows, ns * hidden_rows)

    shared_two = jnp.concatenate([by_owner(shared_gate), by_owner(shared_up)], -1)
    in_blocks, token_blocks, out_local, shared_two, local_down = gather_in(
        in_weight, pack, tokens[0], out_weight, shared_two, shared_down, ns, ne, inner, 0
    )
    out_local = out_local.reshape(hw, model)
    shared_two = shared_two.reshape(model, 2 * ns * hidden_rows)
    local_gate, local_up = shared_two[:, : ns * hidden_rows], shared_two[:, ns * hidden_rows :]
    local_down = local_down.reshape(ns * hidden_rows, model)
    grad_low = out_grad[0]
    in_local = in_blocks.reshape(model, -1)
    full_pack = in_local[:, 2 * hw + state2 :]
    full_router = full_pack[:, heads : heads + experts]
    full_norm_mix = full_pack[:, heads + experts].astype(F32)
    full_norm_ffn = full_pack[:, heads + experts + 1].astype(F32)
    full_small = full_pack[:, at_small : at_small + 16].reshape(total, 16 * rows).astype(F32)
    full_conv = full_small[:, : (width + 1) * channels].reshape(total, width + 1, channels)
    full_conv = jnp.swapaxes(full_conv, 0, 1).reshape(width + 1, total * channels)
    at_gain = (width + 1) * channels
    full_norm_gate = full_small[:, at_gain : at_gain + gains].reshape(inner)
    local_conv = jnp.concatenate(
        [lax.dynamic_slice_in_dim(full_conv, s * hw, hw, 1), full_conv[:, inner:]], 1
    )
    local_gain = lax.dynamic_slice_in_dim(full_norm_gate, s * hw, hw)
    at_head = s * local_heads
    local_bias = lax.dynamic_slice_in_dim(step_bias, at_head, local_heads)
    local_decay = lax.dynamic_slice_in_dim(decay_log, at_head, local_heads)
    local_skip = lax.dynamic_slice_in_dim(skip_gain, at_head, local_heads)

    table = jnp.concatenate(
        [
            local_conv,
            jnp.pad(
                jnp.stack([local_gain, jnp.repeat(local_skip, hw // local_heads)]),
                ((0, 6 - width - 1), (0, state2)),
            ),
        ],
        0,
    )
    head_table = jnp.pad(
        jnp.stack([local_bias, -jnp.exp(local_decay)]), ((0, 6), (0, 128 - local_heads))
    )

    token_rows = tokens[0].astype(F32)
    sequence = token_blocks.reshape(whole, model).astype(F32)
    scale_one = lax.rsqrt(jnp.mean(sequence * sequence, -1, keepdims=True) + EPSILON)
    lowered = (sequence * scale_one * full_norm_mix).astype(BF)
    projected = matmul_plain(lowered, in_local)
    scanned, mixed, entries, mixed_raw, squares, grad_all = mix_forward(
        projected, table, head_table, out_local, grad_low, ns, ne, hw, state2, local_heads, width, 1
    )
    scale_gate = lax.rsqrt(squares[0] / inner + EPSILON)
    mixer_out = mixed_raw * scale_gate[:, None]
    resid = token_rows + mixer_out
    scale_two = lax.rsqrt(jnp.mean(resid * resid, -1, keepdims=True) + EPSILON)
    ffn_in = (resid * scale_two * full_norm_ffn).astype(BF)

    logits = matmul_plain(ffn_in, full_router)
    named = jnp.any(
        routes[0][:, :, None] == jnp.arange(experts, dtype=jnp.int32)[None, None, :], 1
    )
    top = jnp.max(jnp.where(named, logits, -jnp.inf), -1, keepdims=True)
    raised = jnp.where(named, jnp.exp(jnp.where(named, logits - top, 0.0)), 0.0)
    gates = (raised / jnp.sum(raised, -1, keepdims=True)).T

    gates_out = jnp.pad(
        gates.reshape(ne, local_experts, length), ((0, 0), (0, 8 - local_experts), (0, 0))
    )
    back_sum, gate_grads, out_part, weight_grads, grad_shared_down = experts_both_ways(
        ffn_in, gates_out, grad_all, expert_gate, expert_up, expert_down, shared_two, local_down, ne, 2
    )
    gate_grads = gate_grads[:, :local_experts].reshape(experts, length)
    weight_grads = lax.psum_scatter(weight_grads, "seq", scatter_dimension=0, tiled=True)
    grad_shared_down = lax.psum_scatter(
        grad_shared_down, "seq", scatter_dimension=0, tiled=True
    ).astype(F32)
    experts_wide = 3 * local_experts * expert_gate.shape[2]
    shared_parts = lax.all_to_all(
        weight_grads[:, experts_wide:].reshape(ne, rows, -1),
        "exp",
        split_axis=0,
        concat_axis=0,
        tiled=True,
    ).astype(F32)
    expert_parts = weight_grads[:, :experts_wide].astype(F32)
    expert_parts = expert_parts.reshape(model // ns, local_experts, 3, -1)
    expert_parts = [
        jnp.swapaxes(expert_parts[:, :, 0], 0, 1),
        jnp.swapaxes(expert_parts[:, :, 1], 0, 1),
        jnp.transpose(expert_parts[:, :, 2], (1, 2, 0)),
    ]

    def to_rows(piece):
        piece = piece.reshape(ne, rows, ns, hidden_rows)
        return jnp.transpose(piece, (1, 2, 0, 3)).reshape(rows, total * hidden_rows)

    grad_shared_gate = to_rows(shared_parts[:, :, : ns * hidden_rows])
    grad_shared_up = to_rows(shared_parts[:, :, ns * hidden_rows :])

    picked_grad = gates * (gate_grads - jnp.sum(gates * gate_grads, 0, keepdims=True))
    logit_grad = picked_grad.T.astype(BF)
    grad_router = matmul_rows(ffn_in, logit_grad)
    ffn_in_grad = matmul_cols(logit_grad, full_router) + back_sum
    resid_norm_grad, grad_norm_ffn = rms_back(resid, full_norm_ffn, ffn_in_grad)
    resid_grad = grad_low.astype(F32) + resid_norm_grad
    resid_low = resid_grad.astype(BF)
    inside = jnp.sum(resid_low.astype(F32) * mixer_out, -1) / (scale_gate * inner)
    scales = jnp.concatenate(
        [scale_gate[None], inside[None], jnp.zeros((6, length), F32)], 0
    )

    ffn_out, projected_grad, grad_out, table_grad, head_grad = mix_backward(
        projected,
        table,
        head_table,
        scanned,
        mixed,
        entries,
        out_local,
        resid_low,
        scales,
        out_part,
        ns,
        ne,
        hw,
        state2,
        local_heads,
        width,
        4,
    )
    result = (resid + ffn_out).astype(BF)
    stat_terms = jnp.stack(
        [jnp.sum(resid * resid), jnp.sum(mixer_out * mixer_out), jnp.sum(ffn_out * ffn_out)]
    )
    grad_gain = table_grad[width + 1, :hw]
    grad_skip = jnp.sum(table_grad[width + 2, :hw].reshape(local_heads, -1), -1)
    grad_step_bias = head_grad[0, :local_heads]
    grad_decay = head_grad[1, :local_heads] * head_table[1, :local_heads]
    lowered_part = matmul_cols(projected_grad, in_local).astype(BF)
    lowered_grad, _ = sum_seq(
        lowered_part.reshape(ns, length, model), jnp.zeros((ns, 8, length), F32), ns, 5
    )
    tokens_norm_grad, grad_norm_mix = rms_back(token_rows, full_norm_mix, lowered_grad)
    tokens_grad = (resid_grad + tokens_norm_grad).astype(BF)

    conv_grads = table_grad[: width + 1]
    wide = jnp.zeros((width + 1, total * channels), F32)
    wide = lax.dynamic_update_slice(wide, conv_grads[:, :hw], (0, s * hw))
    wide = lax.dynamic_update_slice(wide, conv_grads[:, hw:], (0, inner))
    wide_gain = lax.dynamic_update_slice(jnp.zeros((inner,), F32), grad_gain, (s * hw,))
    wide_heads = lax.dynamic_update_slice(
        jnp.zeros((3, heads), F32),
        jnp.stack([grad_step_bias, grad_decay, grad_skip]),
        (0, at_head),
    )
    sums = lax.psum(
        (wide, wide_gain, wide_heads, grad_router, grad_norm_mix, grad_norm_ffn, stat_terms),
        ("seq", "exp"),
    )
    wide, wide_gain, wide_heads, grad_router, grad_norm_mix, grad_norm_ffn, stat_terms = sums
    conv_grads = lax.dynamic_slice_in_dim(wide, place * channels, channels, 1)

    grad_in = matmul_rows(lowered, projected_grad).astype(BF)
    pieces, grad_out = sum_weights(
        grad_in.reshape(ns, ne, rows, -1),
        grad_out.reshape(ne, hw // ne, model),
        ns,
        ne,
        6,
    )
    pieces = pieces.astype(F32)
    grad_in = jnp.concatenate(
        [
            jnp.swapaxes(pieces[:, :, :hw], 0, 1).reshape(rows, inner),
            jnp.swapaxes(pieces[:, :, hw : 2 * hw], 0, 1).reshape(rows, inner),
            jnp.sum(pieces[:, :, 2 * hw : 2 * hw + state2], 0),
        ],
        1,
    )
    grad_step = jnp.sum(pieces[:, :, 2 * hw + state2 : 2 * hw + state2 + heads], 0)
    return (
        result[None],
        tokens_grad[None],
        lax.dynamic_slice_in_dim(grad_norm_mix, place * rows, rows),
        grad_in,
        grad_step,
        conv_grads[:width],
        conv_grads[width],
        wide_heads[0],
        wide_heads[1],
        wide_heads[2],
        lax.dynamic_slice_in_dim(wide_gain, place * gains, gains),
        grad_out,
        lax.dynamic_slice_in_dim(grad_norm_ffn, place * rows, rows),
        lax.dynamic_slice_in_dim(grad_router, place * rows, rows),
        grad_shared_gate,
        grad_shared_up,
        grad_shared_down,
        expert_parts[0],
        expert_parts[1],
        expert_parts[2],
        stat_terms / (total * length * model),
    )


def solution(mesh):
    both = ("seq", "exp")
    return jax.shard_map(
        on_device,
        mesh=mesh,
        in_specs=(
            P("exp", "seq", None),
            P("exp", "seq", None),
            P("exp", "seq", None),
            P(both),
            P(both, None),
            P(both, None),
            P(None, both),
            P(both),
            P(),
            P(),
            P(),
            P(both),
            P(both, None),
            P(both),
            P(both, None),
            P(both, None),
            P(both, None),
            P(both, None),
            P("exp", None, None),
            P("exp", None, None),
            P("exp", None, None),
        ),
        out_specs=(
            P("exp", "seq", None),
            P("exp", "seq", None),
            P(both),
            P(both, None),
            P(both, None),
            P(None, both),
            P(both),
            P(),
            P(),
            P(),
            P(both),
            P(both, None),
            P(both),
            P(both, None),
            P(both, None),
            P(both, None),
            P(both, None),
            P("exp", "seq", None),
            P("exp", "seq", None),
            P("exp", None, "seq"),
            P(),
        ),
        check_vma=False,
    )
```

```python
import functools

import jax
import jax.numpy as jnp
from jax import lax
from jax.experimental import pallas as pl
from jax.experimental.pallas import tpu as pltpu
from jax.sharding import PartitionSpec as P

GROUP = 128
EPSILON = 1e-05
PRECISE = lax.Precision.HIGHEST
MESH = pl.DeviceIdType.MESH
BF = jnp.bfloat16
F32 = jnp.float32
ANY = pl.BlockSpec(memory_space=pl.ANY)
VMEM = pl.BlockSpec(memory_space=pltpu.VMEM)
DMA = pltpu.SemaphoreType.DMA


def ring_place(e, n):
    odd = e % 2
    return (1 - odd) * (e // 2) + odd * (n - 1 - e // 2)


def ring_index(p, n):
    back = p // (n // 2)
    return (1 - back) * (2 * p) + back * (2 * (n - 1 - p) + 1)


def ring_sides(e, n):
    p = ring_place(e, n)
    return p, ring_index((p + 1) % n, n), ring_index((p + n - 1) % n, n)


def greet(partners):
    barrier = pltpu.get_barrier_semaphore()
    for partner in partners:
        pl.semaphore_signal(barrier, inc=1, device_id=partner, device_id_type=MESH)
    pl.semaphore_wait(barrier, len(partners))


def remote(src, dst, send, recv, device):
    copy = pltpu.make_async_remote_copy(
        src_ref=src,
        dst_ref=dst,
        send_sem=send,
        recv_sem=recv,
        device_id=device,
        device_id_type=MESH,
    )
    copy.start()
    return copy


def params(cid, mib=48):
    return pltpu.CompilerParams(
        collective_id=cid, has_side_effects=True, vmem_limit_bytes=mib << 20
    )


class Loads:
    def __init__(self, sources, held, sems):
        self.copies = [
            pltpu.make_async_copy(src, dst, sems.at[i])
            for i, (src, dst) in enumerate(zip(sources, held))
        ]

    @staticmethod
    def scratch(arrays):
        return [pltpu.VMEM(v.shape, v.dtype) for v in arrays] + [DMA((len(arrays),))]

    def begin(self):
        for copy in self.copies:
            copy.start()

    def wait(self, *which):
        for i in which:
            self.copies[i].wait()


def tile_rows(rows, most=16):
    return most if rows % most == 0 else rows


def gather_in_kernel(
    ns,
    ne,
    hw,
    inner,
    in_ref,
    pack_ref,
    tok_ref,
    out_ref,
    two_ref,
    down_ref,
    w_ref,
    x_ref,
    o_ref,
    shared_ref,
    sd_ref,
    lsem,
    ssem0,
    rsem0,
    ssem,
    rsem,
    sa,
    ra,
    sb,
    rb,
):
    s, e = lax.axis_index("seq"), lax.axis_index("exp")
    p, right, left = ring_sides(e, ne)
    width = in_ref.shape[1] - 2 * inner
    half = out_ref.shape[1] // 2
    parts = (
        (lambda to: in_ref.at[:, pl.ds(pl.multiple_of(to * hw, 128), hw)], 0, hw),
        (lambda to: in_ref.at[:, pl.ds(pl.multiple_of(inner + to * hw, 128), hw)], hw, hw),
        (lambda to: in_ref.at[:, pl.ds(2 * inner, width)], 2 * hw, width),
        (lambda to: pack_ref, 2 * hw + width, pack_ref.shape[1]),
    )
    greet([((s + t) % ns, e) for t in range(1, ns)] + [(s, (e + t) % ne) for t in range(1, ne)])
    own = []
    for i, (piece, start, size) in enumerate(parts):
        own.append(
            pltpu.make_async_copy(piece(s), w_ref.at[s, e, :, pl.ds(start, size)], lsem.at[i])
        )
    own.append(pltpu.make_async_copy(out_ref, o_ref.at[e], lsem.at[4]))
    own.append(pltpu.make_async_copy(two_ref.at[e], shared_ref.at[s, e], lsem.at[5]))
    own.append(pltpu.make_async_copy(tok_ref, x_ref.at[s], lsem.at[6]))
    own.append(pltpu.make_async_copy(down_ref, sd_ref.at[s], lsem.at[7]))
    for copy in own:
        copy.start()
    first = {}
    for t in range(1, ns):
        to = (s + t) % ns
        for i, (piece, start, size) in enumerate(parts):
            first[t, i] = remote(
                piece(to),
                w_ref.at[s, e, :, pl.ds(start, size)],
                ssem0.at[t - 1, i],
                rsem0.at[t - 1, i],
                (to, e),
            )
    for copy in own:
        copy.wait()
    sent = {}
    across = {}
    along = {}
    for k in range(ne - 1):
        for t in range(ns + 2):
            way = t % 2
            to = (s, right if way == 0 else left)
            place = (p - k + ne) % ne if way == 0 else (p + k) % ne
            slot = ring_index(place, ne)
            if k > 0:
                sent[k - 1, t].wait_recv()
            elif 0 < t < ns:
                for i in range(len(parts)):
                    first[t, i].wait_recv()
            if t < ns:
                block = w_ref.at[(s + ns - t) % ns, slot]
            else:
                block = o_ref.at[slot, :, pl.ds(way * half, half)]
            sent[k, t] = remote(block, block, ssem.at[k, t], rsem.at[k, t], to)
        if k == 0:
            for t in range(1, ns):
                to = ((s + t) % ns, e)
                first[t, 4] = remote(
                    tok_ref, x_ref.at[s], ssem0.at[t - 1, 4], rsem0.at[t - 1, 4], to
                )
                first[t, 5] = remote(
                    down_ref, sd_ref.at[s], ssem0.at[t - 1, 5], rsem0.at[t - 1, 5], to
                )
            for t in range(1, ne):
                to = (e + t) % ne
                across[t] = remote(
                    two_ref.at[to], shared_ref.at[s, e], sa.at[t - 1], ra.at[t - 1], (s, to)
                )
        if k == 2:
            for t in range(1, ne):
                across[t].wait_recv()
            for t in range(1, ns):
                along[t] = remote(
                    shared_ref.at[s], shared_ref.at[s], sb.at[t - 1], rb.at[t - 1], ((s + t) % ns, e)
                )
    for t in range(ns + 2):
        sent[ne - 2, t].wait_recv()
    for t in range(1, ns):
        first[t, 4].wait_recv()
        first[t, 5].wait_recv()
        along[t].wait_recv()
    for group in (first, sent, across, along):
        for copy in group.values():
            copy.wait_send()


def gather_in(in_weight, pack, tokens, out_weight, shared_two, shared_down, ns, ne, inner, cid):
    rows, columns = in_weight.shape
    hw = inner // ns
    wide = 2 * hw + columns - 2 * inner + pack.shape[1]
    return pl.pallas_call(
        functools.partial(gather_in_kernel, ns, ne, hw, inner),
        out_shape=(
            jax.ShapeDtypeStruct((ns, ne, rows, wide), BF),
            jax.ShapeDtypeStruct((ns,) + tokens.shape, BF),
            jax.ShapeDtypeStruct((ne,) + out_weight.shape, BF),
            jax.ShapeDtypeStruct((ns,) + shared_two.shape, BF),
            jax.ShapeDtypeStruct((ns,) + shared_down.shape, BF),
        ),
        in_specs=[ANY] * 6,
        out_specs=(ANY,) * 5,
        scratch_shapes=[
            DMA((8,)),
            DMA((ns - 1, 6)),
            DMA((ns - 1, 6)),
            DMA((ne - 1, ns + 2)),
            DMA((ne - 1, ns + 2)),
            DMA((ne - 1,)),
            DMA((ne - 1,)),
            DMA((ns - 1,)),
            DMA((ns - 1,)),
        ],
        compiler_params=params(cid, 8),
        name="gather_in",
    )(in_weight, pack, tokens, out_weight, shared_two, shared_down)


class SeqSum:
    def __init__(self, ns, subs, part, aux, one, two, aux_in, s1, r1, s2, r2, sa, ra):
        self.s, self.e = lax.axis_index("seq"), lax.axis_index("exp")
        self.ns, self.ny, self.subs = ns, ns // 2, subs
        self.y, self.c = self.s // 2, self.s % 2
        self.part, self.aux, self.one, self.two, self.aux_in = part, aux, one, two, aux_in
        self.sems = (s1, r1, s2, r2, sa, ra)
        self.step = part.shape[1] // subs
        self.tile = tile_rows(self.step)
        self.first, self.second, self.extra = {}, {}, []

    @staticmethod
    def scratch(ns, subs, rows, width, aux_shape):
        ny = ns // 2
        return [
            pltpu.VMEM((ny, rows, width), BF),
            pltpu.VMEM((max(ny - 1, 1), rows, width), BF),
            pltpu.VMEM((ns - 1,) + aux_shape, F32),
            DMA((ny, subs)),
            DMA((ny, subs)),
            DMA((max(ny - 1, 1), subs)),
            DMA((max(ny - 1, 1), subs)),
            DMA((ns - 1,)),
            DMA((ns - 1,)),
        ]

    def rows(self, u):
        return pl.ds(u * self.step, self.step)

    def send_aux(self):
        s1, r1, s2, r2, sa, ra = self.sems
        for t in range(1, self.ns):
            to = (self.s + t) % self.ns
            self.extra.append(
                remote(
                    self.aux.at[to], self.aux_in.at[t - 1], sa.at[t - 1], ra.at[t - 1], (to, self.e)
                )
            )

    def order(self):
        return list(range(1, self.ny)) + [0]

    def far(self, j):
        return 2 * ((self.y + j) % self.ny) + 1 - self.c

    def near(self, j):
        return 2 * ((self.y + j) % self.ny) + self.c

    def send(self, j):
        s1, r1, s2, r2, sa, ra = self.sems
        mate = (2 * self.y + 1 - self.c, self.e)
        for u in range(self.subs):
            self.first[j, u] = remote(
                self.part.at[self.far(j), self.rows(u)],
                self.one.at[j, self.rows(u)],
                s1.at[j, u],
                r1.at[j, u],
                mate,
            )

    def begin(self, fill):
        self.send_aux()
        for j in self.order():
            fill(self.far(j))
            self.send(j)
        for j in self.order():
            fill(self.near(j))

    def join(self, j, u):
        s1, r1, s2, r2, sa, ra = self.sems
        to = self.near(j)
        self.first[j, u].wait_recv()

        def add(i, carry):
            r = pl.ds(pl.multiple_of(u * self.step + i * self.tile, self.tile), self.tile)
            total = self.one[j, r, :].astype(F32) + self.part[to, r, :].astype(F32)
            self.one[j, r, :] = total.astype(BF)
            return carry

        lax.fori_loop(0, self.step // self.tile, add, 0)
        self.second[j, u] = remote(
            self.one.at[j, self.rows(u)],
            self.two.at[j - 1, self.rows(u)],
            s2.at[j - 1, u],
            r2.at[j - 1, u],
            (to, self.e),
        )

    def middle(self):
        for j in range(1, self.ny):
            for u in range(self.subs):
                self.join(j, u)

    def close(self, u, out):
        self.first[0, u].wait_recv()
        for j in range(1, self.ny):
            self.second[j, u].wait_recv()

        def add(i, carry):
            r = pl.ds(pl.multiple_of(u * self.step + i * self.tile, self.tile), self.tile)
            total = self.one[0, r, :].astype(F32) + self.part[self.s, r, :].astype(F32)
            for j in range(1, self.ny):
                total = total + self.two[j - 1, r, :].astype(F32)
            out[r, :] = total
            return carry

        lax.fori_loop(0, self.step // self.tile, add, 0)

    def finish(self, out, aux_out):
        for u in range(self.subs):
            self.close(u, out)
        total = self.aux[self.s]
        for t in range(1, self.ns):
            self.extra[t - 1].wait_recv()
            total = total + self.aux_in[t - 1]
        aux_out[...] = total

    def drain(self):
        for copy in list(self.first.values()) + list(self.second.values()) + self.extra:
            copy.wait_send()


class BlockSum:
    def __init__(self, ns, sources, outs, scratch):
        self.s, self.e = lax.axis_index("seq"), lax.axis_index("exp")
        self.ns, self.ny = ns, ns // 2
        self.y, self.c = self.s // 2, self.s % 2
        self.sources, self.outs = sources, outs
        self.items = [(m, i) for m, src in enumerate(sources) for i in range(src.shape[1])]
        count = len(sources)
        self.held, self.one, self.two = (
            scratch[:count],
            scratch[count : 2 * count],
            scratch[2 * count : 3 * count],
        )
        self.lsem, self.s1, self.r1, self.s2, self.r2 = scratch[3 * count :]
        self.loads = [
            pltpu.make_async_copy(src, held, self.lsem.at[m])
            for m, (src, held) in enumerate(zip(self.sources, self.held))
        ]
        self.first, self.second = {}, {}

    @staticmethod
    def scratch(ns, shapes):
        ny = ns // 2
        items = sum(shape[1] for shape in shapes)
        return (
            [pltpu.VMEM(shape, BF) for shape in shapes]
            + [pltpu.VMEM((ny,) + shape[1:], BF) for shape in shapes]
            + [pltpu.VMEM((max(ny - 1, 1),) + shape[1:], BF) for shape in shapes]
            + [
                DMA((len(shapes),)),
                DMA((ny, items)),
                DMA((ny, items)),
                DMA((max(ny - 1, 1), items)),
                DMA((max(ny - 1, 1), items)),
            ]
        )

    def load(self):
        for copy in self.loads:
            copy.start()

    def begin(self):
        mate = (2 * self.y + 1 - self.c, self.e)
        for copy in self.loads:
            copy.wait()
        for j in list(range(1, self.ny)) + [0]:
            block = 2 * ((self.y + j) % self.ny) + 1 - self.c
            for n, (m, i) in enumerate(self.items):
                self.first[j, n] = remote(
                    self.held[m].at[block, i],
                    self.one[m].at[j, i],
                    self.s1.at[j, n],
                    self.r1.at[j, n],
                    mate,
                )

    def tiles(self, shape, body):
        if len(shape) == 3:
            lax.fori_loop(0, shape[0], lambda i, carry: body((i,)) or carry, 0)
        else:
            size = 32 if shape[0] % 32 == 0 else shape[0]
            lax.fori_loop(
                0,
                shape[0] // size,
                lambda i, carry: body((pl.ds(pl.multiple_of(i * size, size), size),)) or carry,
                0,
            )

    def join(self, j, n):
        m, i = self.items[n]
        to = 2 * ((self.y + j) % self.ny) + self.c
        self.first[j, n].wait_recv()
        one, held = self.one[m], self.held[m]

        def add(at):
            total = one[(j, i) + at].astype(F32) + held[(to, i) + at].astype(F32)
            one[(j, i) + at] = total.astype(BF)

        self.tiles(one.shape[2:], add)
        self.second[j, n] = remote(
            one.at[j, i],
            self.two[m].at[j - 1, i],
            self.s2.at[j - 1, n],
            self.r2.at[j - 1, n],
            (to, self.e),
        )

    def close(self, n):
        m, i = self.items[n]
        self.first[0, n].wait_recv()
        for j in range(1, self.ny):
            self.second[j, n].wait_recv()
        one, held, two, out = self.one[m], self.held[m], self.two[m], self.outs[m]

        def add(at):
            total = one[(0, i) + at].astype(F32) + held[(self.s, i) + at].astype(F32)
            for j in range(1, self.ny):
                total = total + two[(j - 1, i) + at].astype(F32)
            out[(i,) + at] = total

        self.tiles(one.shape[2:], add)

    def drain(self):
        for copy in list(self.first.values()) + list(self.second.values()):
            copy.wait_send()


class RingGather:
    def __init__(self, ne, v, out, lsem, ssem, rsem):
        self.s, self.e = lax.axis_index("seq"), lax.axis_index("exp")
        self.ne, self.v, self.out = ne, v, out
        self.p, self.right, self.left = ring_sides(self.e, ne)
        self.ssem, self.rsem = ssem, rsem
        self.subs = ssem.shape[2]
        self.step_rows = v.shape[0] // (2 * self.subs)
        self.own = pltpu.make_async_copy(v, out.at[self.e], lsem)

    @staticmethod
    def scratch(ne, subs):
        return [DMA, DMA((ne - 1, 2, subs)), DMA((ne - 1, 2, subs))]

    def copy(self, k, way, u, src=None):
        place = (self.p - k + self.ne) % self.ne if way == 0 else (self.p + k) % self.ne
        slot = ring_index(place, self.ne)
        rows = pl.ds((way * self.subs + u) * self.step_rows, self.step_rows)
        block = self.out.at[slot, rows]
        return pltpu.make_async_remote_copy(
            src_ref=block if src is None else src.at[rows],
            dst_ref=block,
            send_sem=self.ssem.at[k, way, u],
            recv_sem=self.rsem.at[k, way, u],
            device_id=(self.s, self.right if way == 0 else self.left),
            device_id_type=MESH,
        )

    def begin(self):
        self.own.start()
        for u in range(self.subs):
            for way in range(2):
                self.copy(0, way, u, self.v).start()

    def step(self, k):
        for u in range(self.subs):
            for way in range(2):
                self.copy(k - 1, way, u).wait_recv()
                self.copy(k, way, u).start()

    def forward(self, k):
        for u in range(self.subs):
            for way in range(2):
                self.copy(k, way, u).start()

    def arrived(self, k):
        for u in range(self.subs):
            for way in range(2):
                self.copy(k, way, u).wait_recv()

    def drain(self):
        for k in range(self.ne - 1):
            for u in range(self.subs):
                for way in range(2):
                    self.copy(k, way, u).wait_send()

    def finish(self):
        self.arrived(self.ne - 2)
        self.drain()
        self.own.wait()


class RingSum:
    def __init__(self, ne, part, acc, ssem, rsem):
        self.s, self.e = lax.axis_index("seq"), lax.axis_index("exp")
        self.ne, self.part, self.acc = ne, part, acc
        self.p, self.right, self.left = ring_sides(self.e, ne)
        self.ssem, self.rsem = ssem, rsem
        self.subs = ssem.shape[2]
        self.size = part.shape[1] // (2 * self.subs)
        self.tile = tile_rows(self.size)

    @staticmethod
    def scratch(ne, subs, rows, width):
        return [
            pltpu.VMEM((ne - 1, rows, width), BF),
            DMA((ne - 1, 2, subs)),
            DMA((ne - 1, 2, subs)),
        ]

    def slot(self, k, way):
        place = (self.p - 1 - k + 2 * self.ne) % self.ne if way == 0 else (self.p + 1 + k) % self.ne
        return ring_index(place, self.ne)

    def copy(self, k, way, u, src=None):
        rows = pl.ds((way * self.subs + u) * self.size, self.size)
        return pltpu.make_async_remote_copy(
            src_ref=self.acc.at[k, rows] if src is None else src.at[rows],
            dst_ref=self.acc.at[k, rows],
            send_sem=self.ssem.at[k, way, u],
            recv_sem=self.rsem.at[k, way, u],
            device_id=(self.s, self.right if way == 0 else self.left),
            device_id_type=MESH,
        )

    def add(self, k, way, u, out):
        base = (way * self.subs + u) * self.size
        slot = self.slot(k, way)

        def join(i, carry):
            r = pl.ds(pl.multiple_of(base + i * self.tile, self.tile), self.tile)
            total = self.acc[k - 1, r, :].astype(F32) + self.part[slot, r, :].astype(F32)
            if out is None:
                self.acc[k - 1, r, :] = total.astype(BF)
            else:
                out[r, :] = total
            return carry

        lax.fori_loop(0, self.size // self.tile, join, 0)

    def begin(self):
        for u in range(self.subs):
            for way in range(2):
                self.copy(0, way, u, self.part.at[self.slot(0, way)]).start()

    def step(self, k):
        for u in range(self.subs):
            for way in range(2):
                self.copy(k - 1, way, u).wait_recv()
                self.add(k, way, u, None)
                rows = pl.ds((way * self.subs + u) * self.size, self.size)
                pltpu.make_async_remote_copy(
                    src_ref=self.acc.at[k - 1, rows],
                    dst_ref=self.acc.at[k, rows],
                    send_sem=self.ssem.at[k, way, u],
                    recv_sem=self.rsem.at[k, way, u],
                    device_id=(self.s, self.right if way == 0 else self.left),
                    device_id_type=MESH,
                ).start()

    def finish(self, out):
        k = self.ne - 1
        for u in range(self.subs):
            for way in range(2):
                self.copy(k - 1, way, u).wait_recv()
                self.add(k, way, u, out)
        for k in range(self.ne - 1):
            for u in range(self.subs):
                for way in range(2):
                    self.copy(k, way, u).wait_send()


class Exchange:
    def __init__(self, ne, src, dst, lsem, ssem, rsem, pick=None, spread=False):
        s, e = lax.axis_index("seq"), lax.axis_index("exp")
        if pick is None:
            pick = lambda ref, at: ref.at[at]
        give = (lambda ref, at: ref) if spread else pick
        self.own = pltpu.make_async_copy(give(src, e), pick(dst, e), lsem)
        self.copies = []
        for t in range(1, ne):
            to = (e + t) % ne
            self.copies.append(
                pltpu.make_async_remote_copy(
                    src_ref=give(src, to),
                    dst_ref=pick(dst, e),
                    send_sem=ssem.at[t - 1],
                    recv_sem=rsem.at[t - 1],
                    device_id=(s, to),
                    device_id_type=MESH,
                )
            )

    @staticmethod
    def scratch(ne):
        return [DMA, DMA((ne - 1,)), DMA((ne - 1,))]

    def begin(self):
        self.own.start()
        for copy in self.copies:
            copy.start()

    def arrived(self):
        self.own.wait()
        for copy in self.copies:
            copy.wait_recv()

    def drain(self):
        for copy in self.copies:
            copy.wait_send()


def experts_kernel(
    ne,
    count,
    ffn_ref,
    gate_ref,
    grad_hbm,
    eg_hbm,
    eu_hbm,
    ed_hbm,
    two_hbm,
    sd_hbm,
    back_ref,
    gate_back,
    out_ref,
    dgu_ref,
    dd_ref,
    ds_ref,
    dsd_ref,
    x_ref,
    gates,
    hid_ref,
    da_ref,
    db_ref,
    part_ref,
    gate_part,
    stage_gu,
    stage_d,
    stage_s,
    stage_sem,
    out_stage,
    out_sem,
    *scratch,
):
    s, e = lax.axis_index("seq"), lax.axis_index("exp")
    length, model = ffn_ref.shape
    half = length // 2
    sources = (eg_hbm, eu_hbm, grad_hbm, ed_hbm, two_hbm, sd_hbm)
    eg_ref, eu_ref, grad_ref, ed_ref, two_ref, sd_ref = scratch[12:18]
    loads = Loads(sources, scratch[12:18], scratch[18])
    loads.begin()
    width = eg_ref.shape[2]
    narrow = sd_ref.shape[0]
    tile_width = min(width, 256)
    greet([(s, (e + t) % ne) for t in range(1, ne)])
    ring = RingGather(ne, ffn_ref, x_ref, *scratch[:3])
    there = Exchange(ne, gate_ref, gates, *scratch[3:6])
    back = Exchange(ne, gate_part, gate_back, *scratch[6:9])
    total = RingSum(ne, part_ref, *scratch[9:12])
    ring.begin()
    there.begin()
    gate_part[...] = jnp.zeros_like(gate_part)
    ring.own.wait()
    there.own.wait()
    lane = lax.broadcasted_iota(jnp.int32, (8, length), 1)
    wide_lane = lax.broadcasted_iota(jnp.int32, (2 * length, 128), 1)

    def quarters(i):
        found = []
        for k in (2 * i, 2 * i + 1):
            found.append((ring_index((ring.p - k + ne) % ne, ne), 0))
            found.append((ring_index((ring.p + k) % ne, ne), half))
        return found

    def out_copies(i):
        slot = i % 2
        return [
            pltpu.make_async_copy(
                out_stage.at[slot, pl.ds(n * half, half)],
                out_ref.at[block, pl.ds(first, half)],
                out_sem.at[slot, n],
            )
            for n, (block, first) in enumerate(quarters(i))
        ]

    def rows_of(ref, places, cols):
        return jnp.concatenate(
            [ref[block, first : first + half, cols] for block, first in places], 0
        )

    def store(ref, places, cols, value):
        for n, (block, first) in enumerate(places):
            ref[block, first : first + half, cols] = value[n * half : (n + 1) * half]

    def compute(i):
        places = quarters(i)
        every = slice(0, model)
        x = rows_of(x_ref, places, every)
        g = rows_of(grad_ref, places, every)
        table = jnp.concatenate(
            [
                jnp.where(lane < half, gates[places[n][0]], gates[places[n + 1][0]]).T
                for n in (0, 2)
            ],
            0,
        )
        slots = jnp.zeros((2 * length, 128), F32)
        for j in range(count + 1):
            size = width if j < count else narrow
            column = table[:, j : j + 1] if j < count else None
            for f in range(0, size, tile_width):
                wide = min(tile_width, size - f)
                if j < count:
                    a = mm(x, eg_ref[j, :, f : f + wide])
                    b = mm(x, eu_ref[j, :, f : f + wide])
                    h = mm_t(g, ed_ref[j, f : f + wide, :])
                else:
                    both = mm(x, two_ref[...])
                    a, b = both[:, :narrow], both[:, narrow:]
                    h = mm_t(g, sd_ref[...])
                sig = sigmoid(a)
                silu = a * sig
                act = silu * b
                if j < count:
                    found = jnp.sum(act * h, 1, keepdims=True)
                    slots = slots + jnp.where(wide_lane == j, found, 0.0)
                    act = act * column
                    h = h * column
                cols = slice(j * width + f, j * width + f + wide)
                store(hid_ref, places, cols, act.astype(BF))
                store(da_ref, places, cols, (h * b * (sig + silu * (1 - sig))).astype(BF))
                store(db_ref, places, cols, (h * silu).astype(BF))
        found = slots.T[:8]
        for n in (0, 2):
            part = found[:, (n // 2) * length : (n // 2 + 1) * length]
            one, two = places[n][0], places[n + 1][0]
            gate_part[one] = jnp.where(lane < half, part, gate_part[one])
            gate_part[two] = jnp.where(lane >= half, part, gate_part[two])

    def compute_back(i):
        places = quarters(i)

        @pl.when(i >= 2)
        def _():
            for copy in out_copies(i - 2):
                copy.wait()

        last = slice(count * width, count * width + narrow)
        for d in range(0, model, 256):
            cols = slice(d, d + 256)
            out = mm(rows_of(hid_ref, places, last), sd_ref[:, cols])
            row = mm_t(rows_of(da_ref, places, last), two_ref[cols, :narrow])
            row = row + mm_t(rows_of(db_ref, places, last), two_ref[cols, narrow:])
            for j in range(count):
                mine = slice(j * width, (j + 1) * width)
                out = out + mm(rows_of(hid_ref, places, mine), ed_ref[j, :, cols])
                row = row + mm_t(rows_of(da_ref, places, mine), eg_ref[j, cols, :])
                row = row + mm_t(rows_of(db_ref, places, mine), eu_ref[j, cols, :])
            out_stage[i % 2, :, cols] = out.astype(BF)
            store(part_ref, places, cols, row.astype(BF))
        for copy in out_copies(i):
            copy.start()

    def arrive(i, carry):
        ring.arrived(2 * i)

        @pl.when(2 * i + 1 < ne - 1)
        def _():
            ring.forward(2 * i + 1)

        @pl.when(i == 0)
        def _():
            loads.wait(*range(6))
            for copy in there.copies:
                copy.wait_recv()

        compute(i)

        @pl.when(2 * i + 1 < ne - 1)
        def _():
            ring.arrived(2 * i + 1)
            ring.forward(2 * i + 2)

        compute_back(i)
        return carry

    lax.fori_loop(0, ne // 2, arrive, 0)
    ring.drain()
    back.begin()
    total.begin()
    part_rows = stage_gu.shape[4]
    per = stage_gu.shape[1]
    tile = per * part_rows
    tiles = model // tile
    every = ne * length

    def stage_copies(i):
        slot = i % 2
        blocks = pl.ds(i * per, per)
        return [
            pltpu.make_async_copy(stage_gu.at[slot], dgu_ref.at[blocks], stage_sem.at[slot, 0]),
            pltpu.make_async_copy(stage_d.at[slot], dd_ref.at[blocks], stage_sem.at[slot, 1]),
            pltpu.make_async_copy(stage_s.at[slot], ds_ref.at[i], stage_sem.at[slot, 2]),
        ]

    def weights(i):
        @pl.when(i >= 2)
        def _():
            for copy in stage_copies(i - 2):
                copy.wait()

        cols = pl.ds(pl.multiple_of(i * tile, 128), tile)
        slot = i % 2
        x_t = x_ref[:, :, cols].reshape(every, tile).T
        g_t = grad_ref[:, :, cols].reshape(every, tile).T
        for j in range(count):
            at = slice(j * width, (j + 1) * width)
            gate = mm(x_t, da_ref[:, :, at].reshape(every, width)).astype(BF)
            up = mm(x_t, db_ref[:, :, at].reshape(every, width)).astype(BF)
            down = mm(g_t, hid_ref[:, :, at].reshape(every, width)).T.astype(BF)
            for q in range(per):
                rows = slice(q * part_rows, (q + 1) * part_rows)
                stage_gu[slot, q, j, 0] = gate[rows]
                stage_gu[slot, q, j, 1] = up[rows]
                stage_d[slot, q, j] = down[:, rows]
        at = slice(count * width, count * width + narrow)
        both = jnp.concatenate(
            [da_ref[:, :, at].reshape(every, narrow), db_ref[:, :, at].reshape(every, narrow)], 1
        )
        stage_s[slot] = mm(x_t, both).astype(BF)
        for copy in stage_copies(i):
            copy.start()

    def back_step(k, carry):
        @pl.when(k > 0)
        def _():
            total.step(k)

        @pl.when(k < tiles)
        def _():
            weights(k)

        return carry

    lax.fori_loop(0, ne - 1, back_step, 0)
    at = slice(count * width, count * width + narrow)
    hid_t = hid_ref[:, :, at].reshape(every, narrow).T
    for d in range(0, model, 512):
        dsd_ref[:, d : d + 512] = mm(hid_t, grad_ref[:, :, d : d + 512].reshape(every, 512)).astype(BF)
    for i in range(ne - 1, tiles):
        weights(i)
    for i in range(max(tiles - 2, 0), tiles):
        for copy in stage_copies(i):
            copy.wait()
    for i in (ne // 2 - 2, ne // 2 - 1):
        for copy in out_copies(i):
            copy.wait()
    total.finish(back_ref)
    back.arrived()
    back.drain()
    there.drain()


def experts_both_ways(
    ffn_in, gates, grad_all, expert_gate, expert_up, expert_down, shared_two, shared_down, ns, ne, cid
):
    length, model = ffn_in.shape
    count, _, width = expert_gate.shape
    narrow = shared_down.shape[0]
    hidden = count * width + narrow
    part = model // ns
    per = 1 if part % 128 == 0 else 2
    return pl.pallas_call(
        functools.partial(experts_kernel, ne, count),
        out_shape=(
            jax.ShapeDtypeStruct((length, model), F32),
            jax.ShapeDtypeStruct((ne, 8, length), F32),
            jax.ShapeDtypeStruct((ne, length, model), BF),
            jax.ShapeDtypeStruct((ns, count, 2, part, width), BF),
            jax.ShapeDtypeStruct((ns, count, width, part), BF),
            jax.ShapeDtypeStruct((ns // per, per * part, 2 * narrow), BF),
            jax.ShapeDtypeStruct((narrow, model), BF),
        ),
        in_specs=[VMEM] * 2 + [ANY] * 6,
        out_specs=(VMEM, VMEM, ANY, ANY, ANY, ANY, VMEM),
        scratch_shapes=[
            pltpu.VMEM((ne, length, model), BF),
            pltpu.VMEM((ne, 8, length), F32),
            pltpu.VMEM((ne, length, hidden), BF),
            pltpu.VMEM((ne, length, hidden), BF),
            pltpu.VMEM((ne, length, hidden), BF),
            pltpu.VMEM((ne, length, model), BF),
            pltpu.VMEM((ne, 8, length), F32),
            pltpu.VMEM((2, per, count, 2, part, width), BF),
            pltpu.VMEM((2, per, count, width, part), BF),
            pltpu.VMEM((2, per * part, 2 * narrow), BF),
            DMA((2, 3)),
            pltpu.VMEM((2, 2 * length, model), BF),
            DMA((2, 4)),
        ]
        + RingGather.scratch(ne, 2)
        + Exchange.scratch(ne)
        + Exchange.scratch(ne)
        + RingSum.scratch(ne, 2, length, model)
        + Loads.scratch(
            [expert_gate, expert_up, grad_all, expert_down, shared_two, shared_down]
        ),
        compiler_params=params(cid, 60),
        name="experts",
    )(ffn_in, gates, grad_all, expert_gate, expert_up, expert_down, shared_two, shared_down)


class SeqGather:
    def __init__(self, ns, v, aux, out, aux_out, lsem, s1, r1, s2, r2, sa, ra):
        s, e = lax.axis_index("seq"), lax.axis_index("exp")
        ny = ns // 2
        y, c = s // 2, s % 2
        mate = (2 * y + 1 - c, e)

        def make(src, dst, send, recv, device):
            return pltpu.make_async_remote_copy(
                src_ref=src,
                dst_ref=dst,
                send_sem=send,
                recv_sem=recv,
                device_id=device,
                device_id_type=MESH,
            )

        self.own = [
            pltpu.make_async_copy(v, out.at[s], lsem.at[0]),
            pltpu.make_async_copy(aux, aux_out.at[s], lsem.at[1]),
        ]
        self.first = [
            make(v, out.at[s], s1.at[j], r1.at[j], (2 * ((y + j) % ny) + c, e))
            for j in range(1, ny)
        ]
        self.first.append(make(v, out.at[s], s1.at[0], r1.at[0], mate))
        self.extra = [
            make(aux, aux_out.at[s], sa.at[t - 1], ra.at[t - 1], ((s + t) % ns, e))
            for t in range(1, ns)
        ]
        self.second = []
        for j in range(1, ny):
            block = out.at[2 * ((y + ny - j) % ny) + c]
            self.second.append(make(block, block, s2.at[j - 1], r2.at[j - 1], mate))

    @staticmethod
    def scratch(ns):
        ny = ns // 2
        return [
            DMA((2,)),
            DMA((ny,)),
            DMA((ny,)),
            DMA((max(ny - 1, 1),)),
            DMA((max(ny - 1, 1),)),
            DMA((ns - 1,)),
            DMA((ns - 1,)),
        ]

    def begin(self):
        for copy in self.first + self.extra + self.own:
            copy.start()

    def middle(self):
        for arrived, onward in zip(self.first[:-1], self.second):
            arrived.wait_recv()
            onward.start()

    def finish(self):
        for copy in [self.first[-1]] + self.second + self.extra:
            copy.wait_recv()
        for copy in self.own:
            copy.wait()

    def drain(self):
        for copy in self.first + self.second + self.extra:
            copy.wait_send()


def sum_weights_kernel(
    ns,
    ne,
    blocks,
    gin,
    gout,
    dproj_ref,
    in_ref,
    tok_ref,
    resid_ref,
    gain_ref,
    aux_ref,
    *refs,
):
    sources = refs[:blocks]
    out, out_rows, tok_out, aux_out, shared_out = refs[blocks : blocks + 5]
    block_outs = refs[blocks + 5 : 2 * blocks + 4]
    sum_weights_body(
        ns,
        ne,
        sources,
        block_outs,
        gin,
        gout,
        dproj_ref,
        in_ref,
        tok_ref,
        resid_ref,
        gain_ref,
        aux_ref,
        out,
        out_rows,
        tok_out,
        aux_out,
        shared_out,
        *refs[2 * blocks + 4 :],
    )


def sum_weights_body(
    ns,
    ne,
    sources,
    block_outs,
    gin,
    gout,
    dproj_ref,
    in_ref,
    tok_ref,
    resid_ref,
    gain_ref,
    aux_ref,
    out,
    out_rows,
    tok_out,
    aux_out,
    shared_out,
    acc,
    acc_out,
    fin,
    part_ref,
    lowered_grad,
    aux_part,
    aux_in,
    aux_sum,
    shared_sum,
    shared_low,
    dproj,
    in_held,
    load_sems,
    ssem,
    rsem,
    so,
    ro,
    sx,
    rx,
    ss,
    rs,
    *scratch,
):
    s, e = lax.axis_index("seq"), lax.axis_index("exp")
    p, right, left = ring_sides(e, ne)
    count = len(SeqSum.scratch(ns, 2, 8, 128, (8, 128)))
    job = SeqSum(ns, 2, part_ref, None, *scratch[:count])
    there = Exchange(ne, aux_part, aux_in, *scratch[count : count + 3])
    back = Exchange(
        ne,
        aux_sum,
        aux_out,
        *scratch[count + 3 : count + 6],
        pick=lambda ref, at: ref.at[s, at],
        spread=True,
    )
    along = []
    more = BlockSum(ns, sources, tuple(block_outs) + (shared_sum,), scratch[count + 9 :])
    across = Exchange(ne, shared_low, shared_out, *scratch[count + 6 : count + 9])
    loads = Loads((dproj_ref, in_ref), (dproj, in_held), load_sems)
    loads.begin()
    more.load()
    greet([((s + t) % ns, e) for t in range(1, ns)] + [(s, (e + t) % ne) for t in range(1, ne)])

    def fill(block):
        rows = pl.ds(pl.multiple_of(block * GROUP, GROUP), GROUP)
        part_ref[block] = mm_t(dproj[rows, :], in_held[...]).astype(BF)

    def tokens_back():
        value = tok_ref[...].astype(F32)
        grad = lowered_grad[...]
        width = value.shape[1]
        scale = lax.rsqrt(jnp.sum(value * value, 1, keepdims=True) / width + EPSILON)
        inside = gain_ref[0:1, :] * grad
        mean = jnp.sum(value * inside, 1, keepdims=True) / width
        tok_out[...] = (resid_ref[...] + scale * inside - value * (scale * scale * scale * mean)).astype(BF)
        gain_grad = jnp.sum(value * scale * grad, 0, keepdims=True)
        aux_part[...] = aux_ref[...]
        for i in range(width // 128):
            row = 6 + i // ne
            aux_part[i % ne, row : row + 1, :128] = gain_grad[:, i * 128 : (i + 1) * 128]
        there.begin()

    def sums():
        there.arrived()
        total = aux_in[0]
        for i in range(1, ne):
            total = total + aux_in[i]
        aux_sum[...] = total
        back.begin()

    def spread():
        back.arrived()
        for t in range(1, ns):
            along.append(
                remote(aux_out.at[s], aux_out.at[s], ss.at[t - 1], rs.at[t - 1], ((s + t) % ns, e))
            )

    def swap():
        shared_low[...] = shared_sum[0].astype(BF)
        across.begin()

    def far_task(j):
        def run():
            fill(job.far(j))
            job.send(j)

        return run

    items = len(more.items)
    lanes = range(1, ns // 2)
    tasks = [(0.0, lambda: loads.wait(0, 1))]
    tasks += [(0.0, far_task(j)) for j in job.order()]
    tasks += [(0.03, functools.partial(fill, job.near(j))) for j in job.order()]
    tasks += [(0.10, more.begin)]
    tasks += [(0.14, functools.partial(job.join, j, u)) for j in lanes for u in range(job.subs)]
    tasks += [
        (0.22 + 0.2 * n / items, functools.partial(more.join, j, n))
        for n in reversed(range(items))
        for j in lanes
    ]
    tasks += [(0.36, functools.partial(job.close, u, lowered_grad)) for u in range(job.subs)]
    tasks += [(0.40, tokens_back), (0.54, sums), (0.68, spread)]
    tasks += [(0.74, functools.partial(more.close, items - 1)), (0.75, swap)]
    tasks += [
        (0.80 + 0.18 * (items - 1 - n) / items, functools.partial(more.close, n))
        for n in range(items - 1)
    ]
    tasks.sort(key=lambda task: task[0])
    rows = gin.shape[2]
    tile = tile_rows(rows)
    half = gout.shape[2] // 2
    tile_out = tile_rows(gout.shape[1])
    sent = {}
    last = {}
    done = 0
    for k in range(ne):
        for t in list(range(1, ns)) + [0, ns, ns + 1]:
            while k > 0 and tasks and tasks[0][0] <= done / (ne * (ns + 2)):
                tasks.pop(0)[1]()
            done += 1
            way = t % 2
            to = right if way == 0 else left
            place = (p - 1 - k + 2 * ne) % ne if way == 0 else (p + 1 + k) % ne
            slot = ring_index(place, ne)
            if t < ns:
                piece = (s + t) % ns
                if k > 0:
                    sent[k - 1, t].wait_recv()

                    def join(i, carry):
                        r = pl.ds(pl.multiple_of(i * tile, tile), tile)
                        total = acc[k - 1, t, r, :].astype(F32) + gin[piece, slot, r, :].astype(
                            F32
                        )
                        if k < ne - 1:
                            acc[k - 1, t, r, :] = total.astype(BF)
                        elif t == 0:
                            out[s, r, :] = total.astype(BF)
                        else:
                            fin[t - 1, r, :] = total.astype(BF)
                        return carry

                    lax.fori_loop(0, rows // tile, join, 0)
                if k < ne - 1:
                    src = gin.at[piece, slot] if k == 0 else acc.at[k - 1, t]
                    sent[k, t] = remote(
                        src, acc.at[k, t], ssem.at[k, t], rsem.at[k, t], (s, to)
                    )
                elif t > 0:
                    last[t] = remote(
                        fin.at[t - 1], out.at[s], sx.at[t - 1], rx.at[t - 1], (piece, e)
                    )
            else:
                part_columns = pl.ds(way * half, half)
                if k > 0:
                    sent[k - 1, t].wait_recv()

                    def join_out(i, carry):
                        r = pl.ds(pl.multiple_of(i * tile_out, tile_out), tile_out)
                        total = acc_out[k - 1, r, part_columns].astype(F32)
                        total = total + gout[slot, r, part_columns].astype(F32)
                        if k < ne - 1:
                            acc_out[k - 1, r, part_columns] = total.astype(BF)
                        else:
                            out_rows[r, part_columns] = total
                        return carry

                    lax.fori_loop(0, gout.shape[1] // tile_out, join_out, 0)
                if k < ne - 1:
                    src = (
                        gout.at[slot, :, part_columns]
                        if k == 0
                        else acc_out.at[k - 1, :, part_columns]
                    )
                    sent[k, t] = remote(
                        src,
                        acc_out.at[k, :, part_columns],
                        so.at[k, way],
                        ro.at[k, way],
                        (s, to),
                    )
    for _, task in tasks:
        task()
    for copy in list(last.values()) + along:
        copy.wait_recv()
    for copy in list(sent.values()) + list(last.values()) + along:
        copy.wait_send()
    across.arrived()
    more.drain()
    job.drain()
    there.drain()
    back.drain()
    across.drain()


def sum_weights(
    gin, gout, projected_grad, in_local, tokens, resid_grad, gain, aux, sources, ns, ne, cid
):
    rows, wide = gin.shape[2:]
    length, model = tokens.shape
    blocks = len(sources)
    return pl.pallas_call(
        functools.partial(sum_weights_kernel, ns, ne, blocks),
        out_shape=(
            jax.ShapeDtypeStruct((ns, rows, wide), BF),
            jax.ShapeDtypeStruct(gout.shape[1:], F32),
            jax.ShapeDtypeStruct(tokens.shape, BF),
            jax.ShapeDtypeStruct((ns,) + aux.shape, F32),
            jax.ShapeDtypeStruct(sources[-1].shape[2:], BF),
        )
        + tuple(jax.ShapeDtypeStruct(v.shape[1:], F32) for v in sources[:-1]),
        in_specs=[VMEM] * 2 + [ANY] * 2 + [VMEM] * 4 + [ANY] * blocks,
        out_specs=(VMEM,) * (4 + blocks),
        scratch_shapes=[
            pltpu.VMEM((ne - 1, ns, rows, wide), BF),
            pltpu.VMEM((ne - 1,) + gout.shape[1:], BF),
            pltpu.VMEM((ns - 1, rows, wide), BF),
            pltpu.VMEM((ns, length, model), BF),
            pltpu.VMEM((length, model), F32),
            pltpu.VMEM(aux.shape, F32),
            pltpu.VMEM(aux.shape, F32),
            pltpu.VMEM(aux.shape[1:], F32),
            pltpu.VMEM(sources[-1].shape[1:], F32),
            pltpu.VMEM(sources[-1].shape[2:], BF),
        ]
        + Loads.scratch([projected_grad, in_local])
        + [
            DMA((ne - 1, ns)),
            DMA((ne - 1, ns)),
            DMA((ne - 1, 2)),
            DMA((ne - 1, 2)),
            DMA((ns - 1,)),
            DMA((ns - 1,)),
            DMA((ns - 1,)),
            DMA((ns - 1,)),
        ]
        + SeqSum.scratch(ns, 2, length, model, (8, 128))
        + Exchange.scratch(ne)
        + Exchange.scratch(ne)
        + Exchange.scratch(ne)
        + BlockSum.scratch(ns, [v.shape for v in sources]),
        compiler_params=params(cid, 60),
        name="sum_weights",
    )(gin, gout, projected_grad, in_local, tokens, resid_grad, gain, aux, *sources)


def matmul_plain(left, right):
    return jnp.dot(left, right, preferred_element_type=F32)


def matmul_rows(left, right):
    return lax.dot_general(left, right, (((0,), (0,)), ((), ())), preferred_element_type=F32)


def matmul_cols(left, right):
    return lax.dot_general(left, right, (((1,), (1,)), ((), ())), preferred_element_type=F32)


def mm(left, right):
    return jnp.dot(left, right, preferred_element_type=F32)


def mm_t(left, right):
    return lax.dot_general(left, right, (((1,), (1,)), ((), ())), preferred_element_type=F32)


def t_mm(left, right):
    return lax.dot_general(left, right, (((0,), (0,)), ((), ())), preferred_element_type=F32)


def exact(left, right):
    return jnp.dot(left, right, precision=PRECISE, preferred_element_type=F32)


def spread_heads(table, heads, head_dim):
    rows = table.shape[0]
    per = 128 // head_dim
    lane = lax.broadcasted_iota(jnp.int32, (rows, 128), 1)
    tiles = []
    for h in range(0, heads, per):
        tile = jnp.broadcast_to(table[:, h : h + 1], (rows, 128))
        for i in range(1, per):
            other = jnp.broadcast_to(table[:, h + i : h + i + 1], (rows, 128))
            tile = jnp.where(lane >= i * head_dim, other, tile)
        tiles.append(tile)
    return jnp.concatenate(tiles, 1)


def sigmoid(v):
    return 1.0 / (1.0 + jnp.exp(-v))


def softplus(v):
    return jnp.maximum(v, 0.0) + jnp.log1p(jnp.exp(-jnp.abs(v)))


def triangle(flip=False):
    t = lax.broadcasted_iota(jnp.int32, (GROUP, GROUP), 0)
    u = lax.broadcasted_iota(jnp.int32, (GROUP, GROUP), 1)
    return u >= t if flip else t >= u


def step_table(pack, bias, heads, s):
    turned = pltpu.roll(pack, (128 - heads * s) % 128, 1)
    lane = lax.broadcasted_iota(jnp.int32, turned.shape, 1)
    raw = jnp.where(lane < heads, turned + bias, 0.0)
    return raw, jnp.where(lane < heads, softplus(raw), 0.0)


def convolved(ext, table, width):
    mixed = table[width : width + 1]
    for j in range(width):
        mixed = mixed + table[j : j + 1] * ext[8 - width + 1 + j : 8 - width + 1 + j + GROUP]
    return mixed


def with_before(proj_ref, at, columns, first):
    before = proj_ref[pl.ds(pl.multiple_of(jnp.maximum(at - 8, 0), 8), 8), columns]
    before = jnp.where(first, 0.0, before)
    return jnp.concatenate([before, proj_ref[pl.ds(at, GROUP), columns]], 0)


def mix_forward_kernel(
    ns,
    ne,
    hw,
    state2,
    heads,
    width,
    proj_ref,
    table_ref,
    head_ref,
    out_ref,
    grad_ref,
    scan_ref,
    mix_ref,
    entry_ref,
    sum_ref,
    square_out,
    grad_all,
    state,
    low_ref,
    square_ref,
    part_ref,
    *sems,
):
    s, e = lax.axis_index("seq"), lax.axis_index("exp")
    p, right, left = ring_sides(e, ne)
    greet([((s + t) % ns, e) for t in range(1, ns)] + [(s, right), (s, left)])
    ring = RingGather(ne, grad_ref, grad_all, *sems[:3])
    job = SeqSum(ns, 2, part_ref, square_ref, *sems[3:])
    ring.begin()
    blocks = proj_ref.shape[0] // GROUP
    head_dim = hw // heads
    n = state2 // 2
    state[...] = jnp.zeros_like(state)
    lane = lax.broadcasted_iota(jnp.int32, (GROUP, 128), 1)
    table = table_ref[...]
    skip = table[width + 2 : width + 3, :hw]
    gain = table[width + 1 : width + 2, :hw]
    bias, rate = head_ref[0:1, :], head_ref[1:2, :]

    def chunk(c, carry):
        at = pl.multiple_of(c * GROUP, GROUP)
        rows = pl.ds(at, GROUP)
        causal = triangle()
        ext = with_before(proj_ref, at, slice(hw, 2 * hw + state2), c == 0)
        mixed = convolved(ext, table, width)
        mix_ref[rows, :] = mixed
        conv = mixed * sigmoid(mixed)
        values = conv[:, :hw]
        b = conv[:, hw : hw + n].astype(BF)
        ct = conv[:, hw + n :].astype(BF)
        _, steps = step_table(proj_ref[rows, 2 * hw + state2 :], bias, heads, s)
        logs = exact(causal.astype(F32), steps * rate)
        logs_t, steps_t = logs.T, steps.T
        end = logs[GROUP - 1 : GROUP, :]
        before = state[...]
        entry_ref[c] = before
        carried = mm(ct, before.astype(BF)) * spread_heads(jnp.exp(logs), heads, head_dim)
        tails = spread_heads(jnp.exp(end - logs) * steps, heads, head_dim)
        fresh = t_mm(b, (values * tails).astype(BF))
        state[...] = spread_heads(jnp.exp(end), heads, head_dim) * before + fresh
        cross = mm_t(ct, b)
        low = values.astype(BF)
        tiles = []
        per = 128 // head_dim
        for h in range(0, heads, per):
            tile = None
            part = low[:, h * head_dim : h * head_dim + 128]
            for i in range(per):
                gap = logs[:, h + i : h + i + 1] - logs_t[h + i : h + i + 1, :]
                kernel = jnp.exp(jnp.where(causal, gap, -1e30))
                weights = cross * kernel * steps_t[h + i : h + i + 1, :]
                one = mm(weights.astype(BF), part)
                tile = one if i == 0 else jnp.where(lane >= i * head_dim, one, tile)
            tiles.append(tile)
        scanned = jnp.concatenate(tiles, 1) + carried + skip * values
        scan_ref[rows, :] = scanned
        gate = proj_ref[rows, :hw]
        gated = scanned * (gate * sigmoid(gate))
        low_ref[rows, :] = (gated * gain).astype(BF)
        square_ref[c] = lax.dot_general(
            jnp.ones((8, hw), F32),
            gated * gated,
            (((1,), (1,)), ((), ())),
            precision=PRECISE,
            preferred_element_type=F32,
        )

        @pl.when(c % 2 == 1)
        def _():
            ring.step((c + 1) // 2)

        return carry

    lax.fori_loop(0, blocks, chunk, 0)

    def fill(block):
        rows = pl.ds(pl.multiple_of(block * GROUP, GROUP), GROUP)
        part_ref[block] = mm(low_ref[rows, :], out_ref[...]).astype(BF)

    k = blocks // 2 + 1
    job.begin(fill)
    for stage in (job.middle, lambda: job.finish(sum_ref, square_out)):
        if k < ne - 1:
            ring.step(k)
            k += 1
        stage()
    while k < ne - 1:
        ring.step(k)
        k += 1
    ring.finish()
    job.drain()


def mix_forward(proj, table, head_table, out_local, grad_low, ns, ne, hw, state2, heads, width, cid):
    whole = proj.shape[0]
    blocks = whole // GROUP
    n = state2 // 2
    rows, model = grad_low.shape
    return pl.pallas_call(
        functools.partial(mix_forward_kernel, ns, ne, hw, state2, heads, width),
        out_shape=(
            jax.ShapeDtypeStruct((whole, hw), F32),
            jax.ShapeDtypeStruct((whole, hw + state2), F32),
            jax.ShapeDtypeStruct((blocks, n, hw), F32),
            jax.ShapeDtypeStruct((rows, model), F32),
            jax.ShapeDtypeStruct((8, rows), F32),
            jax.ShapeDtypeStruct((ne, rows, model), BF),
        ),
        in_specs=[VMEM] * 5,
        out_specs=(VMEM,) * 6,
        scratch_shapes=[
            pltpu.VMEM((n, hw), F32),
            pltpu.VMEM((whole, hw), BF),
            pltpu.VMEM((blocks, 8, GROUP), F32),
            pltpu.VMEM((ns, rows, model), BF),
        ]
        + RingGather.scratch(ne, 2)
        + SeqSum.scratch(ns, 2, rows, model, (8, rows)),
        compiler_params=params(cid),
        name="mix_forward",
    )(proj, table, head_table, out_local, grad_low)


def mix_backward_kernel(
    ns,
    ne,
    hw,
    state2,
    heads,
    width,
    proj_hbm,
    table_ref,
    head_ref,
    scan_hbm,
    mix_hbm,
    entry_hbm,
    out_hbm,
    resid_ref,
    rows_ref,
    part_ref,
    sum_ref,
    dproj_ref,
    grad_out_ref,
    dtable_ref,
    dhead_ref,
    adjoint,
    after,
    low_ref,
    resid_all,
    scale_ref,
    *scratch,
):
    s, e = lax.axis_index("seq"), lax.axis_index("exp")
    p, right, left = ring_sides(e, ne)
    loads = Loads((proj_hbm, scan_hbm, mix_hbm, entry_hbm, out_hbm), scratch[:5], scratch[5])
    proj_ref, scan_ref, mix_ref, entry_ref, out_ref = scratch[:5]
    loads.begin()
    greet([((s + t) % ns, e) for t in range(1, ns)] + [(s, right), (s, left)])
    ring = RingSum(ne, part_ref, *scratch[6:9])
    rows_in = SeqGather(ns, resid_ref, rows_ref, resid_all, scale_ref, *scratch[9:])
    rows_in.begin()
    ring.begin()
    ring.step(1)
    rows_in.middle()
    ring.step(2)
    rows_in.finish()
    loads.wait(*range(5))
    blocks = proj_ref.shape[0] // GROUP
    head_dim = hw // heads
    n = state2 // 2
    per = 128 // head_dim
    adjoint[...] = jnp.zeros_like(adjoint)
    after[...] = jnp.zeros_like(after)
    dtable_ref[...] = jnp.zeros_like(dtable_ref)
    dhead_ref[...] = jnp.zeros_like(dhead_ref)
    lane = lax.broadcasted_iota(jnp.int32, (GROUP, 128), 1)
    row = lax.broadcasted_iota(jnp.int32, (GROUP, 128), 0)
    table = table_ref[...]
    skip = table[width + 2 : width + 3, :hw]
    gain = table[width + 1 : width + 2, :hw]
    bias, rate = head_ref[0:1, :], head_ref[1:2, :]

    def chunk(lap, carry):
        c = blocks - 1 - lap
        at = pl.multiple_of(c * GROUP, GROUP)
        rows = pl.ds(at, GROUP)
        causal = triangle()
        head_of = lax.broadcasted_iota(jnp.int32, (hw, 128), 0) // head_dim
        pick = (head_of == lax.broadcasted_iota(jnp.int32, (hw, 128), 1)).astype(F32)
        gate = proj_ref[rows, :hw]
        gate_sig = sigmoid(gate)
        gate_silu = gate * gate_sig
        scanned = scan_ref[rows, :]
        gated = scanned * gate_silu
        scales = scale_ref[c].T
        r, inside = scales[:, 0:1], scales[:, 1:2]
        q = mm_t(resid_all[c], out_ref[...])
        dgated = r * (gain * q) - gated * (r * r * r * inside)
        low_ref[rows, :] = (gated * gain * r).astype(BF)
        dtable_ref[width + 1 : width + 2, :hw] += jnp.sum(gated * r * q, 0, keepdims=True)
        dy = dgated * gate_silu
        dproj_ref[rows, :hw] = (dgated * scanned * (gate_sig + gate_silu * (1 - gate_sig))).astype(BF)

        mixed = mix_ref[rows, :]
        sig = sigmoid(mixed)
        conv = mixed * sig
        values = conv[:, :hw]
        b = conv[:, hw : hw + n].astype(BF)
        ct = conv[:, hw + n :].astype(BF)
        dtable_ref[width + 2 : width + 3, :hw] += jnp.sum(dy * values, 0, keepdims=True)
        raw, steps = step_table(proj_ref[rows, 2 * hw + state2 :], bias, heads, s)
        logs = exact(causal.astype(F32), steps * rate)
        logs_t, steps_t = logs.T, steps.T
        end = logs[GROUP - 1 : GROUP, :]
        rest = jnp.exp(end - logs)
        tail = rest * steps
        ends = jnp.exp(end)
        before = entry_ref[c]
        before_low = before.astype(BF)
        later = adjoint[...]
        later_low = later.astype(BF)
        tails = spread_heads(tail, heads, head_dim)
        dy_carried = dy * spread_heads(jnp.exp(logs), heads, head_dim)
        dy_carried_low = dy_carried.astype(BF)
        carried = mm(ct, before_low)
        back = mm(b, later_low)
        dvalues = tails * back + skip * dy
        dc = mm_t(dy_carried_low, before_low)
        db = mm_t((values * tails).astype(BF), later_low)
        kept = jnp.sum(later * before, 0, keepdims=True)
        adjoint[...] = spread_heads(ends, heads, head_dim) * later + t_mm(ct, dy_carried_low)
        sums = exact(jnp.concatenate([dy_carried * carried, values * back, jnp.broadcast_to(kept, (8, hw))], 0), pick)
        from_carried, dtail, kept = sums[:GROUP], sums[GROUP : 2 * GROUP], sums[2 * GROUP : 2 * GROUP + 1]
        cross = mm_t(ct, b)
        low = values.astype(BF)
        dy_low = dy.astype(BF)
        dcross = jnp.zeros((GROUP, GROUP), F32)
        dlogs = from_carried - dtail * tail
        columns = []
        tiles = []
        for h in range(0, heads, per):
            part = low[:, h * head_dim : h * head_dim + 128]
            dy_part = dy_low[:, h * head_dim : h * head_dim + 128]
            tile = None
            for i in range(per):
                gap = logs[:, h + i : h + i + 1] - logs_t[h + i : h + i + 1, :]
                kernel = jnp.exp(jnp.where(causal, gap, -1e30))
                scaled = kernel * steps_t[h + i : h + i + 1, :]
                weights = cross * scaled
                inside_head = (lane >= i * head_dim) & (lane < (i + 1) * head_dim)
                one = t_mm(weights.astype(BF), dy_part)
                tile = one if i == 0 else jnp.where(lane >= i * head_dim, one, tile)
                dweights = mm_t(jnp.where(inside_head, dy_part, jnp.zeros_like(dy_part)), part)
                dcross = dcross + dweights * scaled
                unscaled = dweights * (cross * kernel)
                total = jnp.sum(dweights * weights, 1, keepdims=True)
                dlogs = dlogs + jnp.where(lane == h + i, total, 0.0)
                columns.append(jnp.sum(unscaled, 0, keepdims=True))
            tiles.append(tile)
        dvalues = dvalues + jnp.concatenate(tiles, 1)
        columns = jnp.concatenate(columns + [jnp.zeros((128 - heads, GROUP), F32)], 0).T
        dlogs = dlogs - columns * steps
        at_end = jnp.sum(dtail * tail, 0, keepdims=True) + ends * kept
        dlogs = dlogs + jnp.where(row == GROUP - 1, at_end, 0.0)
        da = exact(triangle(True).astype(F32), dlogs)
        dsteps = columns + dtail * rest + da * rate
        dhead_ref[1:2, :] += jnp.sum(da * steps, 0, keepdims=True)
        draw = jnp.where(lane < heads, dsteps * sigmoid(raw), 0.0)
        dhead_ref[0:1, :] += jnp.sum(draw, 0, keepdims=True)
        dproj_ref[rows, 2 * hw + state2 :] = pltpu.roll(draw, heads * s, 1).astype(BF)
        dcross_low = dcross.astype(BF)
        dc = dc + mm(dcross_low, b)
        db = db + t_mm(dcross_low, ct)
        dmix = jnp.concatenate([dvalues, db, dc], 1) * (sig + conv * (1 - sig))
        dtable_ref[width : width + 1, :] += jnp.sum(dmix, 0, keepdims=True)
        ext = with_before(proj_ref, at, slice(hw, 2 * hw + state2), c == 0)
        dext = jnp.concatenate([dmix, after[...]], 0)
        dconv = 0.0
        for j in range(width):
            first = 8 - width + 1 + j
            dtable_ref[j : j + 1, :] += jnp.sum(dmix * ext[first : first + GROUP], 0, keepdims=True)
            dconv = dconv + table[j : j + 1] * dext[width - 1 - j : width - 1 - j + GROUP]
        after[...] = dmix[:8]
        dproj_ref[rows, hw : 2 * hw + state2] = dconv.astype(BF)
        ring.step(lap + 3)
        return carry

    lax.fori_loop(0, blocks, chunk, 0)
    model = resid_all.shape[2]
    every = resid_all[...].reshape(blocks * GROUP, model)
    for d in range(0, hw, 128):
        low_t = low_ref[:, d : d + 128].T
        grad_out_ref[d : d + 128, :] = mm(low_t, every).astype(BF)
    for k in range(blocks + 3, ne - 1):
        ring.step(k)
    ring.finish(sum_ref)
    rows_in.drain()


def mix_backward(
    proj,
    table,
    head_table,
    scanned,
    mixed,
    entries,
    out_local,
    resid_low,
    scales,
    out_part,
    ns,
    ne,
    hw,
    state2,
    heads,
    width,
    cid,
):
    whole = proj.shape[0]
    n = state2 // 2
    rows, model = resid_low.shape
    return pl.pallas_call(
        functools.partial(mix_backward_kernel, ns, ne, hw, state2, heads, width),
        out_shape=(
            jax.ShapeDtypeStruct((rows, model), F32),
            jax.ShapeDtypeStruct(proj.shape, BF),
            jax.ShapeDtypeStruct((hw, model), BF),
            jax.ShapeDtypeStruct((8, hw + state2), F32),
            jax.ShapeDtypeStruct((8, 128), F32),
        ),
        in_specs=[ANY, VMEM, VMEM] + [ANY] * 4 + [VMEM] * 3,
        out_specs=(VMEM,) * 5,
        scratch_shapes=[
            pltpu.VMEM((n, hw), F32),
            pltpu.VMEM((8, hw + state2), F32),
            pltpu.VMEM((whole, hw), BF),
            pltpu.VMEM((ns, rows, model), BF),
            pltpu.VMEM((ns, 8, rows), F32),
        ]
        + Loads.scratch([proj, scanned, mixed, entries, out_local])
        + RingSum.scratch(ne, 2, rows, model)
        + SeqGather.scratch(ns),
        compiler_params=params(cid),
        name="mix_backward",
    )(
        proj,
        table,
        head_table,
        scanned,
        mixed,
        entries,
        out_local,
        resid_low,
        scales,
        out_part,
    )


def rms_back(value, gain, grad):
    scale = lax.rsqrt(jnp.mean(value * value, -1, keepdims=True) + EPSILON)
    inside = gain * grad
    back = scale * inside - value * scale**3 * jnp.mean(value * inside, -1, keepdims=True)
    return back, jnp.sum(value * scale * grad, 0)


def swiglu_back(a, b, grad):
    sig = jax.nn.sigmoid(a)
    return grad * b * sig * (1 + a * (1 - sig)), grad * a * sig


def on_device(
    tokens,
    routes,
    out_grad,
    norm_mix,
    in_weight,
    step_weight,
    conv_weight,
    conv_bias,
    step_bias,
    decay_log,
    skip_gain,
    norm_gate,
    out_weight,
    norm_ffn,
    router_weight,
    shared_gate,
    shared_up,
    shared_down,
    expert_gate,
    expert_up,
    expert_down,
):
    ns, ne = lax.axis_size("seq"), lax.axis_size("exp")
    s, e = lax.axis_index("seq"), lax.axis_index("exp")
    total = ns * ne
    rows, columns = in_weight.shape
    model = tokens.shape[2]
    length = tokens.shape[1]
    whole = length * ns
    width, channels = conv_weight.shape
    gains = norm_gate.shape[0]
    inner = gains * total
    hw = inner // ns
    heads = step_bias.shape[0]
    local_heads = heads // ns
    state2 = columns - 2 * inner
    experts = router_weight.shape[1]
    local_experts = expert_gate.shape[0]
    place = s * ne + e

    small = jnp.concatenate([conv_weight.reshape(-1), conv_bias, norm_gate])
    small = jnp.pad(small, (0, 16 * rows - small.shape[0])).reshape(rows, 16)
    pack = jnp.concatenate(
        [step_weight, router_weight, norm_mix[:, None], norm_ffn[:, None], small], 1
    )
    at_small = heads + experts + 2
    pack = jnp.pad(pack, ((0, 0), (0, 128 - pack.shape[1])))
    hidden_rows = shared_down.shape[0]

    def by_owner(weight):
        split = weight.reshape(rows, ns, ne, hidden_rows)
        return jnp.transpose(split, (2, 0, 1, 3)).reshape(ne, rows, ns * hidden_rows)

    shared_two = jnp.concatenate([by_owner(shared_gate), by_owner(shared_up)], -1)
    in_blocks, token_blocks, out_local, shared_two, local_down = gather_in(
        in_weight, pack, tokens[0], out_weight, shared_two, shared_down, ns, ne, inner, 0
    )
    out_local = out_local.reshape(hw, model)
    shared_two = shared_two.reshape(model, 2 * ns * hidden_rows)
    local_gate, local_up = shared_two[:, : ns * hidden_rows], shared_two[:, ns * hidden_rows :]
    local_down = local_down.reshape(ns * hidden_rows, model)
    grad_low = out_grad[0]
    in_local = in_blocks.reshape(model, -1)
    full_pack = in_local[:, 2 * hw + state2 :]
    full_router = full_pack[:, heads : heads + experts]
    full_norm_mix = full_pack[:, heads + experts].astype(F32)
    full_norm_ffn = full_pack[:, heads + experts + 1].astype(F32)
    full_small = full_pack[:, at_small : at_small + 16].reshape(total, 16 * rows).astype(F32)
    full_conv = full_small[:, : (width + 1) * channels].reshape(total, width + 1, channels)
    full_conv = jnp.swapaxes(full_conv, 0, 1).reshape(width + 1, total * channels)
    at_gain = (width + 1) * channels
    full_norm_gate = full_small[:, at_gain : at_gain + gains].reshape(inner)
    local_conv = jnp.concatenate(
        [lax.dynamic_slice_in_dim(full_conv, s * hw, hw, 1), full_conv[:, inner:]], 1
    )
    local_gain = lax.dynamic_slice_in_dim(full_norm_gate, s * hw, hw)
    at_head = s * local_heads
    local_bias = lax.dynamic_slice_in_dim(step_bias, at_head, local_heads)
    local_decay = lax.dynamic_slice_in_dim(decay_log, at_head, local_heads)
    local_skip = lax.dynamic_slice_in_dim(skip_gain, at_head, local_heads)

    table = jnp.concatenate(
        [
            local_conv,
            jnp.pad(
                jnp.stack([local_gain, jnp.repeat(local_skip, hw // local_heads)]),
                ((0, 6 - width - 1), (0, state2)),
            ),
        ],
        0,
    )
    head_table = jnp.pad(
        jnp.stack([local_bias, -jnp.exp(local_decay)]), ((0, 6), (0, 128 - local_heads))
    )

    token_rows = tokens[0].astype(F32)
    sequence = token_blocks.reshape(whole, model).astype(F32)
    scale_one = lax.rsqrt(jnp.mean(sequence * sequence, -1, keepdims=True) + EPSILON)
    lowered = (sequence * scale_one * full_norm_mix).astype(BF)
    projected = matmul_plain(lowered, in_local)
    scanned, mixed, entries, mixed_raw, squares, grad_all = mix_forward(
        projected, table, head_table, out_local, grad_low, ns, ne, hw, state2, local_heads, width, 1
    )
    scale_gate = lax.rsqrt(squares[0] / inner + EPSILON)
    mixer_out = mixed_raw * scale_gate[:, None]
    resid = token_rows + mixer_out
    scale_two = lax.rsqrt(jnp.mean(resid * resid, -1, keepdims=True) + EPSILON)
    ffn_in = (resid * scale_two * full_norm_ffn).astype(BF)

    logits = matmul_plain(ffn_in, full_router)
    named = jnp.any(
        routes[0][:, :, None] == jnp.arange(experts, dtype=jnp.int32)[None, None, :], 1
    )
    top = jnp.max(jnp.where(named, logits, -jnp.inf), -1, keepdims=True)
    raised = jnp.where(named, jnp.exp(jnp.where(named, logits - top, 0.0)), 0.0)
    gates = (raised / jnp.sum(raised, -1, keepdims=True)).T

    gates_out = jnp.pad(
        gates.reshape(ne, local_experts, length), ((0, 0), (0, 8 - local_experts), (0, 0))
    )
    back_sum, gate_grads, out_part, grad_gate_up, grad_down, shared_part, grad_shared_down = (
        experts_both_ways(
            ffn_in,
            gates_out,
            grad_all,
            expert_gate,
            expert_up,
            expert_down,
            shared_two,
            local_down,
            ns,
            ne,
            2,
        )
    )
    gate_grads = gate_grads[:, :local_experts].reshape(experts, length)
    picked_grad = gates * (gate_grads - jnp.sum(gates * gate_grads, 0, keepdims=True))
    logit_grad = picked_grad.T.astype(BF)
    grad_router = matmul_rows(ffn_in, logit_grad)
    ffn_in_grad = matmul_cols(logit_grad, full_router) + back_sum
    resid_norm_grad, grad_norm_ffn = rms_back(resid, full_norm_ffn, ffn_in_grad)
    resid_grad = grad_low.astype(F32) + resid_norm_grad
    resid_low = resid_grad.astype(BF)
    inside = jnp.sum(resid_low.astype(F32) * mixer_out, -1) / (scale_gate * inner)
    scales = jnp.concatenate(
        [scale_gate[None], inside[None], jnp.zeros((6, length), F32)], 0
    )

    ffn_out, projected_grad, grad_out, table_grad, head_grad = mix_backward(
        projected,
        table,
        head_table,
        scanned,
        mixed,
        entries,
        out_local,
        resid_low,
        scales,
        out_part,
        ns,
        ne,
        hw,
        state2,
        local_heads,
        width,
        4,
    )
    result = (resid + ffn_out).astype(BF)
    stat_terms = jnp.stack(
        [jnp.sum(resid * resid), jnp.sum(mixer_out * mixer_out), jnp.sum(ffn_out * ffn_out)]
    )
    grad_skip = jnp.sum(table_grad[width + 2, :hw].reshape(local_heads, -1), -1)
    grad_decay = head_grad[1, :local_heads] * head_table[1, :local_heads]

    small_parts = [
        table_grad[: width + 1],
        table_grad[width + 1, :hw],
        head_grad[0, :local_heads],
        grad_decay,
        grad_skip,
        grad_norm_ffn,
        stat_terms,
    ]
    ends = []
    at = 0
    for part in small_parts:
        ends.append((at, at + part.size, part.shape))
        at += part.size
    room = 6 * 256
    aux = jnp.concatenate([part.reshape(-1) for part in small_parts])
    aux = jnp.pad(aux, (0, ne * room - at)).reshape(ne, 6, 256)
    aux = jnp.pad(aux, ((0, 0), (0, 2), (0, 0)))

    in_grad = matmul_rows(lowered, projected_grad)
    at_router = 2 * hw + state2 + heads
    in_grad = in_grad + jnp.pad(
        grad_router, ((0, 0), (at_router, in_grad.shape[1] - at_router - experts))
    )
    pieces, grad_out, tokens_grad, sums, shared_part, grad_gate_up, grad_down, grad_shared_down = (
        sum_weights(
            in_grad.astype(BF).reshape(ns, ne, rows, -1),
            grad_out.reshape(ne, hw // ne, model),
            projected_grad,
            in_local,
            tokens[0],
            resid_grad,
            jnp.broadcast_to(full_norm_mix[None], (8, model)),
            aux,
            [
                grad_gate_up.reshape(ns, 2 * local_experts, model // ns, -1),
                grad_down,
                grad_shared_down.reshape(ns, 1, hidden_rows, model),
                shared_part.reshape(ns, 1, ne, rows, -1),
            ],
            ns,
            ne,
            6,
        )
    )
    pieces = pieces.astype(F32)
    grad_in = jnp.concatenate(
        [
            jnp.swapaxes(pieces[:, :, :hw], 0, 1).reshape(rows, inner),
            jnp.swapaxes(pieces[:, :, hw : 2 * hw], 0, 1).reshape(rows, inner),
            jnp.sum(pieces[:, :, 2 * hw : 2 * hw + state2], 0),
        ],
        1,
    )
    grad_pack = jnp.sum(pieces[:, :, 2 * hw + state2 : at_router + experts], 0)
    grad_step, grad_router = grad_pack[:, :heads], grad_pack[:, heads:]
    flat = sums[:, :, :6].reshape(ns, ne * room)
    table_all, gain_all, bias_all, decay_all, skip_all, ffn_all, stat_all = [
        flat[:, start:end].reshape((ns,) + shape) for start, end, shape in ends
    ]
    conv_all = jnp.concatenate(
        [
            jnp.swapaxes(table_all[:, :, :hw], 0, 1).reshape(width + 1, inner),
            jnp.sum(table_all[:, :, hw:], 0),
        ],
        1,
    )
    conv_grads = lax.dynamic_slice_in_dim(conv_all, place * channels, channels, 1)
    mix_sums = jnp.sum(sums[:, :, 6:, :128], 0)
    grad_norm_mix = jnp.swapaxes(mix_sums, 0, 1).reshape(-1)[:model]
    shared_part = shared_part.astype(F32).reshape(ne, rows, 2, ns, hidden_rows)
    shared_grads = jnp.transpose(shared_part, (2, 1, 3, 0, 4)).reshape(2, rows, total * hidden_rows)
    return (
        result[None],
        tokens_grad[None],
        lax.dynamic_slice_in_dim(grad_norm_mix, place * rows, rows),
        grad_in,
        grad_step,
        conv_grads[:width],
        conv_grads[width],
        bias_all.reshape(heads),
        decay_all.reshape(heads),
        skip_all.reshape(heads),
        lax.dynamic_slice_in_dim(gain_all.reshape(inner), place * gains, gains),
        grad_out,
        lax.dynamic_slice_in_dim(jnp.sum(ffn_all, 0), place * rows, rows),
        grad_router,
        shared_grads[0],
        shared_grads[1],
        grad_shared_down[0],
        grad_gate_up[0::2],
        grad_gate_up[1::2],
        grad_down,
        jnp.sum(stat_all, 0) / (total * length * model),
    )


def solution(mesh):
    both = ("seq", "exp")
    return jax.shard_map(
        on_device,
        mesh=mesh,
        in_specs=(
            P("exp", "seq", None),
            P("exp", "seq", None),
            P("exp", "seq", None),
            P(both),
            P(both, None),
            P(both, None),
            P(None, both),
            P(both),
            P(),
            P(),
            P(),
            P(both),
            P(both, None),
            P(both),
            P(both, None),
            P(both, None),
            P(both, None),
            P(both, None),
            P("exp", None, None),
            P("exp", None, None),
            P("exp", None, None),
        ),
        out_specs=(
            P("exp", "seq", None),
            P("exp", "seq", None),
            P(both),
            P(both, None),
            P(both, None),
            P(None, both),
            P(both),
            P(),
            P(),
            P(),
            P(both),
            P(both, None),
            P(both),
            P(both, None),
            P(both, None),
            P(both, None),
            P(both, None),
            P("exp", "seq", None),
            P("exp", "seq", None),
            P("exp", None, "seq"),
            P(),
        ),
        check_vma=False,
    )
```

```python
import functools

import jax
import jax.numpy as jnp
from jax import lax
from jax.experimental import pallas as pl
from jax.experimental.pallas import tpu as pltpu
from jax.sharding import PartitionSpec as P

GROUP = 128
EPSILON = 1e-05
PRECISE = lax.Precision.HIGHEST
MESH = pl.DeviceIdType.MESH
BF = jnp.bfloat16
F32 = jnp.float32
ANY = pl.BlockSpec(memory_space=pl.ANY)
VMEM = pl.BlockSpec(memory_space=pltpu.VMEM)
DMA = pltpu.SemaphoreType.DMA


def ring_place(e, n):
    odd = e % 2
    return (1 - odd) * (e // 2) + odd * (n - 1 - e // 2)


def ring_index(p, n):
    back = p // (n // 2)
    return (1 - back) * (2 * p) + back * (2 * (n - 1 - p) + 1)


def ring_sides(e, n):
    p = ring_place(e, n)
    return p, ring_index((p + 1) % n, n), ring_index((p + n - 1) % n, n)


def greet(partners):
    barrier = pltpu.get_barrier_semaphore()
    for partner in partners:
        pl.semaphore_signal(barrier, inc=1, device_id=partner, device_id_type=MESH)
    pl.semaphore_wait(barrier, len(partners))


def remote(src, dst, send, recv, device):
    copy = pltpu.make_async_remote_copy(
        src_ref=src,
        dst_ref=dst,
        send_sem=send,
        recv_sem=recv,
        device_id=device,
        device_id_type=MESH,
    )
    copy.start()
    return copy


def params(cid, mib=48):
    return pltpu.CompilerParams(
        collective_id=cid, has_side_effects=True, vmem_limit_bytes=mib << 20
    )


class Loads:
    def __init__(self, sources, held, sems):
        self.copies = [
            pltpu.make_async_copy(src, dst, sems.at[i])
            for i, (src, dst) in enumerate(zip(sources, held))
        ]

    @staticmethod
    def scratch(arrays):
        return [pltpu.VMEM(v.shape, v.dtype) for v in arrays] + [DMA((len(arrays),))]

    def begin(self):
        for copy in self.copies:
            copy.start()

    def wait(self, *which):
        for i in which:
            self.copies[i].wait()


def tile_rows(rows, most=16):
    return most if rows % most == 0 else rows


def gather_in_kernel(
    ns,
    ne,
    hw,
    inner,
    in_ref,
    pack_ref,
    tok_ref,
    out_ref,
    two_ref,
    down_ref,
    w_ref,
    c_ref,
    x_ref,
    o_ref,
    shared_ref,
    sd_ref,
    lsem,
    ssem0,
    rsem0,
    ssem,
    rsem,
    sa,
    ra,
    sb,
    rb,
    sc,
    rc,
):
    s, e = lax.axis_index("seq"), lax.axis_index("exp")
    p, right, left = ring_sides(e, ne)
    width = in_ref.shape[1] - 2 * inner
    half = out_ref.shape[1] // 2
    parts = (
        (lambda to: in_ref.at[:, pl.ds(pl.multiple_of(to * hw, 128), hw)], 0),
        (lambda to: in_ref.at[:, pl.ds(pl.multiple_of(inner + to * hw, 128), hw)], hw),
    )
    greet([((s + t) % ns, e) for t in range(1, ns)] + [(s, (e + t) % ne) for t in range(1, ne)])
    own = []
    for i, (piece, start) in enumerate(parts):
        own.append(
            pltpu.make_async_copy(piece(s), w_ref.at[s, e, :, pl.ds(start, hw)], lsem.at[i])
        )
    own.append(
        pltpu.make_async_copy(
            in_ref.at[:, pl.ds(2 * inner, width)], c_ref.at[s, e, :, pl.ds(0, width)], lsem.at[2]
        )
    )
    own.append(
        pltpu.make_async_copy(
            pack_ref, c_ref.at[s, e, :, pl.ds(width, pack_ref.shape[1])], lsem.at[3]
        )
    )
    own.append(pltpu.make_async_copy(out_ref, o_ref.at[e], lsem.at[4]))
    own.append(pltpu.make_async_copy(two_ref.at[e], shared_ref.at[s, e], lsem.at[5]))
    own.append(pltpu.make_async_copy(tok_ref, x_ref.at[s], lsem.at[6]))
    own.append(pltpu.make_async_copy(down_ref, sd_ref.at[s], lsem.at[7]))
    for copy in own:
        copy.start()
    first = {}
    for t in range(1, ns):
        to = (s + t) % ns
        for i, (piece, start) in enumerate(parts):
            first[t, i] = remote(
                piece(to),
                w_ref.at[s, e, :, pl.ds(start, hw)],
                ssem0.at[t - 1, i],
                rsem0.at[t - 1, i],
                (to, e),
            )
    for copy in own:
        copy.wait()
    sent = {}
    across = {}
    along = {}
    common = {}

    def place_of(k, way):
        return ring_index((p - k + ne) % ne if way == 0 else (p + k) % ne, ne)

    def share(k):
        block = c_ref.at[s, place_of(k, 1)]
        for t in range(1, ns):
            common[k, t] = remote(
                block, block, sc.at[k, t - 1], rc.at[k, t - 1], ((s + t) % ns, e)
            )

    for k in range(ne - 1):
        for t in range(ns + 3):
            way = 1 if t == ns else (t - ns - 1 if t > ns else t % 2)
            to = (s, right if way == 0 else left)
            slot = place_of(k, way)
            if k > 0:
                sent[k - 1, t].wait_recv()
            elif 0 < t < ns:
                for i in range(len(parts)):
                    first[t, i].wait_recv()
            if t < ns:
                block = w_ref.at[(s + ns - t) % ns, slot]
            elif t == ns:
                block = c_ref.at[s, slot]
            else:
                block = o_ref.at[slot, :, pl.ds(way * half, half)]
            sent[k, t] = remote(block, block, ssem.at[k, t], rsem.at[k, t], to)
            if t == ns:
                share(k)
        if k == 0:
            for t in range(1, ns):
                to = ((s + t) % ns, e)
                first[t, 2] = remote(
                    tok_ref, x_ref.at[s], ssem0.at[t - 1, 2], rsem0.at[t - 1, 2], to
                )
                first[t, 3] = remote(
                    down_ref, sd_ref.at[s], ssem0.at[t - 1, 3], rsem0.at[t - 1, 3], to
                )
            for t in range(1, ne):
                to = (e + t) % ne
                across[t] = remote(
                    two_ref.at[to], shared_ref.at[s, e], sa.at[t - 1], ra.at[t - 1], (s, to)
                )
        if k == 2:
            for t in range(1, ne):
                across[t].wait_recv()
            for t in range(1, ns):
                along[t] = remote(
                    shared_ref.at[s], shared_ref.at[s], sb.at[t - 1], rb.at[t - 1], ((s + t) % ns, e)
                )
    sent[ne - 2, ns].wait_recv()
    share(ne - 1)
    for t in range(ns + 3):
        if t != ns:
            sent[ne - 2, t].wait_recv()
    for t in range(1, ns):
        first[t, 2].wait_recv()
        first[t, 3].wait_recv()
        along[t].wait_recv()
    for copy in common.values():
        copy.wait_recv()
    for group in (first, sent, across, along, common):
        for copy in group.values():
            copy.wait_send()


def gather_in(in_weight, pack, tokens, out_weight, shared_two, shared_down, ns, ne, inner, cid):
    rows, columns = in_weight.shape
    hw = inner // ns
    wide = columns - 2 * inner + pack.shape[1]
    return pl.pallas_call(
        functools.partial(gather_in_kernel, ns, ne, hw, inner),
        out_shape=(
            jax.ShapeDtypeStruct((ns, ne, rows, 2 * hw), BF),
            jax.ShapeDtypeStruct((ns, ne, rows, wide), BF),
            jax.ShapeDtypeStruct((ns,) + tokens.shape, BF),
            jax.ShapeDtypeStruct((ne,) + out_weight.shape, BF),
            jax.ShapeDtypeStruct((ns,) + shared_two.shape, BF),
            jax.ShapeDtypeStruct((ns,) + shared_down.shape, BF),
        ),
        in_specs=[ANY] * 6,
        out_specs=(ANY,) * 6,
        scratch_shapes=[
            DMA((8,)),
            DMA((ns - 1, 4)),
            DMA((ns - 1, 4)),
            DMA((ne - 1, ns + 3)),
            DMA((ne - 1, ns + 3)),
            DMA((ne - 1,)),
            DMA((ne - 1,)),
            DMA((ns - 1,)),
            DMA((ns - 1,)),
            DMA((ne, ns - 1)),
            DMA((ne, ns - 1)),
        ],
        compiler_params=params(cid, 8),
        name="gather_in",
    )(in_weight, pack, tokens, out_weight, shared_two, shared_down)


class SeqSum:
    def __init__(self, ns, subs, part, aux, one, two, aux_in, s1, r1, s2, r2, sa, ra):
        self.s, self.e = lax.axis_index("seq"), lax.axis_index("exp")
        self.ns, self.ny, self.subs = ns, ns // 2, subs
        self.y, self.c = self.s // 2, self.s % 2
        self.part, self.aux, self.one, self.two, self.aux_in = part, aux, one, two, aux_in
        self.sems = (s1, r1, s2, r2, sa, ra)
        self.step = part.shape[1] // subs
        self.tile = tile_rows(self.step)
        self.first, self.second, self.extra = {}, {}, []

    @staticmethod
    def scratch(ns, subs, rows, width, aux_shape):
        ny = ns // 2
        return [
            pltpu.VMEM((ny, rows, width), BF),
            pltpu.VMEM((max(ny - 1, 1), rows, width), BF),
            pltpu.VMEM((ns - 1,) + aux_shape, F32),
            DMA((ny, subs)),
            DMA((ny, subs)),
            DMA((max(ny - 1, 1), subs)),
            DMA((max(ny - 1, 1), subs)),
            DMA((ns - 1,)),
            DMA((ns - 1,)),
        ]

    def rows(self, u):
        return pl.ds(u * self.step, self.step)

    def send_aux(self):
        s1, r1, s2, r2, sa, ra = self.sems
        for t in range(1, self.ns):
            to = (self.s + t) % self.ns
            self.extra.append(
                remote(
                    self.aux.at[to], self.aux_in.at[t - 1], sa.at[t - 1], ra.at[t - 1], (to, self.e)
                )
            )

    def order(self):
        return list(range(1, self.ny)) + [0]

    def far(self, j):
        return 2 * ((self.y + j) % self.ny) + 1 - self.c

    def near(self, j):
        return 2 * ((self.y + j) % self.ny) + self.c

    def send(self, j):
        s1, r1, s2, r2, sa, ra = self.sems
        mate = (2 * self.y + 1 - self.c, self.e)
        for u in range(self.subs):
            self.first[j, u] = remote(
                self.part.at[self.far(j), self.rows(u)],
                self.one.at[j, self.rows(u)],
                s1.at[j, u],
                r1.at[j, u],
                mate,
            )

    def begin(self, fill):
        self.send_aux()
        for j in self.order():
            fill(self.far(j))
            self.send(j)
        for j in self.order():
            fill(self.near(j))

    def join(self, j, u):
        s1, r1, s2, r2, sa, ra = self.sems
        to = self.near(j)
        self.first[j, u].wait_recv()

        def add(i, carry):
            r = pl.ds(pl.multiple_of(u * self.step + i * self.tile, self.tile), self.tile)
            total = self.one[j, r, :].astype(F32) + self.part[to, r, :].astype(F32)
            self.one[j, r, :] = total.astype(BF)
            return carry

        lax.fori_loop(0, self.step // self.tile, add, 0)
        self.second[j, u] = remote(
            self.one.at[j, self.rows(u)],
            self.two.at[j - 1, self.rows(u)],
            s2.at[j - 1, u],
            r2.at[j - 1, u],
            (to, self.e),
        )

    def middle(self):
        for j in range(1, self.ny):
            for u in range(self.subs):
                self.join(j, u)

    def close(self, u, out):
        self.first[0, u].wait_recv()
        for j in range(1, self.ny):
            self.second[j, u].wait_recv()

        def add(i, carry):
            r = pl.ds(pl.multiple_of(u * self.step + i * self.tile, self.tile), self.tile)
            total = self.one[0, r, :].astype(F32) + self.part[self.s, r, :].astype(F32)
            for j in range(1, self.ny):
                total = total + self.two[j - 1, r, :].astype(F32)
            out[r, :] = total
            return carry

        lax.fori_loop(0, self.step // self.tile, add, 0)

    def finish(self, out, aux_out):
        for u in range(self.subs):
            self.close(u, out)
        total = self.aux[self.s]
        for t in range(1, self.ns):
            self.extra[t - 1].wait_recv()
            total = total + self.aux_in[t - 1]
        aux_out[...] = total

    def drain(self):
        for copy in list(self.first.values()) + list(self.second.values()) + self.extra:
            copy.wait_send()


class BlockSum:
    def __init__(self, ns, sources, outs, scratch):
        self.s, self.e = lax.axis_index("seq"), lax.axis_index("exp")
        self.ns, self.ny = ns, ns // 2
        self.y, self.c = self.s // 2, self.s % 2
        self.sources, self.outs = sources, outs
        self.items = [(m, i) for m, src in enumerate(sources) for i in range(src.shape[1])]
        count = len(sources)
        self.held, self.one, self.two = (
            scratch[:count],
            scratch[count : 2 * count],
            scratch[2 * count : 3 * count],
        )
        self.lsem, self.s1, self.r1, self.s2, self.r2 = scratch[3 * count :]
        self.loads = [
            pltpu.make_async_copy(src, held, self.lsem.at[m])
            for m, (src, held) in enumerate(zip(self.sources, self.held))
        ]
        self.first, self.second = {}, {}

    @staticmethod
    def scratch(ns, shapes):
        ny = ns // 2
        items = sum(shape[1] for shape in shapes)
        return (
            [pltpu.VMEM(shape, BF) for shape in shapes]
            + [pltpu.VMEM((ny,) + shape[1:], BF) for shape in shapes]
            + [pltpu.VMEM((max(ny - 1, 1),) + shape[1:], BF) for shape in shapes]
            + [
                DMA((len(shapes),)),
                DMA((ny, items)),
                DMA((ny, items)),
                DMA((max(ny - 1, 1), items)),
                DMA((max(ny - 1, 1), items)),
            ]
        )

    def load(self):
        for copy in self.loads:
            copy.start()

    def begin(self):
        mate = (2 * self.y + 1 - self.c, self.e)
        for copy in self.loads:
            copy.wait()
        for j in list(range(1, self.ny)) + [0]:
            block = 2 * ((self.y + j) % self.ny) + 1 - self.c
            for n, (m, i) in enumerate(self.items):
                self.first[j, n] = remote(
                    self.held[m].at[block, i],
                    self.one[m].at[j, i],
                    self.s1.at[j, n],
                    self.r1.at[j, n],
                    mate,
                )

    def tiles(self, shape, body):
        if len(shape) == 3:
            lax.fori_loop(0, shape[0], lambda i, carry: body((i,)) or carry, 0)
        else:
            size = 32 if shape[0] % 32 == 0 else shape[0]
            lax.fori_loop(
                0,
                shape[0] // size,
                lambda i, carry: body((pl.ds(pl.multiple_of(i * size, size), size),)) or carry,
                0,
            )

    def join(self, j, n):
        m, i = self.items[n]
        to = 2 * ((self.y + j) % self.ny) + self.c
        self.first[j, n].wait_recv()
        one, held = self.one[m], self.held[m]

        def add(at):
            total = one[(j, i) + at].astype(F32) + held[(to, i) + at].astype(F32)
            one[(j, i) + at] = total.astype(BF)

        self.tiles(one.shape[2:], add)
        self.second[j, n] = remote(
            one.at[j, i],
            self.two[m].at[j - 1, i],
            self.s2.at[j - 1, n],
            self.r2.at[j - 1, n],
            (to, self.e),
        )

    def close(self, n):
        m, i = self.items[n]
        self.first[0, n].wait_recv()
        for j in range(1, self.ny):
            self.second[j, n].wait_recv()
        one, held, two, out = self.one[m], self.held[m], self.two[m], self.outs[m]

        def add(at):
            total = one[(0, i) + at].astype(F32) + held[(self.s, i) + at].astype(F32)
            for j in range(1, self.ny):
                total = total + two[(j - 1, i) + at].astype(F32)
            out[(i,) + at] = total

        self.tiles(one.shape[2:], add)

    def drain(self):
        for copy in list(self.first.values()) + list(self.second.values()):
            copy.wait_send()


class RingGather:
    def __init__(self, ne, v, out, lsem, ssem, rsem):
        self.s, self.e = lax.axis_index("seq"), lax.axis_index("exp")
        self.ne, self.v, self.out = ne, v, out
        self.p, self.right, self.left = ring_sides(self.e, ne)
        self.ssem, self.rsem = ssem, rsem
        self.subs = ssem.shape[2]
        self.step_rows = v.shape[0] // (2 * self.subs)
        self.own = pltpu.make_async_copy(v, out.at[self.e], lsem)

    @staticmethod
    def scratch(ne, subs):
        return [DMA, DMA((ne - 1, 2, subs)), DMA((ne - 1, 2, subs))]

    def copy(self, k, way, u, src=None):
        place = (self.p - k + self.ne) % self.ne if way == 0 else (self.p + k) % self.ne
        slot = ring_index(place, self.ne)
        rows = pl.ds((way * self.subs + u) * self.step_rows, self.step_rows)
        block = self.out.at[slot, rows]
        return pltpu.make_async_remote_copy(
            src_ref=block if src is None else src.at[rows],
            dst_ref=block,
            send_sem=self.ssem.at[k, way, u],
            recv_sem=self.rsem.at[k, way, u],
            device_id=(self.s, self.right if way == 0 else self.left),
            device_id_type=MESH,
        )

    def begin(self):
        self.own.start()
        for u in range(self.subs):
            for way in range(2):
                self.copy(0, way, u, self.v).start()

    def step(self, k):
        for u in range(self.subs):
            for way in range(2):
                self.copy(k - 1, way, u).wait_recv()
                self.copy(k, way, u).start()

    def forward(self, k):
        for u in range(self.subs):
            for way in range(2):
                self.copy(k, way, u).start()

    def arrived(self, k):
        for u in range(self.subs):
            for way in range(2):
                self.copy(k, way, u).wait_recv()

    def drain(self):
        for k in range(self.ne - 1):
            for u in range(self.subs):
                for way in range(2):
                    self.copy(k, way, u).wait_send()

    def finish(self):
        self.arrived(self.ne - 2)
        self.drain()
        self.own.wait()


class RingSum:
    def __init__(self, ne, part, acc, ssem, rsem):
        self.s, self.e = lax.axis_index("seq"), lax.axis_index("exp")
        self.ne, self.part, self.acc = ne, part, acc
        self.p, self.right, self.left = ring_sides(self.e, ne)
        self.ssem, self.rsem = ssem, rsem
        self.subs = ssem.shape[2]
        self.size = part.shape[1] // (2 * self.subs)
        self.tile = tile_rows(self.size)

    @staticmethod
    def scratch(ne, subs, rows, width):
        return [
            pltpu.VMEM((ne - 1, rows, width), BF),
            DMA((ne - 1, 2, subs)),
            DMA((ne - 1, 2, subs)),
        ]

    def slot(self, k, way):
        place = (self.p - 1 - k + 2 * self.ne) % self.ne if way == 0 else (self.p + 1 + k) % self.ne
        return ring_index(place, self.ne)

    def copy(self, k, way, u, src=None):
        rows = pl.ds((way * self.subs + u) * self.size, self.size)
        return pltpu.make_async_remote_copy(
            src_ref=self.acc.at[k, rows] if src is None else src.at[rows],
            dst_ref=self.acc.at[k, rows],
            send_sem=self.ssem.at[k, way, u],
            recv_sem=self.rsem.at[k, way, u],
            device_id=(self.s, self.right if way == 0 else self.left),
            device_id_type=MESH,
        )

    def add(self, k, way, u, out):
        base = (way * self.subs + u) * self.size
        slot = self.slot(k, way)

        def join(i, carry):
            r = pl.ds(pl.multiple_of(base + i * self.tile, self.tile), self.tile)
            total = self.acc[k - 1, r, :].astype(F32) + self.part[slot, r, :].astype(F32)
            if out is None:
                self.acc[k - 1, r, :] = total.astype(BF)
            else:
                out[r, :] = total
            return carry

        lax.fori_loop(0, self.size // self.tile, join, 0)

    def begin(self):
        for u in range(self.subs):
            for way in range(2):
                self.copy(0, way, u, self.part.at[self.slot(0, way)]).start()

    def step(self, k):
        for u in range(self.subs):
            for way in range(2):
                self.copy(k - 1, way, u).wait_recv()
                self.add(k, way, u, None)
                rows = pl.ds((way * self.subs + u) * self.size, self.size)
                pltpu.make_async_remote_copy(
                    src_ref=self.acc.at[k - 1, rows],
                    dst_ref=self.acc.at[k, rows],
                    send_sem=self.ssem.at[k, way, u],
                    recv_sem=self.rsem.at[k, way, u],
                    device_id=(self.s, self.right if way == 0 else self.left),
                    device_id_type=MESH,
                ).start()

    def finish(self, out):
        k = self.ne - 1
        for u in range(self.subs):
            for way in range(2):
                self.copy(k - 1, way, u).wait_recv()
                self.add(k, way, u, out)
        for k in range(self.ne - 1):
            for u in range(self.subs):
                for way in range(2):
                    self.copy(k, way, u).wait_send()


class Exchange:
    def __init__(self, ne, src, dst, lsem, ssem, rsem, pick=None, spread=False):
        s, e = lax.axis_index("seq"), lax.axis_index("exp")
        if pick is None:
            pick = lambda ref, at: ref.at[at]
        give = (lambda ref, at: ref) if spread else pick
        self.own = pltpu.make_async_copy(give(src, e), pick(dst, e), lsem)
        self.copies = []
        for t in range(1, ne):
            to = (e + t) % ne
            self.copies.append(
                pltpu.make_async_remote_copy(
                    src_ref=give(src, to),
                    dst_ref=pick(dst, e),
                    send_sem=ssem.at[t - 1],
                    recv_sem=rsem.at[t - 1],
                    device_id=(s, to),
                    device_id_type=MESH,
                )
            )

    @staticmethod
    def scratch(ne):
        return [DMA, DMA((ne - 1,)), DMA((ne - 1,))]

    def begin(self):
        self.own.start()
        for copy in self.copies:
            copy.start()

    def arrived(self):
        self.own.wait()
        for copy in self.copies:
            copy.wait_recv()

    def drain(self):
        for copy in self.copies:
            copy.wait_send()


def experts_kernel(
    ne,
    count,
    ffn_ref,
    gate_ref,
    grad_hbm,
    eg_hbm,
    eu_hbm,
    ed_hbm,
    two_hbm,
    sd_hbm,
    back_ref,
    gate_back,
    out_ref,
    dg_ref,
    du_ref,
    dd_ref,
    ds_ref,
    dsd_ref,
    x_ref,
    gates,
    hid_ref,
    da_ref,
    db_ref,
    part_ref,
    gate_part,
    stage_g,
    stage_u,
    stage_d,
    stage_s,
    stage_sem,
    out_stage,
    out_sem,
    *scratch,
):
    s, e = lax.axis_index("seq"), lax.axis_index("exp")
    length, model = ffn_ref.shape
    half = length // 2
    sources = (eg_hbm, eu_hbm, grad_hbm, ed_hbm, two_hbm, sd_hbm)
    eg_ref, eu_ref, grad_ref, ed_ref, two_ref, sd_ref = scratch[12:18]
    loads = Loads(sources, scratch[12:18], scratch[18])
    loads.begin()
    width = eg_ref.shape[2]
    narrow = sd_ref.shape[0]
    tile_width = min(width, 256)
    greet([(s, (e + t) % ne) for t in range(1, ne)])
    ring = RingGather(ne, ffn_ref, x_ref, *scratch[:3])
    there = Exchange(ne, gate_ref, gates, *scratch[3:6])
    back = Exchange(ne, gate_part, gate_back, *scratch[6:9])
    total = RingSum(ne, part_ref, *scratch[9:12])
    ring.begin()
    there.begin()
    gate_part[...] = jnp.zeros_like(gate_part)
    ring.own.wait()
    there.own.wait()
    lane = lax.broadcasted_iota(jnp.int32, (8, length), 1)
    wide_lane = lax.broadcasted_iota(jnp.int32, (2 * length, 128), 1)

    def quarters(i):
        found = []
        for k in (2 * i, 2 * i + 1):
            found.append((ring_index((ring.p - k + ne) % ne, ne), 0))
            found.append((ring_index((ring.p + k) % ne, ne), half))
        return found

    def out_copies(i):
        slot = i % 2
        return [
            pltpu.make_async_copy(
                out_stage.at[slot, pl.ds(n * half, half)],
                out_ref.at[block, pl.ds(first, half)],
                out_sem.at[slot, n],
            )
            for n, (block, first) in enumerate(quarters(i))
        ]

    def rows_of(ref, places, cols):
        return jnp.concatenate(
            [ref[block, first : first + half, cols] for block, first in places], 0
        )

    def store(ref, places, cols, value):
        for n, (block, first) in enumerate(places):
            ref[block, first : first + half, cols] = value[n * half : (n + 1) * half]

    def compute(i):
        places = quarters(i)
        every = slice(0, model)
        x = rows_of(x_ref, places, every)
        g = rows_of(grad_ref, places, every)
        table = jnp.concatenate(
            [
                jnp.where(lane < half, gates[places[n][0]], gates[places[n + 1][0]]).T
                for n in (0, 2)
            ],
            0,
        )
        slots = jnp.zeros((2 * length, 128), F32)
        for j in range(count + 1):
            size = width if j < count else narrow
            column = table[:, j : j + 1] if j < count else None
            for f in range(0, size, tile_width):
                wide = min(tile_width, size - f)
                if j < count:
                    a = mm(x, eg_ref[j, :, f : f + wide])
                    b = mm(x, eu_ref[j, :, f : f + wide])
                    h = mm_t(g, ed_ref[j, f : f + wide, :])
                else:
                    both = mm(x, two_ref[...])
                    a, b = both[:, :narrow], both[:, narrow:]
                    h = mm_t(g, sd_ref[...])
                sig = sigmoid(a)
                silu = a * sig
                act = silu * b
                if j < count:
                    found = jnp.sum(act * h, 1, keepdims=True)
                    slots = slots + jnp.where(wide_lane == j, found, 0.0)
                    act = act * column
                    h = h * column
                cols = slice(j * width + f, j * width + f + wide)
                store(hid_ref, places, cols, act.astype(BF))
                store(da_ref, places, cols, (h * b * (sig + silu * (1 - sig))).astype(BF))
                store(db_ref, places, cols, (h * silu).astype(BF))
        found = slots.T[:8]
        for n in (0, 2):
            part = found[:, (n // 2) * length : (n // 2 + 1) * length]
            one, two = places[n][0], places[n + 1][0]
            gate_part[one] = jnp.where(lane < half, part, gate_part[one])
            gate_part[two] = jnp.where(lane >= half, part, gate_part[two])

    def compute_back(i):
        places = quarters(i)

        @pl.when(i >= 2)
        def _():
            for copy in out_copies(i - 2):
                copy.wait()

        last = slice(count * width, count * width + narrow)
        for d in range(0, model, 256):
            cols = slice(d, d + 256)
            out = mm(rows_of(hid_ref, places, last), sd_ref[:, cols])
            row = mm_t(rows_of(da_ref, places, last), two_ref[cols, :narrow])
            row = row + mm_t(rows_of(db_ref, places, last), two_ref[cols, narrow:])
            for j in range(count):
                mine = slice(j * width, (j + 1) * width)
                out = out + mm(rows_of(hid_ref, places, mine), ed_ref[j, :, cols])
                row = row + mm_t(rows_of(da_ref, places, mine), eg_ref[j, cols, :])
                row = row + mm_t(rows_of(db_ref, places, mine), eu_ref[j, cols, :])
            out_stage[i % 2, :, cols] = out.astype(BF)
            store(part_ref, places, cols, row.astype(BF))
        for copy in out_copies(i):
            copy.start()

    def arrive(i, carry):
        ring.arrived(2 * i)

        @pl.when(2 * i + 1 < ne - 1)
        def _():
            ring.forward(2 * i + 1)

        @pl.when(i == 0)
        def _():
            loads.wait(*range(6))
            for copy in there.copies:
                copy.wait_recv()

        compute(i)

        @pl.when(2 * i + 1 < ne - 1)
        def _():
            ring.arrived(2 * i + 1)
            ring.forward(2 * i + 2)

        compute_back(i)
        return carry

    lax.fori_loop(0, ne // 2, arrive, 0)
    ring.drain()
    back.begin()
    total.begin()
    part_rows = stage_g.shape[3]
    per = stage_g.shape[1]
    tile = per * part_rows
    tiles = model // tile
    every = ne * length

    def stage_copies(i):
        slot = i % 2
        blocks = pl.ds(i * per, per)
        return [
            pltpu.make_async_copy(stage_g.at[slot], dg_ref.at[blocks], stage_sem.at[slot, 0]),
            pltpu.make_async_copy(stage_u.at[slot], du_ref.at[blocks], stage_sem.at[slot, 3]),
            pltpu.make_async_copy(stage_d.at[slot], dd_ref.at[blocks], stage_sem.at[slot, 1]),
            pltpu.make_async_copy(stage_s.at[slot], ds_ref.at[i], stage_sem.at[slot, 2]),
        ]

    def weights(i):
        @pl.when(i >= 2)
        def _():
            for copy in stage_copies(i - 2):
                copy.wait()

        cols = pl.ds(pl.multiple_of(i * tile, 128), tile)
        slot = i % 2
        x_t = x_ref[:, :, cols].reshape(every, tile).T
        g_t = grad_ref[:, :, cols].reshape(every, tile).T
        for j in range(count):
            at = slice(j * width, (j + 1) * width)
            gate = mm(x_t, da_ref[:, :, at].reshape(every, width)).astype(BF)
            up = mm(x_t, db_ref[:, :, at].reshape(every, width)).astype(BF)
            down = mm(g_t, hid_ref[:, :, at].reshape(every, width)).T.astype(BF)
            for q in range(per):
                rows = slice(q * part_rows, (q + 1) * part_rows)
                stage_g[slot, q, j] = gate[rows]
                stage_u[slot, q, j] = up[rows]
                stage_d[slot, q, j] = down[:, rows]
        at = slice(count * width, count * width + narrow)
        both = jnp.concatenate(
            [da_ref[:, :, at].reshape(every, narrow), db_ref[:, :, at].reshape(every, narrow)], 1
        )
        stage_s[slot] = mm(x_t, both).astype(BF)
        for copy in stage_copies(i):
            copy.start()

    def back_step(k, carry):
        @pl.when(k > 0)
        def _():
            total.step(k)

        @pl.when(k < tiles)
        def _():
            weights(k)

        return carry

    lax.fori_loop(0, ne - 1, back_step, 0)
    at = slice(count * width, count * width + narrow)
    hid_t = hid_ref[:, :, at].reshape(every, narrow).T
    for d in range(0, model, 512):
        dsd_ref[:, d : d + 512] = mm(hid_t, grad_ref[:, :, d : d + 512].reshape(every, 512)).astype(BF)
    for i in range(ne - 1, tiles):
        weights(i)
    for i in range(max(tiles - 2, 0), tiles):
        for copy in stage_copies(i):
            copy.wait()
    for i in (ne // 2 - 2, ne // 2 - 1):
        for copy in out_copies(i):
            copy.wait()
    total.finish(back_ref)
    back.arrived()
    back.drain()
    there.drain()


def experts_both_ways(
    ffn_in, gates, grad_all, expert_gate, expert_up, expert_down, shared_two, shared_down, ns, ne, cid
):
    length, model = ffn_in.shape
    count, _, width = expert_gate.shape
    narrow = shared_down.shape[0]
    hidden = count * width + narrow
    part = model // ns
    per = 1 if part % 128 == 0 else 2
    return pl.pallas_call(
        functools.partial(experts_kernel, ne, count),
        out_shape=(
            jax.ShapeDtypeStruct((length, model), F32),
            jax.ShapeDtypeStruct((ne, 8, length), F32),
            jax.ShapeDtypeStruct((ne, length, model), BF),
            jax.ShapeDtypeStruct((ns, count, part, width), BF),
            jax.ShapeDtypeStruct((ns, count, part, width), BF),
            jax.ShapeDtypeStruct((ns, count, width, part), BF),
            jax.ShapeDtypeStruct((ns // per, per * part, 2 * narrow), BF),
            jax.ShapeDtypeStruct((narrow, model), BF),
        ),
        in_specs=[VMEM] * 2 + [ANY] * 6,
        out_specs=(VMEM, VMEM, ANY, ANY, ANY, ANY, ANY, VMEM),
        scratch_shapes=[
            pltpu.VMEM((ne, length, model), BF),
            pltpu.VMEM((ne, 8, length), F32),
            pltpu.VMEM((ne, length, hidden), BF),
            pltpu.VMEM((ne, length, hidden), BF),
            pltpu.VMEM((ne, length, hidden), BF),
            pltpu.VMEM((ne, length, model), BF),
            pltpu.VMEM((ne, 8, length), F32),
            pltpu.VMEM((2, per, count, part, width), BF),
            pltpu.VMEM((2, per, count, part, width), BF),
            pltpu.VMEM((2, per, count, width, part), BF),
            pltpu.VMEM((2, per * part, 2 * narrow), BF),
            DMA((2, 4)),
            pltpu.VMEM((2, 2 * length, model), BF),
            DMA((2, 4)),
        ]
        + RingGather.scratch(ne, 2)
        + Exchange.scratch(ne)
        + Exchange.scratch(ne)
        + RingSum.scratch(ne, 2, length, model)
        + Loads.scratch(
            [expert_gate, expert_up, grad_all, expert_down, shared_two, shared_down]
        ),
        compiler_params=params(cid, 60),
        name="experts",
    )(ffn_in, gates, grad_all, expert_gate, expert_up, expert_down, shared_two, shared_down)


class SeqGather:
    def __init__(self, ns, v, aux, out, aux_out, lsem, s1, r1, s2, r2, sa, ra):
        s, e = lax.axis_index("seq"), lax.axis_index("exp")
        ny = ns // 2
        y, c = s // 2, s % 2
        mate = (2 * y + 1 - c, e)

        def make(src, dst, send, recv, device):
            return pltpu.make_async_remote_copy(
                src_ref=src,
                dst_ref=dst,
                send_sem=send,
                recv_sem=recv,
                device_id=device,
                device_id_type=MESH,
            )

        self.own = [
            pltpu.make_async_copy(v, out.at[s], lsem.at[0]),
            pltpu.make_async_copy(aux, aux_out.at[s], lsem.at[1]),
        ]
        self.first = [
            make(v, out.at[s], s1.at[j], r1.at[j], (2 * ((y + j) % ny) + c, e))
            for j in range(1, ny)
        ]
        self.first.append(make(v, out.at[s], s1.at[0], r1.at[0], mate))
        self.extra = [
            make(aux, aux_out.at[s], sa.at[t - 1], ra.at[t - 1], ((s + t) % ns, e))
            for t in range(1, ns)
        ]
        self.second = []
        for j in range(1, ny):
            block = out.at[2 * ((y + ny - j) % ny) + c]
            self.second.append(make(block, block, s2.at[j - 1], r2.at[j - 1], mate))

    @staticmethod
    def scratch(ns):
        ny = ns // 2
        return [
            DMA((2,)),
            DMA((ny,)),
            DMA((ny,)),
            DMA((max(ny - 1, 1),)),
            DMA((max(ny - 1, 1),)),
            DMA((ns - 1,)),
            DMA((ns - 1,)),
        ]

    def begin(self):
        for copy in self.first + self.extra + self.own:
            copy.start()

    def middle(self):
        for arrived, onward in zip(self.first[:-1], self.second):
            arrived.wait_recv()
            onward.start()

    def finish(self):
        for copy in [self.first[-1]] + self.second + self.extra:
            copy.wait_recv()
        for copy in self.own:
            copy.wait()

    def drain(self):
        for copy in self.first + self.second + self.extra:
            copy.wait_send()


def sum_weights_kernel(
    ns,
    ne,
    blocks,
    gin,
    gcommon,
    gout,
    dproj_ref,
    in_ref,
    common_ref,
    tok_ref,
    resid_ref,
    gain_ref,
    aux_ref,
    *refs,
):
    sources = refs[:blocks]
    in_out, pack_out, out_rows, tok_out, aux_out, shared_out = refs[blocks : blocks + 6]
    block_outs = refs[blocks + 6 : 2 * blocks + 5]
    sum_weights_body(
        ns,
        ne,
        sources,
        block_outs,
        gin,
        gcommon,
        gout,
        dproj_ref,
        in_ref,
        common_ref,
        tok_ref,
        resid_ref,
        gain_ref,
        aux_ref,
        in_out,
        pack_out,
        out_rows,
        tok_out,
        aux_out,
        shared_out,
        *refs[2 * blocks + 5 :],
    )


def sum_weights_body(
    ns,
    ne,
    sources,
    block_outs,
    gin,
    gcommon,
    gout,
    dproj_ref,
    in_ref,
    common_ref,
    tok_ref,
    resid_ref,
    gain_ref,
    aux_ref,
    in_out,
    pack_out,
    out_rows,
    tok_out,
    aux_out,
    shared_out,
    out,
    acc,
    acc_out,
    acc_common,
    common_sum,
    common_low,
    fin,
    part_ref,
    lowered_grad,
    aux_part,
    aux_in,
    aux_sum,
    shared_sum,
    shared_low,
    dproj,
    in_held,
    common_held,
    load_sems,
    ssem,
    rsem,
    so,
    ro,
    sc,
    rc,
    sx,
    rx,
    ss,
    rs,
    *scratch,
):
    s, e = lax.axis_index("seq"), lax.axis_index("exp")
    p, right, left = ring_sides(e, ne)
    count = len(SeqSum.scratch(ns, 2, 8, 128, (8, 128)))
    job = SeqSum(ns, 2, part_ref, None, *scratch[:count])
    there = Exchange(ne, aux_part, aux_in, *scratch[count : count + 3])
    back = Exchange(
        ne,
        aux_sum,
        aux_out,
        *scratch[count + 3 : count + 6],
        pick=lambda ref, at: ref.at[s, at],
        spread=True,
    )
    along = []
    at = count + 9 + len(BlockSum.scratch(ns, [gcommon.shape]))
    shared_cols = BlockSum(ns, (gcommon,), (common_sum,), scratch[count + 9 : at])
    more = BlockSum(ns, sources, tuple(block_outs) + (shared_sum,), scratch[at:])
    across = Exchange(ne, shared_low, shared_out, *scratch[count + 6 : count + 9])
    loads = Loads((dproj_ref, in_ref, common_ref), (dproj, in_held, common_held), load_sems)
    shared_cols.load()
    loads.begin()
    more.load()
    greet([((s + t) % ns, e) for t in range(1, ns)] + [(s, (e + t) % ne) for t in range(1, ne)])

    def fill(block):
        rows = pl.ds(pl.multiple_of(block * GROUP, GROUP), GROUP)
        main = in_held.shape[1]
        part = mm_t(dproj[rows, :main], in_held[...])
        part_ref[block] = (part + mm_t(dproj[rows, main:], common_held[...])).astype(BF)

    def tokens_back():
        value = tok_ref[...].astype(F32)
        grad = lowered_grad[...]
        width = value.shape[1]
        scale = lax.rsqrt(jnp.sum(value * value, 1, keepdims=True) / width + EPSILON)
        inside = gain_ref[0:1, :] * grad
        mean = jnp.sum(value * inside, 1, keepdims=True) / width
        tok_out[...] = (resid_ref[...] + scale * inside - value * (scale * scale * scale * mean)).astype(BF)
        gain_grad = jnp.sum(value * scale * grad, 0, keepdims=True)
        aux_part[...] = aux_ref[...]
        for i in range(width // 128):
            row = 6 + i // ne
            aux_part[i % ne, row : row + 1, :128] = gain_grad[:, i * 128 : (i + 1) * 128]
        there.begin()

    def sums():
        there.arrived()
        total = aux_in[0]
        for i in range(1, ne):
            total = total + aux_in[i]
        aux_sum[...] = total
        back.begin()

    def spread():
        back.arrived()
        for t in range(1, ns):
            along.append(
                remote(aux_out.at[s], aux_out.at[s], ss.at[t - 1], rs.at[t - 1], ((s + t) % ns, e))
            )

    def swap():
        shared_low[...] = shared_sum[0].astype(BF)
        across.begin()

    def far_task(j):
        def run():
            fill(job.far(j))
            job.send(j)

        return run

    def common_ready():
        shared_cols.close(0)
        common_low[...] = common_sum[0].astype(BF)
        ready.append(True)

    ready = []
    items = len(more.items)
    lanes = range(1, ns // 2)
    tasks = [(0.0, lambda: loads.wait(0, 1, 2))]
    tasks += [(0.05, functools.partial(shared_cols.join, j, 0)) for j in lanes]
    tasks += [(0.17, common_ready)]
    tasks += [(0.02 * i, far_task(j)) for i, j in enumerate(job.order())]
    tasks += [
        (0.02 * (i + ns // 2), functools.partial(fill, job.near(j)))
        for i, j in enumerate(job.order())
    ]
    tasks += [(0.13, more.begin)]
    tasks += [(0.14, functools.partial(job.join, j, u)) for j in lanes for u in range(job.subs)]
    tasks += [
        (0.22 + 0.15 * (items - 1 - n) / items, functools.partial(more.join, j, n))
        for n in reversed(range(items))
        for j in lanes
    ]
    tasks += [(0.36, functools.partial(job.close, u, lowered_grad)) for u in range(job.subs)]
    tasks += [(0.40, tokens_back), (0.54, sums), (0.68, spread)]
    tasks += [(0.74, functools.partial(more.close, items - 1)), (0.75, swap)]
    tasks += [
        (0.80 + 0.18 * (items - 1 - n) / items, functools.partial(more.close, n))
        for n in range(items - 1)
    ]
    tasks.sort(key=lambda task: task[0])
    shared_cols.begin()
    rows = gin.shape[2]
    main = gin.shape[3]
    tile = tile_rows(rows)
    half = gout.shape[2] // 2
    tile_out = tile_rows(gout.shape[1])
    sent = {}
    last = {}
    done = 0
    lag = 2
    for k in range(ne + lag):
        for t in list(range(1, ns)) + [0, ns, ns + 1, ns + 2]:
            while k > 0 and tasks and tasks[0][0] <= done / (ne * (ns + 3)):
                tasks.pop(0)[1]()
            if t == ns + 2:
                hop = k - lag
                way = 1
            else:
                hop = k
                way = t % 2
            if hop < 0 or hop >= ne:
                continue
            while t == ns + 2 and not ready:
                tasks.pop(0)[1]()
            done += 1
            to = right if way == 0 else left
            place = (p - 1 - hop + 2 * ne) % ne if way == 0 else (p + 1 + hop) % ne
            slot = ring_index(place, ne)
            if hop > 0:
                sent[hop - 1, t].wait_recv()
            if t < ns:
                piece = (s + t) % ns
                if hop > 0:

                    def join(i, carry):
                        r = pl.ds(pl.multiple_of(i * tile, tile), tile)
                        total = acc[hop - 1, t, r, :].astype(F32)
                        total = total + gin[piece, slot, r, :].astype(F32)
                        if hop < ne - 1:
                            acc[hop - 1, t, r, :] = total.astype(BF)
                        elif t == 0:
                            out[s, r, :] = total.astype(BF)
                        else:
                            fin[t - 1, r, :] = total.astype(BF)
                        return carry

                    lax.fori_loop(0, rows // tile, join, 0)
                if hop < ne - 1:
                    src = gin.at[piece, slot] if hop == 0 else acc.at[hop - 1, t]
                    sent[hop, t] = remote(
                        src, acc.at[hop, t], ssem.at[hop, t], rsem.at[hop, t], (s, to)
                    )
                elif t > 0:
                    last[t] = remote(
                        fin.at[t - 1], out.at[s], sx.at[t - 1], rx.at[t - 1], (piece, e)
                    )
            elif t == ns + 2:
                if hop > 0:
                    total = acc_common[hop - 1].astype(F32) + common_low[slot].astype(F32)
                    if hop < ne - 1:
                        acc_common[hop - 1] = total.astype(BF)
                    else:
                        wide = total.shape[1] - pack_out.shape[1]
                        in_out[:, in_out.shape[1] - wide :] = total[:, :wide]
                        pack_out[...] = total[:, wide:]
                if hop < ne - 1:
                    src = common_low.at[slot] if hop == 0 else acc_common.at[hop - 1]
                    sent[hop, t] = remote(
                        src, acc_common.at[hop], sc.at[hop], rc.at[hop], (s, to)
                    )
            else:
                part_columns = pl.ds(way * half, half)
                if hop > 0:

                    def join_out(i, carry):
                        r = pl.ds(pl.multiple_of(i * tile_out, tile_out), tile_out)
                        total = acc_out[hop - 1, r, part_columns].astype(F32)
                        total = total + gout[slot, r, part_columns].astype(F32)
                        if hop < ne - 1:
                            acc_out[hop - 1, r, part_columns] = total.astype(BF)
                        else:
                            out_rows[r, part_columns] = total
                        return carry

                    lax.fori_loop(0, gout.shape[1] // tile_out, join_out, 0)
                if hop < ne - 1:
                    src = (
                        gout.at[slot, :, part_columns]
                        if hop == 0
                        else acc_out.at[hop - 1, :, part_columns]
                    )
                    sent[hop, t] = remote(
                        src,
                        acc_out.at[hop, :, part_columns],
                        so.at[hop, way],
                        ro.at[hop, way],
                        (s, to),
                    )
    for _, task in tasks:
        task()
    for copy in list(last.values()) + along:
        copy.wait_recv()
    head = main // 2
    inner = head * ns
    for block in range(ns):
        in_out[:, block * head : (block + 1) * head] = out[block, :, :head].astype(F32)
        in_out[:, inner + block * head : inner + (block + 1) * head] = out[block, :, head:].astype(F32)
    for copy in list(sent.values()) + list(last.values()) + along:
        copy.wait_send()
    across.arrived()
    more.drain()
    shared_cols.drain()
    job.drain()
    there.drain()
    back.drain()
    across.drain()


def sum_weights(
    gin,
    gcommon,
    gout,
    projected_grad,
    in_local,
    in_common,
    tokens,
    resid_grad,
    gain,
    aux,
    sources,
    pack,
    ns,
    ne,
    cid,
):
    rows, wide = gin.shape[2:]
    narrow = gcommon.shape[4]
    length, model = tokens.shape
    blocks = len(sources)
    return pl.pallas_call(
        functools.partial(sum_weights_kernel, ns, ne, blocks),
        out_shape=(
            jax.ShapeDtypeStruct((rows, ns * wide + narrow - pack), F32),
            jax.ShapeDtypeStruct((rows, pack), F32),
            jax.ShapeDtypeStruct(gout.shape[1:], F32),
            jax.ShapeDtypeStruct(tokens.shape, BF),
            jax.ShapeDtypeStruct((ns,) + aux.shape, F32),
            jax.ShapeDtypeStruct(sources[-1].shape[2:], BF),
        )
        + tuple(jax.ShapeDtypeStruct(v.shape[1:], F32) for v in sources[:-1]),
        in_specs=[VMEM, ANY, VMEM] + [ANY] * 3 + [VMEM] * 4 + [ANY] * blocks,
        out_specs=(VMEM,) * (5 + blocks),
        scratch_shapes=[
            pltpu.VMEM((ns, rows, wide), BF),
            pltpu.VMEM((ne - 1, ns, rows, wide), BF),
            pltpu.VMEM((ne - 1,) + gout.shape[1:], BF),
            pltpu.VMEM((ne - 1, rows, narrow), BF),
            pltpu.VMEM(gcommon.shape[1:], F32),
            pltpu.VMEM(gcommon.shape[2:], BF),
            pltpu.VMEM((ns - 1, rows, wide), BF),
            pltpu.VMEM((ns, length, model), BF),
            pltpu.VMEM((length, model), F32),
            pltpu.VMEM(aux.shape, F32),
            pltpu.VMEM(aux.shape, F32),
            pltpu.VMEM(aux.shape[1:], F32),
            pltpu.VMEM(sources[-1].shape[1:], F32),
            pltpu.VMEM(sources[-1].shape[2:], BF),
        ]
        + Loads.scratch([projected_grad, in_local, in_common])
        + [
            DMA((ne - 1, ns)),
            DMA((ne - 1, ns)),
            DMA((ne - 1, 2)),
            DMA((ne - 1, 2)),
            DMA((ne - 1,)),
            DMA((ne - 1,)),
            DMA((ns - 1,)),
            DMA((ns - 1,)),
            DMA((ns - 1,)),
            DMA((ns - 1,)),
        ]
        + SeqSum.scratch(ns, 2, length, model, (8, 128))
        + Exchange.scratch(ne)
        + Exchange.scratch(ne)
        + Exchange.scratch(ne)
        + BlockSum.scratch(ns, [gcommon.shape])
        + BlockSum.scratch(ns, [v.shape for v in sources]),
        compiler_params=params(cid, 60),
        name="sum_weights",
    )(
        gin,
        gcommon,
        gout,
        projected_grad,
        in_local,
        in_common,
        tokens,
        resid_grad,
        gain,
        aux,
        *sources,
    )


def matmul_plain(left, right):
    return jnp.dot(left, right, preferred_element_type=F32)


def matmul_rows(left, right):
    return lax.dot_general(left, right, (((0,), (0,)), ((), ())), preferred_element_type=F32)


def matmul_cols(left, right):
    return lax.dot_general(left, right, (((1,), (1,)), ((), ())), preferred_element_type=F32)


def mm(left, right):
    return jnp.dot(left, right, preferred_element_type=F32)


def mm_t(left, right):
    return lax.dot_general(left, right, (((1,), (1,)), ((), ())), preferred_element_type=F32)


def t_mm(left, right):
    return lax.dot_general(left, right, (((0,), (0,)), ((), ())), preferred_element_type=F32)


def exact(left, right):
    return jnp.dot(left, right, precision=PRECISE, preferred_element_type=F32)


def spread_heads(table, heads, head_dim):
    rows = table.shape[0]
    per = 128 // head_dim
    lane = lax.broadcasted_iota(jnp.int32, (rows, 128), 1)
    tiles = []
    for h in range(0, heads, per):
        tile = jnp.broadcast_to(table[:, h : h + 1], (rows, 128))
        for i in range(1, per):
            other = jnp.broadcast_to(table[:, h + i : h + i + 1], (rows, 128))
            tile = jnp.where(lane >= i * head_dim, other, tile)
        tiles.append(tile)
    return jnp.concatenate(tiles, 1)


def sigmoid(v):
    return 1.0 / (1.0 + jnp.exp(-v))


def softplus(v):
    return jnp.maximum(v, 0.0) + jnp.log1p(jnp.exp(-jnp.abs(v)))


def triangle(flip=False):
    t = lax.broadcasted_iota(jnp.int32, (GROUP, GROUP), 0)
    u = lax.broadcasted_iota(jnp.int32, (GROUP, GROUP), 1)
    return u >= t if flip else t >= u


def step_table(pack, bias, heads, s):
    turned = pltpu.roll(pack, (128 - heads * s) % 128, 1)
    lane = lax.broadcasted_iota(jnp.int32, turned.shape, 1)
    raw = jnp.where(lane < heads, turned + bias, 0.0)
    return raw, jnp.where(lane < heads, softplus(raw), 0.0)


def convolved(ext, table, width):
    mixed = table[width : width + 1]
    for j in range(width):
        mixed = mixed + table[j : j + 1] * ext[8 - width + 1 + j : 8 - width + 1 + j + GROUP]
    return mixed


def with_before(proj_ref, at, columns, first):
    before = proj_ref[pl.ds(pl.multiple_of(jnp.maximum(at - 8, 0), 8), 8), columns]
    before = jnp.where(first, 0.0, before)
    return jnp.concatenate([before, proj_ref[pl.ds(at, GROUP), columns]], 0)


def mix_forward_kernel(
    ns,
    ne,
    hw,
    state2,
    heads,
    width,
    norm_at,
    x_ref,
    w_hbm,
    c_hbm,
    table_ref,
    head_ref,
    out_hbm,
    grad_ref,
    proj_hbm,
    lowered_hbm,
    scan_hbm,
    mix_hbm,
    entry_hbm,
    sum_ref,
    square_out,
    grad_all,
    proj_ref,
    lowered_ref,
    scan_ref,
    mix_ref,
    entry_ref,
    state,
    low_ref,
    square_ref,
    part_ref,
    store_sem,
    w_ref,
    c_ref,
    out_ref,
    load_sem,
    *sems,
):
    s, e = lax.axis_index("seq"), lax.axis_index("exp")
    p, right, left = ring_sides(e, ne)
    loads = Loads((w_hbm, c_hbm, out_hbm), (w_ref, c_ref, out_ref), load_sem)
    loads.begin()
    greet([((s + t) % ns, e) for t in range(1, ns)] + [(s, right), (s, left)])
    ring = RingGather(ne, grad_ref, grad_all, *sems[:3])
    job = SeqSum(ns, 2, part_ref, square_ref, *sems[3:])
    ring.begin()
    pairs = (
        (proj_ref, proj_hbm),
        (lowered_ref, lowered_hbm),
        (scan_ref, scan_hbm),
        (mix_ref, mix_hbm),
    )

    def stores(c):
        rows = pl.ds(pl.multiple_of(c * GROUP, GROUP), GROUP)
        copies = [
            pltpu.make_async_copy(ref.at[rows], hbm.at[rows], store_sem.at[c, i])
            for i, (ref, hbm) in enumerate(pairs)
        ]
        copies.append(
            pltpu.make_async_copy(entry_ref.at[c], entry_hbm.at[c], store_sem.at[c, len(pairs)])
        )
        return copies

    loads.wait(0, 1)
    norm = c_ref[:, state2:].astype(F32).T[norm_at : norm_at + 1, :]
    blocks = x_ref.shape[0] // GROUP
    head_dim = hw // heads
    n = state2 // 2
    state[...] = jnp.zeros_like(state)
    lane = lax.broadcasted_iota(jnp.int32, (GROUP, 128), 1)
    table = table_ref[...]
    skip = table[width + 2 : width + 3, :hw]
    gain = table[width + 1 : width + 2, :hw]
    bias, rate = head_ref[0:1, :], head_ref[1:2, :]

    def chunk(c, carry):
        at = pl.multiple_of(c * GROUP, GROUP)
        rows = pl.ds(at, GROUP)
        causal = triangle()
        x = x_ref[rows, :].astype(F32)
        scale = lax.rsqrt(jnp.sum(x * x, 1, keepdims=True) / x.shape[1] + EPSILON)
        lowered = (x * scale * norm).astype(BF)
        lowered_ref[rows, :] = lowered
        proj_ref[rows, : 2 * hw] = mm(lowered, w_ref[...])
        proj_ref[rows, 2 * hw :] = mm(lowered, c_ref[...])
        ext = with_before(proj_ref, at, slice(hw, 2 * hw + state2), c == 0)
        mixed = convolved(ext, table, width)
        mix_ref[rows, :] = mixed
        conv = mixed * sigmoid(mixed)
        values = conv[:, :hw]
        b = conv[:, hw : hw + n].astype(BF)
        ct = conv[:, hw + n :].astype(BF)
        _, steps = step_table(proj_ref[rows, 2 * hw + state2 :], bias, heads, s)
        logs = exact(causal.astype(F32), steps * rate)
        logs_t, steps_t = logs.T, steps.T
        end = logs[GROUP - 1 : GROUP, :]
        before = state[...]
        entry_ref[c] = before
        carried = mm(ct, before.astype(BF)) * spread_heads(jnp.exp(logs), heads, head_dim)
        tails = spread_heads(jnp.exp(end - logs) * steps, heads, head_dim)
        fresh = t_mm(b, (values * tails).astype(BF))
        state[...] = spread_heads(jnp.exp(end), heads, head_dim) * before + fresh
        cross = mm_t(ct, b)
        low = values.astype(BF)
        tiles = []
        per = 128 // head_dim
        for h in range(0, heads, per):
            tile = None
            part = low[:, h * head_dim : h * head_dim + 128]
            for i in range(per):
                gap = logs[:, h + i : h + i + 1] - logs_t[h + i : h + i + 1, :]
                kernel = jnp.exp(jnp.where(causal, gap, -1e30))
                weights = cross * kernel * steps_t[h + i : h + i + 1, :]
                one = mm(weights.astype(BF), part)
                tile = one if i == 0 else jnp.where(lane >= i * head_dim, one, tile)
            tiles.append(tile)
        scanned = jnp.concatenate(tiles, 1) + carried + skip * values
        scan_ref[rows, :] = scanned
        gate = proj_ref[rows, :hw]
        gated = scanned * (gate * sigmoid(gate))
        low_ref[rows, :] = (gated * gain).astype(BF)
        square_ref[c] = lax.dot_general(
            jnp.ones((8, hw), F32),
            gated * gated,
            (((1,), (1,)), ((), ())),
            precision=PRECISE,
            preferred_element_type=F32,
        )

        for copy in stores(c):
            copy.start()
        ring.step(c + 1)

        return carry

    lax.fori_loop(0, blocks, chunk, 0)

    def fill(block):
        rows = pl.ds(pl.multiple_of(block * GROUP, GROUP), GROUP)
        part_ref[block] = mm(low_ref[rows, :], out_ref[...]).astype(BF)

    k = blocks + 1
    loads.wait(2)
    job.begin(fill)
    for stage in (job.middle, lambda: job.finish(sum_ref, square_out)):
        if k < ne - 1:
            ring.step(k)
            k += 1
        stage()
    while k < ne - 1:
        ring.step(k)
        k += 1
    ring.finish()
    job.drain()
    for c in range(blocks):
        for copy in stores(c):
            copy.wait()


def mix_forward(
    sequence,
    in_local,
    in_common,
    table,
    head_table,
    out_local,
    grad_low,
    ns,
    ne,
    hw,
    state2,
    heads,
    width,
    norm_at,
    cid,
):
    whole, model = sequence.shape
    blocks = whole // GROUP
    n = state2 // 2
    rows = grad_low.shape[0]
    columns = in_local.shape[1] + in_common.shape[1]
    kept = [
        jax.ShapeDtypeStruct((whole, columns), F32),
        jax.ShapeDtypeStruct((whole, model), BF),
        jax.ShapeDtypeStruct((whole, hw), F32),
        jax.ShapeDtypeStruct((whole, hw + state2), F32),
        jax.ShapeDtypeStruct((blocks, n, hw), F32),
    ]
    return pl.pallas_call(
        functools.partial(mix_forward_kernel, ns, ne, hw, state2, heads, width, norm_at),
        out_shape=tuple(kept)
        + (
            jax.ShapeDtypeStruct((rows, model), F32),
            jax.ShapeDtypeStruct((8, rows), F32),
            jax.ShapeDtypeStruct((ne, rows, model), BF),
        ),
        in_specs=[VMEM, ANY, ANY, VMEM, VMEM, ANY, VMEM],
        out_specs=(ANY,) * 5 + (VMEM,) * 3,
        scratch_shapes=[pltpu.VMEM(v.shape, v.dtype) for v in kept]
        + [
            pltpu.VMEM((n, hw), F32),
            pltpu.VMEM((whole, hw), BF),
            pltpu.VMEM((blocks, 8, GROUP), F32),
            pltpu.VMEM((ns, rows, model), BF),
            DMA((blocks, 5)),
        ]
        + Loads.scratch([in_local, in_common, out_local])
        + RingGather.scratch(ne, 2)
        + SeqSum.scratch(ns, 2, rows, model, (8, rows)),
        compiler_params=params(cid, 56),
        name="mix_forward",
    )(sequence, in_local, in_common, table, head_table, out_local, grad_low)


def mix_backward_kernel(
    ns,
    ne,
    hw,
    state2,
    heads,
    width,
    proj_hbm,
    table_ref,
    head_ref,
    scan_hbm,
    mix_hbm,
    entry_hbm,
    out_hbm,
    resid_ref,
    rows_ref,
    part_ref,
    expert_ref,
    sum_ref,
    expert_out,
    dproj_ref,
    grad_out_ref,
    dtable_ref,
    dhead_ref,
    adjoint,
    after,
    low_ref,
    resid_all,
    scale_ref,
    *scratch,
):
    s, e = lax.axis_index("seq"), lax.axis_index("exp")
    p, right, left = ring_sides(e, ne)
    loads = Loads((proj_hbm, scan_hbm, mix_hbm, entry_hbm, out_hbm), scratch[:5], scratch[5])
    proj_ref, scan_ref, mix_ref, entry_ref, out_ref = scratch[:5]
    loads.begin()
    greet([((s + t) % ns, e) for t in range(1, ns)] + [(s, right), (s, left)])
    ring = RingSum(ne, part_ref, *scratch[6:9])
    at = 9 + len(SeqGather.scratch(ns))
    rows_in = SeqGather(ns, resid_ref, rows_ref, resid_all, scale_ref, *scratch[9:at])
    experts = BlockSum(ns, (expert_ref,), (expert_out,), scratch[at:])
    experts.load()
    rows_in.begin()
    ring.begin()
    ring.step(1)
    rows_in.middle()
    experts.begin()
    ring.step(2)
    rows_in.finish()
    for j in range(1, ns // 2):
        for n in range(len(experts.items)):
            experts.join(j, n)
    loads.wait(*range(5))
    blocks = proj_ref.shape[0] // GROUP
    head_dim = hw // heads
    n = state2 // 2
    per = 128 // head_dim
    adjoint[...] = jnp.zeros_like(adjoint)
    after[...] = jnp.zeros_like(after)
    dtable_ref[...] = jnp.zeros_like(dtable_ref)
    dhead_ref[...] = jnp.zeros_like(dhead_ref)
    lane = lax.broadcasted_iota(jnp.int32, (GROUP, 128), 1)
    row = lax.broadcasted_iota(jnp.int32, (GROUP, 128), 0)
    table = table_ref[...]
    skip = table[width + 2 : width + 3, :hw]
    gain = table[width + 1 : width + 2, :hw]
    bias, rate = head_ref[0:1, :], head_ref[1:2, :]

    def chunk(lap, carry):
        c = blocks - 1 - lap
        at = pl.multiple_of(c * GROUP, GROUP)
        rows = pl.ds(at, GROUP)
        causal = triangle()
        head_of = lax.broadcasted_iota(jnp.int32, (hw, 128), 0) // head_dim
        pick = (head_of == lax.broadcasted_iota(jnp.int32, (hw, 128), 1)).astype(F32)
        gate = proj_ref[rows, :hw]
        gate_sig = sigmoid(gate)
        gate_silu = gate * gate_sig
        scanned = scan_ref[rows, :]
        gated = scanned * gate_silu
        scales = scale_ref[c].T
        r, inside = scales[:, 0:1], scales[:, 1:2]
        q = mm_t(resid_all[c], out_ref[...])
        dgated = r * (gain * q) - gated * (r * r * r * inside)
        low_ref[rows, :] = (gated * gain * r).astype(BF)
        dtable_ref[width + 1 : width + 2, :hw] += jnp.sum(gated * r * q, 0, keepdims=True)
        dy = dgated * gate_silu
        dproj_ref[rows, :hw] = (dgated * scanned * (gate_sig + gate_silu * (1 - gate_sig))).astype(BF)

        mixed = mix_ref[rows, :]
        sig = sigmoid(mixed)
        conv = mixed * sig
        values = conv[:, :hw]
        b = conv[:, hw : hw + n].astype(BF)
        ct = conv[:, hw + n :].astype(BF)
        dtable_ref[width + 2 : width + 3, :hw] += jnp.sum(dy * values, 0, keepdims=True)
        raw, steps = step_table(proj_ref[rows, 2 * hw + state2 :], bias, heads, s)
        logs = exact(causal.astype(F32), steps * rate)
        logs_t, steps_t = logs.T, steps.T
        end = logs[GROUP - 1 : GROUP, :]
        rest = jnp.exp(end - logs)
        tail = rest * steps
        ends = jnp.exp(end)
        before = entry_ref[c]
        before_low = before.astype(BF)
        later = adjoint[...]
        later_low = later.astype(BF)
        tails = spread_heads(tail, heads, head_dim)
        dy_carried = dy * spread_heads(jnp.exp(logs), heads, head_dim)
        dy_carried_low = dy_carried.astype(BF)
        carried = mm(ct, before_low)
        back = mm(b, later_low)
        dvalues = tails * back + skip * dy
        dc = mm_t(dy_carried_low, before_low)
        db = mm_t((values * tails).astype(BF), later_low)
        kept = jnp.sum(later * before, 0, keepdims=True)
        adjoint[...] = spread_heads(ends, heads, head_dim) * later + t_mm(ct, dy_carried_low)
        sums = exact(jnp.concatenate([dy_carried * carried, values * back, jnp.broadcast_to(kept, (8, hw))], 0), pick)
        from_carried, dtail, kept = sums[:GROUP], sums[GROUP : 2 * GROUP], sums[2 * GROUP : 2 * GROUP + 1]
        cross = mm_t(ct, b)
        low = values.astype(BF)
        dy_low = dy.astype(BF)
        dcross = jnp.zeros((GROUP, GROUP), F32)
        dlogs = from_carried - dtail * tail
        columns = []
        tiles = []
        for h in range(0, heads, per):
            part = low[:, h * head_dim : h * head_dim + 128]
            dy_part = dy_low[:, h * head_dim : h * head_dim + 128]
            tile = None
            for i in range(per):
                gap = logs[:, h + i : h + i + 1] - logs_t[h + i : h + i + 1, :]
                kernel = jnp.exp(jnp.where(causal, gap, -1e30))
                scaled = kernel * steps_t[h + i : h + i + 1, :]
                weights = cross * scaled
                inside_head = (lane >= i * head_dim) & (lane < (i + 1) * head_dim)
                one = t_mm(weights.astype(BF), dy_part)
                tile = one if i == 0 else jnp.where(lane >= i * head_dim, one, tile)
                dweights = mm_t(jnp.where(inside_head, dy_part, jnp.zeros_like(dy_part)), part)
                dcross = dcross + dweights * scaled
                unscaled = dweights * (cross * kernel)
                total = jnp.sum(dweights * weights, 1, keepdims=True)
                dlogs = dlogs + jnp.where(lane == h + i, total, 0.0)
                columns.append(jnp.sum(unscaled, 0, keepdims=True))
            tiles.append(tile)
        dvalues = dvalues + jnp.concatenate(tiles, 1)
        columns = jnp.concatenate(columns + [jnp.zeros((128 - heads, GROUP), F32)], 0).T
        dlogs = dlogs - columns * steps
        at_end = jnp.sum(dtail * tail, 0, keepdims=True) + ends * kept
        dlogs = dlogs + jnp.where(row == GROUP - 1, at_end, 0.0)
        da = exact(triangle(True).astype(F32), dlogs)
        dsteps = columns + dtail * rest + da * rate
        dhead_ref[1:2, :] += jnp.sum(da * steps, 0, keepdims=True)
        draw = jnp.where(lane < heads, dsteps * sigmoid(raw), 0.0)
        dhead_ref[0:1, :] += jnp.sum(draw, 0, keepdims=True)
        dproj_ref[rows, 2 * hw + state2 :] = pltpu.roll(draw, heads * s, 1).astype(BF)
        dcross_low = dcross.astype(BF)
        dc = dc + mm(dcross_low, b)
        db = db + t_mm(dcross_low, ct)
        dmix = jnp.concatenate([dvalues, db, dc], 1) * (sig + conv * (1 - sig))
        dtable_ref[width : width + 1, :] += jnp.sum(dmix, 0, keepdims=True)
        ext = with_before(proj_ref, at, slice(hw, 2 * hw + state2), c == 0)
        dext = jnp.concatenate([dmix, after[...]], 0)
        dconv = 0.0
        for j in range(width):
            first = 8 - width + 1 + j
            dtable_ref[j : j + 1, :] += jnp.sum(dmix * ext[first : first + GROUP], 0, keepdims=True)
            dconv = dconv + table[j : j + 1] * dext[width - 1 - j : width - 1 - j + GROUP]
        after[...] = dmix[:8]
        dproj_ref[rows, hw : 2 * hw + state2] = dconv.astype(BF)
        ring.step(lap + 3)
        return carry

    lax.fori_loop(0, blocks, chunk, 0)
    model = resid_all.shape[2]
    every = resid_all[...].reshape(blocks * GROUP, model)
    for d in range(0, hw, 128):
        low_t = low_ref[:, d : d + 128].T
        grad_out_ref[d : d + 128, :] = mm(low_t, every).astype(BF)
    for k in range(blocks + 3, ne - 1):
        ring.step(k)
    ring.finish(sum_ref)
    for n in range(len(experts.items)):
        experts.close(n)
    experts.drain()
    rows_in.drain()


def mix_backward(
    proj,
    table,
    head_table,
    scanned,
    mixed,
    entries,
    out_local,
    resid_low,
    scales,
    out_part,
    expert_part,
    ns,
    ne,
    hw,
    state2,
    heads,
    width,
    cid,
):
    whole = proj.shape[0]
    n = state2 // 2
    rows, model = resid_low.shape
    return pl.pallas_call(
        functools.partial(mix_backward_kernel, ns, ne, hw, state2, heads, width),
        out_shape=(
            jax.ShapeDtypeStruct((rows, model), F32),
            jax.ShapeDtypeStruct(expert_part.shape[1:], F32),
            jax.ShapeDtypeStruct(proj.shape, BF),
            jax.ShapeDtypeStruct((hw, model), BF),
            jax.ShapeDtypeStruct((8, hw + state2), F32),
            jax.ShapeDtypeStruct((8, 128), F32),
        ),
        in_specs=[ANY, VMEM, VMEM] + [ANY] * 4 + [VMEM] * 3 + [ANY],
        out_specs=(VMEM,) * 6,
        scratch_shapes=[
            pltpu.VMEM((n, hw), F32),
            pltpu.VMEM((8, hw + state2), F32),
            pltpu.VMEM((whole, hw), BF),
            pltpu.VMEM((ns, rows, model), BF),
            pltpu.VMEM((ns, 8, rows), F32),
        ]
        + Loads.scratch([proj, scanned, mixed, entries, out_local])
        + RingSum.scratch(ne, 2, rows, model)
        + SeqGather.scratch(ns)
        + BlockSum.scratch(ns, [expert_part.shape]),
        compiler_params=params(cid, 56),
        name="mix_backward",
    )(
        proj,
        table,
        head_table,
        scanned,
        mixed,
        entries,
        out_local,
        resid_low,
        scales,
        out_part,
        expert_part,
    )


def rms_back(value, gain, grad):
    scale = lax.rsqrt(jnp.mean(value * value, -1, keepdims=True) + EPSILON)
    inside = gain * grad
    back = scale * inside - value * scale**3 * jnp.mean(value * inside, -1, keepdims=True)
    return back, jnp.sum(value * scale * grad, 0)


def swiglu_back(a, b, grad):
    sig = jax.nn.sigmoid(a)
    return grad * b * sig * (1 + a * (1 - sig)), grad * a * sig


def on_device(
    tokens,
    routes,
    out_grad,
    norm_mix,
    in_weight,
    step_weight,
    conv_weight,
    conv_bias,
    step_bias,
    decay_log,
    skip_gain,
    norm_gate,
    out_weight,
    norm_ffn,
    router_weight,
    shared_gate,
    shared_up,
    shared_down,
    expert_gate,
    expert_up,
    expert_down,
):
    ns, ne = lax.axis_size("seq"), lax.axis_size("exp")
    s, e = lax.axis_index("seq"), lax.axis_index("exp")
    total = ns * ne
    rows, columns = in_weight.shape
    model = tokens.shape[2]
    length = tokens.shape[1]
    whole = length * ns
    width, channels = conv_weight.shape
    gains = norm_gate.shape[0]
    inner = gains * total
    hw = inner // ns
    heads = step_bias.shape[0]
    local_heads = heads // ns
    state2 = columns - 2 * inner
    experts = router_weight.shape[1]
    local_experts = expert_gate.shape[0]
    place = s * ne + e

    small = jnp.concatenate([conv_weight.reshape(-1), conv_bias, norm_gate])
    small = jnp.pad(small, (0, 16 * rows - small.shape[0])).reshape(rows, 16)
    pack = jnp.concatenate(
        [step_weight, router_weight, norm_mix[:, None], norm_ffn[:, None], small], 1
    )
    at_small = heads + experts + 2
    pack = jnp.pad(pack, ((0, 0), (0, 128 - pack.shape[1])))
    hidden_rows = shared_down.shape[0]

    def by_owner(weight):
        split = weight.reshape(rows, ns, ne, hidden_rows)
        return jnp.transpose(split, (2, 0, 1, 3)).reshape(ne, rows, ns * hidden_rows)

    shared_two = jnp.concatenate([by_owner(shared_gate), by_owner(shared_up)], -1)
    in_blocks, common_blocks, token_blocks, out_local, shared_two, local_down = gather_in(
        in_weight, pack, tokens[0], out_weight, shared_two, shared_down, ns, ne, inner, 0
    )
    out_local = out_local.reshape(hw, model)
    shared_two = shared_two.reshape(model, 2 * ns * hidden_rows)
    local_gate, local_up = shared_two[:, : ns * hidden_rows], shared_two[:, ns * hidden_rows :]
    local_down = local_down.reshape(ns * hidden_rows, model)
    grad_low = out_grad[0]
    in_local = in_blocks.reshape(model, -1)
    in_common = common_blocks.reshape(model, -1)
    full_pack = in_common[:, state2:]
    full_router = full_pack[:, heads : heads + experts]
    full_norm_mix = full_pack[:, heads + experts].astype(F32)
    full_norm_ffn = full_pack[:, heads + experts + 1].astype(F32)
    full_small = full_pack[:, at_small : at_small + 16].reshape(total, 16 * rows).astype(F32)
    full_conv = full_small[:, : (width + 1) * channels].reshape(total, width + 1, channels)
    full_conv = jnp.swapaxes(full_conv, 0, 1).reshape(width + 1, total * channels)
    at_gain = (width + 1) * channels
    full_norm_gate = full_small[:, at_gain : at_gain + gains].reshape(inner)
    local_conv = jnp.concatenate(
        [lax.dynamic_slice_in_dim(full_conv, s * hw, hw, 1), full_conv[:, inner:]], 1
    )
    local_gain = lax.dynamic_slice_in_dim(full_norm_gate, s * hw, hw)
    at_head = s * local_heads
    local_bias = lax.dynamic_slice_in_dim(step_bias, at_head, local_heads)
    local_decay = lax.dynamic_slice_in_dim(decay_log, at_head, local_heads)
    local_skip = lax.dynamic_slice_in_dim(skip_gain, at_head, local_heads)

    table = jnp.concatenate(
        [
            local_conv,
            jnp.pad(
                jnp.stack([local_gain, jnp.repeat(local_skip, hw // local_heads)]),
                ((0, 6 - width - 1), (0, state2)),
            ),
        ],
        0,
    )
    head_table = jnp.pad(
        jnp.stack([local_bias, -jnp.exp(local_decay)]), ((0, 6), (0, 128 - local_heads))
    )

    token_rows = tokens[0].astype(F32)
    projected, lowered, scanned, mixed, entries, mixed_raw, squares, grad_all = mix_forward(
        token_blocks.reshape(whole, model),
        in_local,
        in_common,
        table,
        head_table,
        out_local,
        grad_low,
        ns,
        ne,
        hw,
        state2,
        local_heads,
        width,
        heads + experts,
        1,
    )
    scale_gate = lax.rsqrt(squares[0] / inner + EPSILON)
    mixer_out = mixed_raw * scale_gate[:, None]
    resid = token_rows + mixer_out
    scale_two = lax.rsqrt(jnp.mean(resid * resid, -1, keepdims=True) + EPSILON)
    ffn_in = (resid * scale_two * full_norm_ffn).astype(BF)

    logits = matmul_plain(ffn_in, full_router)
    named = jnp.any(
        routes[0][:, :, None] == jnp.arange(experts, dtype=jnp.int32)[None, None, :], 1
    )
    top = jnp.max(jnp.where(named, logits, -jnp.inf), -1, keepdims=True)
    raised = jnp.where(named, jnp.exp(jnp.where(named, logits - top, 0.0)), 0.0)
    gates = (raised / jnp.sum(raised, -1, keepdims=True)).T

    gates_out = jnp.pad(
        gates.reshape(ne, local_experts, length), ((0, 0), (0, 8 - local_experts), (0, 0))
    )
    back_sum, gate_grads, out_part, grad_gate, grad_up, grad_down, shared_part, grad_shared_down = (
        experts_both_ways(
            ffn_in,
            gates_out,
            grad_all,
            expert_gate,
            expert_up,
            expert_down,
            shared_two,
            local_down,
            ns,
            ne,
            2,
        )
    )
    gate_grads = gate_grads[:, :local_experts].reshape(experts, length)
    picked_grad = gates * (gate_grads - jnp.sum(gates * gate_grads, 0, keepdims=True))
    logit_grad = picked_grad.T.astype(BF)
    grad_router = matmul_rows(ffn_in, logit_grad)
    ffn_in_grad = matmul_cols(logit_grad, full_router) + back_sum
    resid_norm_grad, grad_norm_ffn = rms_back(resid, full_norm_ffn, ffn_in_grad)
    resid_grad = grad_low.astype(F32) + resid_norm_grad
    resid_low = resid_grad.astype(BF)
    inside = jnp.sum(resid_low.astype(F32) * mixer_out, -1) / (scale_gate * inner)
    scales = jnp.concatenate(
        [scale_gate[None], inside[None], jnp.zeros((6, length), F32)], 0
    )

    ffn_out, grad_gate, projected_grad, grad_out, table_grad, head_grad = mix_backward(
        projected,
        table,
        head_table,
        scanned,
        mixed,
        entries,
        out_local,
        resid_low,
        scales,
        out_part,
        grad_gate,
        ns,
        ne,
        hw,
        state2,
        local_heads,
        width,
        4,
    )
    result = (resid + ffn_out).astype(BF)
    stat_terms = jnp.stack(
        [jnp.sum(resid * resid), jnp.sum(mixer_out * mixer_out), jnp.sum(ffn_out * ffn_out)]
    )
    grad_skip = jnp.sum(table_grad[width + 2, :hw].reshape(local_heads, -1), -1)
    grad_decay = head_grad[1, :local_heads] * head_table[1, :local_heads]

    small_parts = [
        table_grad[: width + 1],
        table_grad[width + 1, :hw],
        head_grad[0, :local_heads],
        grad_decay,
        grad_skip,
        grad_norm_ffn,
        stat_terms,
    ]
    ends = []
    at = 0
    for part in small_parts:
        ends.append((at, at + part.size, part.shape))
        at += part.size
    room = 6 * 256
    aux = jnp.concatenate([part.reshape(-1) for part in small_parts])
    aux = jnp.pad(aux, (0, ne * room - at)).reshape(ne, 6, 256)
    aux = jnp.pad(aux, ((0, 0), (0, 2), (0, 0)))

    in_grad = matmul_rows(lowered, projected_grad[:, : 2 * hw]).astype(BF)
    common_grad = matmul_rows(lowered, projected_grad[:, 2 * hw :])
    common_grad = common_grad + jnp.pad(
        grad_router, ((0, 0), (state2 + heads, 128 - heads - experts))
    )
    (
        grad_in,
        grad_pack,
        grad_out,
        tokens_grad,
        sums,
        shared_part,
        grad_up,
        grad_down,
        grad_shared_down,
    ) = sum_weights(
        in_grad.reshape(ns, ne, rows, -1),
        common_grad.astype(BF).reshape(ns, 1, ne, rows, -1),
        grad_out.reshape(ne, hw // ne, model),
        projected_grad,
        in_local,
        in_common,
        tokens[0],
        resid_grad,
        jnp.broadcast_to(full_norm_mix[None], (8, model)),
        aux,
        [
            grad_up,
            grad_down,
            grad_shared_down.reshape(ns, 1, hidden_rows, model),
            shared_part.reshape(ns, 1, ne, rows, -1),
        ],
        128,
        ns,
        ne,
        6,
    )
    grad_step = grad_pack[:, :heads]
    grad_router = grad_pack[:, heads : heads + experts]
    flat = sums[:, :, :6].reshape(ns, ne * room)
    table_all, gain_all, bias_all, decay_all, skip_all, ffn_all, stat_all = [
        flat[:, start:end].reshape((ns,) + shape) for start, end, shape in ends
    ]
    conv_all = jnp.concatenate(
        [
            jnp.swapaxes(table_all[:, :, :hw], 0, 1).reshape(width + 1, inner),
            jnp.sum(table_all[:, :, hw:], 0),
        ],
        1,
    )
    conv_grads = lax.dynamic_slice_in_dim(conv_all, place * channels, channels, 1)
    mix_sums = jnp.sum(sums[:, :, 6:, :128], 0)
    grad_norm_mix = jnp.swapaxes(mix_sums, 0, 1).reshape(-1)[:model]
    shared_part = shared_part.astype(F32).reshape(ne, rows, 2, ns, hidden_rows)
    shared_grads = jnp.transpose(shared_part, (2, 1, 3, 0, 4)).reshape(2, rows, total * hidden_rows)
    return (
        result[None],
        tokens_grad[None],
        lax.dynamic_slice_in_dim(grad_norm_mix, place * rows, rows),
        grad_in,
        grad_step,
        conv_grads[:width],
        conv_grads[width],
        bias_all.reshape(heads),
        decay_all.reshape(heads),
        skip_all.reshape(heads),
        lax.dynamic_slice_in_dim(gain_all.reshape(inner), place * gains, gains),
        grad_out,
        lax.dynamic_slice_in_dim(jnp.sum(ffn_all, 0), place * rows, rows),
        grad_router,
        shared_grads[0],
        shared_grads[1],
        grad_shared_down[0],
        grad_gate,
        grad_up,
        grad_down,
        jnp.sum(stat_all, 0) / (total * length * model),
    )


def solution(mesh):
    both = ("seq", "exp")
    return jax.shard_map(
        on_device,
        mesh=mesh,
        in_specs=(
            P("exp", "seq", None),
            P("exp", "seq", None),
            P("exp", "seq", None),
            P(both),
            P(both, None),
            P(both, None),
            P(None, both),
            P(both),
            P(),
            P(),
            P(),
            P(both),
            P(both, None),
            P(both),
            P(both, None),
            P(both, None),
            P(both, None),
            P(both, None),
            P("exp", None, None),
            P("exp", None, None),
            P("exp", None, None),
        ),
        out_specs=(
            P("exp", "seq", None),
            P("exp", "seq", None),
            P(both),
            P(both, None),
            P(both, None),
            P(None, both),
            P(both),
            P(),
            P(),
            P(),
            P(both),
            P(both, None),
            P(both),
            P(both, None),
            P(both, None),
            P(both, None),
            P(both, None),
            P("exp", "seq", None),
            P("exp", "seq", None),
            P("exp", None, "seq"),
            P(),
        ),
        check_vma=False,
    )
```

```python
import functools

import jax
import jax.numpy as jnp
from jax import lax
from jax.experimental import pallas as pl
from jax.experimental.pallas import tpu as pltpu
from jax.sharding import PartitionSpec as P

GROUP = 128
EPSILON = 1e-05
PRECISE = lax.Precision.HIGHEST
MESH = pl.DeviceIdType.MESH
BF = jnp.bfloat16
F32 = jnp.float32
ANY = pl.BlockSpec(memory_space=pl.ANY)
VMEM = pl.BlockSpec(memory_space=pltpu.VMEM)
DMA = pltpu.SemaphoreType.DMA


def ring_place(e, n):
    odd = e % 2
    return (1 - odd) * (e // 2) + odd * (n - 1 - e // 2)


def ring_index(p, n):
    back = p // (n // 2)
    return (1 - back) * (2 * p) + back * (2 * (n - 1 - p) + 1)


def ring_sides(e, n):
    p = ring_place(e, n)
    return p, ring_index((p + 1) % n, n), ring_index((p + n - 1) % n, n)


def greet(partners):
    barrier = pltpu.get_barrier_semaphore()
    for partner in partners:
        pl.semaphore_signal(barrier, inc=1, device_id=partner, device_id_type=MESH)
    pl.semaphore_wait(barrier, len(partners))


def remote(src, dst, send, recv, device):
    copy = pltpu.make_async_remote_copy(
        src_ref=src,
        dst_ref=dst,
        send_sem=send,
        recv_sem=recv,
        device_id=device,
        device_id_type=MESH,
    )
    copy.start()
    return copy


def params(cid, mib=48):
    return pltpu.CompilerParams(
        collective_id=cid, has_side_effects=True, vmem_limit_bytes=mib << 20
    )


class Loads:
    def __init__(self, sources, held, sems):
        self.copies = [
            pltpu.make_async_copy(src, dst, sems.at[i])
            for i, (src, dst) in enumerate(zip(sources, held))
        ]

    @staticmethod
    def scratch(arrays):
        return [pltpu.VMEM(v.shape, v.dtype) for v in arrays] + [DMA((len(arrays),))]

    def begin(self):
        for copy in self.copies:
            copy.start()

    def wait(self, *which):
        for i in which:
            self.copies[i].wait()


def tile_rows(rows, most=16):
    return most if rows % most == 0 else rows


def gather_in_kernel(
    ns,
    ne,
    hw,
    inner,
    in_ref,
    pack_ref,
    tok_ref,
    out_ref,
    two_ref,
    down_ref,
    w_ref,
    c_ref,
    x_ref,
    o_ref,
    shared_ref,
    sd_ref,
    lsem,
    ssem0,
    rsem0,
    ssem,
    rsem,
    sa,
    ra,
    sb,
    rb,
    sc,
    rc,
):
    s, e = lax.axis_index("seq"), lax.axis_index("exp")
    p, right, left = ring_sides(e, ne)
    width = in_ref.shape[1] - 2 * inner
    half = out_ref.shape[1] // 2
    parts = (
        (lambda to: in_ref.at[:, pl.ds(pl.multiple_of(to * hw, 128), hw)], 0),
        (lambda to: in_ref.at[:, pl.ds(pl.multiple_of(inner + to * hw, 128), hw)], hw),
    )
    greet([((s + t) % ns, e) for t in range(1, ns)] + [(s, (e + t) % ne) for t in range(1, ne)])
    own = []
    for i, (piece, start) in enumerate(parts):
        own.append(
            pltpu.make_async_copy(piece(s), w_ref.at[s, e, :, pl.ds(start, hw)], lsem.at[i])
        )
    own.append(
        pltpu.make_async_copy(
            in_ref.at[:, pl.ds(2 * inner, width)], c_ref.at[s, e, :, pl.ds(0, width)], lsem.at[2]
        )
    )
    own.append(
        pltpu.make_async_copy(
            pack_ref, c_ref.at[s, e, :, pl.ds(width, pack_ref.shape[1])], lsem.at[3]
        )
    )
    own.append(pltpu.make_async_copy(out_ref, o_ref.at[e], lsem.at[4]))
    own.append(pltpu.make_async_copy(two_ref.at[e], shared_ref.at[s, e], lsem.at[5]))
    own.append(pltpu.make_async_copy(tok_ref, x_ref.at[s], lsem.at[6]))
    own.append(pltpu.make_async_copy(down_ref, sd_ref.at[s], lsem.at[7]))
    for copy in own:
        copy.start()
    first = {}
    for t in range(1, ns):
        to = (s + t) % ns
        for i, (piece, start) in enumerate(parts):
            first[t, i] = remote(
                piece(to),
                w_ref.at[s, e, :, pl.ds(start, hw)],
                ssem0.at[t - 1, i],
                rsem0.at[t - 1, i],
                (to, e),
            )
    for copy in own:
        copy.wait()
    sent = {}
    across = {}
    along = {}
    common = {}

    def place_of(k, way):
        return ring_index((p - k + ne) % ne if way == 0 else (p + k) % ne, ne)

    def share(k):
        block = c_ref.at[s, place_of(k, 1)]
        for t in range(1, ns):
            common[k, t] = remote(
                block, block, sc.at[k, t - 1], rc.at[k, t - 1], ((s + t) % ns, e)
            )

    for k in range(ne - 1):
        for t in [0, ns, ns + 1, ns + 2] + list(range(1, ns)):
            way = 1 if t == ns else (t - ns - 1 if t > ns else t % 2)
            to = (s, right if way == 0 else left)
            slot = place_of(k, way)
            if k > 0:
                sent[k - 1, t].wait_recv()
            elif 0 < t < ns:
                for i in range(len(parts)):
                    first[t, i].wait_recv()
            if t < ns:
                block = w_ref.at[(s + ns - t) % ns, slot]
            elif t == ns:
                block = c_ref.at[s, slot]
            else:
                block = o_ref.at[slot, :, pl.ds(way * half, half)]
            sent[k, t] = remote(block, block, ssem.at[k, t], rsem.at[k, t], to)
            if t == ns:
                share(k)
        if k == 0:
            for t in range(1, ns):
                to = ((s + t) % ns, e)
                first[t, 2] = remote(
                    tok_ref, x_ref.at[s], ssem0.at[t - 1, 2], rsem0.at[t - 1, 2], to
                )
                first[t, 3] = remote(
                    down_ref, sd_ref.at[s], ssem0.at[t - 1, 3], rsem0.at[t - 1, 3], to
                )
            for t in range(1, ne):
                to = (e + t) % ne
                across[t] = remote(
                    two_ref.at[to], shared_ref.at[s, e], sa.at[t - 1], ra.at[t - 1], (s, to)
                )
        if k == 2:
            for t in range(1, ne):
                across[t].wait_recv()
            for t in range(1, ns):
                along[t] = remote(
                    shared_ref.at[s], shared_ref.at[s], sb.at[t - 1], rb.at[t - 1], ((s + t) % ns, e)
                )
    sent[ne - 2, ns].wait_recv()
    share(ne - 1)
    for t in range(ns + 3):
        if t != ns:
            sent[ne - 2, t].wait_recv()
    for t in range(1, ns):
        first[t, 2].wait_recv()
        first[t, 3].wait_recv()
        along[t].wait_recv()
    for copy in common.values():
        copy.wait_recv()
    for group in (first, sent, across, along, common):
        for copy in group.values():
            copy.wait_send()


def gather_in(in_weight, pack, tokens, out_weight, shared_two, shared_down, ns, ne, inner, cid):
    rows, columns = in_weight.shape
    hw = inner // ns
    wide = columns - 2 * inner + pack.shape[1]
    return pl.pallas_call(
        functools.partial(gather_in_kernel, ns, ne, hw, inner),
        out_shape=(
            jax.ShapeDtypeStruct((ns, ne, rows, 2 * hw), BF),
            jax.ShapeDtypeStruct((ns, ne, rows, wide), BF),
            jax.ShapeDtypeStruct((ns,) + tokens.shape, BF),
            jax.ShapeDtypeStruct((ne,) + out_weight.shape, BF),
            jax.ShapeDtypeStruct((ns,) + shared_two.shape, BF),
            jax.ShapeDtypeStruct((ns,) + shared_down.shape, BF),
        ),
        in_specs=[ANY] * 6,
        out_specs=(ANY,) * 6,
        scratch_shapes=[
            DMA((8,)),
            DMA((ns - 1, 4)),
            DMA((ns - 1, 4)),
            DMA((ne - 1, ns + 3)),
            DMA((ne - 1, ns + 3)),
            DMA((ne - 1,)),
            DMA((ne - 1,)),
            DMA((ns - 1,)),
            DMA((ns - 1,)),
            DMA((ne, ns - 1)),
            DMA((ne, ns - 1)),
        ],
        compiler_params=params(cid, 8),
        name="gather_in",
    )(in_weight, pack, tokens, out_weight, shared_two, shared_down)


class SeqSum:
    def __init__(self, ns, subs, part, aux, one, two, aux_in, s1, r1, s2, r2, sa, ra):
        self.s, self.e = lax.axis_index("seq"), lax.axis_index("exp")
        self.ns, self.ny, self.subs = ns, ns // 2, subs
        self.y, self.c = self.s // 2, self.s % 2
        self.part, self.aux, self.one, self.two, self.aux_in = part, aux, one, two, aux_in
        self.sems = (s1, r1, s2, r2, sa, ra)
        self.step = part.shape[1] // subs
        self.tile = tile_rows(self.step)
        self.first, self.second, self.extra = {}, {}, []

    @staticmethod
    def scratch(ns, subs, rows, width, aux_shape):
        ny = ns // 2
        return [
            pltpu.VMEM((ny, rows, width), BF),
            pltpu.VMEM((max(ny - 1, 1), rows, width), BF),
            pltpu.VMEM((ns - 1,) + aux_shape, F32),
            DMA((ny, subs)),
            DMA((ny, subs)),
            DMA((max(ny - 1, 1), subs)),
            DMA((max(ny - 1, 1), subs)),
            DMA((ns - 1,)),
            DMA((ns - 1,)),
        ]

    def rows(self, u):
        return pl.ds(u * self.step, self.step)

    def send_aux(self):
        s1, r1, s2, r2, sa, ra = self.sems
        for t in range(1, self.ns):
            to = (self.s + t) % self.ns
            self.extra.append(
                remote(
                    self.aux.at[to], self.aux_in.at[t - 1], sa.at[t - 1], ra.at[t - 1], (to, self.e)
                )
            )

    def order(self):
        return list(range(1, self.ny)) + [0]

    def far(self, j):
        return 2 * ((self.y + j) % self.ny) + 1 - self.c

    def near(self, j):
        return 2 * ((self.y + j) % self.ny) + self.c

    def send(self, j):
        s1, r1, s2, r2, sa, ra = self.sems
        mate = (2 * self.y + 1 - self.c, self.e)
        for u in range(self.subs):
            self.first[j, u] = remote(
                self.part.at[self.far(j), self.rows(u)],
                self.one.at[j, self.rows(u)],
                s1.at[j, u],
                r1.at[j, u],
                mate,
            )

    def begin(self, fill):
        self.send_aux()
        for j in self.order():
            fill(self.far(j))
            self.send(j)
        for j in self.order():
            fill(self.near(j))

    def join(self, j, u):
        s1, r1, s2, r2, sa, ra = self.sems
        to = self.near(j)
        self.first[j, u].wait_recv()

        def add(i, carry):
            r = pl.ds(pl.multiple_of(u * self.step + i * self.tile, self.tile), self.tile)
            total = self.one[j, r, :].astype(F32) + self.part[to, r, :].astype(F32)
            self.one[j, r, :] = total.astype(BF)
            return carry

        lax.fori_loop(0, self.step // self.tile, add, 0)
        self.second[j, u] = remote(
            self.one.at[j, self.rows(u)],
            self.two.at[j - 1, self.rows(u)],
            s2.at[j - 1, u],
            r2.at[j - 1, u],
            (to, self.e),
        )

    def middle(self):
        for j in range(1, self.ny):
            for u in range(self.subs):
                self.join(j, u)

    def close(self, u, out):
        self.first[0, u].wait_recv()
        for j in range(1, self.ny):
            self.second[j, u].wait_recv()

        def add(i, carry):
            r = pl.ds(pl.multiple_of(u * self.step + i * self.tile, self.tile), self.tile)
            total = self.one[0, r, :].astype(F32) + self.part[self.s, r, :].astype(F32)
            for j in range(1, self.ny):
                total = total + self.two[j - 1, r, :].astype(F32)
            out[r, :] = total
            return carry

        lax.fori_loop(0, self.step // self.tile, add, 0)

    def finish(self, out, aux_out):
        for u in range(self.subs):
            self.close(u, out)
        total = self.aux[self.s]
        for t in range(1, self.ns):
            self.extra[t - 1].wait_recv()
            total = total + self.aux_in[t - 1]
        aux_out[...] = total

    def drain(self):
        for copy in list(self.first.values()) + list(self.second.values()) + self.extra:
            copy.wait_send()


class BlockSum:
    def __init__(self, ns, sources, outs, scratch):
        self.s, self.e = lax.axis_index("seq"), lax.axis_index("exp")
        self.ns, self.ny = ns, ns // 2
        self.y, self.c = self.s // 2, self.s % 2
        self.sources, self.outs = sources, outs
        self.items = [(m, i) for m, src in enumerate(sources) for i in range(src.shape[1])]
        count = len(sources)
        self.held, self.one, self.two = (
            scratch[:count],
            scratch[count : 2 * count],
            scratch[2 * count : 3 * count],
        )
        self.lsem, self.s1, self.r1, self.s2, self.r2 = scratch[3 * count :]
        self.loads = [
            pltpu.make_async_copy(src, held, self.lsem.at[m])
            for m, (src, held) in enumerate(zip(self.sources, self.held))
        ]
        self.first, self.second = {}, {}

    @staticmethod
    def scratch(ns, shapes):
        ny = ns // 2
        items = sum(shape[1] for shape in shapes)
        return (
            [pltpu.VMEM(shape, BF) for shape in shapes]
            + [pltpu.VMEM((ny,) + shape[1:], BF) for shape in shapes]
            + [pltpu.VMEM((max(ny - 1, 1),) + shape[1:], BF) for shape in shapes]
            + [
                DMA((len(shapes),)),
                DMA((ny, items)),
                DMA((ny, items)),
                DMA((max(ny - 1, 1), items)),
                DMA((max(ny - 1, 1), items)),
            ]
        )

    def load(self):
        for copy in self.loads:
            copy.start()

    def begin(self):
        mate = (2 * self.y + 1 - self.c, self.e)
        for copy in self.loads:
            copy.wait()
        for j in list(range(1, self.ny)) + [0]:
            block = 2 * ((self.y + j) % self.ny) + 1 - self.c
            for n, (m, i) in enumerate(self.items):
                self.first[j, n] = remote(
                    self.held[m].at[block, i],
                    self.one[m].at[j, i],
                    self.s1.at[j, n],
                    self.r1.at[j, n],
                    mate,
                )

    def tiles(self, shape, body):
        if len(shape) == 3:
            lax.fori_loop(0, shape[0], lambda i, carry: body((i,)) or carry, 0)
        else:
            size = 32 if shape[0] % 32 == 0 else shape[0]
            lax.fori_loop(
                0,
                shape[0] // size,
                lambda i, carry: body((pl.ds(pl.multiple_of(i * size, size), size),)) or carry,
                0,
            )

    def join(self, j, n):
        m, i = self.items[n]
        to = 2 * ((self.y + j) % self.ny) + self.c
        self.first[j, n].wait_recv()
        one, held = self.one[m], self.held[m]

        def add(at):
            total = one[(j, i) + at].astype(F32) + held[(to, i) + at].astype(F32)
            one[(j, i) + at] = total.astype(BF)

        self.tiles(one.shape[2:], add)
        self.second[j, n] = remote(
            one.at[j, i],
            self.two[m].at[j - 1, i],
            self.s2.at[j - 1, n],
            self.r2.at[j - 1, n],
            (to, self.e),
        )

    def close(self, n):
        m, i = self.items[n]
        self.first[0, n].wait_recv()
        for j in range(1, self.ny):
            self.second[j, n].wait_recv()
        one, held, two, out = self.one[m], self.held[m], self.two[m], self.outs[m]

        def add(at):
            total = one[(0, i) + at].astype(F32) + held[(self.s, i) + at].astype(F32)
            for j in range(1, self.ny):
                total = total + two[(j - 1, i) + at].astype(F32)
            out[(i,) + at] = total

        self.tiles(one.shape[2:], add)

    def drain(self):
        for copy in list(self.first.values()) + list(self.second.values()):
            copy.wait_send()


class RingGather:
    def __init__(self, ne, v, out, lsem, ssem, rsem):
        self.s, self.e = lax.axis_index("seq"), lax.axis_index("exp")
        self.ne, self.v, self.out = ne, v, out
        self.p, self.right, self.left = ring_sides(self.e, ne)
        self.ssem, self.rsem = ssem, rsem
        self.subs = ssem.shape[2]
        self.step_rows = v.shape[0] // (2 * self.subs)
        self.own = pltpu.make_async_copy(v, out.at[self.e], lsem)

    @staticmethod
    def scratch(ne, subs):
        return [DMA, DMA((ne - 1, 2, subs)), DMA((ne - 1, 2, subs))]

    def copy(self, k, way, u, src=None):
        place = (self.p - k + self.ne) % self.ne if way == 0 else (self.p + k) % self.ne
        slot = ring_index(place, self.ne)
        rows = pl.ds((way * self.subs + u) * self.step_rows, self.step_rows)
        block = self.out.at[slot, rows]
        return pltpu.make_async_remote_copy(
            src_ref=block if src is None else src.at[rows],
            dst_ref=block,
            send_sem=self.ssem.at[k, way, u],
            recv_sem=self.rsem.at[k, way, u],
            device_id=(self.s, self.right if way == 0 else self.left),
            device_id_type=MESH,
        )

    def begin(self):
        self.own.start()
        for u in range(self.subs):
            for way in range(2):
                self.copy(0, way, u, self.v).start()

    def step(self, k):
        for u in range(self.subs):
            for way in range(2):
                self.copy(k - 1, way, u).wait_recv()
                self.copy(k, way, u).start()

    def forward(self, k):
        for u in range(self.subs):
            for way in range(2):
                self.copy(k, way, u).start()

    def arrived(self, k):
        for u in range(self.subs):
            for way in range(2):
                self.copy(k, way, u).wait_recv()

    def drain(self):
        for k in range(self.ne - 1):
            for u in range(self.subs):
                for way in range(2):
                    self.copy(k, way, u).wait_send()

    def finish(self):
        self.arrived(self.ne - 2)
        self.drain()
        self.own.wait()


class RingSum:
    def __init__(self, ne, part, acc, ssem, rsem):
        self.s, self.e = lax.axis_index("seq"), lax.axis_index("exp")
        self.ne, self.part, self.acc = ne, part, acc
        self.p, self.right, self.left = ring_sides(self.e, ne)
        self.ssem, self.rsem = ssem, rsem
        self.subs = ssem.shape[2]
        self.size = part.shape[1] // (2 * self.subs)
        self.tile = tile_rows(self.size)

    @staticmethod
    def scratch(ne, subs, rows, width):
        return [
            pltpu.VMEM((ne - 1, rows, width), BF),
            DMA((ne - 1, 2, subs)),
            DMA((ne - 1, 2, subs)),
        ]

    def slot(self, k, way):
        place = (self.p - 1 - k + 2 * self.ne) % self.ne if way == 0 else (self.p + 1 + k) % self.ne
        return ring_index(place, self.ne)

    def copy(self, k, way, u, src=None):
        rows = pl.ds((way * self.subs + u) * self.size, self.size)
        return pltpu.make_async_remote_copy(
            src_ref=self.acc.at[k, rows] if src is None else src.at[rows],
            dst_ref=self.acc.at[k, rows],
            send_sem=self.ssem.at[k, way, u],
            recv_sem=self.rsem.at[k, way, u],
            device_id=(self.s, self.right if way == 0 else self.left),
            device_id_type=MESH,
        )

    def add(self, k, way, u, out):
        base = (way * self.subs + u) * self.size
        slot = self.slot(k, way)

        def join(i, carry):
            r = pl.ds(pl.multiple_of(base + i * self.tile, self.tile), self.tile)
            total = self.acc[k - 1, r, :].astype(F32) + self.part[slot, r, :].astype(F32)
            if out is None:
                self.acc[k - 1, r, :] = total.astype(BF)
            else:
                out[r, :] = total
            return carry

        lax.fori_loop(0, self.size // self.tile, join, 0)

    def begin(self):
        for u in range(self.subs):
            for way in range(2):
                self.copy(0, way, u, self.part.at[self.slot(0, way)]).start()

    def step(self, k):
        for u in range(self.subs):
            for way in range(2):
                self.copy(k - 1, way, u).wait_recv()
                self.add(k, way, u, None)
                rows = pl.ds((way * self.subs + u) * self.size, self.size)
                pltpu.make_async_remote_copy(
                    src_ref=self.acc.at[k - 1, rows],
                    dst_ref=self.acc.at[k, rows],
                    send_sem=self.ssem.at[k, way, u],
                    recv_sem=self.rsem.at[k, way, u],
                    device_id=(self.s, self.right if way == 0 else self.left),
                    device_id_type=MESH,
                ).start()

    def finish(self, out):
        k = self.ne - 1
        for u in range(self.subs):
            for way in range(2):
                self.copy(k - 1, way, u).wait_recv()
                self.add(k, way, u, out)
        for k in range(self.ne - 1):
            for u in range(self.subs):
                for way in range(2):
                    self.copy(k, way, u).wait_send()


class Exchange:
    def __init__(self, ne, src, dst, lsem, ssem, rsem, pick=None, spread=False):
        s, e = lax.axis_index("seq"), lax.axis_index("exp")
        if pick is None:
            pick = lambda ref, at: ref.at[at]
        give = (lambda ref, at: ref) if spread else pick
        self.own = pltpu.make_async_copy(give(src, e), pick(dst, e), lsem)
        self.copies = []
        for t in range(1, ne):
            to = (e + t) % ne
            self.copies.append(
                pltpu.make_async_remote_copy(
                    src_ref=give(src, to),
                    dst_ref=pick(dst, e),
                    send_sem=ssem.at[t - 1],
                    recv_sem=rsem.at[t - 1],
                    device_id=(s, to),
                    device_id_type=MESH,
                )
            )

    @staticmethod
    def scratch(ne):
        return [DMA, DMA((ne - 1,)), DMA((ne - 1,))]

    def begin(self):
        self.own.start()
        for copy in self.copies:
            copy.start()

    def arrived(self):
        self.own.wait()
        for copy in self.copies:
            copy.wait_recv()

    def drain(self):
        for copy in self.copies:
            copy.wait_send()


def experts_kernel(
    ne,
    count,
    ffn_ref,
    gate_ref,
    grad_hbm,
    eg_hbm,
    eu_hbm,
    ed_hbm,
    two_hbm,
    sd_hbm,
    back_ref,
    gate_back,
    out_ref,
    dg_ref,
    du_ref,
    dd_ref,
    ds_ref,
    dsd_ref,
    x_ref,
    gates,
    hid_ref,
    da_ref,
    db_ref,
    part_ref,
    gate_part,
    stage_g,
    stage_u,
    stage_d,
    stage_s,
    stage_sem,
    out_stage,
    out_sem,
    *scratch,
):
    s, e = lax.axis_index("seq"), lax.axis_index("exp")
    length, model = ffn_ref.shape
    half = length // 2
    sources = (eg_hbm, eu_hbm, grad_hbm, ed_hbm, two_hbm, sd_hbm)
    eg_ref, eu_ref, grad_ref, ed_ref, two_ref, sd_ref = scratch[12:18]
    loads = Loads(sources, scratch[12:18], scratch[18])
    loads.begin()
    width = eg_ref.shape[2]
    narrow = sd_ref.shape[0]
    tile_width = min(width, 256)
    greet([(s, (e + t) % ne) for t in range(1, ne)])
    ring = RingGather(ne, ffn_ref, x_ref, *scratch[:3])
    there = Exchange(ne, gate_ref, gates, *scratch[3:6])
    back = Exchange(ne, gate_part, gate_back, *scratch[6:9])
    total = RingSum(ne, part_ref, *scratch[9:12])
    ring.begin()
    there.begin()
    gate_part[...] = jnp.zeros_like(gate_part)
    ring.own.wait()
    there.own.wait()
    lane = lax.broadcasted_iota(jnp.int32, (8, length), 1)
    wide_lane = lax.broadcasted_iota(jnp.int32, (2 * length, 128), 1)

    def quarters(i):
        found = []
        for k in (2 * i, 2 * i + 1):
            found.append((ring_index((ring.p - k + ne) % ne, ne), 0))
            found.append((ring_index((ring.p + k) % ne, ne), half))
        return found

    def out_copies(i):
        slot = i % 2
        return [
            pltpu.make_async_copy(
                out_stage.at[slot, pl.ds(n * half, half)],
                out_ref.at[block, pl.ds(first, half)],
                out_sem.at[slot, n],
            )
            for n, (block, first) in enumerate(quarters(i))
        ]

    def rows_of(ref, places, cols):
        return jnp.concatenate(
            [ref[block, first : first + half, cols] for block, first in places], 0
        )

    def store(ref, places, cols, value):
        for n, (block, first) in enumerate(places):
            ref[block, first : first + half, cols] = value[n * half : (n + 1) * half]

    def compute(i):
        places = quarters(i)
        every = slice(0, model)
        x = rows_of(x_ref, places, every)
        g = rows_of(grad_ref, places, every)
        table = jnp.concatenate(
            [
                jnp.where(lane < half, gates[places[n][0]], gates[places[n + 1][0]]).T
                for n in (0, 2)
            ],
            0,
        )
        slots = jnp.zeros((2 * length, 128), F32)
        for j in range(count + 1):
            size = width if j < count else narrow
            column = table[:, j : j + 1] if j < count else None
            for f in range(0, size, tile_width):
                wide = min(tile_width, size - f)
                if j < count:
                    a = mm(x, eg_ref[j, :, f : f + wide])
                    b = mm(x, eu_ref[j, :, f : f + wide])
                    h = mm_t(g, ed_ref[j, f : f + wide, :])
                else:
                    both = mm(x, two_ref[...])
                    a, b = both[:, :narrow], both[:, narrow:]
                    h = mm_t(g, sd_ref[...])
                sig = sigmoid(a)
                silu = a * sig
                act = silu * b
                if j < count:
                    found = jnp.sum(act * h, 1, keepdims=True)
                    slots = slots + jnp.where(wide_lane == j, found, 0.0)
                    act = act * column
                    h = h * column
                cols = slice(j * width + f, j * width + f + wide)
                store(hid_ref, places, cols, act.astype(BF))
                store(da_ref, places, cols, (h * b * (sig + silu * (1 - sig))).astype(BF))
                store(db_ref, places, cols, (h * silu).astype(BF))
        found = slots.T[:8]
        for n in (0, 2):
            part = found[:, (n // 2) * length : (n // 2 + 1) * length]
            one, two = places[n][0], places[n + 1][0]
            gate_part[one] = jnp.where(lane < half, part, gate_part[one])
            gate_part[two] = jnp.where(lane >= half, part, gate_part[two])

    def compute_back(i):
        places = quarters(i)

        @pl.when(i >= 2)
        def _():
            for copy in out_copies(i - 2):
                copy.wait()

        last = slice(count * width, count * width + narrow)
        for d in range(0, model, 256):
            cols = slice(d, d + 256)
            out = mm(rows_of(hid_ref, places, last), sd_ref[:, cols])
            row = mm_t(rows_of(da_ref, places, last), two_ref[cols, :narrow])
            row = row + mm_t(rows_of(db_ref, places, last), two_ref[cols, narrow:])
            for j in range(count):
                mine = slice(j * width, (j + 1) * width)
                out = out + mm(rows_of(hid_ref, places, mine), ed_ref[j, :, cols])
                row = row + mm_t(rows_of(da_ref, places, mine), eg_ref[j, cols, :])
                row = row + mm_t(rows_of(db_ref, places, mine), eu_ref[j, cols, :])
            out_stage[i % 2, :, cols] = out.astype(BF)
            store(part_ref, places, cols, row.astype(BF))
        for copy in out_copies(i):
            copy.start()

    def arrive(i, carry):
        ring.arrived(2 * i)

        @pl.when(2 * i + 1 < ne - 1)
        def _():
            ring.forward(2 * i + 1)

        @pl.when(i == 0)
        def _():
            loads.wait(*range(6))
            for copy in there.copies:
                copy.wait_recv()

        @pl.when(i == ne // 2 - 1)
        def _():
            total.begin()

        compute(i)

        @pl.when(2 * i + 1 < ne - 1)
        def _():
            ring.arrived(2 * i + 1)
            ring.forward(2 * i + 2)

        @pl.when(i == ne // 2 - 1)
        def _():
            total.step(1)

        compute_back(i)
        return carry

    lax.fori_loop(0, ne // 2, arrive, 0)
    ring.drain()
    back.begin()
    part_rows = stage_g.shape[3]
    per = stage_g.shape[1]
    tile = per * part_rows
    tiles = model // tile
    every = ne * length

    def stage_copies(i):
        slot = i % 2
        blocks = pl.ds(i * per, per)
        return [
            pltpu.make_async_copy(stage_g.at[slot], dg_ref.at[blocks], stage_sem.at[slot, 0]),
            pltpu.make_async_copy(stage_u.at[slot], du_ref.at[blocks], stage_sem.at[slot, 3]),
            pltpu.make_async_copy(stage_d.at[slot], dd_ref.at[blocks], stage_sem.at[slot, 1]),
            pltpu.make_async_copy(stage_s.at[slot], ds_ref.at[i], stage_sem.at[slot, 2]),
        ]

    def weights(i):
        @pl.when(i >= 2)
        def _():
            for copy in stage_copies(i - 2):
                copy.wait()

        cols = pl.ds(pl.multiple_of(i * tile, 128), tile)
        slot = i % 2
        x_t = x_ref[:, :, cols].reshape(every, tile).T
        g_t = grad_ref[:, :, cols].reshape(every, tile).T
        for j in range(count):
            at = slice(j * width, (j + 1) * width)
            gate = mm(x_t, da_ref[:, :, at].reshape(every, width)).astype(BF)
            up = mm(x_t, db_ref[:, :, at].reshape(every, width)).astype(BF)
            down = mm(g_t, hid_ref[:, :, at].reshape(every, width)).T.astype(BF)
            for q in range(per):
                rows = slice(q * part_rows, (q + 1) * part_rows)
                stage_g[slot, q, j] = gate[rows]
                stage_u[slot, q, j] = up[rows]
                stage_d[slot, q, j] = down[:, rows]
        at = slice(count * width, count * width + narrow)
        both = jnp.concatenate(
            [da_ref[:, :, at].reshape(every, narrow), db_ref[:, :, at].reshape(every, narrow)], 1
        )
        stage_s[slot] = mm(x_t, both).astype(BF)
        for copy in stage_copies(i):
            copy.start()

    def back_step(k, carry):
        total.step(k)

        @pl.when(k - 2 < tiles)
        def _():
            weights(k - 2)

        return carry

    lax.fori_loop(2, ne - 1, back_step, 0)
    at = slice(count * width, count * width + narrow)
    hid_t = hid_ref[:, :, at].reshape(every, narrow).T
    for d in range(0, model, 512):
        dsd_ref[:, d : d + 512] = mm(hid_t, grad_ref[:, :, d : d + 512].reshape(every, 512)).astype(BF)
    for i in range(ne - 3, tiles):
        weights(i)
    for i in range(max(tiles - 2, 0), tiles):
        for copy in stage_copies(i):
            copy.wait()
    for i in (ne // 2 - 2, ne // 2 - 1):
        for copy in out_copies(i):
            copy.wait()
    total.finish(back_ref)
    back.arrived()
    back.drain()
    there.drain()


def experts_both_ways(
    ffn_in, gates, grad_all, expert_gate, expert_up, expert_down, shared_two, shared_down, ns, ne, cid
):
    length, model = ffn_in.shape
    count, _, width = expert_gate.shape
    narrow = shared_down.shape[0]
    hidden = count * width + narrow
    part = model // ns
    per = 1 if part % 128 == 0 else 2
    return pl.pallas_call(
        functools.partial(experts_kernel, ne, count),
        out_shape=(
            jax.ShapeDtypeStruct((length, model), F32),
            jax.ShapeDtypeStruct((ne, 8, length), F32),
            jax.ShapeDtypeStruct((ne, length, model), BF),
            jax.ShapeDtypeStruct((ns, count, part, width), BF),
            jax.ShapeDtypeStruct((ns, count, part, width), BF),
            jax.ShapeDtypeStruct((ns, count, width, part), BF),
            jax.ShapeDtypeStruct((ns // per, per * part, 2 * narrow), BF),
            jax.ShapeDtypeStruct((narrow, model), BF),
        ),
        in_specs=[VMEM] * 2 + [ANY] * 6,
        out_specs=(VMEM, VMEM, ANY, ANY, ANY, ANY, ANY, VMEM),
        scratch_shapes=[
            pltpu.VMEM((ne, length, model), BF),
            pltpu.VMEM((ne, 8, length), F32),
            pltpu.VMEM((ne, length, hidden), BF),
            pltpu.VMEM((ne, length, hidden), BF),
            pltpu.VMEM((ne, length, hidden), BF),
            pltpu.VMEM((ne, length, model), BF),
            pltpu.VMEM((ne, 8, length), F32),
            pltpu.VMEM((2, per, count, part, width), BF),
            pltpu.VMEM((2, per, count, part, width), BF),
            pltpu.VMEM((2, per, count, width, part), BF),
            pltpu.VMEM((2, per * part, 2 * narrow), BF),
            DMA((2, 4)),
            pltpu.VMEM((2, 2 * length, model), BF),
            DMA((2, 4)),
        ]
        + RingGather.scratch(ne, 2)
        + Exchange.scratch(ne)
        + Exchange.scratch(ne)
        + RingSum.scratch(ne, 2, length, model)
        + Loads.scratch(
            [expert_gate, expert_up, grad_all, expert_down, shared_two, shared_down]
        ),
        compiler_params=params(cid, 60),
        name="experts",
    )(ffn_in, gates, grad_all, expert_gate, expert_up, expert_down, shared_two, shared_down)


class SeqGather:
    def __init__(self, ns, v, aux, out, aux_out, lsem, s1, r1, s2, r2, sa, ra):
        s, e = lax.axis_index("seq"), lax.axis_index("exp")
        ny = ns // 2
        y, c = s // 2, s % 2
        mate = (2 * y + 1 - c, e)

        def make(src, dst, send, recv, device):
            return pltpu.make_async_remote_copy(
                src_ref=src,
                dst_ref=dst,
                send_sem=send,
                recv_sem=recv,
                device_id=device,
                device_id_type=MESH,
            )

        self.own = [
            pltpu.make_async_copy(v, out.at[s], lsem.at[0]),
            pltpu.make_async_copy(aux, aux_out.at[s], lsem.at[1]),
        ]
        self.first = [
            make(v, out.at[s], s1.at[j], r1.at[j], (2 * ((y + j) % ny) + c, e))
            for j in range(1, ny)
        ]
        self.first.append(make(v, out.at[s], s1.at[0], r1.at[0], mate))
        self.extra = [
            make(aux, aux_out.at[s], sa.at[t - 1], ra.at[t - 1], ((s + t) % ns, e))
            for t in range(1, ns)
        ]
        self.second = []
        for j in range(1, ny):
            block = out.at[2 * ((y + ny - j) % ny) + c]
            self.second.append(make(block, block, s2.at[j - 1], r2.at[j - 1], mate))

    @staticmethod
    def scratch(ns):
        ny = ns // 2
        return [
            DMA((2,)),
            DMA((ny,)),
            DMA((ny,)),
            DMA((max(ny - 1, 1),)),
            DMA((max(ny - 1, 1),)),
            DMA((ns - 1,)),
            DMA((ns - 1,)),
        ]

    def begin(self):
        for copy in self.first + self.extra + self.own:
            copy.start()

    def middle(self):
        for arrived, onward in zip(self.first[:-1], self.second):
            arrived.wait_recv()
            onward.start()

    def finish(self):
        for copy in [self.first[-1]] + self.second + self.extra:
            copy.wait_recv()
        for copy in self.own:
            copy.wait()

    def drain(self):
        for copy in self.first + self.second + self.extra:
            copy.wait_send()


def sum_weights_kernel(
    ns,
    ne,
    blocks,
    gin,
    gcommon,
    gout,
    dproj_ref,
    in_ref,
    common_ref,
    tok_ref,
    resid_ref,
    gain_ref,
    aux_ref,
    *refs,
):
    sources = refs[:blocks]
    in_out, pack_out, out_rows, tok_out, aux_out, shared_out = refs[blocks : blocks + 6]
    block_outs = refs[blocks + 6 : 2 * blocks + 5]
    sum_weights_body(
        ns,
        ne,
        sources,
        block_outs,
        gin,
        gcommon,
        gout,
        dproj_ref,
        in_ref,
        common_ref,
        tok_ref,
        resid_ref,
        gain_ref,
        aux_ref,
        in_out,
        pack_out,
        out_rows,
        tok_out,
        aux_out,
        shared_out,
        *refs[2 * blocks + 5 :],
    )


def sum_weights_body(
    ns,
    ne,
    sources,
    block_outs,
    gin,
    gcommon,
    gout,
    dproj_ref,
    in_ref,
    common_ref,
    tok_ref,
    resid_ref,
    gain_ref,
    aux_ref,
    in_out,
    pack_out,
    out_rows,
    tok_out,
    aux_out,
    shared_out,
    out,
    acc,
    acc_out,
    acc_common,
    common_sum,
    common_low,
    fin,
    part_ref,
    lowered_grad,
    aux_part,
    aux_in,
    aux_sum,
    shared_sum,
    shared_low,
    dproj,
    in_held,
    common_held,
    load_sems,
    ssem,
    rsem,
    so,
    ro,
    sc,
    rc,
    sx,
    rx,
    ss,
    rs,
    *scratch,
):
    s, e = lax.axis_index("seq"), lax.axis_index("exp")
    p, right, left = ring_sides(e, ne)
    count = len(SeqSum.scratch(ns, 2, 8, 128, (8, 128)))
    job = SeqSum(ns, 2, part_ref, None, *scratch[:count])
    there = Exchange(ne, aux_part, aux_in, *scratch[count : count + 3])
    back = Exchange(
        ne,
        aux_sum,
        aux_out,
        *scratch[count + 3 : count + 6],
        pick=lambda ref, at: ref.at[s, at],
        spread=True,
    )
    along = []
    at = count + 9 + len(BlockSum.scratch(ns, [gcommon.shape]))
    shared_cols = BlockSum(ns, (gcommon,), (common_sum,), scratch[count + 9 : at])
    more = BlockSum(ns, sources, tuple(block_outs) + (shared_sum,), scratch[at:])
    across = Exchange(ne, shared_low, shared_out, *scratch[count + 6 : count + 9])
    loads = Loads((dproj_ref, in_ref, common_ref), (dproj, in_held, common_held), load_sems)
    shared_cols.load()
    loads.begin()
    more.load()
    greet([((s + t) % ns, e) for t in range(1, ns)] + [(s, (e + t) % ne) for t in range(1, ne)])

    def fill(block):
        rows = pl.ds(pl.multiple_of(block * GROUP, GROUP), GROUP)
        main = in_held.shape[1]
        part = mm_t(dproj[rows, :main], in_held[...])
        part_ref[block] = (part + mm_t(dproj[rows, main:], common_held[...])).astype(BF)

    def tokens_back():
        value = tok_ref[...].astype(F32)
        grad = lowered_grad[...]
        width = value.shape[1]
        scale = lax.rsqrt(jnp.sum(value * value, 1, keepdims=True) / width + EPSILON)
        inside = gain_ref[0:1, :] * grad
        mean = jnp.sum(value * inside, 1, keepdims=True) / width
        tok_out[...] = (resid_ref[...] + scale * inside - value * (scale * scale * scale * mean)).astype(BF)
        gain_grad = jnp.sum(value * scale * grad, 0, keepdims=True)
        aux_part[...] = aux_ref[...]
        for i in range(width // 128):
            row = 6 + i // ne
            aux_part[i % ne, row : row + 1, :128] = gain_grad[:, i * 128 : (i + 1) * 128]
        there.begin()

    def sums():
        there.arrived()
        total = aux_in[0]
        for i in range(1, ne):
            total = total + aux_in[i]
        aux_sum[...] = total
        back.begin()

    def spread():
        back.arrived()
        for t in range(1, ns):
            along.append(
                remote(aux_out.at[s], aux_out.at[s], ss.at[t - 1], rs.at[t - 1], ((s + t) % ns, e))
            )

    def swap():
        shared_low[...] = shared_sum[0].astype(BF)
        across.begin()

    def far_task(j):
        def run():
            fill(job.far(j))
            job.send(j)

        return run

    def common_ready():
        shared_cols.close(0)
        common_low[...] = common_sum[0].astype(BF)
        ready.append(True)

    ready = []
    items = len(more.items)
    lanes = range(1, ns // 2)
    tasks = [(0.0, lambda: loads.wait(0, 1, 2))]
    tasks += [(0.05, functools.partial(shared_cols.join, j, 0)) for j in lanes]
    tasks += [(0.17, common_ready)]
    tasks += [(0.02 * i, far_task(j)) for i, j in enumerate(job.order())]
    tasks += [
        (0.02 * (i + ns // 2), functools.partial(fill, job.near(j)))
        for i, j in enumerate(job.order())
    ]
    tasks += [(0.13, more.begin)]
    tasks += [(0.14, functools.partial(job.join, j, u)) for j in lanes for u in range(job.subs)]
    tasks += [
        (0.22 + 0.15 * (items - 1 - n) / items, functools.partial(more.join, j, n))
        for n in reversed(range(items))
        for j in lanes
    ]
    tasks += [(0.36, functools.partial(job.close, u, lowered_grad)) for u in range(job.subs)]
    tasks += [(0.40, tokens_back), (0.54, sums), (0.68, spread)]
    tasks += [(0.74, functools.partial(more.close, items - 1)), (0.75, swap)]
    tasks += [
        (0.80 + 0.18 * (items - 1 - n) / items, functools.partial(more.close, n))
        for n in range(items - 1)
    ]
    tasks.sort(key=lambda task: task[0])
    shared_cols.begin()
    rows = gin.shape[2]
    main = gin.shape[3]
    tile = tile_rows(rows)
    half = gout.shape[2] // 2
    tile_out = tile_rows(gout.shape[1])
    sent = {}
    last = {}
    done = 0
    lag = 2
    for k in range(ne + lag):
        for t in list(range(1, ns)) + [0, ns, ns + 1, ns + 2]:
            while k > 0 and tasks and tasks[0][0] <= done / (ne * (ns + 3)):
                tasks.pop(0)[1]()
            if t == ns + 2:
                hop = k - lag
                way = 1
            else:
                hop = k
                way = t % 2
            if hop < 0 or hop >= ne:
                continue
            while t == ns + 2 and not ready:
                tasks.pop(0)[1]()
            done += 1
            to = right if way == 0 else left
            place = (p - 1 - hop + 2 * ne) % ne if way == 0 else (p + 1 + hop) % ne
            slot = ring_index(place, ne)
            if hop > 0:
                sent[hop - 1, t].wait_recv()
            if t < ns:
                piece = (s + t) % ns
                if hop > 0:

                    def join(i, carry):
                        r = pl.ds(pl.multiple_of(i * tile, tile), tile)
                        total = acc[hop - 1, t, r, :].astype(F32)
                        total = total + gin[piece, slot, r, :].astype(F32)
                        if hop < ne - 1:
                            acc[hop - 1, t, r, :] = total.astype(BF)
                        elif t == 0:
                            out[s, r, :] = total.astype(BF)
                        else:
                            fin[t - 1, r, :] = total.astype(BF)
                        return carry

                    lax.fori_loop(0, rows // tile, join, 0)
                if hop < ne - 1:
                    src = gin.at[piece, slot] if hop == 0 else acc.at[hop - 1, t]
                    sent[hop, t] = remote(
                        src, acc.at[hop, t], ssem.at[hop, t], rsem.at[hop, t], (s, to)
                    )
                elif t > 0:
                    last[t] = remote(
                        fin.at[t - 1], out.at[s], sx.at[t - 1], rx.at[t - 1], (piece, e)
                    )
            elif t == ns + 2:
                if hop > 0:
                    total = acc_common[hop - 1].astype(F32) + common_low[slot].astype(F32)
                    if hop < ne - 1:
                        acc_common[hop - 1] = total.astype(BF)
                    else:
                        wide = total.shape[1] - pack_out.shape[1]
                        in_out[:, in_out.shape[1] - wide :] = total[:, :wide]
                        pack_out[...] = total[:, wide:]
                if hop < ne - 1:
                    src = common_low.at[slot] if hop == 0 else acc_common.at[hop - 1]
                    sent[hop, t] = remote(
                        src, acc_common.at[hop], sc.at[hop], rc.at[hop], (s, to)
                    )
            else:
                part_columns = pl.ds(way * half, half)
                if hop > 0:

                    def join_out(i, carry):
                        r = pl.ds(pl.multiple_of(i * tile_out, tile_out), tile_out)
                        total = acc_out[hop - 1, r, part_columns].astype(F32)
                        total = total + gout[slot, r, part_columns].astype(F32)
                        if hop < ne - 1:
                            acc_out[hop - 1, r, part_columns] = total.astype(BF)
                        else:
                            out_rows[r, part_columns] = total
                        return carry

                    lax.fori_loop(0, gout.shape[1] // tile_out, join_out, 0)
                if hop < ne - 1:
                    src = (
                        gout.at[slot, :, part_columns]
                        if hop == 0
                        else acc_out.at[hop - 1, :, part_columns]
                    )
                    sent[hop, t] = remote(
                        src,
                        acc_out.at[hop, :, part_columns],
                        so.at[hop, way],
                        ro.at[hop, way],
                        (s, to),
                    )
    for _, task in tasks:
        task()
    for copy in list(last.values()) + along:
        copy.wait_recv()
    head = main // 2
    inner = head * ns
    for block in range(ns):
        in_out[:, block * head : (block + 1) * head] = out[block, :, :head].astype(F32)
        in_out[:, inner + block * head : inner + (block + 1) * head] = out[block, :, head:].astype(F32)
    for copy in list(sent.values()) + list(last.values()) + along:
        copy.wait_send()
    across.arrived()
    more.drain()
    shared_cols.drain()
    job.drain()
    there.drain()
    back.drain()
    across.drain()


def sum_weights(
    gin,
    gcommon,
    gout,
    projected_grad,
    in_local,
    in_common,
    tokens,
    resid_grad,
    gain,
    aux,
    sources,
    pack,
    ns,
    ne,
    cid,
):
    rows, wide = gin.shape[2:]
    narrow = gcommon.shape[4]
    length, model = tokens.shape
    blocks = len(sources)
    return pl.pallas_call(
        functools.partial(sum_weights_kernel, ns, ne, blocks),
        out_shape=(
            jax.ShapeDtypeStruct((rows, ns * wide + narrow - pack), F32),
            jax.ShapeDtypeStruct((rows, pack), F32),
            jax.ShapeDtypeStruct(gout.shape[1:], F32),
            jax.ShapeDtypeStruct(tokens.shape, BF),
            jax.ShapeDtypeStruct((ns,) + aux.shape, F32),
            jax.ShapeDtypeStruct(sources[-1].shape[2:], BF),
        )
        + tuple(jax.ShapeDtypeStruct(v.shape[1:], F32) for v in sources[:-1]),
        in_specs=[VMEM, ANY, VMEM] + [ANY] * 3 + [VMEM] * 4 + [ANY] * blocks,
        out_specs=(VMEM,) * (5 + blocks),
        scratch_shapes=[
            pltpu.VMEM((ns, rows, wide), BF),
            pltpu.VMEM((ne - 1, ns, rows, wide), BF),
            pltpu.VMEM((ne - 1,) + gout.shape[1:], BF),
            pltpu.VMEM((ne - 1, rows, narrow), BF),
            pltpu.VMEM(gcommon.shape[1:], F32),
            pltpu.VMEM(gcommon.shape[2:], BF),
            pltpu.VMEM((ns - 1, rows, wide), BF),
            pltpu.VMEM((ns, length, model), BF),
            pltpu.VMEM((length, model), F32),
            pltpu.VMEM(aux.shape, F32),
            pltpu.VMEM(aux.shape, F32),
            pltpu.VMEM(aux.shape[1:], F32),
            pltpu.VMEM(sources[-1].shape[1:], F32),
            pltpu.VMEM(sources[-1].shape[2:], BF),
        ]
        + Loads.scratch([projected_grad, in_local, in_common])
        + [
            DMA((ne - 1, ns)),
            DMA((ne - 1, ns)),
            DMA((ne - 1, 2)),
            DMA((ne - 1, 2)),
            DMA((ne - 1,)),
            DMA((ne - 1,)),
            DMA((ns - 1,)),
            DMA((ns - 1,)),
            DMA((ns - 1,)),
            DMA((ns - 1,)),
        ]
        + SeqSum.scratch(ns, 2, length, model, (8, 128))
        + Exchange.scratch(ne)
        + Exchange.scratch(ne)
        + Exchange.scratch(ne)
        + BlockSum.scratch(ns, [gcommon.shape])
        + BlockSum.scratch(ns, [v.shape for v in sources]),
        compiler_params=params(cid, 60),
        name="sum_weights",
    )(
        gin,
        gcommon,
        gout,
        projected_grad,
        in_local,
        in_common,
        tokens,
        resid_grad,
        gain,
        aux,
        *sources,
    )


def matmul_plain(left, right):
    return jnp.dot(left, right, preferred_element_type=F32)


def matmul_rows(left, right):
    return lax.dot_general(left, right, (((0,), (0,)), ((), ())), preferred_element_type=F32)


def matmul_cols(left, right):
    return lax.dot_general(left, right, (((1,), (1,)), ((), ())), preferred_element_type=F32)


def mm(left, right):
    return jnp.dot(left, right, preferred_element_type=F32)


def mm_t(left, right):
    return lax.dot_general(left, right, (((1,), (1,)), ((), ())), preferred_element_type=F32)


def t_mm(left, right):
    return lax.dot_general(left, right, (((0,), (0,)), ((), ())), preferred_element_type=F32)


def exact(left, right):
    return jnp.dot(left, right, precision=PRECISE, preferred_element_type=F32)


def spread_heads(table, heads, head_dim):
    rows = table.shape[0]
    per = 128 // head_dim
    lane = lax.broadcasted_iota(jnp.int32, (rows, 128), 1)
    tiles = []
    for h in range(0, heads, per):
        tile = jnp.broadcast_to(table[:, h : h + 1], (rows, 128))
        for i in range(1, per):
            other = jnp.broadcast_to(table[:, h + i : h + i + 1], (rows, 128))
            tile = jnp.where(lane >= i * head_dim, other, tile)
        tiles.append(tile)
    return jnp.concatenate(tiles, 1)


def sigmoid(v):
    return 1.0 / (1.0 + jnp.exp(-v))


def softplus(v):
    return jnp.maximum(v, 0.0) + jnp.log1p(jnp.exp(-jnp.abs(v)))


def two_parts(v):
    high = v.astype(BF)
    return high, (v - high.astype(F32)).astype(BF)


def triangle(flip=False):
    t = lax.broadcasted_iota(jnp.int32, (GROUP, GROUP), 0)
    u = lax.broadcasted_iota(jnp.int32, (GROUP, GROUP), 1)
    return u >= t if flip else t >= u


def step_table(pack, bias, heads, s):
    turned = pltpu.roll(pack, (128 - heads * s) % 128, 1)
    lane = lax.broadcasted_iota(jnp.int32, turned.shape, 1)
    raw = jnp.where(lane < heads, turned + bias, 0.0)
    return raw, jnp.where(lane < heads, softplus(raw), 0.0)


def convolved(ext, table, width):
    mixed = table[width : width + 1]
    for j in range(width):
        mixed = mixed + table[j : j + 1] * ext[8 - width + 1 + j : 8 - width + 1 + j + GROUP]
    return mixed


def with_before(proj_ref, at, columns, first):
    before = proj_ref[pl.ds(pl.multiple_of(jnp.maximum(at - 8, 0), 8), 8), columns]
    before = jnp.where(first, 0.0, before)
    return jnp.concatenate([before, proj_ref[pl.ds(at, GROUP), columns]], 0)


def mix_forward_kernel(
    ns,
    ne,
    hw,
    state2,
    heads,
    width,
    norm_at,
    x_ref,
    w_hbm,
    c_hbm,
    table_ref,
    head_ref,
    out_hbm,
    grad_ref,
    proj_hbm,
    lowered_hbm,
    scan_hbm,
    mix_hbm,
    entry_hbm,
    sum_ref,
    square_out,
    grad_all,
    proj_ref,
    lowered_ref,
    scan_ref,
    mix_ref,
    entry_ref,
    state,
    low_ref,
    square_ref,
    part_ref,
    store_sem,
    w_ref,
    c_ref,
    out_ref,
    load_sem,
    *sems,
):
    s, e = lax.axis_index("seq"), lax.axis_index("exp")
    p, right, left = ring_sides(e, ne)
    loads = Loads((w_hbm, c_hbm, out_hbm), (w_ref, c_ref, out_ref), load_sem)
    loads.begin()
    greet([((s + t) % ns, e) for t in range(1, ns)] + [(s, right), (s, left)])
    ring = RingGather(ne, grad_ref, grad_all, *sems[:3])
    job = SeqSum(ns, 2, part_ref, square_ref, *sems[3:])
    ring.begin()
    pairs = (
        (proj_ref, proj_hbm),
        (lowered_ref, lowered_hbm),
        (scan_ref, scan_hbm),
        (mix_ref, mix_hbm),
    )

    def stores(c):
        rows = pl.ds(pl.multiple_of(c * GROUP, GROUP), GROUP)
        copies = [
            pltpu.make_async_copy(ref.at[rows], hbm.at[rows], store_sem.at[c, i])
            for i, (ref, hbm) in enumerate(pairs)
        ]
        copies.append(
            pltpu.make_async_copy(entry_ref.at[c], entry_hbm.at[c], store_sem.at[c, len(pairs)])
        )
        return copies

    loads.wait(0, 1)
    norm = c_ref[:, state2:].astype(F32).T[norm_at : norm_at + 1, :]
    blocks = x_ref.shape[0] // GROUP
    head_dim = hw // heads
    n = state2 // 2
    state[...] = jnp.zeros_like(state)
    lane = lax.broadcasted_iota(jnp.int32, (GROUP, 128), 1)
    table = table_ref[...]
    skip = table[width + 2 : width + 3, :hw]
    gain = table[width + 1 : width + 2, :hw]
    bias, rate = head_ref[0:1, :], head_ref[1:2, :]

    def chunk(c, carry):
        at = pl.multiple_of(c * GROUP, GROUP)
        rows = pl.ds(at, GROUP)
        causal = triangle()
        x = x_ref[rows, :].astype(F32)
        scale = lax.rsqrt(jnp.sum(x * x, 1, keepdims=True) / x.shape[1] + EPSILON)
        lowered = (x * scale * norm).astype(BF)
        lowered_ref[rows, :] = lowered
        proj_ref[rows, : 2 * hw] = mm(lowered, w_ref[...])
        proj_ref[rows, 2 * hw :] = mm(lowered, c_ref[...])
        ext = with_before(proj_ref, at, slice(hw, 2 * hw + state2), c == 0)
        mixed = convolved(ext, table, width)
        mix_ref[rows, :] = mixed
        conv = mixed * sigmoid(mixed)
        values = conv[:, :hw]
        b = conv[:, hw : hw + n].astype(BF)
        ct = conv[:, hw + n :].astype(BF)
        _, steps = step_table(proj_ref[rows, 2 * hw + state2 :], bias, heads, s)
        logs = exact(causal.astype(F32), steps * rate)
        logs_t, steps_t = logs.T, steps.T
        end = logs[GROUP - 1 : GROUP, :]
        before = state[...]
        entry_ref[c] = before
        carried = mm(ct, before.astype(BF)) * spread_heads(jnp.exp(logs), heads, head_dim)
        tails = spread_heads(jnp.exp(end - logs) * steps, heads, head_dim)
        fresh = t_mm(b, (values * tails).astype(BF))
        state[...] = spread_heads(jnp.exp(end), heads, head_dim) * before + fresh
        cross = mm_t(ct, b)
        low = values.astype(BF)
        tiles = []
        per = 128 // head_dim
        for h in range(0, heads, per):
            tile = None
            part = low[:, h * head_dim : h * head_dim + 128]
            for i in range(per):
                gap = logs[:, h + i : h + i + 1] - logs_t[h + i : h + i + 1, :]
                kernel = jnp.exp(jnp.where(causal, gap, -1e30))
                weights = cross * kernel * steps_t[h + i : h + i + 1, :]
                one = mm(weights.astype(BF), part)
                tile = one if i == 0 else jnp.where(lane >= i * head_dim, one, tile)
            tiles.append(tile)
        scanned = jnp.concatenate(tiles, 1) + carried + skip * values
        scan_ref[rows, :] = scanned
        gate = proj_ref[rows, :hw]
        gated = scanned * (gate * sigmoid(gate))
        low_ref[rows, :] = (gated * gain).astype(BF)
        square_ref[c] = lax.dot_general(
            jnp.ones((8, hw), F32),
            gated * gated,
            (((1,), (1,)), ((), ())),
            precision=PRECISE,
            preferred_element_type=F32,
        )

        for copy in stores(c):
            copy.start()
        ring.step(c + 1)

        return carry

    lax.fori_loop(0, blocks, chunk, 0)

    def fill(block):
        rows = pl.ds(pl.multiple_of(block * GROUP, GROUP), GROUP)
        part_ref[block] = mm(low_ref[rows, :], out_ref[...]).astype(BF)

    k = blocks + 1
    loads.wait(2)
    job.begin(fill)
    for stage in (job.middle, lambda: job.finish(sum_ref, square_out)):
        if k < ne - 1:
            ring.step(k)
            k += 1
        stage()
    while k < ne - 1:
        ring.step(k)
        k += 1
    ring.finish()
    job.drain()
    for c in range(blocks):
        for copy in stores(c):
            copy.wait()


def mix_forward(
    sequence,
    in_local,
    in_common,
    table,
    head_table,
    out_local,
    grad_low,
    ns,
    ne,
    hw,
    state2,
    heads,
    width,
    norm_at,
    cid,
):
    whole, model = sequence.shape
    blocks = whole // GROUP
    n = state2 // 2
    rows = grad_low.shape[0]
    columns = in_local.shape[1] + in_common.shape[1]
    kept = [
        jax.ShapeDtypeStruct((whole, columns), F32),
        jax.ShapeDtypeStruct((whole, model), BF),
        jax.ShapeDtypeStruct((whole, hw), F32),
        jax.ShapeDtypeStruct((whole, hw + state2), F32),
        jax.ShapeDtypeStruct((blocks, n, hw), F32),
    ]
    return pl.pallas_call(
        functools.partial(mix_forward_kernel, ns, ne, hw, state2, heads, width, norm_at),
        out_shape=tuple(kept)
        + (
            jax.ShapeDtypeStruct((rows, model), F32),
            jax.ShapeDtypeStruct((8, rows), F32),
            jax.ShapeDtypeStruct((ne, rows, model), BF),
        ),
        in_specs=[VMEM, ANY, ANY, VMEM, VMEM, ANY, VMEM],
        out_specs=(ANY,) * 5 + (VMEM,) * 3,
        scratch_shapes=[pltpu.VMEM(v.shape, v.dtype) for v in kept]
        + [
            pltpu.VMEM((n, hw), F32),
            pltpu.VMEM((whole, hw), BF),
            pltpu.VMEM((blocks, 8, GROUP), F32),
            pltpu.VMEM((ns, rows, model), BF),
            DMA((blocks, 5)),
        ]
        + Loads.scratch([in_local, in_common, out_local])
        + RingGather.scratch(ne, 2)
        + SeqSum.scratch(ns, 2, rows, model, (8, rows)),
        compiler_params=params(cid, 50),
        name="mix_forward",
    )(sequence, in_local, in_common, table, head_table, out_local, grad_low)


def mix_backward_kernel(
    ns,
    ne,
    hw,
    state2,
    heads,
    width,
    proj_hbm,
    table_ref,
    head_ref,
    scan_hbm,
    mix_hbm,
    entry_hbm,
    out_hbm,
    resid_ref,
    rows_ref,
    part_ref,
    expert_ref,
    lowered_hbm,
    router_ref,
    sum_ref,
    expert_out,
    dproj_ref,
    grad_out_ref,
    grad_in_ref,
    grad_common_ref,
    dtable_ref,
    dhead_ref,
    adjoint,
    after,
    low_ref,
    resid_all,
    scale_ref,
    *scratch,
):
    s, e = lax.axis_index("seq"), lax.axis_index("exp")
    p, right, left = ring_sides(e, ne)
    loads = Loads(
        (proj_hbm, scan_hbm, mix_hbm, entry_hbm, out_hbm, lowered_hbm), scratch[:6], scratch[6]
    )
    proj_ref, scan_ref, mix_ref, entry_ref, out_ref, lowered_ref = scratch[:6]
    loads.begin()
    greet([((s + t) % ns, e) for t in range(1, ns)] + [(s, right), (s, left)])
    ring = RingSum(ne, part_ref, *scratch[7:10])
    at = 10 + len(SeqGather.scratch(ns))
    rows_in = SeqGather(ns, resid_ref, rows_ref, resid_all, scale_ref, *scratch[10:at])
    experts = BlockSum(ns, (expert_ref,), (expert_out,), scratch[at:])
    experts.load()
    rows_in.begin()
    ring.begin()
    ring.step(1)
    rows_in.middle()
    experts.begin()
    ring.step(2)
    rows_in.finish()
    for j in range(1, ns // 2):
        for n in range(len(experts.items)):
            experts.join(j, n)
    loads.wait(*range(6))
    blocks = proj_ref.shape[0] // GROUP
    head_dim = hw // heads
    n = state2 // 2
    per = 128 // head_dim
    adjoint[...] = jnp.zeros_like(adjoint)
    after[...] = jnp.zeros_like(after)
    dtable_ref[...] = jnp.zeros_like(dtable_ref)
    dhead_ref[...] = jnp.zeros_like(dhead_ref)
    lane = lax.broadcasted_iota(jnp.int32, (GROUP, 128), 1)
    row = lax.broadcasted_iota(jnp.int32, (GROUP, 128), 0)
    table = table_ref[...]
    skip = table[width + 2 : width + 3, :hw]
    gain = table[width + 1 : width + 2, :hw]
    bias, rate = head_ref[0:1, :], head_ref[1:2, :]

    def chunk(lap, carry):
        c = blocks - 1 - lap
        at = pl.multiple_of(c * GROUP, GROUP)
        rows = pl.ds(at, GROUP)
        causal = triangle()
        head_of = lax.broadcasted_iota(jnp.int32, (hw, 128), 0) // head_dim
        pick = (head_of == lax.broadcasted_iota(jnp.int32, (hw, 128), 1)).astype(F32)
        gate = proj_ref[rows, :hw]
        gate_sig = sigmoid(gate)
        gate_silu = gate * gate_sig
        scanned = scan_ref[rows, :]
        gated = scanned * gate_silu
        scales = scale_ref[c].T
        r, inside = scales[:, 0:1], scales[:, 1:2]
        q = mm_t(resid_all[c], out_ref[...])
        dgated = r * (gain * q) - gated * (r * r * r * inside)
        low_ref[rows, :] = (gated * gain * r).astype(BF)
        dtable_ref[width + 1 : width + 2, :hw] += jnp.sum(gated * r * q, 0, keepdims=True)
        dy = dgated * gate_silu
        dproj_ref[rows, :hw] = (dgated * scanned * (gate_sig + gate_silu * (1 - gate_sig))).astype(BF)

        mixed = mix_ref[rows, :]
        sig = sigmoid(mixed)
        conv = mixed * sig
        values = conv[:, :hw]
        b, b_rest = two_parts(conv[:, hw : hw + n])
        ct, ct_rest = two_parts(conv[:, hw + n :])
        dtable_ref[width + 2 : width + 3, :hw] += jnp.sum(dy * values, 0, keepdims=True)
        raw, steps = step_table(proj_ref[rows, 2 * hw + state2 :], bias, heads, s)
        logs = exact(causal.astype(F32), steps * rate)
        logs_t, steps_t = logs.T, steps.T
        end = logs[GROUP - 1 : GROUP, :]
        rest = jnp.exp(end - logs)
        tail = rest * steps
        ends = jnp.exp(end)
        before = entry_ref[c]
        before_low, before_rest = two_parts(before)
        later = adjoint[...]
        later_low, later_rest = two_parts(later)
        tails = spread_heads(tail, heads, head_dim)
        dy_carried = dy * spread_heads(jnp.exp(logs), heads, head_dim)
        dy_carried_low = dy_carried.astype(BF)
        carried = mm(ct, before_low)
        back = mm(b, later_low)
        dvalues = tails * back + skip * dy
        dc = mm_t(dy_carried_low, before_low) + mm_t(dy_carried_low, before_rest)
        values_tail = (values * tails).astype(BF)
        db = mm_t(values_tail, later_low) + mm_t(values_tail, later_rest)
        kept = jnp.sum(later * before, 0, keepdims=True)
        adjoint[...] = spread_heads(ends, heads, head_dim) * later + t_mm(ct, dy_carried_low)
        sums = exact(jnp.concatenate([dy_carried * carried, values * back, jnp.broadcast_to(kept, (8, hw))], 0), pick)
        from_carried, dtail, kept = sums[:GROUP], sums[GROUP : 2 * GROUP], sums[2 * GROUP : 2 * GROUP + 1]
        cross = mm_t(ct, b)
        low = values.astype(BF)
        dy_low = dy.astype(BF)
        dcross = jnp.zeros((GROUP, GROUP), F32)
        dlogs = from_carried - dtail * tail
        columns = []
        tiles = []
        for h in range(0, heads, per):
            part = low[:, h * head_dim : h * head_dim + 128]
            dy_part = dy_low[:, h * head_dim : h * head_dim + 128]
            tile = None
            for i in range(per):
                gap = logs[:, h + i : h + i + 1] - logs_t[h + i : h + i + 1, :]
                kernel = jnp.exp(jnp.where(causal, gap, -1e30))
                scaled = kernel * steps_t[h + i : h + i + 1, :]
                weights = cross * scaled
                inside_head = (lane >= i * head_dim) & (lane < (i + 1) * head_dim)
                one = t_mm(weights.astype(BF), dy_part)
                tile = one if i == 0 else jnp.where(lane >= i * head_dim, one, tile)
                dweights = mm_t(jnp.where(inside_head, dy_part, jnp.zeros_like(dy_part)), part)
                dcross = dcross + dweights * scaled
                unscaled = dweights * (cross * kernel)
                total = jnp.sum(dweights * weights, 1, keepdims=True)
                dlogs = dlogs + jnp.where(lane == h + i, total, 0.0)
                columns.append(jnp.sum(unscaled, 0, keepdims=True))
            tiles.append(tile)
        dvalues = dvalues + jnp.concatenate(tiles, 1)
        columns = jnp.concatenate(columns + [jnp.zeros((128 - heads, GROUP), F32)], 0).T
        dlogs = dlogs - columns * steps
        at_end = jnp.sum(dtail * tail, 0, keepdims=True) + ends * kept
        dlogs = dlogs + jnp.where(row == GROUP - 1, at_end, 0.0)
        da = exact(triangle(True).astype(F32), dlogs)
        dsteps = columns + dtail * rest + da * rate
        dhead_ref[1:2, :] += jnp.sum(da * steps, 0, keepdims=True)
        draw = jnp.where(lane < heads, dsteps * sigmoid(raw), 0.0)
        dhead_ref[0:1, :] += jnp.sum(draw, 0, keepdims=True)
        dproj_ref[rows, 2 * hw + state2 :] = pltpu.roll(draw, heads * s, 1).astype(BF)
        dcross_low = dcross.astype(BF)
        dc = dc + mm(dcross_low, b) + mm(dcross_low, b_rest)
        dcross_t = dcross.T.astype(BF)
        db = db + mm(dcross_t, ct) + mm(dcross_t, ct_rest)
        dmix = jnp.concatenate([dvalues, db, dc], 1) * (sig + conv * (1 - sig))
        dtable_ref[width : width + 1, :] += jnp.sum(dmix, 0, keepdims=True)
        ext = with_before(proj_ref, at, slice(hw, 2 * hw + state2), c == 0)
        dext = jnp.concatenate([dmix, after[...]], 0)
        dconv = 0.0
        for j in range(width):
            first = 8 - width + 1 + j
            dtable_ref[j : j + 1, :] += jnp.sum(dmix * ext[first : first + GROUP], 0, keepdims=True)
            dconv = dconv + table[j : j + 1] * dext[width - 1 - j : width - 1 - j + GROUP]
        after[...] = dmix[:8]
        dproj_ref[rows, hw : 2 * hw + state2] = dconv.astype(BF)
        ring.step(lap + 3)
        return carry

    lax.fori_loop(0, blocks, chunk, 0)
    model = resid_all.shape[2]
    every = resid_all[...].reshape(blocks * GROUP, model)
    for d in range(0, hw, 128):
        low_t = low_ref[:, d : d + 128].T
        grad_out_ref[d : d + 128, :] = mm(low_t, every).astype(BF)
    for k in range(blocks + 3, ne - 1):
        ring.step(k)
    wide = grad_common_ref.shape[1]
    main = dproj_ref.shape[1] - wide
    for d in range(0, model, 384):
        rows = slice(d, d + 384)
        lowered_t = lowered_ref[:, rows].T
        grad_in_ref[rows, :] = mm(lowered_t, dproj_ref[:, :main]).astype(BF)
        common = mm(lowered_t, dproj_ref[:, main:])
        grad_common_ref[rows, : wide - 128] = common[:, : wide - 128].astype(BF)
        grad_common_ref[rows, wide - 128 :] = (common[:, wide - 128 :] + router_ref[rows, :]).astype(BF)
    ring.finish(sum_ref)
    for n in range(len(experts.items)):
        experts.close(n)
    experts.drain()
    rows_in.drain()


def mix_backward(
    proj,
    table,
    head_table,
    scanned,
    mixed,
    entries,
    out_local,
    resid_low,
    scales,
    out_part,
    expert_part,
    lowered,
    router_grad,
    ns,
    ne,
    hw,
    state2,
    heads,
    width,
    cid,
):
    whole = proj.shape[0]
    n = state2 // 2
    rows, model = resid_low.shape
    return pl.pallas_call(
        functools.partial(mix_backward_kernel, ns, ne, hw, state2, heads, width),
        out_shape=(
            jax.ShapeDtypeStruct((rows, model), F32),
            jax.ShapeDtypeStruct(expert_part.shape[1:], F32),
            jax.ShapeDtypeStruct(proj.shape, BF),
            jax.ShapeDtypeStruct((hw, model), BF),
            jax.ShapeDtypeStruct((model, 2 * hw), BF),
            jax.ShapeDtypeStruct((model, proj.shape[1] - 2 * hw), BF),
            jax.ShapeDtypeStruct((8, hw + state2), F32),
            jax.ShapeDtypeStruct((8, 128), F32),
        ),
        in_specs=[ANY, VMEM, VMEM] + [ANY] * 4 + [VMEM] * 3 + [ANY] * 2 + [VMEM],
        out_specs=(VMEM,) * 8,
        scratch_shapes=[
            pltpu.VMEM((n, hw), F32),
            pltpu.VMEM((8, hw + state2), F32),
            pltpu.VMEM((whole, hw), BF),
            pltpu.VMEM((ns, rows, model), BF),
            pltpu.VMEM((ns, 8, rows), F32),
        ]
        + Loads.scratch([proj, scanned, mixed, entries, out_local, lowered])
        + RingSum.scratch(ne, 2, rows, model)
        + SeqGather.scratch(ns)
        + BlockSum.scratch(ns, [expert_part.shape]),
        compiler_params=params(cid, 50),
        name="mix_backward",
    )(
        proj,
        table,
        head_table,
        scanned,
        mixed,
        entries,
        out_local,
        resid_low,
        scales,
        out_part,
        expert_part,
        lowered,
        router_grad,
    )


def rms_back(value, gain, grad):
    scale = lax.rsqrt(jnp.mean(value * value, -1, keepdims=True) + EPSILON)
    inside = gain * grad
    back = scale * inside - value * scale**3 * jnp.mean(value * inside, -1, keepdims=True)
    return back, jnp.sum(value * scale * grad, 0)


def swiglu_back(a, b, grad):
    sig = jax.nn.sigmoid(a)
    return grad * b * sig * (1 + a * (1 - sig)), grad * a * sig


def on_device(
    tokens,
    routes,
    out_grad,
    norm_mix,
    in_weight,
    step_weight,
    conv_weight,
    conv_bias,
    step_bias,
    decay_log,
    skip_gain,
    norm_gate,
    out_weight,
    norm_ffn,
    router_weight,
    shared_gate,
    shared_up,
    shared_down,
    expert_gate,
    expert_up,
    expert_down,
):
    ns, ne = lax.axis_size("seq"), lax.axis_size("exp")
    s, e = lax.axis_index("seq"), lax.axis_index("exp")
    total = ns * ne
    rows, columns = in_weight.shape
    model = tokens.shape[2]
    length = tokens.shape[1]
    whole = length * ns
    width, channels = conv_weight.shape
    gains = norm_gate.shape[0]
    inner = gains * total
    hw = inner // ns
    heads = step_bias.shape[0]
    local_heads = heads // ns
    state2 = columns - 2 * inner
    experts = router_weight.shape[1]
    local_experts = expert_gate.shape[0]
    place = s * ne + e

    small = jnp.concatenate([conv_weight.reshape(-1), conv_bias, norm_gate])
    small = jnp.pad(small, (0, 16 * rows - small.shape[0])).reshape(rows, 16)
    pack = jnp.concatenate(
        [step_weight, router_weight, norm_mix[:, None], norm_ffn[:, None], small], 1
    )
    at_small = heads + experts + 2
    pack = jnp.pad(pack, ((0, 0), (0, 128 - pack.shape[1])))
    hidden_rows = shared_down.shape[0]

    def by_owner(weight):
        split = weight.reshape(rows, ns, ne, hidden_rows)
        return jnp.transpose(split, (2, 0, 1, 3)).reshape(ne, rows, ns * hidden_rows)

    shared_two = jnp.concatenate([by_owner(shared_gate), by_owner(shared_up)], -1)
    in_blocks, common_blocks, token_blocks, out_local, shared_two, local_down = gather_in(
        in_weight, pack, tokens[0], out_weight, shared_two, shared_down, ns, ne, inner, 0
    )
    out_local = out_local.reshape(hw, model)
    shared_two = shared_two.reshape(model, 2 * ns * hidden_rows)
    local_gate, local_up = shared_two[:, : ns * hidden_rows], shared_two[:, ns * hidden_rows :]
    local_down = local_down.reshape(ns * hidden_rows, model)
    grad_low = out_grad[0]
    in_local = in_blocks.reshape(model, -1)
    in_common = common_blocks.reshape(model, -1)
    full_pack = in_common[:, state2:]
    full_router = full_pack[:, heads : heads + experts]
    full_norm_mix = full_pack[:, heads + experts].astype(F32)
    full_norm_ffn = full_pack[:, heads + experts + 1].astype(F32)
    full_small = full_pack[:, at_small : at_small + 16].reshape(total, 16 * rows).astype(F32)
    full_conv = full_small[:, : (width + 1) * channels].reshape(total, width + 1, channels)
    full_conv = jnp.swapaxes(full_conv, 0, 1).reshape(width + 1, total * channels)
    at_gain = (width + 1) * channels
    full_norm_gate = full_small[:, at_gain : at_gain + gains].reshape(inner)
    local_conv = jnp.concatenate(
        [lax.dynamic_slice_in_dim(full_conv, s * hw, hw, 1), full_conv[:, inner:]], 1
    )
    local_gain = lax.dynamic_slice_in_dim(full_norm_gate, s * hw, hw)
    at_head = s * local_heads
    local_bias = lax.dynamic_slice_in_dim(step_bias, at_head, local_heads)
    local_decay = lax.dynamic_slice_in_dim(decay_log, at_head, local_heads)
    local_skip = lax.dynamic_slice_in_dim(skip_gain, at_head, local_heads)

    table = jnp.concatenate(
        [
            local_conv,
            jnp.pad(
                jnp.stack([local_gain, jnp.repeat(local_skip, hw // local_heads)]),
                ((0, 6 - width - 1), (0, state2)),
            ),
        ],
        0,
    )
    head_table = jnp.pad(
        jnp.stack([local_bias, -jnp.exp(local_decay)]), ((0, 6), (0, 128 - local_heads))
    )

    token_rows = tokens[0].astype(F32)
    projected, lowered, scanned, mixed, entries, mixed_raw, squares, grad_all = mix_forward(
        token_blocks.reshape(whole, model),
        in_local,
        in_common,
        table,
        head_table,
        out_local,
        grad_low,
        ns,
        ne,
        hw,
        state2,
        local_heads,
        width,
        heads + experts,
        1,
    )
    scale_gate = lax.rsqrt(squares[0] / inner + EPSILON)
    mixer_out = mixed_raw * scale_gate[:, None]
    resid = token_rows + mixer_out
    scale_two = lax.rsqrt(jnp.mean(resid * resid, -1, keepdims=True) + EPSILON)
    ffn_in = (resid * scale_two * full_norm_ffn).astype(BF)

    logits = matmul_plain(ffn_in, full_router)
    named = jnp.any(
        routes[0][:, :, None] == jnp.arange(experts, dtype=jnp.int32)[None, None, :], 1
    )
    top = jnp.max(jnp.where(named, logits, -jnp.inf), -1, keepdims=True)
    raised = jnp.where(named, jnp.exp(jnp.where(named, logits - top, 0.0)), 0.0)
    gates = (raised / jnp.sum(raised, -1, keepdims=True)).T

    gates_out = jnp.pad(
        gates.reshape(ne, local_experts, length), ((0, 0), (0, 8 - local_experts), (0, 0))
    )
    back_sum, gate_grads, out_part, grad_gate, grad_up, grad_down, shared_part, grad_shared_down = (
        experts_both_ways(
            ffn_in,
            gates_out,
            grad_all,
            expert_gate,
            expert_up,
            expert_down,
            shared_two,
            local_down,
            ns,
            ne,
            2,
        )
    )
    gate_grads = gate_grads[:, :local_experts].reshape(experts, length)
    picked_grad = gates * (gate_grads - jnp.sum(gates * gate_grads, 0, keepdims=True))
    logit_grad = picked_grad.T.astype(BF)
    grad_router = matmul_rows(ffn_in, logit_grad)
    ffn_in_grad = matmul_cols(logit_grad, full_router) + back_sum
    resid_norm_grad, grad_norm_ffn = rms_back(resid, full_norm_ffn, ffn_in_grad)
    resid_grad = grad_low.astype(F32) + resid_norm_grad
    resid_low = resid_grad.astype(BF)
    inside = jnp.sum(resid_low.astype(F32) * mixer_out, -1) / (scale_gate * inner)
    scales = jnp.concatenate(
        [scale_gate[None], inside[None], jnp.zeros((6, length), F32)], 0
    )

    ffn_out, grad_gate, projected_grad, grad_out, in_grad, common_grad, table_grad, head_grad = mix_backward(
        projected,
        table,
        head_table,
        scanned,
        mixed,
        entries,
        out_local,
        resid_low,
        scales,
        out_part,
        grad_gate,
        lowered,
        jnp.pad(grad_router, ((0, 0), (heads, 128 - heads - experts))),
        ns,
        ne,
        hw,
        state2,
        local_heads,
        width,
        4,
    )
    result = (resid + ffn_out).astype(BF)
    stat_terms = jnp.stack(
        [jnp.sum(resid * resid), jnp.sum(mixer_out * mixer_out), jnp.sum(ffn_out * ffn_out)]
    )
    grad_skip = jnp.sum(table_grad[width + 2, :hw].reshape(local_heads, -1), -1)
    grad_decay = head_grad[1, :local_heads] * head_table[1, :local_heads]

    small_parts = [
        table_grad[: width + 1],
        table_grad[width + 1, :hw],
        head_grad[0, :local_heads],
        grad_decay,
        grad_skip,
        grad_norm_ffn,
        stat_terms,
    ]
    ends = []
    at = 0
    for part in small_parts:
        ends.append((at, at + part.size, part.shape))
        at += part.size
    room = 6 * 256
    aux = jnp.concatenate([part.reshape(-1) for part in small_parts])
    aux = jnp.pad(aux, (0, ne * room - at)).reshape(ne, 6, 256)
    aux = jnp.pad(aux, ((0, 0), (0, 2), (0, 0)))

    (
        grad_in,
        grad_pack,
        grad_out,
        tokens_grad,
        sums,
        shared_part,
        grad_up,
        grad_down,
        grad_shared_down,
    ) = sum_weights(
        in_grad.reshape(ns, ne, rows, -1),
        common_grad.reshape(ns, 1, ne, rows, -1),
        grad_out.reshape(ne, hw // ne, model),
        projected_grad,
        in_local,
        in_common,
        tokens[0],
        resid_grad,
        jnp.broadcast_to(full_norm_mix[None], (8, model)),
        aux,
        [
            grad_up,
            grad_down,
            grad_shared_down.reshape(ns, 1, hidden_rows, model),
            shared_part.reshape(ns, 1, ne, rows, -1),
        ],
        128,
        ns,
        ne,
        6,
    )
    grad_step = grad_pack[:, :heads]
    grad_router = grad_pack[:, heads : heads + experts]
    flat = sums[:, :, :6].reshape(ns, ne * room)
    table_all, gain_all, bias_all, decay_all, skip_all, ffn_all, stat_all = [
        flat[:, start:end].reshape((ns,) + shape) for start, end, shape in ends
    ]
    conv_all = jnp.concatenate(
        [
            jnp.swapaxes(table_all[:, :, :hw], 0, 1).reshape(width + 1, inner),
            jnp.sum(table_all[:, :, hw:], 0),
        ],
        1,
    )
    conv_grads = lax.dynamic_slice_in_dim(conv_all, place * channels, channels, 1)
    mix_sums = jnp.sum(sums[:, :, 6:, :128], 0)
    grad_norm_mix = jnp.swapaxes(mix_sums, 0, 1).reshape(-1)[:model]
    shared_part = shared_part.astype(F32).reshape(ne, rows, 2, ns, hidden_rows)
    shared_grads = jnp.transpose(shared_part, (2, 1, 3, 0, 4)).reshape(2, rows, total * hidden_rows)
    return (
        result[None],
        tokens_grad[None],
        lax.dynamic_slice_in_dim(grad_norm_mix, place * rows, rows),
        grad_in,
        grad_step,
        conv_grads[:width],
        conv_grads[width],
        bias_all.reshape(heads),
        decay_all.reshape(heads),
        skip_all.reshape(heads),
        lax.dynamic_slice_in_dim(gain_all.reshape(inner), place * gains, gains),
        grad_out,
        lax.dynamic_slice_in_dim(jnp.sum(ffn_all, 0), place * rows, rows),
        grad_router,
        shared_grads[0],
        shared_grads[1],
        grad_shared_down[0],
        grad_gate,
        grad_up,
        grad_down,
        jnp.sum(stat_all, 0) / (total * length * model),
    )


def solution(mesh):
    both = ("seq", "exp")
    return jax.shard_map(
        on_device,
        mesh=mesh,
        in_specs=(
            P("exp", "seq", None),
            P("exp", "seq", None),
            P("exp", "seq", None),
            P(both),
            P(both, None),
            P(both, None),
            P(None, both),
            P(both),
            P(),
            P(),
            P(),
            P(both),
            P(both, None),
            P(both),
            P(both, None),
            P(both, None),
            P(both, None),
            P(both, None),
            P("exp", None, None),
            P("exp", None, None),
            P("exp", None, None),
        ),
        out_specs=(
            P("exp", "seq", None),
            P("exp", "seq", None),
            P(both),
            P(both, None),
            P(both, None),
            P(None, both),
            P(both),
            P(),
            P(),
            P(),
            P(both),
            P(both, None),
            P(both),
            P(both, None),
            P(both, None),
            P(both, None),
            P(both, None),
            P("exp", "seq", None),
            P("exp", "seq", None),
            P("exp", None, "seq"),
            P(),
        ),
        check_vma=False,
    )
```

```python
import functools

import jax
import jax.numpy as jnp
from jax import lax
from jax.experimental import pallas as pl
from jax.experimental.pallas import tpu as pltpu
from jax.sharding import PartitionSpec as P

GROUP = 128
EPSILON = 1e-05
PRECISE = lax.Precision.HIGHEST
MESH = pl.DeviceIdType.MESH
BF = jnp.bfloat16
F32 = jnp.float32
ANY = pl.BlockSpec(memory_space=pl.ANY)
VMEM = pl.BlockSpec(memory_space=pltpu.VMEM)
DMA = pltpu.SemaphoreType.DMA


def ring_place(e, n):
    odd = e % 2
    return (1 - odd) * (e // 2) + odd * (n - 1 - e // 2)


def ring_index(p, n):
    back = p // (n // 2)
    return (1 - back) * (2 * p) + back * (2 * (n - 1 - p) + 1)


def ring_sides(e, n):
    p = ring_place(e, n)
    return p, ring_index((p + 1) % n, n), ring_index((p + n - 1) % n, n)


def greet(partners):
    barrier = pltpu.get_barrier_semaphore()
    for partner in partners:
        pl.semaphore_signal(barrier, inc=1, device_id=partner, device_id_type=MESH)
    pl.semaphore_wait(barrier, len(partners))


def remote(src, dst, send, recv, device):
    copy = pltpu.make_async_remote_copy(
        src_ref=src,
        dst_ref=dst,
        send_sem=send,
        recv_sem=recv,
        device_id=device,
        device_id_type=MESH,
    )
    copy.start()
    return copy


def params(cid, mib=48):
    return pltpu.CompilerParams(
        collective_id=cid, has_side_effects=True, vmem_limit_bytes=mib << 20
    )


class Loads:
    def __init__(self, sources, held, sems):
        self.copies = [
            pltpu.make_async_copy(src, dst, sems.at[i])
            for i, (src, dst) in enumerate(zip(sources, held))
        ]

    @staticmethod
    def scratch(arrays):
        return [pltpu.VMEM(v.shape, v.dtype) for v in arrays] + [DMA((len(arrays),))]

    def begin(self):
        for copy in self.copies:
            copy.start()

    def wait(self, *which):
        for i in which:
            self.copies[i].wait()


def tile_rows(rows, most=16):
    return most if rows % most == 0 else rows


def gather_in_kernel(
    ns,
    ne,
    hw,
    inner,
    in_ref,
    pack_ref,
    tok_ref,
    out_ref,
    two_ref,
    down_ref,
    w_ref,
    c_ref,
    x_ref,
    o_ref,
    shared_ref,
    sd_ref,
    lsem,
    ssem0,
    rsem0,
    ssem,
    rsem,
    sa,
    ra,
    sb,
    rb,
    sc,
    rc,
):
    s, e = lax.axis_index("seq"), lax.axis_index("exp")
    p, right, left = ring_sides(e, ne)
    width = in_ref.shape[1] - 2 * inner
    half = out_ref.shape[1] // 2
    parts = (
        (lambda to: in_ref.at[:, pl.ds(pl.multiple_of(to * hw, 128), hw)], 0),
        (lambda to: in_ref.at[:, pl.ds(pl.multiple_of(inner + to * hw, 128), hw)], hw),
    )
    greet([((s + t) % ns, e) for t in range(1, ns)] + [(s, (e + t) % ne) for t in range(1, ne)])
    own = []
    for i, (piece, start) in enumerate(parts):
        own.append(
            pltpu.make_async_copy(piece(s), w_ref.at[s, e, :, pl.ds(start, hw)], lsem.at[i])
        )
    own.append(
        pltpu.make_async_copy(
            in_ref.at[:, pl.ds(2 * inner, width)], c_ref.at[s, e, :, pl.ds(0, width)], lsem.at[2]
        )
    )
    own.append(
        pltpu.make_async_copy(
            pack_ref, c_ref.at[s, e, :, pl.ds(width, pack_ref.shape[1])], lsem.at[3]
        )
    )
    own.append(pltpu.make_async_copy(out_ref, o_ref.at[e], lsem.at[4]))
    own.append(pltpu.make_async_copy(two_ref.at[e], shared_ref.at[s, e], lsem.at[5]))
    own.append(pltpu.make_async_copy(tok_ref, x_ref.at[s], lsem.at[6]))
    own.append(pltpu.make_async_copy(down_ref, sd_ref.at[s], lsem.at[7]))
    for copy in own:
        copy.start()
    first = {}
    for t in range(1, ns):
        to = (s + t) % ns
        for i, (piece, start) in enumerate(parts):
            first[t, i] = remote(
                piece(to),
                w_ref.at[s, e, :, pl.ds(start, hw)],
                ssem0.at[t - 1, i],
                rsem0.at[t - 1, i],
                (to, e),
            )
    for copy in own:
        copy.wait()
    sent = {}
    across = {}
    along = {}
    common = {}

    def place_of(k, way):
        return ring_index((p - k + ne) % ne if way == 0 else (p + k) % ne, ne)

    def share(k):
        block = c_ref.at[s, place_of(k, 1)]
        for t in range(1, ns):
            common[k, t] = remote(
                block, block, sc.at[k, t - 1], rc.at[k, t - 1], ((s + t) % ns, e)
            )

    for k in range(ne - 1):
        for t in [0, ns, ns + 1, ns + 2] + list(range(1, ns)):
            way = 1 if t == ns else (t - ns - 1 if t > ns else t % 2)
            to = (s, right if way == 0 else left)
            slot = place_of(k, way)
            if k > 0:
                sent[k - 1, t].wait_recv()
            elif 0 < t < ns:
                for i in range(len(parts)):
                    first[t, i].wait_recv()
            if t < ns:
                block = w_ref.at[(s + ns - t) % ns, slot]
            elif t == ns:
                block = c_ref.at[s, slot]
            else:
                block = o_ref.at[slot, :, pl.ds(way * half, half)]
            sent[k, t] = remote(block, block, ssem.at[k, t], rsem.at[k, t], to)
            if t == ns:
                share(k)
        if k == 0:
            for t in range(1, ns):
                to = ((s + t) % ns, e)
                first[t, 2] = remote(
                    tok_ref, x_ref.at[s], ssem0.at[t - 1, 2], rsem0.at[t - 1, 2], to
                )
                first[t, 3] = remote(
                    down_ref, sd_ref.at[s], ssem0.at[t - 1, 3], rsem0.at[t - 1, 3], to
                )
            for t in range(1, ne):
                to = (e + t) % ne
                across[t] = remote(
                    two_ref.at[to], shared_ref.at[s, e], sa.at[t - 1], ra.at[t - 1], (s, to)
                )
        if k == 2:
            for t in range(1, ne):
                across[t].wait_recv()
            for t in range(1, ns):
                along[t] = remote(
                    shared_ref.at[s], shared_ref.at[s], sb.at[t - 1], rb.at[t - 1], ((s + t) % ns, e)
                )
    sent[ne - 2, ns].wait_recv()
    share(ne - 1)
    for t in range(ns + 3):
        if t != ns:
            sent[ne - 2, t].wait_recv()
    for t in range(1, ns):
        first[t, 2].wait_recv()
        first[t, 3].wait_recv()
        along[t].wait_recv()
    for copy in common.values():
        copy.wait_recv()
    for group in (first, sent, across, along, common):
        for copy in group.values():
            copy.wait_send()


def gather_in(in_weight, pack, tokens, out_weight, shared_two, shared_down, ns, ne, inner, cid):
    rows, columns = in_weight.shape
    hw = inner // ns
    wide = columns - 2 * inner + pack.shape[1]
    return pl.pallas_call(
        functools.partial(gather_in_kernel, ns, ne, hw, inner),
        out_shape=(
            jax.ShapeDtypeStruct((ns, ne, rows, 2 * hw), BF),
            jax.ShapeDtypeStruct((ns, ne, rows, wide), BF),
            jax.ShapeDtypeStruct((ns,) + tokens.shape, BF),
            jax.ShapeDtypeStruct((ne,) + out_weight.shape, BF),
            jax.ShapeDtypeStruct((ns,) + shared_two.shape, BF),
            jax.ShapeDtypeStruct((ns,) + shared_down.shape, BF),
        ),
        in_specs=[ANY] * 6,
        out_specs=(ANY,) * 6,
        scratch_shapes=[
            DMA((8,)),
            DMA((ns - 1, 4)),
            DMA((ns - 1, 4)),
            DMA((ne - 1, ns + 3)),
            DMA((ne - 1, ns + 3)),
            DMA((ne - 1,)),
            DMA((ne - 1,)),
            DMA((ns - 1,)),
            DMA((ns - 1,)),
            DMA((ne, ns - 1)),
            DMA((ne, ns - 1)),
        ],
        compiler_params=params(cid, 8),
        name="gather_in",
    )(in_weight, pack, tokens, out_weight, shared_two, shared_down)


class SeqSum:
    def __init__(self, ns, subs, part, aux, one, two, aux_in, s1, r1, s2, r2, sa, ra):
        self.s, self.e = lax.axis_index("seq"), lax.axis_index("exp")
        self.ns, self.ny, self.subs = ns, ns // 2, subs
        self.y, self.c = self.s // 2, self.s % 2
        self.part, self.aux, self.one, self.two, self.aux_in = part, aux, one, two, aux_in
        self.sems = (s1, r1, s2, r2, sa, ra)
        self.step = part.shape[1] // subs
        self.tile = tile_rows(self.step)
        self.first, self.second, self.extra = {}, {}, []

    @staticmethod
    def scratch(ns, subs, rows, width, aux_shape):
        ny = ns // 2
        return [
            pltpu.VMEM((ny, rows, width), BF),
            pltpu.VMEM((max(ny - 1, 1), rows, width), BF),
            pltpu.VMEM((ns - 1,) + aux_shape, F32),
            DMA((ny, subs)),
            DMA((ny, subs)),
            DMA((max(ny - 1, 1), subs)),
            DMA((max(ny - 1, 1), subs)),
            DMA((ns - 1,)),
            DMA((ns - 1,)),
        ]

    def rows(self, u):
        return pl.ds(u * self.step, self.step)

    def send_aux(self):
        s1, r1, s2, r2, sa, ra = self.sems
        for t in range(1, self.ns):
            to = (self.s + t) % self.ns
            self.extra.append(
                remote(
                    self.aux.at[to], self.aux_in.at[t - 1], sa.at[t - 1], ra.at[t - 1], (to, self.e)
                )
            )

    def order(self):
        return list(range(1, self.ny)) + [0]

    def far(self, j):
        return 2 * ((self.y + j) % self.ny) + 1 - self.c

    def near(self, j):
        return 2 * ((self.y + j) % self.ny) + self.c

    def send(self, j):
        s1, r1, s2, r2, sa, ra = self.sems
        mate = (2 * self.y + 1 - self.c, self.e)
        for u in range(self.subs):
            self.first[j, u] = remote(
                self.part.at[self.far(j), self.rows(u)],
                self.one.at[j, self.rows(u)],
                s1.at[j, u],
                r1.at[j, u],
                mate,
            )

    def begin(self, fill):
        self.send_aux()
        for j in self.order():
            fill(self.far(j))
            self.send(j)
        for j in self.order():
            fill(self.near(j))

    def join(self, j, u):
        s1, r1, s2, r2, sa, ra = self.sems
        to = self.near(j)
        self.first[j, u].wait_recv()

        def add(i, carry):
            r = pl.ds(pl.multiple_of(u * self.step + i * self.tile, self.tile), self.tile)
            total = self.one[j, r, :].astype(F32) + self.part[to, r, :].astype(F32)
            self.one[j, r, :] = total.astype(BF)
            return carry

        lax.fori_loop(0, self.step // self.tile, add, 0)
        self.second[j, u] = remote(
            self.one.at[j, self.rows(u)],
            self.two.at[j - 1, self.rows(u)],
            s2.at[j - 1, u],
            r2.at[j - 1, u],
            (to, self.e),
        )

    def middle(self):
        for j in range(1, self.ny):
            for u in range(self.subs):
                self.join(j, u)

    def close(self, u, out):
        self.first[0, u].wait_recv()
        for j in range(1, self.ny):
            self.second[j, u].wait_recv()

        def add(i, carry):
            r = pl.ds(pl.multiple_of(u * self.step + i * self.tile, self.tile), self.tile)
            total = self.one[0, r, :].astype(F32) + self.part[self.s, r, :].astype(F32)
            for j in range(1, self.ny):
                total = total + self.two[j - 1, r, :].astype(F32)
            out[r, :] = total
            return carry

        lax.fori_loop(0, self.step // self.tile, add, 0)

    def finish(self, out, aux_out):
        for u in range(self.subs):
            self.close(u, out)
        total = self.aux[self.s]
        for t in range(1, self.ns):
            self.extra[t - 1].wait_recv()
            total = total + self.aux_in[t - 1]
        aux_out[...] = total

    def drain(self):
        for copy in list(self.first.values()) + list(self.second.values()) + self.extra:
            copy.wait_send()


class BlockSum:
    def __init__(self, ns, sources, outs, scratch):
        self.s, self.e = lax.axis_index("seq"), lax.axis_index("exp")
        self.ns, self.ny = ns, ns // 2
        self.y, self.c = self.s // 2, self.s % 2
        self.sources, self.outs = sources, outs
        self.items = [(m, i) for m, src in enumerate(sources) for i in range(src.shape[1])]
        count = len(sources)
        self.held, self.one, self.two = (
            scratch[:count],
            scratch[count : 2 * count],
            scratch[2 * count : 3 * count],
        )
        self.lsem, self.s1, self.r1, self.s2, self.r2 = scratch[3 * count :]
        self.loads = [
            pltpu.make_async_copy(src, held, self.lsem.at[m])
            for m, (src, held) in enumerate(zip(self.sources, self.held))
        ]
        self.first, self.second = {}, {}

    @staticmethod
    def scratch(ns, shapes):
        ny = ns // 2
        items = sum(shape[1] for shape in shapes)
        return (
            [pltpu.VMEM(shape, BF) for shape in shapes]
            + [pltpu.VMEM((ny,) + shape[1:], BF) for shape in shapes]
            + [pltpu.VMEM((max(ny - 1, 1),) + shape[1:], BF) for shape in shapes]
            + [
                DMA((len(shapes),)),
                DMA((ny, items)),
                DMA((ny, items)),
                DMA((max(ny - 1, 1), items)),
                DMA((max(ny - 1, 1), items)),
            ]
        )

    def load(self):
        for copy in self.loads:
            copy.start()

    def begin(self):
        mate = (2 * self.y + 1 - self.c, self.e)
        for copy in self.loads:
            copy.wait()
        for j in list(range(1, self.ny)) + [0]:
            block = 2 * ((self.y + j) % self.ny) + 1 - self.c
            for n, (m, i) in enumerate(self.items):
                self.first[j, n] = remote(
                    self.held[m].at[block, i],
                    self.one[m].at[j, i],
                    self.s1.at[j, n],
                    self.r1.at[j, n],
                    mate,
                )

    def tiles(self, shape, body):
        if len(shape) == 3:
            lax.fori_loop(0, shape[0], lambda i, carry: body((i,)) or carry, 0)
        else:
            size = 32 if shape[0] % 32 == 0 else shape[0]
            lax.fori_loop(
                0,
                shape[0] // size,
                lambda i, carry: body((pl.ds(pl.multiple_of(i * size, size), size),)) or carry,
                0,
            )

    def join(self, j, n):
        m, i = self.items[n]
        to = 2 * ((self.y + j) % self.ny) + self.c
        self.first[j, n].wait_recv()
        one, held = self.one[m], self.held[m]

        def add(at):
            total = one[(j, i) + at].astype(F32) + held[(to, i) + at].astype(F32)
            one[(j, i) + at] = total.astype(BF)

        self.tiles(one.shape[2:], add)
        self.second[j, n] = remote(
            one.at[j, i],
            self.two[m].at[j - 1, i],
            self.s2.at[j - 1, n],
            self.r2.at[j - 1, n],
            (to, self.e),
        )

    def close(self, n):
        m, i = self.items[n]
        self.first[0, n].wait_recv()
        for j in range(1, self.ny):
            self.second[j, n].wait_recv()
        one, held, two, out = self.one[m], self.held[m], self.two[m], self.outs[m]

        def add(at):
            total = one[(0, i) + at].astype(F32) + held[(self.s, i) + at].astype(F32)
            for j in range(1, self.ny):
                total = total + two[(j - 1, i) + at].astype(F32)
            out[(i,) + at] = total

        self.tiles(one.shape[2:], add)

    def drain(self):
        for copy in list(self.first.values()) + list(self.second.values()):
            copy.wait_send()


class RingGather:
    def __init__(self, ne, v, out, lsem, ssem, rsem):
        self.s, self.e = lax.axis_index("seq"), lax.axis_index("exp")
        self.ne, self.v, self.out = ne, v, out
        self.p, self.right, self.left = ring_sides(self.e, ne)
        self.ssem, self.rsem = ssem, rsem
        self.subs = ssem.shape[2]
        self.step_rows = v.shape[0] // (2 * self.subs)
        self.own = pltpu.make_async_copy(v, out.at[self.e], lsem)

    @staticmethod
    def scratch(ne, subs):
        return [DMA, DMA((ne - 1, 2, subs)), DMA((ne - 1, 2, subs))]

    def copy(self, k, way, u, src=None):
        place = (self.p - k + self.ne) % self.ne if way == 0 else (self.p + k) % self.ne
        slot = ring_index(place, self.ne)
        rows = pl.ds((way * self.subs + u) * self.step_rows, self.step_rows)
        block = self.out.at[slot, rows]
        return pltpu.make_async_remote_copy(
            src_ref=block if src is None else src.at[rows],
            dst_ref=block,
            send_sem=self.ssem.at[k, way, u],
            recv_sem=self.rsem.at[k, way, u],
            device_id=(self.s, self.right if way == 0 else self.left),
            device_id_type=MESH,
        )

    def begin(self):
        self.own.start()
        for u in range(self.subs):
            for way in range(2):
                self.copy(0, way, u, self.v).start()

    def step(self, k):
        for u in range(self.subs):
            for way in range(2):
                self.copy(k - 1, way, u).wait_recv()
                self.copy(k, way, u).start()

    def forward(self, k):
        for u in range(self.subs):
            for way in range(2):
                self.copy(k, way, u).start()

    def arrived(self, k):
        for u in range(self.subs):
            for way in range(2):
                self.copy(k, way, u).wait_recv()

    def drain(self):
        for k in range(self.ne - 1):
            for u in range(self.subs):
                for way in range(2):
                    self.copy(k, way, u).wait_send()

    def finish(self):
        self.arrived(self.ne - 2)
        self.drain()
        self.own.wait()


class RingSum:
    def __init__(self, ne, part, acc, ssem, rsem):
        self.s, self.e = lax.axis_index("seq"), lax.axis_index("exp")
        self.ne, self.part, self.acc = ne, part, acc
        self.p, self.right, self.left = ring_sides(self.e, ne)
        self.ssem, self.rsem = ssem, rsem
        self.subs = ssem.shape[2]
        self.size = part.shape[1] // (2 * self.subs)
        self.tile = tile_rows(self.size)

    @staticmethod
    def scratch(ne, subs, rows, width):
        return [
            pltpu.VMEM((ne - 1, rows, width), BF),
            DMA((ne - 1, 2, subs)),
            DMA((ne - 1, 2, subs)),
        ]

    def slot(self, k, way):
        place = (self.p - 1 - k + 2 * self.ne) % self.ne if way == 0 else (self.p + 1 + k) % self.ne
        return ring_index(place, self.ne)

    def copy(self, k, way, u, src=None):
        rows = pl.ds((way * self.subs + u) * self.size, self.size)
        return pltpu.make_async_remote_copy(
            src_ref=self.acc.at[k, rows] if src is None else src.at[rows],
            dst_ref=self.acc.at[k, rows],
            send_sem=self.ssem.at[k, way, u],
            recv_sem=self.rsem.at[k, way, u],
            device_id=(self.s, self.right if way == 0 else self.left),
            device_id_type=MESH,
        )

    def add(self, k, way, u, out):
        base = (way * self.subs + u) * self.size
        slot = self.slot(k, way)

        def join(i, carry):
            r = pl.ds(pl.multiple_of(base + i * self.tile, self.tile), self.tile)
            total = self.acc[k - 1, r, :].astype(F32) + self.part[slot, r, :].astype(F32)
            if out is None:
                self.acc[k - 1, r, :] = total.astype(BF)
            else:
                out[r, :] = total
            return carry

        lax.fori_loop(0, self.size // self.tile, join, 0)

    def begin(self):
        for u in range(self.subs):
            for way in range(2):
                self.copy(0, way, u, self.part.at[self.slot(0, way)]).start()

    def step(self, k):
        for u in range(self.subs):
            for way in range(2):
                self.copy(k - 1, way, u).wait_recv()
                self.add(k, way, u, None)
                rows = pl.ds((way * self.subs + u) * self.size, self.size)
                pltpu.make_async_remote_copy(
                    src_ref=self.acc.at[k - 1, rows],
                    dst_ref=self.acc.at[k, rows],
                    send_sem=self.ssem.at[k, way, u],
                    recv_sem=self.rsem.at[k, way, u],
                    device_id=(self.s, self.right if way == 0 else self.left),
                    device_id_type=MESH,
                ).start()

    def finish(self, out):
        k = self.ne - 1
        for u in range(self.subs):
            for way in range(2):
                self.copy(k - 1, way, u).wait_recv()
                self.add(k, way, u, out)
        for k in range(self.ne - 1):
            for u in range(self.subs):
                for way in range(2):
                    self.copy(k, way, u).wait_send()


class Exchange:
    def __init__(self, ne, src, dst, lsem, ssem, rsem, pick=None, spread=False):
        s, e = lax.axis_index("seq"), lax.axis_index("exp")
        if pick is None:
            pick = lambda ref, at: ref.at[at]
        give = (lambda ref, at: ref) if spread else pick
        self.own = pltpu.make_async_copy(give(src, e), pick(dst, e), lsem)
        self.copies = []
        for t in range(1, ne):
            to = (e + t) % ne
            self.copies.append(
                pltpu.make_async_remote_copy(
                    src_ref=give(src, to),
                    dst_ref=pick(dst, e),
                    send_sem=ssem.at[t - 1],
                    recv_sem=rsem.at[t - 1],
                    device_id=(s, to),
                    device_id_type=MESH,
                )
            )

    @staticmethod
    def scratch(ne):
        return [DMA, DMA((ne - 1,)), DMA((ne - 1,))]

    def begin(self):
        self.own.start()
        for copy in self.copies:
            copy.start()

    def arrived(self):
        self.own.wait()
        for copy in self.copies:
            copy.wait_recv()

    def drain(self):
        for copy in self.copies:
            copy.wait_send()


def experts_kernel(
    ne,
    count,
    ffn_ref,
    gate_ref,
    grad_hbm,
    eg_hbm,
    eu_hbm,
    ed_hbm,
    two_hbm,
    sd_hbm,
    back_ref,
    gate_back,
    out_ref,
    dg_ref,
    du_ref,
    dd_ref,
    ds_ref,
    dsd_ref,
    x_ref,
    gates,
    hid_ref,
    da_ref,
    db_ref,
    part_ref,
    gate_part,
    stage_g,
    stage_u,
    stage_d,
    stage_s,
    stage_sem,
    out_stage,
    out_sem,
    *scratch,
):
    s, e = lax.axis_index("seq"), lax.axis_index("exp")
    length, model = ffn_ref.shape
    half = length // 2
    sources = (eg_hbm, eu_hbm, grad_hbm, ed_hbm, two_hbm, sd_hbm)
    eg_ref, eu_ref, grad_ref, ed_ref, two_ref, sd_ref = scratch[12:18]
    loads = Loads(sources, scratch[12:18], scratch[18])
    loads.begin()
    width = eg_ref.shape[2]
    narrow = sd_ref.shape[0]
    tile_width = min(width, 256)
    greet([(s, (e + t) % ne) for t in range(1, ne)])
    ring = RingGather(ne, ffn_ref, x_ref, *scratch[:3])
    there = Exchange(ne, gate_ref, gates, *scratch[3:6])
    back = Exchange(ne, gate_part, gate_back, *scratch[6:9])
    total = RingSum(ne, part_ref, *scratch[9:12])
    ring.begin()
    there.begin()
    gate_part[...] = jnp.zeros_like(gate_part)
    ring.own.wait()
    there.own.wait()
    lane = lax.broadcasted_iota(jnp.int32, (8, length), 1)
    wide_lane = lax.broadcasted_iota(jnp.int32, (2 * length, 128), 1)

    def quarters(i):
        found = []
        for k in (2 * i, 2 * i + 1):
            found.append((ring_index((ring.p - k + ne) % ne, ne), 0))
            found.append((ring_index((ring.p + k) % ne, ne), half))
        return found

    def out_copies(i):
        slot = i % 2
        return [
            pltpu.make_async_copy(
                out_stage.at[slot, pl.ds(n * half, half)],
                out_ref.at[block, pl.ds(first, half)],
                out_sem.at[slot, n],
            )
            for n, (block, first) in enumerate(quarters(i))
        ]

    def rows_of(ref, places, cols):
        return jnp.concatenate(
            [ref[block, first : first + half, cols] for block, first in places], 0
        )

    def store(ref, places, cols, value):
        for n, (block, first) in enumerate(places):
            ref[block, first : first + half, cols] = value[n * half : (n + 1) * half]

    def compute(i):
        places = quarters(i)
        every = slice(0, model)
        x = rows_of(x_ref, places, every)
        g = rows_of(grad_ref, places, every)
        table = jnp.concatenate(
            [
                jnp.where(lane < half, gates[places[n][0]], gates[places[n + 1][0]]).T
                for n in (0, 2)
            ],
            0,
        )
        slots = jnp.zeros((2 * length, 128), F32)
        for j in range(count + 1):
            size = width if j < count else narrow
            column = table[:, j : j + 1] if j < count else None
            for f in range(0, size, tile_width):
                wide = min(tile_width, size - f)
                if j < count:
                    a = mm(x, eg_ref[j, :, f : f + wide])
                    b = mm(x, eu_ref[j, :, f : f + wide])
                    h = mm_t(g, ed_ref[j, f : f + wide, :])
                else:
                    both = mm(x, two_ref[...])
                    a, b = both[:, :narrow], both[:, narrow:]
                    h = mm_t(g, sd_ref[...])
                sig = sigmoid(a)
                silu = a * sig
                act = silu * b
                if j < count:
                    found = jnp.sum(act * h, 1, keepdims=True)
                    slots = slots + jnp.where(wide_lane == j, found, 0.0)
                    act = act * column
                    h = h * column
                cols = slice(j * width + f, j * width + f + wide)
                store(hid_ref, places, cols, act.astype(BF))
                store(da_ref, places, cols, (h * b * (sig + silu * (1 - sig))).astype(BF))
                store(db_ref, places, cols, (h * silu).astype(BF))
        found = slots.T[:8]
        for n in (0, 2):
            part = found[:, (n // 2) * length : (n // 2 + 1) * length]
            one, two = places[n][0], places[n + 1][0]
            gate_part[one] = jnp.where(lane < half, part, gate_part[one])
            gate_part[two] = jnp.where(lane >= half, part, gate_part[two])

    def compute_back(i):
        places = quarters(i)

        @pl.when(i >= 2)
        def _():
            for copy in out_copies(i - 2):
                copy.wait()

        last = slice(count * width, count * width + narrow)
        for d in range(0, model, 256):
            cols = slice(d, d + 256)
            out = mm(rows_of(hid_ref, places, last), sd_ref[:, cols])
            row = mm_t(rows_of(da_ref, places, last), two_ref[cols, :narrow])
            row = row + mm_t(rows_of(db_ref, places, last), two_ref[cols, narrow:])
            for j in range(count):
                mine = slice(j * width, (j + 1) * width)
                out = out + mm(rows_of(hid_ref, places, mine), ed_ref[j, :, cols])
                row = row + mm_t(rows_of(da_ref, places, mine), eg_ref[j, cols, :])
                row = row + mm_t(rows_of(db_ref, places, mine), eu_ref[j, cols, :])
            out_stage[i % 2, :, cols] = out.astype(BF)
            store(part_ref, places, cols, row.astype(BF))
        for copy in out_copies(i):
            copy.start()

    def arrive(i, carry):
        ring.arrived(2 * i)

        @pl.when(2 * i + 1 < ne - 1)
        def _():
            ring.forward(2 * i + 1)

        @pl.when(i == 0)
        def _():
            loads.wait(*range(6))
            for copy in there.copies:
                copy.wait_recv()

        @pl.when(i == ne // 2 - 1)
        def _():
            total.begin()

        compute(i)

        @pl.when(2 * i + 1 < ne - 1)
        def _():
            ring.arrived(2 * i + 1)
            ring.forward(2 * i + 2)

        @pl.when(i == ne // 2 - 1)
        def _():
            total.step(1)

        compute_back(i)
        return carry

    lax.fori_loop(0, ne // 2, arrive, 0)
    ring.drain()
    back.begin()
    part_rows = stage_g.shape[3]
    per = stage_g.shape[1]
    tile = per * part_rows
    tiles = model // tile
    every = ne * length

    def stage_copies(i):
        slot = i % 2
        blocks = pl.ds(i * per, per)
        return [
            pltpu.make_async_copy(stage_g.at[slot], dg_ref.at[blocks], stage_sem.at[slot, 0]),
            pltpu.make_async_copy(stage_u.at[slot], du_ref.at[blocks], stage_sem.at[slot, 3]),
            pltpu.make_async_copy(stage_d.at[slot], dd_ref.at[blocks], stage_sem.at[slot, 1]),
            pltpu.make_async_copy(stage_s.at[slot], ds_ref.at[i], stage_sem.at[slot, 2]),
        ]

    def weights(i):
        @pl.when(i >= 2)
        def _():
            for copy in stage_copies(i - 2):
                copy.wait()

        cols = pl.ds(pl.multiple_of(i * tile, 128), tile)
        slot = i % 2
        x_t = x_ref[:, :, cols].reshape(every, tile).T
        g_t = grad_ref[:, :, cols].reshape(every, tile).T
        for j in range(count):
            at = slice(j * width, (j + 1) * width)
            gate = mm(x_t, da_ref[:, :, at].reshape(every, width)).astype(BF)
            up = mm(x_t, db_ref[:, :, at].reshape(every, width)).astype(BF)
            down = mm(g_t, hid_ref[:, :, at].reshape(every, width)).T.astype(BF)
            for q in range(per):
                rows = slice(q * part_rows, (q + 1) * part_rows)
                stage_g[slot, q, j] = gate[rows]
                stage_u[slot, q, j] = up[rows]
                stage_d[slot, q, j] = down[:, rows]
        at = slice(count * width, count * width + narrow)
        both = jnp.concatenate(
            [da_ref[:, :, at].reshape(every, narrow), db_ref[:, :, at].reshape(every, narrow)], 1
        )
        stage_s[slot] = mm(x_t, both).astype(BF)
        for copy in stage_copies(i):
            copy.start()

    def back_step(k, carry):
        total.step(k)

        @pl.when(k - 2 < tiles)
        def _():
            weights(k - 2)

        return carry

    lax.fori_loop(2, ne - 1, back_step, 0)
    at = slice(count * width, count * width + narrow)
    hid_t = hid_ref[:, :, at].reshape(every, narrow).T
    for d in range(0, model, 512):
        dsd_ref[:, d : d + 512] = mm(hid_t, grad_ref[:, :, d : d + 512].reshape(every, 512)).astype(BF)
    for i in range(ne - 3, tiles):
        weights(i)
    for i in range(max(tiles - 2, 0), tiles):
        for copy in stage_copies(i):
            copy.wait()
    for i in (ne // 2 - 2, ne // 2 - 1):
        for copy in out_copies(i):
            copy.wait()
    total.finish(back_ref)
    back.arrived()
    back.drain()
    there.drain()


def experts_both_ways(
    ffn_in, gates, grad_all, expert_gate, expert_up, expert_down, shared_two, shared_down, ns, ne, cid
):
    length, model = ffn_in.shape
    count, _, width = expert_gate.shape
    narrow = shared_down.shape[0]
    hidden = count * width + narrow
    part = model // ns
    per = 1 if part % 128 == 0 else 2
    return pl.pallas_call(
        functools.partial(experts_kernel, ne, count),
        out_shape=(
            jax.ShapeDtypeStruct((length, model), F32),
            jax.ShapeDtypeStruct((ne, 8, length), F32),
            jax.ShapeDtypeStruct((ne, length, model), BF),
            jax.ShapeDtypeStruct((ns, count, part, width), BF),
            jax.ShapeDtypeStruct((ns, count, part, width), BF),
            jax.ShapeDtypeStruct((ns, count, width, part), BF),
            jax.ShapeDtypeStruct((ns // per, per * part, 2 * narrow), BF),
            jax.ShapeDtypeStruct((narrow, model), BF),
        ),
        in_specs=[VMEM] * 2 + [ANY] * 6,
        out_specs=(VMEM, VMEM, ANY, ANY, ANY, ANY, ANY, VMEM),
        scratch_shapes=[
            pltpu.VMEM((ne, length, model), BF),
            pltpu.VMEM((ne, 8, length), F32),
            pltpu.VMEM((ne, length, hidden), BF),
            pltpu.VMEM((ne, length, hidden), BF),
            pltpu.VMEM((ne, length, hidden), BF),
            pltpu.VMEM((ne, length, model), BF),
            pltpu.VMEM((ne, 8, length), F32),
            pltpu.VMEM((2, per, count, part, width), BF),
            pltpu.VMEM((2, per, count, part, width), BF),
            pltpu.VMEM((2, per, count, width, part), BF),
            pltpu.VMEM((2, per * part, 2 * narrow), BF),
            DMA((2, 4)),
            pltpu.VMEM((2, 2 * length, model), BF),
            DMA((2, 4)),
        ]
        + RingGather.scratch(ne, 2)
        + Exchange.scratch(ne)
        + Exchange.scratch(ne)
        + RingSum.scratch(ne, 2, length, model)
        + Loads.scratch(
            [expert_gate, expert_up, grad_all, expert_down, shared_two, shared_down]
        ),
        compiler_params=params(cid, 60),
        name="experts",
    )(ffn_in, gates, grad_all, expert_gate, expert_up, expert_down, shared_two, shared_down)


class SeqGather:
    def __init__(self, ns, v, aux, out, aux_out, lsem, s1, r1, s2, r2, sa, ra):
        s, e = lax.axis_index("seq"), lax.axis_index("exp")
        ny = ns // 2
        y, c = s // 2, s % 2
        mate = (2 * y + 1 - c, e)

        def make(src, dst, send, recv, device):
            return pltpu.make_async_remote_copy(
                src_ref=src,
                dst_ref=dst,
                send_sem=send,
                recv_sem=recv,
                device_id=device,
                device_id_type=MESH,
            )

        self.own = [
            pltpu.make_async_copy(v, out.at[s], lsem.at[0]),
            pltpu.make_async_copy(aux, aux_out.at[s], lsem.at[1]),
        ]
        self.first = [
            make(v, out.at[s], s1.at[j], r1.at[j], (2 * ((y + j) % ny) + c, e))
            for j in range(1, ny)
        ]
        self.first.append(make(v, out.at[s], s1.at[0], r1.at[0], mate))
        self.extra = [
            make(aux, aux_out.at[s], sa.at[t - 1], ra.at[t - 1], ((s + t) % ns, e))
            for t in range(1, ns)
        ]
        self.second = []
        for j in range(1, ny):
            block = out.at[2 * ((y + ny - j) % ny) + c]
            self.second.append(make(block, block, s2.at[j - 1], r2.at[j - 1], mate))

    @staticmethod
    def scratch(ns):
        ny = ns // 2
        return [
            DMA((2,)),
            DMA((ny,)),
            DMA((ny,)),
            DMA((max(ny - 1, 1),)),
            DMA((max(ny - 1, 1),)),
            DMA((ns - 1,)),
            DMA((ns - 1,)),
        ]

    def begin(self):
        for copy in self.first + self.extra + self.own:
            copy.start()

    def middle(self):
        for arrived, onward in zip(self.first[:-1], self.second):
            arrived.wait_recv()
            onward.start()

    def finish(self):
        for copy in [self.first[-1]] + self.second + self.extra:
            copy.wait_recv()
        for copy in self.own:
            copy.wait()

    def drain(self):
        for copy in self.first + self.second + self.extra:
            copy.wait_send()


def sum_weights_kernel(
    ns,
    ne,
    blocks,
    gin,
    gcommon,
    gout,
    dproj_ref,
    in_ref,
    common_ref,
    tok_ref,
    resid_ref,
    gain_ref,
    aux_ref,
    *refs,
):
    sources = refs[:blocks]
    in_out, pack_out, out_rows, tok_out, aux_out, shared_out = refs[blocks : blocks + 6]
    block_outs = refs[blocks + 6 : 2 * blocks + 5]
    sum_weights_body(
        ns,
        ne,
        sources,
        block_outs,
        gin,
        gcommon,
        gout,
        dproj_ref,
        in_ref,
        common_ref,
        tok_ref,
        resid_ref,
        gain_ref,
        aux_ref,
        in_out,
        pack_out,
        out_rows,
        tok_out,
        aux_out,
        shared_out,
        *refs[2 * blocks + 5 :],
    )


def sum_weights_body(
    ns,
    ne,
    sources,
    block_outs,
    gin,
    gcommon,
    gout,
    dproj_ref,
    in_ref,
    common_ref,
    tok_ref,
    resid_ref,
    gain_ref,
    aux_ref,
    in_out,
    pack_out,
    out_rows,
    tok_out,
    aux_out,
    shared_out,
    out,
    acc,
    acc_out,
    acc_common,
    common_sum,
    common_low,
    fin,
    part_ref,
    lowered_grad,
    aux_part,
    aux_in,
    aux_sum,
    shared_sum,
    shared_low,
    dproj,
    in_held,
    common_held,
    load_sems,
    ssem,
    rsem,
    so,
    ro,
    sc,
    rc,
    sx,
    rx,
    ss,
    rs,
    *scratch,
):
    s, e = lax.axis_index("seq"), lax.axis_index("exp")
    p, right, left = ring_sides(e, ne)
    count = len(SeqSum.scratch(ns, 2, 8, 128, (8, 128)))
    job = SeqSum(ns, 2, part_ref, None, *scratch[:count])
    there = Exchange(ne, aux_part, aux_in, *scratch[count : count + 3])
    back = Exchange(
        ne,
        aux_sum,
        aux_out,
        *scratch[count + 3 : count + 6],
        pick=lambda ref, at: ref.at[s, at],
        spread=True,
    )
    along = []
    at = count + 9 + len(BlockSum.scratch(ns, [gcommon.shape]))
    shared_cols = BlockSum(ns, (gcommon,), (common_sum,), scratch[count + 9 : at])
    more = BlockSum(ns, sources, tuple(block_outs) + (shared_sum,), scratch[at:])
    across = Exchange(ne, shared_low, shared_out, *scratch[count + 6 : count + 9])
    loads = Loads((dproj_ref, in_ref, common_ref), (dproj, in_held, common_held), load_sems)
    shared_cols.load()
    loads.begin()
    more.load()
    greet([((s + t) % ns, e) for t in range(1, ns)] + [(s, (e + t) % ne) for t in range(1, ne)])

    def fill(block):
        rows = pl.ds(pl.multiple_of(block * GROUP, GROUP), GROUP)
        main = in_held.shape[1]
        part = mm_t(dproj[rows, :main], in_held[...])
        part_ref[block] = (part + mm_t(dproj[rows, main:], common_held[...])).astype(BF)

    def tokens_back():
        value = tok_ref[...].astype(F32)
        grad = lowered_grad[...]
        width = value.shape[1]
        scale = lax.rsqrt(jnp.sum(value * value, 1, keepdims=True) / width + EPSILON)
        inside = gain_ref[0:1, :] * grad
        mean = jnp.sum(value * inside, 1, keepdims=True) / width
        tok_out[...] = (resid_ref[...] + scale * inside - value * (scale * scale * scale * mean)).astype(BF)
        gain_grad = jnp.sum(value * scale * grad, 0, keepdims=True)
        aux_part[...] = aux_ref[...]
        for i in range(width // 128):
            q = aux_last + i // 8
            aux_part[q % ne, q // ne, i % 8 : i % 8 + 1, :] = gain_grad[:, i * 128 : (i + 1) * 128]
        there.begin()

    def sums():
        there.arrived()
        total = aux_in[0]
        for i in range(1, ne):
            total = total + aux_in[i]
        aux_sum[...] = total
        back.begin()

    def spread():
        back.arrived()
        for t in range(1, ns):
            along.append(
                remote(aux_out.at[s], aux_out.at[s], ss.at[t - 1], rs.at[t - 1], ((s + t) % ns, e))
            )

    def swap():
        shared_low[...] = shared_sum[0].astype(BF)
        across.begin()

    def far_task(j):
        def run():
            fill(job.far(j))
            job.send(j)

        return run

    def common_ready():
        shared_cols.close(0)
        common_low[...] = common_sum[0].astype(BF)
        ready.append(True)

    ready = []
    aux_last = (gin.shape[3] // 2 + common_ref.shape[1] - pack_out.shape[1]) // 128 + 3
    items = len(more.items)
    lanes = range(1, ns // 2)
    tasks = [(0.0, lambda: loads.wait(0, 1, 2))]
    tasks += [(0.05, functools.partial(shared_cols.join, j, 0)) for j in lanes]
    tasks += [(0.17, common_ready)]
    tasks += [(0.02 * i, far_task(j)) for i, j in enumerate(job.order())]
    tasks += [
        (0.02 * (i + ns // 2), functools.partial(fill, job.near(j)))
        for i, j in enumerate(job.order())
    ]
    tasks += [(0.13, more.begin)]
    tasks += [(0.14, functools.partial(job.join, j, u)) for j in lanes for u in range(job.subs)]
    tasks += [
        (0.22 + 0.15 * (items - 1 - n) / items, functools.partial(more.join, j, n))
        for n in reversed(range(items))
        for j in lanes
    ]
    tasks += [(0.36, functools.partial(job.close, u, lowered_grad)) for u in range(job.subs)]
    tasks += [(0.40, tokens_back), (0.54, sums), (0.68, spread)]
    tasks += [(0.74, functools.partial(more.close, items - 1)), (0.75, swap)]
    tasks += [
        (0.80 + 0.18 * (items - 1 - n) / items, functools.partial(more.close, n))
        for n in range(items - 1)
    ]
    tasks.sort(key=lambda task: task[0])
    shared_cols.begin()
    rows = gin.shape[2]
    main = gin.shape[3]
    tile = tile_rows(rows)
    half = gout.shape[2] // 2
    tile_out = tile_rows(gout.shape[1])
    sent = {}
    last = {}
    done = 0
    lag = 2
    for k in range(ne + lag):
        for t in list(range(1, ns)) + [0, ns, ns + 1, ns + 2]:
            while k > 0 and tasks and tasks[0][0] <= done / (ne * (ns + 3)):
                tasks.pop(0)[1]()
            if t == ns + 2:
                hop = k - lag
                way = 1
            else:
                hop = k
                way = t % 2
            if hop < 0 or hop >= ne:
                continue
            while t == ns + 2 and not ready:
                tasks.pop(0)[1]()
            done += 1
            to = right if way == 0 else left
            place = (p - 1 - hop + 2 * ne) % ne if way == 0 else (p + 1 + hop) % ne
            slot = ring_index(place, ne)
            if hop > 0:
                sent[hop - 1, t].wait_recv()
            if t < ns:
                piece = (s + t) % ns
                if hop > 0:

                    def join(i, carry):
                        r = pl.ds(pl.multiple_of(i * tile, tile), tile)
                        total = acc[hop - 1, t, r, :].astype(F32)
                        total = total + gin[piece, slot, r, :].astype(F32)
                        if hop < ne - 1:
                            acc[hop - 1, t, r, :] = total.astype(BF)
                        elif t == 0:
                            out[s, r, :] = total.astype(BF)
                        else:
                            fin[t - 1, r, :] = total.astype(BF)
                        return carry

                    lax.fori_loop(0, rows // tile, join, 0)
                if hop < ne - 1:
                    src = gin.at[piece, slot] if hop == 0 else acc.at[hop - 1, t]
                    sent[hop, t] = remote(
                        src, acc.at[hop, t], ssem.at[hop, t], rsem.at[hop, t], (s, to)
                    )
                elif t > 0:
                    last[t] = remote(
                        fin.at[t - 1], out.at[s], sx.at[t - 1], rx.at[t - 1], (piece, e)
                    )
            elif t == ns + 2:
                if hop > 0:
                    total = acc_common[hop - 1].astype(F32) + common_low[slot].astype(F32)
                    if hop < ne - 1:
                        acc_common[hop - 1] = total.astype(BF)
                    else:
                        wide = total.shape[1] - pack_out.shape[1]
                        in_out[:, in_out.shape[1] - wide :] = total[:, :wide]
                        pack_out[...] = total[:, wide:]
                if hop < ne - 1:
                    src = common_low.at[slot] if hop == 0 else acc_common.at[hop - 1]
                    sent[hop, t] = remote(
                        src, acc_common.at[hop], sc.at[hop], rc.at[hop], (s, to)
                    )
            else:
                part_columns = pl.ds(way * half, half)
                if hop > 0:

                    def join_out(i, carry):
                        r = pl.ds(pl.multiple_of(i * tile_out, tile_out), tile_out)
                        total = acc_out[hop - 1, r, part_columns].astype(F32)
                        total = total + gout[slot, r, part_columns].astype(F32)
                        if hop < ne - 1:
                            acc_out[hop - 1, r, part_columns] = total.astype(BF)
                        else:
                            out_rows[r, part_columns] = total
                        return carry

                    lax.fori_loop(0, gout.shape[1] // tile_out, join_out, 0)
                if hop < ne - 1:
                    src = (
                        gout.at[slot, :, part_columns]
                        if hop == 0
                        else acc_out.at[hop - 1, :, part_columns]
                    )
                    sent[hop, t] = remote(
                        src,
                        acc_out.at[hop, :, part_columns],
                        so.at[hop, way],
                        ro.at[hop, way],
                        (s, to),
                    )
    for _, task in tasks:
        task()
    for copy in list(last.values()) + along:
        copy.wait_recv()
    head = main // 2
    inner = head * ns
    for block in range(ns):
        in_out[:, block * head : (block + 1) * head] = out[block, :, :head].astype(F32)
        in_out[:, inner + block * head : inner + (block + 1) * head] = out[block, :, head:].astype(F32)
    for copy in list(sent.values()) + list(last.values()) + along:
        copy.wait_send()
    across.arrived()
    more.drain()
    shared_cols.drain()
    job.drain()
    there.drain()
    back.drain()
    across.drain()


def sum_weights(
    gin,
    gcommon,
    gout,
    projected_grad,
    in_local,
    in_common,
    tokens,
    resid_grad,
    gain,
    aux,
    sources,
    pack,
    ns,
    ne,
    cid,
):
    rows, wide = gin.shape[2:]
    narrow = gcommon.shape[4]
    length, model = tokens.shape
    blocks = len(sources)
    return pl.pallas_call(
        functools.partial(sum_weights_kernel, ns, ne, blocks),
        out_shape=(
            jax.ShapeDtypeStruct((rows, ns * wide + narrow - pack), F32),
            jax.ShapeDtypeStruct((rows, pack), F32),
            jax.ShapeDtypeStruct(gout.shape[1:], F32),
            jax.ShapeDtypeStruct(tokens.shape, BF),
            jax.ShapeDtypeStruct((ns,) + aux.shape, F32),
            jax.ShapeDtypeStruct(sources[-1].shape[2:], BF),
        )
        + tuple(jax.ShapeDtypeStruct(v.shape[1:], F32) for v in sources[:-1]),
        in_specs=[VMEM, ANY, VMEM] + [ANY] * 3 + [VMEM] * 4 + [ANY] * blocks,
        out_specs=(VMEM,) * (5 + blocks),
        scratch_shapes=[
            pltpu.VMEM((ns, rows, wide), BF),
            pltpu.VMEM((ne - 1, ns, rows, wide), BF),
            pltpu.VMEM((ne - 1,) + gout.shape[1:], BF),
            pltpu.VMEM((ne - 1, rows, narrow), BF),
            pltpu.VMEM(gcommon.shape[1:], F32),
            pltpu.VMEM(gcommon.shape[2:], BF),
            pltpu.VMEM((ns - 1, rows, wide), BF),
            pltpu.VMEM((ns, length, model), BF),
            pltpu.VMEM((length, model), F32),
            pltpu.VMEM(aux.shape, F32),
            pltpu.VMEM(aux.shape, F32),
            pltpu.VMEM(aux.shape[1:], F32),
            pltpu.VMEM(sources[-1].shape[1:], F32),
            pltpu.VMEM(sources[-1].shape[2:], BF),
        ]
        + Loads.scratch([projected_grad, in_local, in_common])
        + [
            DMA((ne - 1, ns)),
            DMA((ne - 1, ns)),
            DMA((ne - 1, 2)),
            DMA((ne - 1, 2)),
            DMA((ne - 1,)),
            DMA((ne - 1,)),
            DMA((ns - 1,)),
            DMA((ns - 1,)),
            DMA((ns - 1,)),
            DMA((ns - 1,)),
        ]
        + SeqSum.scratch(ns, 2, length, model, (8, 128))
        + Exchange.scratch(ne)
        + Exchange.scratch(ne)
        + Exchange.scratch(ne)
        + BlockSum.scratch(ns, [gcommon.shape])
        + BlockSum.scratch(ns, [v.shape for v in sources]),
        compiler_params=params(cid, 60),
        name="sum_weights",
    )(
        gin,
        gcommon,
        gout,
        projected_grad,
        in_local,
        in_common,
        tokens,
        resid_grad,
        gain,
        aux,
        *sources,
    )


def matmul_plain(left, right):
    return jnp.dot(left, right, preferred_element_type=F32)


def matmul_rows(left, right):
    return lax.dot_general(left, right, (((0,), (0,)), ((), ())), preferred_element_type=F32)


def matmul_cols(left, right):
    return lax.dot_general(left, right, (((1,), (1,)), ((), ())), preferred_element_type=F32)


def mm(left, right):
    return jnp.dot(left, right, preferred_element_type=F32)


def mm_t(left, right):
    return lax.dot_general(left, right, (((1,), (1,)), ((), ())), preferred_element_type=F32)


def t_mm(left, right):
    return lax.dot_general(left, right, (((0,), (0,)), ((), ())), preferred_element_type=F32)


def exact(left, right):
    return jnp.dot(left, right, precision=PRECISE, preferred_element_type=F32)


def spread_heads(table, heads, head_dim):
    rows = table.shape[0]
    per = 128 // head_dim
    lane = lax.broadcasted_iota(jnp.int32, (rows, 128), 1)
    tiles = []
    for h in range(0, heads, per):
        tile = jnp.broadcast_to(table[:, h : h + 1], (rows, 128))
        for i in range(1, per):
            other = jnp.broadcast_to(table[:, h + i : h + i + 1], (rows, 128))
            tile = jnp.where(lane >= i * head_dim, other, tile)
        tiles.append(tile)
    return jnp.concatenate(tiles, 1)


def sigmoid(v):
    return 1.0 / (1.0 + jnp.exp(-v))


def softplus(v):
    return jnp.maximum(v, 0.0) + jnp.log1p(jnp.exp(-jnp.abs(v)))


def two_parts(v):
    high = v.astype(BF)
    return high, (v - high.astype(F32)).astype(BF)


def triangle(flip=False):
    t = lax.broadcasted_iota(jnp.int32, (GROUP, GROUP), 0)
    u = lax.broadcasted_iota(jnp.int32, (GROUP, GROUP), 1)
    return u >= t if flip else t >= u


def step_table(pack, bias, heads, s):
    turned = pltpu.roll(pack, (128 - heads * s) % 128, 1)
    lane = lax.broadcasted_iota(jnp.int32, turned.shape, 1)
    raw = jnp.where(lane < heads, turned + bias, 0.0)
    return raw, jnp.where(lane < heads, softplus(raw), 0.0)


def convolved(ext, table, width):
    mixed = table[width : width + 1]
    for j in range(width):
        mixed = mixed + table[j : j + 1] * ext[8 - width + 1 + j : 8 - width + 1 + j + GROUP]
    return mixed


def with_before(proj_ref, at, columns, first):
    before = proj_ref[pl.ds(pl.multiple_of(jnp.maximum(at - 8, 0), 8), 8), columns]
    before = jnp.where(first, 0.0, before)
    return jnp.concatenate([before, proj_ref[pl.ds(at, GROUP), columns]], 0)


def mix_forward_kernel(
    ns,
    ne,
    hw,
    state2,
    heads,
    width,
    norm_at,
    x_ref,
    w_hbm,
    c_hbm,
    table_ref,
    head_ref,
    out_hbm,
    grad_ref,
    proj_hbm,
    lowered_hbm,
    scan_hbm,
    mix_hbm,
    entry_hbm,
    sum_ref,
    square_out,
    grad_all,
    proj_ref,
    lowered_ref,
    scan_ref,
    mix_ref,
    entry_ref,
    state,
    low_ref,
    square_ref,
    part_ref,
    store_sem,
    w_ref,
    c_ref,
    out_ref,
    load_sem,
    *sems,
):
    s, e = lax.axis_index("seq"), lax.axis_index("exp")
    p, right, left = ring_sides(e, ne)
    loads = Loads((w_hbm, c_hbm, out_hbm), (w_ref, c_ref, out_ref), load_sem)
    loads.begin()
    greet([((s + t) % ns, e) for t in range(1, ns)] + [(s, right), (s, left)])
    ring = RingGather(ne, grad_ref, grad_all, *sems[:3])
    job = SeqSum(ns, 2, part_ref, square_ref, *sems[3:])
    ring.begin()
    pairs = (
        (proj_ref, proj_hbm),
        (lowered_ref, lowered_hbm),
        (scan_ref, scan_hbm),
        (mix_ref, mix_hbm),
    )

    def stores(c):
        rows = pl.ds(pl.multiple_of(c * GROUP, GROUP), GROUP)
        copies = [
            pltpu.make_async_copy(ref.at[rows], hbm.at[rows], store_sem.at[c, i])
            for i, (ref, hbm) in enumerate(pairs)
        ]
        copies.append(
            pltpu.make_async_copy(entry_ref.at[c], entry_hbm.at[c], store_sem.at[c, len(pairs)])
        )
        return copies

    loads.wait(0, 1)
    norm = c_ref[:, state2:].astype(F32).T[norm_at : norm_at + 1, :]
    blocks = x_ref.shape[0] // GROUP
    head_dim = hw // heads
    n = state2 // 2
    state[...] = jnp.zeros_like(state)
    lane = lax.broadcasted_iota(jnp.int32, (GROUP, 128), 1)
    table = table_ref[...]
    skip = table[width + 2 : width + 3, :hw]
    gain = table[width + 1 : width + 2, :hw]
    bias, rate = head_ref[0:1, :], head_ref[1:2, :]

    def chunk(c, carry):
        at = pl.multiple_of(c * GROUP, GROUP)
        rows = pl.ds(at, GROUP)
        causal = triangle()
        x = x_ref[rows, :].astype(F32)
        scale = lax.rsqrt(jnp.sum(x * x, 1, keepdims=True) / x.shape[1] + EPSILON)
        lowered = (x * scale * norm).astype(BF)
        lowered_ref[rows, :] = lowered
        proj_ref[rows, : 2 * hw] = mm(lowered, w_ref[...])
        proj_ref[rows, 2 * hw :] = mm(lowered, c_ref[...])
        ext = with_before(proj_ref, at, slice(hw, 2 * hw + state2), c == 0)
        mixed = convolved(ext, table, width)
        mix_ref[rows, :] = mixed
        conv = mixed * sigmoid(mixed)
        values = conv[:, :hw]
        b = conv[:, hw : hw + n].astype(BF)
        ct = conv[:, hw + n :].astype(BF)
        _, steps = step_table(proj_ref[rows, 2 * hw + state2 :], bias, heads, s)
        logs = exact(causal.astype(F32), steps * rate)
        logs_t, steps_t = logs.T, steps.T
        end = logs[GROUP - 1 : GROUP, :]
        before = state[...]
        entry_ref[c] = before
        carried = mm(ct, before.astype(BF)) * spread_heads(jnp.exp(logs), heads, head_dim)
        tails = spread_heads(jnp.exp(end - logs) * steps, heads, head_dim)
        fresh = t_mm(b, (values * tails).astype(BF))
        state[...] = spread_heads(jnp.exp(end), heads, head_dim) * before + fresh
        cross = mm_t(ct, b)
        low = values.astype(BF)
        tiles = []
        per = 128 // head_dim
        for h in range(0, heads, per):
            tile = None
            part = low[:, h * head_dim : h * head_dim + 128]
            for i in range(per):
                gap = logs[:, h + i : h + i + 1] - logs_t[h + i : h + i + 1, :]
                kernel = jnp.exp(jnp.where(causal, gap, -1e30))
                weights = cross * kernel * steps_t[h + i : h + i + 1, :]
                one = mm(weights.astype(BF), part)
                tile = one if i == 0 else jnp.where(lane >= i * head_dim, one, tile)
            tiles.append(tile)
        scanned = jnp.concatenate(tiles, 1) + carried + skip * values
        scan_ref[rows, :] = scanned
        gate = proj_ref[rows, :hw]
        gated = scanned * (gate * sigmoid(gate))
        low_ref[rows, :] = (gated * gain).astype(BF)
        square_ref[c] = lax.dot_general(
            jnp.ones((8, hw), F32),
            gated * gated,
            (((1,), (1,)), ((), ())),
            precision=PRECISE,
            preferred_element_type=F32,
        )

        for copy in stores(c):
            copy.start()
        ring.step(c + 1)

        return carry

    lax.fori_loop(0, blocks, chunk, 0)

    def fill(block):
        rows = pl.ds(pl.multiple_of(block * GROUP, GROUP), GROUP)
        part_ref[block] = mm(low_ref[rows, :], out_ref[...]).astype(BF)

    k = blocks + 1
    loads.wait(2)
    job.begin(fill)
    for stage in (job.middle, lambda: job.finish(sum_ref, square_out)):
        if k < ne - 1:
            ring.step(k)
            k += 1
        stage()
    while k < ne - 1:
        ring.step(k)
        k += 1
    ring.finish()
    job.drain()
    for c in range(blocks):
        for copy in stores(c):
            copy.wait()


def mix_forward(
    sequence,
    in_local,
    in_common,
    table,
    head_table,
    out_local,
    grad_low,
    ns,
    ne,
    hw,
    state2,
    heads,
    width,
    norm_at,
    cid,
):
    whole, model = sequence.shape
    blocks = whole // GROUP
    n = state2 // 2
    rows = grad_low.shape[0]
    columns = in_local.shape[1] + in_common.shape[1]
    kept = [
        jax.ShapeDtypeStruct((whole, columns), F32),
        jax.ShapeDtypeStruct((whole, model), BF),
        jax.ShapeDtypeStruct((whole, hw), F32),
        jax.ShapeDtypeStruct((whole, hw + state2), F32),
        jax.ShapeDtypeStruct((blocks, n, hw), F32),
    ]
    return pl.pallas_call(
        functools.partial(mix_forward_kernel, ns, ne, hw, state2, heads, width, norm_at),
        out_shape=tuple(kept)
        + (
            jax.ShapeDtypeStruct((rows, model), F32),
            jax.ShapeDtypeStruct((8, rows), F32),
            jax.ShapeDtypeStruct((ne, rows, model), BF),
        ),
        in_specs=[VMEM, ANY, ANY, VMEM, VMEM, ANY, VMEM],
        out_specs=(ANY,) * 5 + (VMEM,) * 3,
        scratch_shapes=[pltpu.VMEM(v.shape, v.dtype) for v in kept]
        + [
            pltpu.VMEM((n, hw), F32),
            pltpu.VMEM((whole, hw), BF),
            pltpu.VMEM((blocks, 8, GROUP), F32),
            pltpu.VMEM((ns, rows, model), BF),
            DMA((blocks, 5)),
        ]
        + Loads.scratch([in_local, in_common, out_local])
        + RingGather.scratch(ne, 2)
        + SeqSum.scratch(ns, 2, rows, model, (8, rows)),
        compiler_params=params(cid, 50),
        name="mix_forward",
    )(sequence, in_local, in_common, table, head_table, out_local, grad_low)


def aux_slots(hw, state2, ne):
    return -(-((hw + state2) // 128 + 5) // ne)


def mix_backward_kernel(
    ns,
    ne,
    hw,
    state2,
    heads,
    width,
    proj_hbm,
    table_ref,
    head_ref,
    scan_hbm,
    mix_hbm,
    entry_hbm,
    out_hbm,
    resid_ref,
    rows_ref,
    part_ref,
    expert_ref,
    lowered_hbm,
    router_ref,
    value_ref,
    ffn_ref,
    stat_ref,
    result_ref,
    expert_out,
    dproj_ref,
    grad_out_ref,
    grad_in_ref,
    grad_common_ref,
    aux_ref,
    sum_ref,
    dtable_ref,
    dhead_ref,
    adjoint,
    after,
    low_ref,
    resid_all,
    scale_ref,
    *scratch,
):
    s, e = lax.axis_index("seq"), lax.axis_index("exp")
    p, right, left = ring_sides(e, ne)
    loads = Loads(
        (proj_hbm, scan_hbm, mix_hbm, entry_hbm, out_hbm, lowered_hbm), scratch[:6], scratch[6]
    )
    proj_ref, scan_ref, mix_ref, entry_ref, out_ref, lowered_ref = scratch[:6]
    loads.begin()
    greet([((s + t) % ns, e) for t in range(1, ns)] + [(s, right), (s, left)])
    ring = RingSum(ne, part_ref, *scratch[7:10])
    at = 10 + len(SeqGather.scratch(ns))
    rows_in = SeqGather(ns, resid_ref, rows_ref, resid_all, scale_ref, *scratch[10:at])
    experts = BlockSum(ns, (expert_ref,), (expert_out,), scratch[at:])
    experts.load()
    rows_in.begin()
    ring.begin()
    ring.step(1)
    rows_in.middle()
    experts.begin()
    ring.step(2)
    rows_in.finish()
    for j in range(1, ns // 2):
        for n in range(len(experts.items)):
            experts.join(j, n)
    loads.wait(*range(6))
    blocks = proj_ref.shape[0] // GROUP
    head_dim = hw // heads
    n = state2 // 2
    per = 128 // head_dim
    adjoint[...] = jnp.zeros_like(adjoint)
    after[...] = jnp.zeros_like(after)
    dtable_ref[...] = jnp.zeros_like(dtable_ref)
    dhead_ref[...] = jnp.zeros_like(dhead_ref)
    lane = lax.broadcasted_iota(jnp.int32, (GROUP, 128), 1)
    row = lax.broadcasted_iota(jnp.int32, (GROUP, 128), 0)
    table = table_ref[...]
    skip = table[width + 2 : width + 3, :hw]
    gain = table[width + 1 : width + 2, :hw]
    bias, rate = head_ref[0:1, :], head_ref[1:2, :]

    def chunk(lap, carry):
        c = blocks - 1 - lap
        at = pl.multiple_of(c * GROUP, GROUP)
        rows = pl.ds(at, GROUP)
        causal = triangle()
        head_of = lax.broadcasted_iota(jnp.int32, (hw, 128), 0) // head_dim
        pick = (head_of == lax.broadcasted_iota(jnp.int32, (hw, 128), 1)).astype(F32)
        gate = proj_ref[rows, :hw]
        gate_sig = sigmoid(gate)
        gate_silu = gate * gate_sig
        scanned = scan_ref[rows, :]
        gated = scanned * gate_silu
        scales = scale_ref[c].T
        r, inside = scales[:, 0:1], scales[:, 1:2]
        q = mm_t(resid_all[c], out_ref[...])
        dgated = r * (gain * q) - gated * (r * r * r * inside)
        low_ref[rows, :] = (gated * gain * r).astype(BF)
        dtable_ref[width + 1 : width + 2, :hw] += jnp.sum(gated * r * q, 0, keepdims=True)
        dy = dgated * gate_silu
        dproj_ref[rows, :hw] = (dgated * scanned * (gate_sig + gate_silu * (1 - gate_sig))).astype(BF)

        mixed = mix_ref[rows, :]
        sig = sigmoid(mixed)
        conv = mixed * sig
        values = conv[:, :hw]
        b, b_rest = two_parts(conv[:, hw : hw + n])
        ct, ct_rest = two_parts(conv[:, hw + n :])
        dtable_ref[width + 2 : width + 3, :hw] += jnp.sum(dy * values, 0, keepdims=True)
        raw, steps = step_table(proj_ref[rows, 2 * hw + state2 :], bias, heads, s)
        logs = exact(causal.astype(F32), steps * rate)
        logs_t, steps_t = logs.T, steps.T
        end = logs[GROUP - 1 : GROUP, :]
        rest = jnp.exp(end - logs)
        tail = rest * steps
        ends = jnp.exp(end)
        before = entry_ref[c]
        before_low, before_rest = two_parts(before)
        later = adjoint[...]
        later_low, later_rest = two_parts(later)
        tails = spread_heads(tail, heads, head_dim)
        dy_carried = dy * spread_heads(jnp.exp(logs), heads, head_dim)
        dy_carried_low = dy_carried.astype(BF)
        carried = mm(ct, before_low)
        back = mm(b, later_low)
        dvalues = tails * back + skip * dy
        dc = mm_t(dy_carried_low, before_low) + mm_t(dy_carried_low, before_rest)
        values_tail = (values * tails).astype(BF)
        db = mm_t(values_tail, later_low) + mm_t(values_tail, later_rest)
        kept = jnp.sum(later * before, 0, keepdims=True)
        adjoint[...] = spread_heads(ends, heads, head_dim) * later + t_mm(ct, dy_carried_low)
        sums = exact(jnp.concatenate([dy_carried * carried, values * back, jnp.broadcast_to(kept, (8, hw))], 0), pick)
        from_carried, dtail, kept = sums[:GROUP], sums[GROUP : 2 * GROUP], sums[2 * GROUP : 2 * GROUP + 1]
        cross = mm_t(ct, b)
        low = values.astype(BF)
        dy_low = dy.astype(BF)
        dcross = jnp.zeros((GROUP, GROUP), F32)
        dlogs = from_carried - dtail * tail
        columns = []
        tiles = []
        for h in range(0, heads, per):
            part = low[:, h * head_dim : h * head_dim + 128]
            dy_part = dy_low[:, h * head_dim : h * head_dim + 128]
            tile = None
            for i in range(per):
                gap = logs[:, h + i : h + i + 1] - logs_t[h + i : h + i + 1, :]
                kernel = jnp.exp(jnp.where(causal, gap, -1e30))
                scaled = kernel * steps_t[h + i : h + i + 1, :]
                weights = cross * scaled
                inside_head = (lane >= i * head_dim) & (lane < (i + 1) * head_dim)
                one = t_mm(weights.astype(BF), dy_part)
                tile = one if i == 0 else jnp.where(lane >= i * head_dim, one, tile)
                dweights = mm_t(jnp.where(inside_head, dy_part, jnp.zeros_like(dy_part)), part)
                dcross = dcross + dweights * scaled
                unscaled = dweights * (cross * kernel)
                total = jnp.sum(dweights * weights, 1, keepdims=True)
                dlogs = dlogs + jnp.where(lane == h + i, total, 0.0)
                columns.append(jnp.sum(unscaled, 0, keepdims=True))
            tiles.append(tile)
        dvalues = dvalues + jnp.concatenate(tiles, 1)
        columns = jnp.concatenate(columns + [jnp.zeros((128 - heads, GROUP), F32)], 0).T
        dlogs = dlogs - columns * steps
        at_end = jnp.sum(dtail * tail, 0, keepdims=True) + ends * kept
        dlogs = dlogs + jnp.where(row == GROUP - 1, at_end, 0.0)
        da = exact(triangle(True).astype(F32), dlogs)
        dsteps = columns + dtail * rest + da * rate
        dhead_ref[1:2, :] += jnp.sum(da * steps, 0, keepdims=True)
        draw = jnp.where(lane < heads, dsteps * sigmoid(raw), 0.0)
        dhead_ref[0:1, :] += jnp.sum(draw, 0, keepdims=True)
        dproj_ref[rows, 2 * hw + state2 :] = pltpu.roll(draw, heads * s, 1).astype(BF)
        dcross_low = dcross.astype(BF)
        dc = dc + mm(dcross_low, b) + mm(dcross_low, b_rest)
        dcross_t = dcross.T.astype(BF)
        db = db + mm(dcross_t, ct) + mm(dcross_t, ct_rest)
        dmix = jnp.concatenate([dvalues, db, dc], 1) * (sig + conv * (1 - sig))
        dtable_ref[width : width + 1, :] += jnp.sum(dmix, 0, keepdims=True)
        ext = with_before(proj_ref, at, slice(hw, 2 * hw + state2), c == 0)
        dext = jnp.concatenate([dmix, after[...]], 0)
        dconv = 0.0
        for j in range(width):
            first = 8 - width + 1 + j
            dtable_ref[j : j + 1, :] += jnp.sum(dmix * ext[first : first + GROUP], 0, keepdims=True)
            dconv = dconv + table[j : j + 1] * dext[width - 1 - j : width - 1 - j + GROUP]
        after[...] = dmix[:8]
        dproj_ref[rows, hw : 2 * hw + state2] = dconv.astype(BF)
        ring.step(lap + 3)
        return carry

    lax.fori_loop(0, blocks, chunk, 0)
    model = resid_all.shape[2]
    every = resid_all[...].reshape(blocks * GROUP, model)
    for d in range(0, hw, 128):
        low_t = low_ref[:, d : d + 128].T
        grad_out_ref[d : d + 128, :] = mm(low_t, every).astype(BF)
    for k in range(blocks + 3, ne - 1):
        ring.step(k)
    wide = grad_common_ref.shape[1]
    main = dproj_ref.shape[1] - wide
    for d in range(0, model, 384):
        rows = slice(d, d + 384)
        lowered_t = lowered_ref[:, rows].T
        grad_in_ref[rows, :] = mm(lowered_t, dproj_ref[:, :main]).astype(BF)
        common = mm(lowered_t, dproj_ref[:, main:])
        grad_common_ref[rows, : wide - 128] = common[:, : wide - 128].astype(BF)
        grad_common_ref[rows, wide - 128 :] = (common[:, wide - 128 :] + router_ref[rows, :]).astype(BF)
    aux_ref[...] = jnp.zeros_like(aux_ref)
    tiles = dtable_ref.shape[1] // 128

    def put(q, tile):
        aux_ref[q % ne, q // ne] = tile

    for q in range(tiles):
        put(q, dtable_ref[:, q * 128 : (q + 1) * 128])
    put(tiles + 1, ffn_ref[:8])
    put(tiles + 2, ffn_ref[8:])
    ring.finish(sum_ref)
    ffn = sum_ref[...]
    result_ref[...] = (value_ref[...] + ffn).astype(BF)
    square = jnp.sum(jnp.sum(ffn * ffn, 1, keepdims=True), 0, keepdims=True)
    tile_row = lax.broadcasted_iota(jnp.int32, (8, 128), 0)
    tile_lane = lax.broadcasted_iota(jnp.int32, (8, 128), 1)
    heads_tile = jnp.where(tile_row == 1, dhead_ref[...] * rate, dhead_ref[...])
    heads_tile = jnp.where(tile_row == 2, stat_ref[...], heads_tile)
    put(tiles, jnp.where((tile_row == 2) & (tile_lane == 2), square, heads_tile))
    for n in range(len(experts.items)):
        experts.close(n)
    experts.drain()
    rows_in.drain()


def mix_backward(
    proj,
    table,
    head_table,
    scanned,
    mixed,
    entries,
    out_local,
    resid_low,
    scales,
    out_part,
    expert_part,
    lowered,
    router_grad,
    resid,
    ffn_grad,
    stat_terms,
    ns,
    ne,
    hw,
    state2,
    heads,
    width,
    cid,
):
    whole = proj.shape[0]
    n = state2 // 2
    rows, model = resid_low.shape
    return pl.pallas_call(
        functools.partial(mix_backward_kernel, ns, ne, hw, state2, heads, width),
        out_shape=(
            jax.ShapeDtypeStruct((rows, model), BF),
            jax.ShapeDtypeStruct(expert_part.shape[1:], F32),
            jax.ShapeDtypeStruct(proj.shape, BF),
            jax.ShapeDtypeStruct((hw, model), BF),
            jax.ShapeDtypeStruct((model, 2 * hw), BF),
            jax.ShapeDtypeStruct((model, proj.shape[1] - 2 * hw), BF),
            jax.ShapeDtypeStruct((ne, aux_slots(hw, state2, ne), 8, 128), F32),
        ),
        in_specs=[ANY, VMEM, VMEM] + [ANY] * 4 + [VMEM] * 3 + [ANY] * 2 + [VMEM] * 4,
        out_specs=(VMEM,) * 7,
        scratch_shapes=[
            pltpu.VMEM((rows, model), F32),
            pltpu.VMEM((8, hw + state2), F32),
            pltpu.VMEM((8, 128), F32),
            pltpu.VMEM((n, hw), F32),
            pltpu.VMEM((8, hw + state2), F32),
            pltpu.VMEM((whole, hw), BF),
            pltpu.VMEM((ns, rows, model), BF),
            pltpu.VMEM((ns, 8, rows), F32),
        ]
        + Loads.scratch([proj, scanned, mixed, entries, out_local, lowered])
        + RingSum.scratch(ne, 2, rows, model)
        + SeqGather.scratch(ns)
        + BlockSum.scratch(ns, [expert_part.shape]),
        compiler_params=params(cid, 53),
        name="mix_backward",
    )(
        proj,
        table,
        head_table,
        scanned,
        mixed,
        entries,
        out_local,
        resid_low,
        scales,
        out_part,
        expert_part,
        lowered,
        router_grad,
        resid,
        ffn_grad,
        stat_terms,
    )


def rms_back(value, gain, grad):
    scale = lax.rsqrt(jnp.mean(value * value, -1, keepdims=True) + EPSILON)
    inside = gain * grad
    back = scale * inside - value * scale**3 * jnp.mean(value * inside, -1, keepdims=True)
    return back, jnp.sum(value * scale * grad, 0)


def swiglu_back(a, b, grad):
    sig = jax.nn.sigmoid(a)
    return grad * b * sig * (1 + a * (1 - sig)), grad * a * sig


def on_device(
    tokens,
    routes,
    out_grad,
    norm_mix,
    in_weight,
    step_weight,
    conv_weight,
    conv_bias,
    step_bias,
    decay_log,
    skip_gain,
    norm_gate,
    out_weight,
    norm_ffn,
    router_weight,
    shared_gate,
    shared_up,
    shared_down,
    expert_gate,
    expert_up,
    expert_down,
):
    ns, ne = lax.axis_size("seq"), lax.axis_size("exp")
    s, e = lax.axis_index("seq"), lax.axis_index("exp")
    total = ns * ne
    rows, columns = in_weight.shape
    model = tokens.shape[2]
    length = tokens.shape[1]
    whole = length * ns
    width, channels = conv_weight.shape
    gains = norm_gate.shape[0]
    inner = gains * total
    hw = inner // ns
    heads = step_bias.shape[0]
    local_heads = heads // ns
    state2 = columns - 2 * inner
    experts = router_weight.shape[1]
    local_experts = expert_gate.shape[0]
    place = s * ne + e

    small = jnp.concatenate([conv_weight.reshape(-1), conv_bias, norm_gate])
    small = jnp.pad(small, (0, 16 * rows - small.shape[0])).reshape(rows, 16)
    pack = jnp.concatenate(
        [step_weight, router_weight, norm_mix[:, None], norm_ffn[:, None], small], 1
    )
    at_small = heads + experts + 2
    pack = jnp.pad(pack, ((0, 0), (0, 128 - pack.shape[1])))
    hidden_rows = shared_down.shape[0]

    def by_owner(weight):
        split = weight.reshape(rows, ns, ne, hidden_rows)
        return jnp.transpose(split, (2, 0, 1, 3)).reshape(ne, rows, ns * hidden_rows)

    shared_two = jnp.concatenate([by_owner(shared_gate), by_owner(shared_up)], -1)
    in_blocks, common_blocks, token_blocks, out_local, shared_two, local_down = gather_in(
        in_weight, pack, tokens[0], out_weight, shared_two, shared_down, ns, ne, inner, 0
    )
    out_local = out_local.reshape(hw, model)
    shared_two = shared_two.reshape(model, 2 * ns * hidden_rows)
    local_gate, local_up = shared_two[:, : ns * hidden_rows], shared_two[:, ns * hidden_rows :]
    local_down = local_down.reshape(ns * hidden_rows, model)
    grad_low = out_grad[0]
    in_local = in_blocks.reshape(model, -1)
    in_common = common_blocks.reshape(model, -1)
    full_pack = in_common[:, state2:]
    full_router = full_pack[:, heads : heads + experts]
    full_norm_mix = full_pack[:, heads + experts].astype(F32)
    full_norm_ffn = full_pack[:, heads + experts + 1].astype(F32)
    full_small = full_pack[:, at_small : at_small + 16].reshape(total, 16 * rows).astype(F32)
    full_conv = full_small[:, : (width + 1) * channels].reshape(total, width + 1, channels)
    full_conv = jnp.swapaxes(full_conv, 0, 1).reshape(width + 1, total * channels)
    at_gain = (width + 1) * channels
    full_norm_gate = full_small[:, at_gain : at_gain + gains].reshape(inner)
    local_conv = jnp.concatenate(
        [lax.dynamic_slice_in_dim(full_conv, s * hw, hw, 1), full_conv[:, inner:]], 1
    )
    local_gain = lax.dynamic_slice_in_dim(full_norm_gate, s * hw, hw)
    at_head = s * local_heads
    local_bias = lax.dynamic_slice_in_dim(step_bias, at_head, local_heads)
    local_decay = lax.dynamic_slice_in_dim(decay_log, at_head, local_heads)
    local_skip = lax.dynamic_slice_in_dim(skip_gain, at_head, local_heads)

    table = jnp.concatenate(
        [
            local_conv,
            jnp.pad(
                jnp.stack([local_gain, jnp.repeat(local_skip, hw // local_heads)]),
                ((0, 6 - width - 1), (0, state2)),
            ),
        ],
        0,
    )
    head_table = jnp.pad(
        jnp.stack([local_bias, -jnp.exp(local_decay)]), ((0, 6), (0, 128 - local_heads))
    )

    token_rows = tokens[0].astype(F32)
    projected, lowered, scanned, mixed, entries, mixed_raw, squares, grad_all = mix_forward(
        token_blocks.reshape(whole, model),
        in_local,
        in_common,
        table,
        head_table,
        out_local,
        grad_low,
        ns,
        ne,
        hw,
        state2,
        local_heads,
        width,
        heads + experts,
        1,
    )
    scale_gate = lax.rsqrt(squares[0] / inner + EPSILON)
    mixer_out = mixed_raw * scale_gate[:, None]
    resid = token_rows + mixer_out
    scale_two = lax.rsqrt(jnp.mean(resid * resid, -1, keepdims=True) + EPSILON)
    ffn_in = (resid * scale_two * full_norm_ffn).astype(BF)

    stat_terms = jnp.stack([jnp.sum(resid * resid), jnp.sum(mixer_out * mixer_out)])
    logits = matmul_plain(ffn_in, full_router)
    named = jnp.any(
        routes[0][:, :, None] == jnp.arange(experts, dtype=jnp.int32)[None, None, :], 1
    )
    top = jnp.max(jnp.where(named, logits, -jnp.inf), -1, keepdims=True)
    raised = jnp.where(named, jnp.exp(jnp.where(named, logits - top, 0.0)), 0.0)
    gates = (raised / jnp.sum(raised, -1, keepdims=True)).T

    gates_out = jnp.pad(
        gates.reshape(ne, local_experts, length), ((0, 0), (0, 8 - local_experts), (0, 0))
    )
    back_sum, gate_grads, out_part, grad_gate, grad_up, grad_down, shared_part, grad_shared_down = (
        experts_both_ways(
            ffn_in,
            gates_out,
            grad_all,
            expert_gate,
            expert_up,
            expert_down,
            shared_two,
            local_down,
            ns,
            ne,
            2,
        )
    )
    gate_grads = gate_grads[:, :local_experts].reshape(experts, length)
    picked_grad = gates * (gate_grads - jnp.sum(gates * gate_grads, 0, keepdims=True))
    logit_grad = picked_grad.T.astype(BF)
    grad_router = matmul_rows(ffn_in, logit_grad)
    ffn_in_grad = matmul_cols(logit_grad, full_router) + back_sum
    resid_norm_grad, grad_norm_ffn = rms_back(resid, full_norm_ffn, ffn_in_grad)
    resid_grad = grad_low.astype(F32) + resid_norm_grad
    resid_low = resid_grad.astype(BF)
    inside = jnp.sum(resid_low.astype(F32) * mixer_out, -1) / (scale_gate * inner)
    scales = jnp.concatenate(
        [scale_gate[None], inside[None], jnp.zeros((6, length), F32)], 0
    )

    result, grad_gate, projected_grad, grad_out, in_grad, common_grad, aux = mix_backward(
        projected,
        table,
        head_table,
        scanned,
        mixed,
        entries,
        out_local,
        resid_low,
        scales,
        out_part,
        grad_gate,
        lowered,
        jnp.pad(grad_router, ((0, 0), (heads, 128 - heads - experts))),
        resid,
        jnp.pad(grad_norm_ffn, (0, 16 * 128 - model)).reshape(16, 128),
        jnp.broadcast_to(jnp.pad(stat_terms, (0, 126))[None], (8, 128)),
        ns,
        ne,
        hw,
        state2,
        local_heads,
        width,
        4,
    )
    (
        grad_in,
        grad_pack,
        grad_out,
        tokens_grad,
        sums,
        shared_part,
        grad_up,
        grad_down,
        grad_shared_down,
    ) = sum_weights(
        in_grad.reshape(ns, ne, rows, -1),
        common_grad.reshape(ns, 1, ne, rows, -1),
        grad_out.reshape(ne, hw // ne, model),
        projected_grad,
        in_local,
        in_common,
        tokens[0],
        resid_grad,
        jnp.broadcast_to(full_norm_mix[None], (8, model)),
        aux,
        [
            grad_up,
            grad_down,
            grad_shared_down.reshape(ns, 1, hidden_rows, model),
            shared_part.reshape(ns, 1, ne, rows, -1),
        ],
        128,
        ns,
        ne,
        6,
    )
    grad_step = grad_pack[:, :heads]
    grad_router = grad_pack[:, heads : heads + experts]
    tiles = (hw + state2) // 128
    sums = jnp.swapaxes(sums, 1, 2).reshape(ns, -1, 8, 128)
    table_all = jnp.swapaxes(sums[:, :tiles], 1, 2).reshape(ns, 8, hw + state2)
    heads_all = sums[:, tiles]
    norm_sums = jnp.sum(sums[:, tiles + 1 : tiles + 5], 0).reshape(2, -1)[:, :model]
    grad_norm_ffn, grad_norm_mix = norm_sums[0], norm_sums[1]
    gain_all = table_all[:, width + 1, :hw]
    skip_all = jnp.sum(table_all[:, width + 2, :hw].reshape(heads, -1), -1)
    table_all = table_all[:, : width + 1]
    conv_all = jnp.concatenate(
        [
            jnp.swapaxes(table_all[:, :, :hw], 0, 1).reshape(width + 1, inner),
            jnp.sum(table_all[:, :, hw:], 0),
        ],
        1,
    )
    conv_grads = lax.dynamic_slice_in_dim(conv_all, place * channels, channels, 1)
    shared_part = shared_part.astype(F32).reshape(ne, rows, 2, ns, hidden_rows)
    shared_grads = jnp.transpose(shared_part, (2, 1, 3, 0, 4)).reshape(2, rows, total * hidden_rows)
    return (
        result[None],
        tokens_grad[None],
        lax.dynamic_slice_in_dim(grad_norm_mix, place * rows, rows),
        grad_in,
        grad_step,
        conv_grads[:width],
        conv_grads[width],
        heads_all[:, 0, :local_heads].reshape(heads),
        heads_all[:, 1, :local_heads].reshape(heads),
        skip_all,
        lax.dynamic_slice_in_dim(gain_all.reshape(inner), place * gains, gains),
        grad_out,
        lax.dynamic_slice_in_dim(grad_norm_ffn, place * rows, rows),
        grad_router,
        shared_grads[0],
        shared_grads[1],
        grad_shared_down[0],
        grad_gate,
        grad_up,
        grad_down,
        jnp.sum(heads_all[:, 2, :3], 0) / (total * length * model),
    )


def solution(mesh):
    both = ("seq", "exp")
    return jax.shard_map(
        on_device,
        mesh=mesh,
        in_specs=(
            P("exp", "seq", None),
            P("exp", "seq", None),
            P("exp", "seq", None),
            P(both),
            P(both, None),
            P(both, None),
            P(None, both),
            P(both),
            P(),
            P(),
            P(),
            P(both),
            P(both, None),
            P(both),
            P(both, None),
            P(both, None),
            P(both, None),
            P(both, None),
            P("exp", None, None),
            P("exp", None, None),
            P("exp", None, None),
        ),
        out_specs=(
            P("exp", "seq", None),
            P("exp", "seq", None),
            P(both),
            P(both, None),
            P(both, None),
            P(None, both),
            P(both),
            P(),
            P(),
            P(),
            P(both),
            P(both, None),
            P(both),
            P(both, None),
            P(both, None),
            P(both, None),
            P(both, None),
            P("exp", "seq", None),
            P("exp", "seq", None),
            P("exp", None, "seq"),
            P(),
        ),
        check_vma=False,
    )
```

```python
import functools

import jax
import jax.numpy as jnp
from jax import lax
from jax.experimental import pallas as pl
from jax.experimental.pallas import tpu as pltpu
from jax.sharding import PartitionSpec as P

GROUP = 128
EPSILON = 1e-05
PRECISE = lax.Precision.HIGHEST
MESH = pl.DeviceIdType.MESH
BF = jnp.bfloat16
F32 = jnp.float32
ANY = pl.BlockSpec(memory_space=pl.ANY)
VMEM = pl.BlockSpec(memory_space=pltpu.VMEM)
DMA = pltpu.SemaphoreType.DMA


def ring_place(e, n):
    odd = e % 2
    return (1 - odd) * (e // 2) + odd * (n - 1 - e // 2)


def ring_index(p, n):
    back = p // (n // 2)
    return (1 - back) * (2 * p) + back * (2 * (n - 1 - p) + 1)


def ring_sides(e, n):
    p = ring_place(e, n)
    return p, ring_index((p + 1) % n, n), ring_index((p + n - 1) % n, n)


def greet(partners):
    barrier = pltpu.get_barrier_semaphore()
    for partner in partners:
        pl.semaphore_signal(barrier, inc=1, device_id=partner, device_id_type=MESH)
    pl.semaphore_wait(barrier, len(partners))


def remote(src, dst, send, recv, device):
    copy = pltpu.make_async_remote_copy(
        src_ref=src,
        dst_ref=dst,
        send_sem=send,
        recv_sem=recv,
        device_id=device,
        device_id_type=MESH,
    )
    copy.start()
    return copy


def params(cid, mib=48):
    return pltpu.CompilerParams(
        collective_id=cid, has_side_effects=True, vmem_limit_bytes=mib << 20
    )


class Loads:
    def __init__(self, sources, held, sems):
        self.copies = [
            pltpu.make_async_copy(src, dst, sems.at[i])
            for i, (src, dst) in enumerate(zip(sources, held))
        ]

    @staticmethod
    def scratch(arrays):
        return [pltpu.VMEM(v.shape, v.dtype) for v in arrays] + [DMA((len(arrays),))]

    def begin(self):
        for copy in self.copies:
            copy.start()

    def wait(self, *which):
        for i in which:
            self.copies[i].wait()


def tile_rows(rows, most=16):
    return most if rows % most == 0 else rows


def gather_in_kernel(
    ns,
    ne,
    hw,
    inner,
    in_ref,
    pack_ref,
    tok_ref,
    out_ref,
    two_ref,
    down_ref,
    w_ref,
    c_ref,
    x_ref,
    o_ref,
    shared_ref,
    sd_ref,
    lsem,
    ssem0,
    rsem0,
    ssem,
    rsem,
    sa,
    ra,
    sb,
    rb,
    sc,
    rc,
):
    s, e = lax.axis_index("seq"), lax.axis_index("exp")
    p, right, left = ring_sides(e, ne)
    width = in_ref.shape[1] - 2 * inner
    half = out_ref.shape[1] // 2
    parts = (
        (lambda to: in_ref.at[:, pl.ds(pl.multiple_of(to * hw, 128), hw)], 0),
        (lambda to: in_ref.at[:, pl.ds(pl.multiple_of(inner + to * hw, 128), hw)], hw),
    )
    greet([((s + t) % ns, e) for t in range(1, ns)] + [(s, (e + t) % ne) for t in range(1, ne)])
    own = []
    for i, (piece, start) in enumerate(parts):
        own.append(
            pltpu.make_async_copy(piece(s), w_ref.at[s, e, :, pl.ds(start, hw)], lsem.at[i])
        )
    own.append(
        pltpu.make_async_copy(
            in_ref.at[:, pl.ds(2 * inner, width)], c_ref.at[s, e, :, pl.ds(0, width)], lsem.at[2]
        )
    )
    own.append(
        pltpu.make_async_copy(
            pack_ref, c_ref.at[s, e, :, pl.ds(width, pack_ref.shape[1])], lsem.at[3]
        )
    )
    own.append(pltpu.make_async_copy(out_ref, o_ref.at[e], lsem.at[4]))
    own.append(pltpu.make_async_copy(two_ref.at[e], shared_ref.at[s, e], lsem.at[5]))
    own.append(pltpu.make_async_copy(tok_ref, x_ref.at[s], lsem.at[6]))
    own.append(pltpu.make_async_copy(down_ref, sd_ref.at[s], lsem.at[7]))
    for copy in own:
        copy.start()
    first = {}
    for t in range(1, ns):
        to = (s + t) % ns
        for i, (piece, start) in enumerate(parts):
            first[t, i] = remote(
                piece(to),
                w_ref.at[s, e, :, pl.ds(start, hw)],
                ssem0.at[t - 1, i],
                rsem0.at[t - 1, i],
                (to, e),
            )
    for copy in own:
        copy.wait()
    sent = {}
    across = {}
    along = {}
    common = {}

    def place_of(k, way):
        return ring_index((p - k + ne) % ne if way == 0 else (p + k) % ne, ne)

    def share(k):
        block = c_ref.at[s, place_of(k, 1)]
        for t in range(1, ns):
            common[k, t] = remote(
                block, block, sc.at[k, t - 1], rc.at[k, t - 1], ((s + t) % ns, e)
            )

    for k in range(ne - 1):
        for t in [0, ns, ns + 1, ns + 2] + list(range(1, ns)):
            way = 1 if t == ns else (t - ns - 1 if t > ns else t % 2)
            to = (s, right if way == 0 else left)
            slot = place_of(k, way)
            if k > 0:
                sent[k - 1, t].wait_recv()
            elif 0 < t < ns:
                for i in range(len(parts)):
                    first[t, i].wait_recv()
            if t < ns:
                block = w_ref.at[(s + ns - t) % ns, slot]
            elif t == ns:
                block = c_ref.at[s, slot]
            else:
                block = o_ref.at[slot, :, pl.ds(way * half, half)]
            sent[k, t] = remote(block, block, ssem.at[k, t], rsem.at[k, t], to)
            if t == ns:
                share(k)
        if k == 0:
            for t in range(1, ns):
                to = ((s + t) % ns, e)
                first[t, 2] = remote(
                    tok_ref, x_ref.at[s], ssem0.at[t - 1, 2], rsem0.at[t - 1, 2], to
                )
                first[t, 3] = remote(
                    down_ref, sd_ref.at[s], ssem0.at[t - 1, 3], rsem0.at[t - 1, 3], to
                )
            for t in range(1, ne):
                to = (e + t) % ne
                across[t] = remote(
                    two_ref.at[to], shared_ref.at[s, e], sa.at[t - 1], ra.at[t - 1], (s, to)
                )
        if k == 2:
            for t in range(1, ne):
                across[t].wait_recv()
            for t in range(1, ns):
                along[t] = remote(
                    shared_ref.at[s], shared_ref.at[s], sb.at[t - 1], rb.at[t - 1], ((s + t) % ns, e)
                )
    sent[ne - 2, ns].wait_recv()
    share(ne - 1)
    for t in range(ns + 3):
        if t != ns:
            sent[ne - 2, t].wait_recv()
    for t in range(1, ns):
        first[t, 2].wait_recv()
        first[t, 3].wait_recv()
        along[t].wait_recv()
    for copy in common.values():
        copy.wait_recv()
    for group in (first, sent, across, along, common):
        for copy in group.values():
            copy.wait_send()


def gather_in(in_weight, pack, tokens, out_weight, shared_two, shared_down, ns, ne, inner, cid):
    rows, columns = in_weight.shape
    hw = inner // ns
    wide = columns - 2 * inner + pack.shape[1]
    return pl.pallas_call(
        functools.partial(gather_in_kernel, ns, ne, hw, inner),
        out_shape=(
            jax.ShapeDtypeStruct((ns, ne, rows, 2 * hw), BF),
            jax.ShapeDtypeStruct((ns, ne, rows, wide), BF),
            jax.ShapeDtypeStruct((ns,) + tokens.shape, BF),
            jax.ShapeDtypeStruct((ne,) + out_weight.shape, BF),
            jax.ShapeDtypeStruct((ns,) + shared_two.shape, BF),
            jax.ShapeDtypeStruct((ns,) + shared_down.shape, BF),
        ),
        in_specs=[ANY] * 6,
        out_specs=(ANY,) * 6,
        scratch_shapes=[
            DMA((8,)),
            DMA((ns - 1, 4)),
            DMA((ns - 1, 4)),
            DMA((ne - 1, ns + 3)),
            DMA((ne - 1, ns + 3)),
            DMA((ne - 1,)),
            DMA((ne - 1,)),
            DMA((ns - 1,)),
            DMA((ns - 1,)),
            DMA((ne, ns - 1)),
            DMA((ne, ns - 1)),
        ],
        compiler_params=params(cid, 8),
        name="gather_in",
    )(in_weight, pack, tokens, out_weight, shared_two, shared_down)


class SeqSum:
    def __init__(self, ns, subs, part, aux, one, two, aux_in, s1, r1, s2, r2, sa, ra):
        self.s, self.e = lax.axis_index("seq"), lax.axis_index("exp")
        self.ns, self.ny, self.subs = ns, ns // 2, subs
        self.y, self.c = self.s // 2, self.s % 2
        self.part, self.aux, self.one, self.two, self.aux_in = part, aux, one, two, aux_in
        self.sems = (s1, r1, s2, r2, sa, ra)
        self.step = part.shape[1] // subs
        self.tile = tile_rows(self.step)
        self.first, self.second, self.extra = {}, {}, []

    @staticmethod
    def scratch(ns, subs, rows, width, aux_shape):
        ny = ns // 2
        return [
            pltpu.VMEM((ny, rows, width), BF),
            pltpu.VMEM((max(ny - 1, 1), rows, width), BF),
            pltpu.VMEM((ns - 1,) + aux_shape, F32),
            DMA((ny, subs)),
            DMA((ny, subs)),
            DMA((max(ny - 1, 1), subs)),
            DMA((max(ny - 1, 1), subs)),
            DMA((ns - 1,)),
            DMA((ns - 1,)),
        ]

    def rows(self, u):
        return pl.ds(u * self.step, self.step)

    def send_aux(self):
        s1, r1, s2, r2, sa, ra = self.sems
        for t in range(1, self.ns):
            to = (self.s + t) % self.ns
            self.extra.append(
                remote(
                    self.aux.at[to], self.aux_in.at[t - 1], sa.at[t - 1], ra.at[t - 1], (to, self.e)
                )
            )

    def order(self):
        return list(range(1, self.ny)) + [0]

    def far(self, j):
        return 2 * ((self.y + j) % self.ny) + 1 - self.c

    def near(self, j):
        return 2 * ((self.y + j) % self.ny) + self.c

    def send(self, j):
        s1, r1, s2, r2, sa, ra = self.sems
        mate = (2 * self.y + 1 - self.c, self.e)
        for u in range(self.subs):
            self.first[j, u] = remote(
                self.part.at[self.far(j), self.rows(u)],
                self.one.at[j, self.rows(u)],
                s1.at[j, u],
                r1.at[j, u],
                mate,
            )

    def begin(self, fill):
        self.send_aux()
        for j in self.order():
            fill(self.far(j))
            self.send(j)
        for j in self.order():
            fill(self.near(j))

    def join(self, j, u):
        s1, r1, s2, r2, sa, ra = self.sems
        to = self.near(j)
        self.first[j, u].wait_recv()

        def add(i, carry):
            r = pl.ds(pl.multiple_of(u * self.step + i * self.tile, self.tile), self.tile)
            total = self.one[j, r, :].astype(F32) + self.part[to, r, :].astype(F32)
            self.one[j, r, :] = total.astype(BF)
            return carry

        lax.fori_loop(0, self.step // self.tile, add, 0)
        self.second[j, u] = remote(
            self.one.at[j, self.rows(u)],
            self.two.at[j - 1, self.rows(u)],
            s2.at[j - 1, u],
            r2.at[j - 1, u],
            (to, self.e),
        )

    def middle(self):
        for j in range(1, self.ny):
            for u in range(self.subs):
                self.join(j, u)

    def close(self, u, out):
        self.first[0, u].wait_recv()
        for j in range(1, self.ny):
            self.second[j, u].wait_recv()

        def add(i, carry):
            r = pl.ds(pl.multiple_of(u * self.step + i * self.tile, self.tile), self.tile)
            total = self.one[0, r, :].astype(F32) + self.part[self.s, r, :].astype(F32)
            for j in range(1, self.ny):
                total = total + self.two[j - 1, r, :].astype(F32)
            out[r, :] = total
            return carry

        lax.fori_loop(0, self.step // self.tile, add, 0)

    def finish(self, out, aux_out):
        for u in range(self.subs):
            self.close(u, out)
        total = self.aux[self.s]
        for t in range(1, self.ns):
            self.extra[t - 1].wait_recv()
            total = total + self.aux_in[t - 1]
        aux_out[...] = total

    def drain(self):
        for copy in list(self.first.values()) + list(self.second.values()) + self.extra:
            copy.wait_send()


class BlockSum:
    def __init__(self, ns, sources, outs, scratch):
        self.s, self.e = lax.axis_index("seq"), lax.axis_index("exp")
        self.ns, self.ny = ns, ns // 2
        self.y, self.c = self.s // 2, self.s % 2
        self.sources, self.outs = sources, outs
        self.items = [(m, i) for m, src in enumerate(sources) for i in range(src.shape[1])]
        count = len(sources)
        self.held, self.one, self.two = (
            scratch[:count],
            scratch[count : 2 * count],
            scratch[2 * count : 3 * count],
        )
        self.lsem, self.s1, self.r1, self.s2, self.r2 = scratch[3 * count :]
        self.loads = [
            pltpu.make_async_copy(src, held, self.lsem.at[m])
            for m, (src, held) in enumerate(zip(self.sources, self.held))
        ]
        self.first, self.second = {}, {}

    @staticmethod
    def scratch(ns, shapes):
        ny = ns // 2
        items = sum(shape[1] for shape in shapes)
        return (
            [pltpu.VMEM(shape, BF) for shape in shapes]
            + [pltpu.VMEM((ny,) + shape[1:], BF) for shape in shapes]
            + [pltpu.VMEM((max(ny - 1, 1),) + shape[1:], BF) for shape in shapes]
            + [
                DMA((len(shapes),)),
                DMA((ny, items)),
                DMA((ny, items)),
                DMA((max(ny - 1, 1), items)),
                DMA((max(ny - 1, 1), items)),
            ]
        )

    def load(self):
        for copy in self.loads:
            copy.start()

    def begin(self):
        mate = (2 * self.y + 1 - self.c, self.e)
        for copy in self.loads:
            copy.wait()
        for j in list(range(1, self.ny)) + [0]:
            block = 2 * ((self.y + j) % self.ny) + 1 - self.c
            for n, (m, i) in enumerate(self.items):
                self.first[j, n] = remote(
                    self.held[m].at[block, i],
                    self.one[m].at[j, i],
                    self.s1.at[j, n],
                    self.r1.at[j, n],
                    mate,
                )

    def tiles(self, shape, body):
        if len(shape) == 3:
            lax.fori_loop(0, shape[0], lambda i, carry: body((i,)) or carry, 0)
        else:
            size = 32 if shape[0] % 32 == 0 else shape[0]
            lax.fori_loop(
                0,
                shape[0] // size,
                lambda i, carry: body((pl.ds(pl.multiple_of(i * size, size), size),)) or carry,
                0,
            )

    def join(self, j, n):
        m, i = self.items[n]
        to = 2 * ((self.y + j) % self.ny) + self.c
        self.first[j, n].wait_recv()
        one, held = self.one[m], self.held[m]

        def add(at):
            total = one[(j, i) + at].astype(F32) + held[(to, i) + at].astype(F32)
            one[(j, i) + at] = total.astype(BF)

        self.tiles(one.shape[2:], add)
        self.second[j, n] = remote(
            one.at[j, i],
            self.two[m].at[j - 1, i],
            self.s2.at[j - 1, n],
            self.r2.at[j - 1, n],
            (to, self.e),
        )

    def close(self, n):
        m, i = self.items[n]
        self.first[0, n].wait_recv()
        for j in range(1, self.ny):
            self.second[j, n].wait_recv()
        one, held, two, out = self.one[m], self.held[m], self.two[m], self.outs[m]

        def add(at):
            total = one[(0, i) + at].astype(F32) + held[(self.s, i) + at].astype(F32)
            for j in range(1, self.ny):
                total = total + two[(j - 1, i) + at].astype(F32)
            out[(i,) + at] = total

        self.tiles(one.shape[2:], add)

    def drain(self):
        for copy in list(self.first.values()) + list(self.second.values()):
            copy.wait_send()


class RingGather:
    def __init__(self, ne, v, out, lsem, ssem, rsem):
        self.s, self.e = lax.axis_index("seq"), lax.axis_index("exp")
        self.ne, self.v, self.out = ne, v, out
        self.p, self.right, self.left = ring_sides(self.e, ne)
        self.ssem, self.rsem = ssem, rsem
        self.subs = ssem.shape[2]
        self.step_rows = v.shape[0] // (2 * self.subs)
        self.own = pltpu.make_async_copy(v, out.at[self.e], lsem)

    @staticmethod
    def scratch(ne, subs):
        return [DMA, DMA((ne - 1, 2, subs)), DMA((ne - 1, 2, subs))]

    def copy(self, k, way, u, src=None):
        place = (self.p - k + self.ne) % self.ne if way == 0 else (self.p + k) % self.ne
        slot = ring_index(place, self.ne)
        rows = pl.ds((way * self.subs + u) * self.step_rows, self.step_rows)
        block = self.out.at[slot, rows]
        return pltpu.make_async_remote_copy(
            src_ref=block if src is None else src.at[rows],
            dst_ref=block,
            send_sem=self.ssem.at[k, way, u],
            recv_sem=self.rsem.at[k, way, u],
            device_id=(self.s, self.right if way == 0 else self.left),
            device_id_type=MESH,
        )

    def begin(self):
        self.own.start()
        for u in range(self.subs):
            for way in range(2):
                self.copy(0, way, u, self.v).start()

    def step(self, k):
        for u in range(self.subs):
            for way in range(2):
                self.copy(k - 1, way, u).wait_recv()
                self.copy(k, way, u).start()

    def forward(self, k):
        for u in range(self.subs):
            for way in range(2):
                self.copy(k, way, u).start()

    def arrived(self, k):
        for u in range(self.subs):
            for way in range(2):
                self.copy(k, way, u).wait_recv()

    def drain(self):
        for k in range(self.ne - 1):
            for u in range(self.subs):
                for way in range(2):
                    self.copy(k, way, u).wait_send()

    def finish(self):
        self.arrived(self.ne - 2)
        self.drain()
        self.own.wait()


class RingSum:
    def __init__(self, ne, part, acc, ssem, rsem):
        self.s, self.e = lax.axis_index("seq"), lax.axis_index("exp")
        self.ne, self.part, self.acc = ne, part, acc
        self.p, self.right, self.left = ring_sides(self.e, ne)
        self.ssem, self.rsem = ssem, rsem
        self.subs = ssem.shape[2]
        self.size = part.shape[1] // (2 * self.subs)
        self.tile = tile_rows(self.size)

    @staticmethod
    def scratch(ne, subs, rows, width):
        return [
            pltpu.VMEM((ne - 1, rows, width), BF),
            DMA((ne - 1, 2, subs)),
            DMA((ne - 1, 2, subs)),
        ]

    def slot(self, k, way):
        place = (self.p - 1 - k + 2 * self.ne) % self.ne if way == 0 else (self.p + 1 + k) % self.ne
        return ring_index(place, self.ne)

    def copy(self, k, way, u, src=None):
        rows = pl.ds((way * self.subs + u) * self.size, self.size)
        return pltpu.make_async_remote_copy(
            src_ref=self.acc.at[k, rows] if src is None else src.at[rows],
            dst_ref=self.acc.at[k, rows],
            send_sem=self.ssem.at[k, way, u],
            recv_sem=self.rsem.at[k, way, u],
            device_id=(self.s, self.right if way == 0 else self.left),
            device_id_type=MESH,
        )

    def add(self, k, way, u, out):
        base = (way * self.subs + u) * self.size
        slot = self.slot(k, way)

        def join(i, carry):
            r = pl.ds(pl.multiple_of(base + i * self.tile, self.tile), self.tile)
            total = self.acc[k - 1, r, :].astype(F32) + self.part[slot, r, :].astype(F32)
            if out is None:
                self.acc[k - 1, r, :] = total.astype(BF)
            else:
                out[r, :] = total
            return carry

        lax.fori_loop(0, self.size // self.tile, join, 0)

    def begin(self):
        for u in range(self.subs):
            for way in range(2):
                self.copy(0, way, u, self.part.at[self.slot(0, way)]).start()

    def step(self, k):
        for u in range(self.subs):
            for way in range(2):
                self.copy(k - 1, way, u).wait_recv()
                self.add(k, way, u, None)
                rows = pl.ds((way * self.subs + u) * self.size, self.size)
                pltpu.make_async_remote_copy(
                    src_ref=self.acc.at[k - 1, rows],
                    dst_ref=self.acc.at[k, rows],
                    send_sem=self.ssem.at[k, way, u],
                    recv_sem=self.rsem.at[k, way, u],
                    device_id=(self.s, self.right if way == 0 else self.left),
                    device_id_type=MESH,
                ).start()

    def finish(self, out):
        k = self.ne - 1
        for u in range(self.subs):
            for way in range(2):
                self.copy(k - 1, way, u).wait_recv()
                self.add(k, way, u, out)
        for k in range(self.ne - 1):
            for u in range(self.subs):
                for way in range(2):
                    self.copy(k, way, u).wait_send()


class Exchange:
    def __init__(self, ne, src, dst, lsem, ssem, rsem, pick=None, spread=False):
        s, e = lax.axis_index("seq"), lax.axis_index("exp")
        if pick is None:
            pick = lambda ref, at: ref.at[at]
        give = (lambda ref, at: ref) if spread else pick
        self.own = pltpu.make_async_copy(give(src, e), pick(dst, e), lsem)
        self.copies = []
        for t in range(1, ne):
            to = (e + t) % ne
            self.copies.append(
                pltpu.make_async_remote_copy(
                    src_ref=give(src, to),
                    dst_ref=pick(dst, e),
                    send_sem=ssem.at[t - 1],
                    recv_sem=rsem.at[t - 1],
                    device_id=(s, to),
                    device_id_type=MESH,
                )
            )

    @staticmethod
    def scratch(ne):
        return [DMA, DMA((ne - 1,)), DMA((ne - 1,))]

    def begin(self):
        self.own.start()
        for copy in self.copies:
            copy.start()

    def arrived(self):
        self.own.wait()
        for copy in self.copies:
            copy.wait_recv()

    def drain(self):
        for copy in self.copies:
            copy.wait_send()


def experts_kernel(
    ne,
    count,
    ffn_ref,
    gate_ref,
    grad_hbm,
    eg_hbm,
    eu_hbm,
    ed_hbm,
    two_hbm,
    sd_hbm,
    back_ref,
    gate_back,
    out_ref,
    dg_ref,
    du_ref,
    dd_ref,
    ds_ref,
    dsd_ref,
    x_ref,
    gates,
    hid_ref,
    da_ref,
    db_ref,
    part_ref,
    gate_part,
    stage_g,
    stage_u,
    stage_d,
    stage_s,
    stage_sem,
    out_stage,
    out_sem,
    *scratch,
):
    s, e = lax.axis_index("seq"), lax.axis_index("exp")
    length, model = ffn_ref.shape
    half = length // 2
    sources = (eg_hbm, eu_hbm, grad_hbm, ed_hbm, two_hbm, sd_hbm)
    eg_ref, eu_ref, grad_ref, ed_ref, two_ref, sd_ref = scratch[12:18]
    loads = Loads(sources, scratch[12:18], scratch[18])
    loads.begin()
    width = eg_ref.shape[2]
    narrow = sd_ref.shape[0]
    tile_width = min(width, 256)
    greet([(s, (e + t) % ne) for t in range(1, ne)])
    ring = RingGather(ne, ffn_ref, x_ref, *scratch[:3])
    there = Exchange(ne, gate_ref, gates, *scratch[3:6])
    back = Exchange(ne, gate_part, gate_back, *scratch[6:9])
    total = RingSum(ne, part_ref, *scratch[9:12])
    ring.begin()
    there.begin()
    gate_part[...] = jnp.zeros_like(gate_part)
    ring.own.wait()
    there.own.wait()
    lane = lax.broadcasted_iota(jnp.int32, (8, length), 1)
    wide_lane = lax.broadcasted_iota(jnp.int32, (2 * length, 128), 1)

    def quarters(i):
        found = []
        for k in (2 * i, 2 * i + 1):
            found.append((ring_index((ring.p - k + ne) % ne, ne), 0))
            found.append((ring_index((ring.p + k) % ne, ne), half))
        return found

    def out_copies(i):
        slot = i % 2
        return [
            pltpu.make_async_copy(
                out_stage.at[slot, pl.ds(n * half, half)],
                out_ref.at[block, pl.ds(first, half)],
                out_sem.at[slot, n],
            )
            for n, (block, first) in enumerate(quarters(i))
        ]

    def rows_of(ref, places, cols):
        return jnp.concatenate(
            [ref[block, first : first + half, cols] for block, first in places], 0
        )

    def store(ref, places, cols, value):
        for n, (block, first) in enumerate(places):
            ref[block, first : first + half, cols] = value[n * half : (n + 1) * half]

    def compute(i):
        places = quarters(i)
        every = slice(0, model)
        x = rows_of(x_ref, places, every)
        g = rows_of(grad_ref, places, every)
        table = jnp.concatenate(
            [
                jnp.where(lane < half, gates[places[n][0]], gates[places[n + 1][0]]).T
                for n in (0, 2)
            ],
            0,
        )
        slots = jnp.zeros((2 * length, 128), F32)
        for j in range(count + 1):
            size = width if j < count else narrow
            column = table[:, j : j + 1] if j < count else None
            for f in range(0, size, tile_width):
                wide = min(tile_width, size - f)
                if j < count:
                    a = mm(x, eg_ref[j, :, f : f + wide])
                    b = mm(x, eu_ref[j, :, f : f + wide])
                    h = mm_t(g, ed_ref[j, f : f + wide, :])
                else:
                    both = mm(x, two_ref[...])
                    a, b = both[:, :narrow], both[:, narrow:]
                    h = mm_t(g, sd_ref[...])
                sig = sigmoid(a)
                silu = a * sig
                act = silu * b
                if j < count:
                    found = jnp.sum(act * h, 1, keepdims=True)
                    slots = slots + jnp.where(wide_lane == j, found, 0.0)
                    act = act * column
                    h = h * column
                cols = slice(j * width + f, j * width + f + wide)
                store(hid_ref, places, cols, act.astype(BF))
                store(da_ref, places, cols, (h * b * (sig + silu * (1 - sig))).astype(BF))
                store(db_ref, places, cols, (h * silu).astype(BF))
        found = slots.T[:8]
        for n in (0, 2):
            part = found[:, (n // 2) * length : (n // 2 + 1) * length]
            one, two = places[n][0], places[n + 1][0]
            gate_part[one] = jnp.where(lane < half, part, gate_part[one])
            gate_part[two] = jnp.where(lane >= half, part, gate_part[two])

    def compute_back(i):
        places = quarters(i)

        @pl.when(i >= 2)
        def _():
            for copy in out_copies(i - 2):
                copy.wait()

        last = slice(count * width, count * width + narrow)
        for d in range(0, model, 256):
            cols = slice(d, d + 256)
            out = mm(rows_of(hid_ref, places, last), sd_ref[:, cols])
            row = mm_t(rows_of(da_ref, places, last), two_ref[cols, :narrow])
            row = row + mm_t(rows_of(db_ref, places, last), two_ref[cols, narrow:])
            for j in range(count):
                mine = slice(j * width, (j + 1) * width)
                out = out + mm(rows_of(hid_ref, places, mine), ed_ref[j, :, cols])
                row = row + mm_t(rows_of(da_ref, places, mine), eg_ref[j, cols, :])
                row = row + mm_t(rows_of(db_ref, places, mine), eu_ref[j, cols, :])
            out_stage[i % 2, :, cols] = out.astype(BF)
            store(part_ref, places, cols, row.astype(BF))
        for copy in out_copies(i):
            copy.start()

    def arrive(i, carry):
        ring.arrived(2 * i)

        @pl.when(2 * i + 1 < ne - 1)
        def _():
            ring.forward(2 * i + 1)

        @pl.when(i == 0)
        def _():
            loads.wait(*range(6))
            for copy in there.copies:
                copy.wait_recv()

        @pl.when(i == ne // 2 - 1)
        def _():
            total.begin()

        compute(i)

        @pl.when(2 * i + 1 < ne - 1)
        def _():
            ring.arrived(2 * i + 1)
            ring.forward(2 * i + 2)

        @pl.when(i == ne // 2 - 1)
        def _():
            total.step(1)

        compute_back(i)
        return carry

    lax.fori_loop(0, ne // 2, arrive, 0)
    ring.drain()
    back.begin()
    part_rows = stage_g.shape[3]
    per = stage_g.shape[1]
    tile = per * part_rows
    tiles = model // tile
    every = ne * length

    def stage_copies(i):
        slot = i % 2
        blocks = pl.ds(i * per, per)
        return [
            pltpu.make_async_copy(stage_g.at[slot], dg_ref.at[blocks], stage_sem.at[slot, 0]),
            pltpu.make_async_copy(stage_u.at[slot], du_ref.at[blocks], stage_sem.at[slot, 3]),
            pltpu.make_async_copy(stage_d.at[slot], dd_ref.at[blocks], stage_sem.at[slot, 1]),
            pltpu.make_async_copy(stage_s.at[slot], ds_ref.at[i], stage_sem.at[slot, 2]),
        ]

    def weights(i):
        @pl.when(i >= 2)
        def _():
            for copy in stage_copies(i - 2):
                copy.wait()

        cols = pl.ds(pl.multiple_of(i * tile, 128), tile)
        slot = i % 2
        x_t = x_ref[:, :, cols].reshape(every, tile).T
        g_t = grad_ref[:, :, cols].reshape(every, tile).T
        for j in range(count):
            at = slice(j * width, (j + 1) * width)
            gate = mm(x_t, da_ref[:, :, at].reshape(every, width)).astype(BF)
            up = mm(x_t, db_ref[:, :, at].reshape(every, width)).astype(BF)
            down = mm(g_t, hid_ref[:, :, at].reshape(every, width)).T.astype(BF)
            for q in range(per):
                rows = slice(q * part_rows, (q + 1) * part_rows)
                stage_g[slot, q, j] = gate[rows]
                stage_u[slot, q, j] = up[rows]
                stage_d[slot, q, j] = down[:, rows]
        at = slice(count * width, count * width + narrow)
        both = jnp.concatenate(
            [da_ref[:, :, at].reshape(every, narrow), db_ref[:, :, at].reshape(every, narrow)], 1
        )
        stage_s[slot] = mm(x_t, both).astype(BF)
        for copy in stage_copies(i):
            copy.start()

    def back_step(k, carry):
        total.step(k)

        @pl.when(k - 2 < tiles)
        def _():
            weights(k - 2)

        return carry

    lax.fori_loop(2, ne - 1, back_step, 0)
    at = slice(count * width, count * width + narrow)
    hid_t = hid_ref[:, :, at].reshape(every, narrow).T
    for d in range(0, model, 512):
        dsd_ref[:, d : d + 512] = mm(hid_t, grad_ref[:, :, d : d + 512].reshape(every, 512)).astype(BF)
    for i in range(ne - 3, tiles):
        weights(i)
    for i in range(max(tiles - 2, 0), tiles):
        for copy in stage_copies(i):
            copy.wait()
    for i in (ne // 2 - 2, ne // 2 - 1):
        for copy in out_copies(i):
            copy.wait()
    total.finish(back_ref)
    back.arrived()
    back.drain()
    there.drain()


def experts_both_ways(
    ffn_in, gates, grad_all, expert_gate, expert_up, expert_down, shared_two, shared_down, ns, ne, cid
):
    length, model = ffn_in.shape
    count, _, width = expert_gate.shape
    narrow = shared_down.shape[0]
    hidden = count * width + narrow
    part = model // ns
    per = 1 if part % 128 == 0 else 2
    return pl.pallas_call(
        functools.partial(experts_kernel, ne, count),
        out_shape=(
            jax.ShapeDtypeStruct((length, model), F32),
            jax.ShapeDtypeStruct((ne, 8, length), F32),
            jax.ShapeDtypeStruct((ne, length, model), BF),
            jax.ShapeDtypeStruct((ns, count, part, width), BF),
            jax.ShapeDtypeStruct((ns, count, part, width), BF),
            jax.ShapeDtypeStruct((ns, count, width, part), BF),
            jax.ShapeDtypeStruct((ns // per, per * part, 2 * narrow), BF),
            jax.ShapeDtypeStruct((narrow, model), BF),
        ),
        in_specs=[VMEM] * 2 + [ANY] * 6,
        out_specs=(VMEM, VMEM, ANY, ANY, ANY, ANY, ANY, VMEM),
        scratch_shapes=[
            pltpu.VMEM((ne, length, model), BF),
            pltpu.VMEM((ne, 8, length), F32),
            pltpu.VMEM((ne, length, hidden), BF),
            pltpu.VMEM((ne, length, hidden), BF),
            pltpu.VMEM((ne, length, hidden), BF),
            pltpu.VMEM((ne, length, model), BF),
            pltpu.VMEM((ne, 8, length), F32),
            pltpu.VMEM((2, per, count, part, width), BF),
            pltpu.VMEM((2, per, count, part, width), BF),
            pltpu.VMEM((2, per, count, width, part), BF),
            pltpu.VMEM((2, per * part, 2 * narrow), BF),
            DMA((2, 4)),
            pltpu.VMEM((2, 2 * length, model), BF),
            DMA((2, 4)),
        ]
        + RingGather.scratch(ne, 2)
        + Exchange.scratch(ne)
        + Exchange.scratch(ne)
        + RingSum.scratch(ne, 2, length, model)
        + Loads.scratch(
            [expert_gate, expert_up, grad_all, expert_down, shared_two, shared_down]
        ),
        compiler_params=params(cid, 60),
        name="experts",
    )(ffn_in, gates, grad_all, expert_gate, expert_up, expert_down, shared_two, shared_down)


class SeqGather:
    def __init__(self, ns, v, aux, out, aux_out, lsem, s1, r1, s2, r2, sa, ra):
        s, e = lax.axis_index("seq"), lax.axis_index("exp")
        ny = ns // 2
        y, c = s // 2, s % 2
        mate = (2 * y + 1 - c, e)

        def make(src, dst, send, recv, device):
            return pltpu.make_async_remote_copy(
                src_ref=src,
                dst_ref=dst,
                send_sem=send,
                recv_sem=recv,
                device_id=device,
                device_id_type=MESH,
            )

        self.own = [
            pltpu.make_async_copy(v, out.at[s], lsem.at[0]),
            pltpu.make_async_copy(aux, aux_out.at[s], lsem.at[1]),
        ]
        self.first = [
            make(v, out.at[s], s1.at[j], r1.at[j], (2 * ((y + j) % ny) + c, e))
            for j in range(1, ny)
        ]
        self.first.append(make(v, out.at[s], s1.at[0], r1.at[0], mate))
        self.extra = [
            make(aux, aux_out.at[s], sa.at[t - 1], ra.at[t - 1], ((s + t) % ns, e))
            for t in range(1, ns)
        ]
        self.second = []
        for j in range(1, ny):
            block = out.at[2 * ((y + ny - j) % ny) + c]
            self.second.append(make(block, block, s2.at[j - 1], r2.at[j - 1], mate))

    @staticmethod
    def scratch(ns):
        ny = ns // 2
        return [
            DMA((2,)),
            DMA((ny,)),
            DMA((ny,)),
            DMA((max(ny - 1, 1),)),
            DMA((max(ny - 1, 1),)),
            DMA((ns - 1,)),
            DMA((ns - 1,)),
        ]

    def begin(self):
        for copy in self.first + self.extra + self.own:
            copy.start()

    def middle(self):
        for arrived, onward in zip(self.first[:-1], self.second):
            arrived.wait_recv()
            onward.start()

    def finish(self):
        for copy in [self.first[-1]] + self.second + self.extra:
            copy.wait_recv()
        for copy in self.own:
            copy.wait()

    def drain(self):
        for copy in self.first + self.second + self.extra:
            copy.wait_send()


def sum_weights_kernel(
    ns,
    ne,
    blocks,
    gin,
    gcommon,
    gout,
    dproj_ref,
    in_ref,
    common_ref,
    tok_ref,
    resid_ref,
    gain_ref,
    aux_ref,
    *refs,
):
    sources = refs[:blocks]
    in_out, pack_out, out_rows, tok_out, aux_out = refs[blocks : blocks + 5]
    shared_outs = refs[blocks + 5 : blocks + 7]
    block_outs = refs[blocks + 7 : 2 * blocks + 6]
    sum_weights_body(
        ns,
        ne,
        sources,
        block_outs,
        gin,
        gcommon,
        gout,
        dproj_ref,
        in_ref,
        common_ref,
        tok_ref,
        resid_ref,
        gain_ref,
        aux_ref,
        in_out,
        pack_out,
        out_rows,
        tok_out,
        aux_out,
        shared_outs,
        *refs[2 * blocks + 6 :],
    )


def sum_weights_body(
    ns,
    ne,
    sources,
    block_outs,
    gin,
    gcommon,
    gout,
    dproj_ref,
    in_ref,
    common_ref,
    tok_ref,
    resid_ref,
    gain_ref,
    aux_ref,
    in_out,
    pack_out,
    out_rows,
    tok_out,
    aux_out,
    shared_outs,
    out,
    acc,
    acc_out,
    acc_common,
    common_sum,
    common_low,
    fin,
    part_ref,
    lowered_grad,
    aux_part,
    aux_in,
    aux_sum,
    shared_sum,
    shared_low,
    shared_all,
    dproj,
    in_held,
    common_held,
    load_sems,
    ssem,
    rsem,
    so,
    ro,
    sc,
    rc,
    sx,
    rx,
    ss,
    rs,
    *scratch,
):
    s, e = lax.axis_index("seq"), lax.axis_index("exp")
    p, right, left = ring_sides(e, ne)
    count = len(SeqSum.scratch(ns, 2, 8, 128, (8, 128)))
    job = SeqSum(ns, 2, part_ref, None, *scratch[:count])
    there = Exchange(ne, aux_part, aux_in, *scratch[count : count + 3])
    back = Exchange(
        ne,
        aux_sum,
        aux_out,
        *scratch[count + 3 : count + 6],
        pick=lambda ref, at: ref.at[s, at],
        spread=True,
    )
    along = []
    at = count + 9 + len(BlockSum.scratch(ns, [gcommon.shape]))
    shared_cols = BlockSum(ns, (gcommon,), (common_sum,), scratch[count + 9 : at])
    more = BlockSum(ns, sources, tuple(block_outs) + (shared_sum,), scratch[at:])
    across = Exchange(ne, shared_low, shared_all, *scratch[count + 6 : count + 9])
    loads = Loads((dproj_ref, in_ref, common_ref), (dproj, in_held, common_held), load_sems)
    shared_cols.load()
    loads.begin()
    more.load()
    greet([((s + t) % ns, e) for t in range(1, ns)] + [(s, (e + t) % ne) for t in range(1, ne)])

    def fill(block):
        rows = pl.ds(pl.multiple_of(block * GROUP, GROUP), GROUP)
        main = in_held.shape[1]
        part = mm_t(dproj[rows, :main], in_held[...])
        part_ref[block] = (part + mm_t(dproj[rows, main:], common_held[...])).astype(BF)

    def tokens_back():
        value = tok_ref[...].astype(F32)
        grad = lowered_grad[...]
        width = value.shape[1]
        scale = lax.rsqrt(jnp.sum(value * value, 1, keepdims=True) / width + EPSILON)
        inside = gain_ref[0:1, :] * grad
        mean = jnp.sum(value * inside, 1, keepdims=True) / width
        tok_out[...] = (resid_ref[...] + scale * inside - value * (scale * scale * scale * mean)).astype(BF)
        gain_grad = jnp.sum(value * scale * grad, 0, keepdims=True)
        aux_part[...] = aux_ref[...]
        for i in range(width // 128):
            q = aux_last + i // 8
            aux_part[q % ne, q // ne, i % 8 : i % 8 + 1, :] = gain_grad[:, i * 128 : (i + 1) * 128]
        there.begin()

    def sums():
        there.arrived()
        total = aux_in[0]
        for i in range(1, ne):
            total = total + aux_in[i]
        aux_sum[...] = total
        back.begin()

    def spread():
        back.arrived()
        for t in range(1, ns):
            along.append(
                remote(aux_out.at[s], aux_out.at[s], ss.at[t - 1], rs.at[t - 1], ((s + t) % ns, e))
            )

    def swap():
        shared_low[...] = shared_sum[0].astype(BF)
        across.begin()

    def far_task(j):
        def run():
            fill(job.far(j))
            job.send(j)

        return run

    def common_ready():
        shared_cols.close(0)
        common_low[...] = common_sum[0].astype(BF)
        ready.append(True)

    ready = []
    aux_last = (gin.shape[3] // 2 + common_ref.shape[1] - pack_out.shape[1]) // 128 + 3
    items = len(more.items)
    lanes = range(1, ns // 2)
    tasks = [(0.0, lambda: loads.wait(0, 1, 2))]
    tasks += [(0.05, functools.partial(shared_cols.join, j, 0)) for j in lanes]
    tasks += [(0.17, common_ready)]
    tasks += [(0.02 * i, far_task(j)) for i, j in enumerate(job.order())]
    tasks += [
        (0.02 * (i + ns // 2), functools.partial(fill, job.near(j)))
        for i, j in enumerate(job.order())
    ]
    tasks += [(0.13, more.begin)]
    tasks += [(0.14, functools.partial(job.join, j, u)) for j in lanes for u in range(job.subs)]
    tasks += [
        (0.22 + 0.15 * (items - 1 - n) / items, functools.partial(more.join, j, n))
        for n in reversed(range(items))
        for j in lanes
    ]
    tasks += [(0.36, functools.partial(job.close, u, lowered_grad)) for u in range(job.subs)]
    tasks += [(0.40, tokens_back), (0.54, sums), (0.68, spread)]
    tasks += [(0.74, functools.partial(more.close, items - 1)), (0.75, swap)]
    tasks += [
        (0.80 + 0.18 * (items - 1 - n) / items, functools.partial(more.close, n))
        for n in range(items - 1)
    ]
    tasks.sort(key=lambda task: task[0])
    shared_cols.begin()
    rows = gin.shape[2]
    main = gin.shape[3]
    tile = tile_rows(rows)
    half = gout.shape[2] // 2
    tile_out = tile_rows(gout.shape[1])
    sent = {}
    last = {}
    done = 0
    lag = 1
    for k in range(ne + lag):
        for t in list(range(1, ns)) + [0, ns, ns + 1, ns + 2]:
            while k > 0 and tasks and tasks[0][0] <= done / (ne * (ns + 3)):
                tasks.pop(0)[1]()
            if t == ns + 2:
                hop = k - lag
                way = 1
            else:
                hop = k
                way = t % 2
            if hop < 0 or hop >= ne:
                continue
            while t == ns + 2 and not ready:
                tasks.pop(0)[1]()
            done += 1
            to = right if way == 0 else left
            place = (p - 1 - hop + 2 * ne) % ne if way == 0 else (p + 1 + hop) % ne
            slot = ring_index(place, ne)
            if hop > 0:
                sent[hop - 1, t].wait_recv()
            if t < ns:
                piece = (s + t) % ns
                if hop > 0:

                    def join(i, carry):
                        r = pl.ds(pl.multiple_of(i * tile, tile), tile)
                        total = acc[hop - 1, t, r, :].astype(F32)
                        total = total + gin[piece, slot, r, :].astype(F32)
                        if hop < ne - 1:
                            acc[hop - 1, t, r, :] = total.astype(BF)
                        elif t == 0:
                            out[s, r, :] = total.astype(BF)
                        else:
                            fin[t - 1, r, :] = total.astype(BF)
                        return carry

                    lax.fori_loop(0, rows // tile, join, 0)
                if hop < ne - 1:
                    src = gin.at[piece, slot] if hop == 0 else acc.at[hop - 1, t]
                    sent[hop, t] = remote(
                        src, acc.at[hop, t], ssem.at[hop, t], rsem.at[hop, t], (s, to)
                    )
                elif t > 0:
                    last[t] = remote(
                        fin.at[t - 1], out.at[s], sx.at[t - 1], rx.at[t - 1], (piece, e)
                    )
            elif t == ns + 2:
                if hop > 0:
                    total = acc_common[hop - 1].astype(F32) + common_low[slot].astype(F32)
                    if hop < ne - 1:
                        acc_common[hop - 1] = total.astype(BF)
                    else:
                        wide = total.shape[1] - pack_out.shape[1]
                        in_out[:, in_out.shape[1] - wide :] = total[:, :wide]
                        pack_out[...] = total[:, wide:]
                if hop < ne - 1:
                    src = common_low.at[slot] if hop == 0 else acc_common.at[hop - 1]
                    sent[hop, t] = remote(
                        src, acc_common.at[hop], sc.at[hop], rc.at[hop], (s, to)
                    )
            else:
                part_columns = pl.ds(way * half, half)
                if hop > 0:

                    def join_out(i, carry):
                        r = pl.ds(pl.multiple_of(i * tile_out, tile_out), tile_out)
                        total = acc_out[hop - 1, r, part_columns].astype(F32)
                        total = total + gout[slot, r, part_columns].astype(F32)
                        if hop < ne - 1:
                            acc_out[hop - 1, r, part_columns] = total.astype(BF)
                        else:
                            out_rows[r, part_columns] = total
                        return carry

                    lax.fori_loop(0, gout.shape[1] // tile_out, join_out, 0)
                if hop < ne - 1:
                    src = (
                        gout.at[slot, :, part_columns]
                        if hop == 0
                        else acc_out.at[hop - 1, :, part_columns]
                    )
                    sent[hop, t] = remote(
                        src,
                        acc_out.at[hop, :, part_columns],
                        so.at[hop, way],
                        ro.at[hop, way],
                        (s, to),
                    )
    for _, task in tasks:
        task()
    across.arrived()
    half_wide = shared_all.shape[2] // 2
    units = half_wide // ns
    for which in range(2):
        for owner in range(ne):
            found = shared_all[owner, :, which * half_wide : (which + 1) * half_wide].astype(F32)
            for block in range(ns):
                first = (block * ne + owner) * units
                shared_outs[which][:, first : first + units] = found[
                    :, block * units : (block + 1) * units
                ]
    for copy in list(last.values()) + along:
        copy.wait_recv()
    head = main // 2
    inner = head * ns
    for block in range(ns):
        in_out[:, block * head : (block + 1) * head] = out[block, :, :head].astype(F32)
        in_out[:, inner + block * head : inner + (block + 1) * head] = out[block, :, head:].astype(F32)
    for copy in list(sent.values()) + list(last.values()) + along:
        copy.wait_send()
    more.drain()
    shared_cols.drain()
    job.drain()
    there.drain()
    back.drain()
    across.drain()


def sum_weights(
    gin,
    gcommon,
    gout,
    projected_grad,
    in_local,
    in_common,
    tokens,
    resid_grad,
    gain,
    aux,
    sources,
    pack,
    ns,
    ne,
    cid,
):
    rows, wide = gin.shape[2:]
    narrow = gcommon.shape[4]
    length, model = tokens.shape
    blocks = len(sources)
    return pl.pallas_call(
        functools.partial(sum_weights_kernel, ns, ne, blocks),
        out_shape=(
            jax.ShapeDtypeStruct((rows, ns * wide + narrow - pack), F32),
            jax.ShapeDtypeStruct((rows, pack), F32),
            jax.ShapeDtypeStruct(gout.shape[1:], F32),
            jax.ShapeDtypeStruct(tokens.shape, BF),
            jax.ShapeDtypeStruct((ns,) + aux.shape, F32),
            jax.ShapeDtypeStruct((rows, ne * sources[-1].shape[4] // 2), F32),
            jax.ShapeDtypeStruct((rows, ne * sources[-1].shape[4] // 2), F32),
        )
        + tuple(jax.ShapeDtypeStruct(v.shape[1:], F32) for v in sources[:-1]),
        in_specs=[VMEM, ANY, VMEM] + [ANY] * 3 + [VMEM] * 4 + [ANY] * blocks,
        out_specs=(VMEM,) * (6 + blocks),
        scratch_shapes=[
            pltpu.VMEM((ns, rows, wide), BF),
            pltpu.VMEM((ne - 1, ns, rows, wide), BF),
            pltpu.VMEM((ne - 1,) + gout.shape[1:], BF),
            pltpu.VMEM((ne - 1, rows, narrow), BF),
            pltpu.VMEM(gcommon.shape[1:], F32),
            pltpu.VMEM(gcommon.shape[2:], BF),
            pltpu.VMEM((ns - 1, rows, wide), BF),
            pltpu.VMEM((ns, length, model), BF),
            pltpu.VMEM((length, model), F32),
            pltpu.VMEM(aux.shape, F32),
            pltpu.VMEM(aux.shape, F32),
            pltpu.VMEM(aux.shape[1:], F32),
            pltpu.VMEM(sources[-1].shape[1:], F32),
            pltpu.VMEM(sources[-1].shape[2:], BF),
            pltpu.VMEM(sources[-1].shape[2:], BF),
        ]
        + Loads.scratch([projected_grad, in_local, in_common])
        + [
            DMA((ne - 1, ns)),
            DMA((ne - 1, ns)),
            DMA((ne - 1, 2)),
            DMA((ne - 1, 2)),
            DMA((ne - 1,)),
            DMA((ne - 1,)),
            DMA((ns - 1,)),
            DMA((ns - 1,)),
            DMA((ns - 1,)),
            DMA((ns - 1,)),
        ]
        + SeqSum.scratch(ns, 2, length, model, (8, 128))
        + Exchange.scratch(ne)
        + Exchange.scratch(ne)
        + Exchange.scratch(ne)
        + BlockSum.scratch(ns, [gcommon.shape])
        + BlockSum.scratch(ns, [v.shape for v in sources]),
        compiler_params=params(cid, 60),
        name="sum_weights",
    )(
        gin,
        gcommon,
        gout,
        projected_grad,
        in_local,
        in_common,
        tokens,
        resid_grad,
        gain,
        aux,
        *sources,
    )


def matmul_plain(left, right):
    return jnp.dot(left, right, preferred_element_type=F32)


def matmul_rows(left, right):
    return lax.dot_general(left, right, (((0,), (0,)), ((), ())), preferred_element_type=F32)


def matmul_cols(left, right):
    return lax.dot_general(left, right, (((1,), (1,)), ((), ())), preferred_element_type=F32)


def mm(left, right):
    return jnp.dot(left, right, preferred_element_type=F32)


def mm_t(left, right):
    return lax.dot_general(left, right, (((1,), (1,)), ((), ())), preferred_element_type=F32)


def t_mm(left, right):
    return lax.dot_general(left, right, (((0,), (0,)), ((), ())), preferred_element_type=F32)


def exact(left, right):
    return jnp.dot(left, right, precision=PRECISE, preferred_element_type=F32)


def spread_heads(table, heads, head_dim):
    rows = table.shape[0]
    per = 128 // head_dim
    lane = lax.broadcasted_iota(jnp.int32, (rows, 128), 1)
    tiles = []
    for h in range(0, heads, per):
        tile = jnp.broadcast_to(table[:, h : h + 1], (rows, 128))
        for i in range(1, per):
            other = jnp.broadcast_to(table[:, h + i : h + i + 1], (rows, 128))
            tile = jnp.where(lane >= i * head_dim, other, tile)
        tiles.append(tile)
    return jnp.concatenate(tiles, 1)


def sigmoid(v):
    return 1.0 / (1.0 + jnp.exp(-v))


def softplus(v):
    return jnp.maximum(v, 0.0) + jnp.log1p(jnp.exp(-jnp.abs(v)))


def two_parts(v):
    high = v.astype(BF)
    return high, (v - high.astype(F32)).astype(BF)


def triangle(flip=False):
    t = lax.broadcasted_iota(jnp.int32, (GROUP, GROUP), 0)
    u = lax.broadcasted_iota(jnp.int32, (GROUP, GROUP), 1)
    return u >= t if flip else t >= u


def step_table(pack, bias, heads, s):
    turned = pltpu.roll(pack, (128 - heads * s) % 128, 1)
    lane = lax.broadcasted_iota(jnp.int32, turned.shape, 1)
    raw = jnp.where(lane < heads, turned + bias, 0.0)
    return raw, jnp.where(lane < heads, softplus(raw), 0.0)


def convolved(ext, table, width):
    mixed = table[width : width + 1]
    for j in range(width):
        mixed = mixed + table[j : j + 1] * ext[8 - width + 1 + j : 8 - width + 1 + j + GROUP]
    return mixed


def with_before(proj_ref, at, columns, first):
    before = proj_ref[pl.ds(pl.multiple_of(jnp.maximum(at - 8, 0), 8), 8), columns]
    before = jnp.where(first, 0.0, before)
    return jnp.concatenate([before, proj_ref[pl.ds(at, GROUP), columns]], 0)


def mix_forward_kernel(
    ns,
    ne,
    hw,
    state2,
    heads,
    width,
    norm_at,
    x_ref,
    w_hbm,
    c_hbm,
    table_ref,
    head_ref,
    out_hbm,
    grad_ref,
    proj_hbm,
    lowered_hbm,
    scan_hbm,
    mix_hbm,
    entry_hbm,
    sum_ref,
    square_out,
    grad_all,
    proj_ref,
    lowered_ref,
    scan_ref,
    mix_ref,
    entry_ref,
    state,
    low_ref,
    square_ref,
    part_ref,
    store_sem,
    w_ref,
    c_ref,
    out_ref,
    load_sem,
    *sems,
):
    s, e = lax.axis_index("seq"), lax.axis_index("exp")
    p, right, left = ring_sides(e, ne)
    loads = Loads((w_hbm, c_hbm, out_hbm), (w_ref, c_ref, out_ref), load_sem)
    loads.begin()
    greet([((s + t) % ns, e) for t in range(1, ns)] + [(s, right), (s, left)])
    ring = RingGather(ne, grad_ref, grad_all, *sems[:3])
    job = SeqSum(ns, 2, part_ref, square_ref, *sems[3:])
    ring.begin()
    pairs = (
        (proj_ref, proj_hbm),
        (lowered_ref, lowered_hbm),
        (scan_ref, scan_hbm),
        (mix_ref, mix_hbm),
    )

    def stores(c):
        rows = pl.ds(pl.multiple_of(c * GROUP, GROUP), GROUP)
        copies = [
            pltpu.make_async_copy(ref.at[rows], hbm.at[rows], store_sem.at[c, i])
            for i, (ref, hbm) in enumerate(pairs)
        ]
        copies.append(
            pltpu.make_async_copy(entry_ref.at[c], entry_hbm.at[c], store_sem.at[c, len(pairs)])
        )
        return copies

    loads.wait(0, 1)
    norm = c_ref[:, state2:].astype(F32).T[norm_at : norm_at + 1, :]
    blocks = x_ref.shape[0] // GROUP
    head_dim = hw // heads
    n = state2 // 2
    state[...] = jnp.zeros_like(state)
    lane = lax.broadcasted_iota(jnp.int32, (GROUP, 128), 1)
    table = table_ref[...]
    skip = table[width + 2 : width + 3, :hw]
    gain = table[width + 1 : width + 2, :hw]
    bias, rate = head_ref[0:1, :], head_ref[1:2, :]

    def chunk(c, carry):
        at = pl.multiple_of(c * GROUP, GROUP)
        rows = pl.ds(at, GROUP)
        causal = triangle()
        x = x_ref[rows, :].astype(F32)
        scale = lax.rsqrt(jnp.sum(x * x, 1, keepdims=True) / x.shape[1] + EPSILON)
        lowered = (x * scale * norm).astype(BF)
        lowered_ref[rows, :] = lowered
        proj_ref[rows, : 2 * hw] = mm(lowered, w_ref[...])
        proj_ref[rows, 2 * hw :] = mm(lowered, c_ref[...])
        ext = with_before(proj_ref, at, slice(hw, 2 * hw + state2), c == 0)
        mixed = convolved(ext, table, width)
        mix_ref[rows, :] = mixed
        conv = mixed * sigmoid(mixed)
        values = conv[:, :hw]
        b = conv[:, hw : hw + n].astype(BF)
        ct = conv[:, hw + n :].astype(BF)
        _, steps = step_table(proj_ref[rows, 2 * hw + state2 :], bias, heads, s)
        logs = exact(causal.astype(F32), steps * rate)
        logs_t, steps_t = logs.T, steps.T
        end = logs[GROUP - 1 : GROUP, :]
        before = state[...]
        entry_ref[c] = before
        carried = mm(ct, before.astype(BF)) * spread_heads(jnp.exp(logs), heads, head_dim)
        tails = spread_heads(jnp.exp(end - logs) * steps, heads, head_dim)
        fresh = t_mm(b, (values * tails).astype(BF))
        state[...] = spread_heads(jnp.exp(end), heads, head_dim) * before + fresh
        cross = mm_t(ct, b)
        low = values.astype(BF)
        tiles = []
        per = 128 // head_dim
        for h in range(0, heads, per):
            tile = None
            part = low[:, h * head_dim : h * head_dim + 128]
            for i in range(per):
                gap = logs[:, h + i : h + i + 1] - logs_t[h + i : h + i + 1, :]
                kernel = jnp.exp(jnp.where(causal, gap, -1e30))
                weights = cross * kernel * steps_t[h + i : h + i + 1, :]
                one = mm(weights.astype(BF), part)
                tile = one if i == 0 else jnp.where(lane >= i * head_dim, one, tile)
            tiles.append(tile)
        scanned = jnp.concatenate(tiles, 1) + carried + skip * values
        scan_ref[rows, :] = scanned
        gate = proj_ref[rows, :hw]
        gated = scanned * (gate * sigmoid(gate))
        low_ref[rows, :] = (gated * gain).astype(BF)
        square_ref[c] = lax.dot_general(
            jnp.ones((8, hw), F32),
            gated * gated,
            (((1,), (1,)), ((), ())),
            precision=PRECISE,
            preferred_element_type=F32,
        )

        for copy in stores(c):
            copy.start()
        ring.step(c + 1)

        return carry

    lax.fori_loop(0, blocks, chunk, 0)

    def fill(block):
        rows = pl.ds(pl.multiple_of(block * GROUP, GROUP), GROUP)
        part_ref[block] = mm(low_ref[rows, :], out_ref[...]).astype(BF)

    k = blocks + 1
    loads.wait(2)
    job.begin(fill)
    for stage in (job.middle, lambda: job.finish(sum_ref, square_out)):
        if k < ne - 1:
            ring.step(k)
            k += 1
        stage()
    while k < ne - 1:
        ring.step(k)
        k += 1
    ring.finish()
    job.drain()
    for c in range(blocks):
        for copy in stores(c):
            copy.wait()


def mix_forward(
    sequence,
    in_local,
    in_common,
    table,
    head_table,
    out_local,
    grad_low,
    ns,
    ne,
    hw,
    state2,
    heads,
    width,
    norm_at,
    cid,
):
    whole, model = sequence.shape
    blocks = whole // GROUP
    n = state2 // 2
    rows = grad_low.shape[0]
    columns = in_local.shape[1] + in_common.shape[1]
    kept = [
        jax.ShapeDtypeStruct((whole, columns), F32),
        jax.ShapeDtypeStruct((whole, model), BF),
        jax.ShapeDtypeStruct((whole, hw), F32),
        jax.ShapeDtypeStruct((whole, hw + state2), F32),
        jax.ShapeDtypeStruct((blocks, n, hw), F32),
    ]
    return pl.pallas_call(
        functools.partial(mix_forward_kernel, ns, ne, hw, state2, heads, width, norm_at),
        out_shape=tuple(kept)
        + (
            jax.ShapeDtypeStruct((rows, model), F32),
            jax.ShapeDtypeStruct((8, rows), F32),
            jax.ShapeDtypeStruct((ne, rows, model), BF),
        ),
        in_specs=[VMEM, ANY, ANY, VMEM, VMEM, ANY, VMEM],
        out_specs=(ANY,) * 5 + (VMEM,) * 3,
        scratch_shapes=[pltpu.VMEM(v.shape, v.dtype) for v in kept]
        + [
            pltpu.VMEM((n, hw), F32),
            pltpu.VMEM((whole, hw), BF),
            pltpu.VMEM((blocks, 8, GROUP), F32),
            pltpu.VMEM((ns, rows, model), BF),
            DMA((blocks, 5)),
        ]
        + Loads.scratch([in_local, in_common, out_local])
        + RingGather.scratch(ne, 2)
        + SeqSum.scratch(ns, 2, rows, model, (8, rows)),
        compiler_params=params(cid, 50),
        name="mix_forward",
    )(sequence, in_local, in_common, table, head_table, out_local, grad_low)


def aux_slots(hw, state2, ne):
    return -(-((hw + state2) // 128 + 5) // ne)


def mix_backward_kernel(
    ns,
    ne,
    hw,
    state2,
    heads,
    width,
    proj_hbm,
    table_ref,
    head_ref,
    scan_hbm,
    mix_hbm,
    entry_hbm,
    out_hbm,
    resid_ref,
    rows_ref,
    part_ref,
    expert_ref,
    lowered_hbm,
    router_ref,
    value_ref,
    ffn_ref,
    stat_ref,
    result_ref,
    expert_out,
    dproj_ref,
    grad_out_ref,
    grad_in_ref,
    grad_common_ref,
    aux_ref,
    sum_ref,
    dtable_ref,
    dhead_ref,
    adjoint,
    after,
    low_ref,
    resid_all,
    scale_ref,
    *scratch,
):
    s, e = lax.axis_index("seq"), lax.axis_index("exp")
    p, right, left = ring_sides(e, ne)
    loads = Loads(
        (proj_hbm, scan_hbm, mix_hbm, entry_hbm, out_hbm, lowered_hbm), scratch[:6], scratch[6]
    )
    proj_ref, scan_ref, mix_ref, entry_ref, out_ref, lowered_ref = scratch[:6]
    loads.begin()
    greet([((s + t) % ns, e) for t in range(1, ns)] + [(s, right), (s, left)])
    ring = RingSum(ne, part_ref, *scratch[7:10])
    at = 10 + len(SeqGather.scratch(ns))
    rows_in = SeqGather(ns, resid_ref, rows_ref, resid_all, scale_ref, *scratch[10:at])
    experts = BlockSum(ns, (expert_ref,), (expert_out,), scratch[at:])
    experts.load()
    rows_in.begin()
    ring.begin()
    ring.step(1)
    rows_in.middle()
    experts.begin()
    ring.step(2)
    rows_in.finish()
    for j in range(1, ns // 2):
        for n in range(len(experts.items)):
            experts.join(j, n)
    loads.wait(*range(6))
    blocks = proj_ref.shape[0] // GROUP
    head_dim = hw // heads
    n = state2 // 2
    per = 128 // head_dim
    adjoint[...] = jnp.zeros_like(adjoint)
    after[...] = jnp.zeros_like(after)
    dtable_ref[...] = jnp.zeros_like(dtable_ref)
    dhead_ref[...] = jnp.zeros_like(dhead_ref)
    lane = lax.broadcasted_iota(jnp.int32, (GROUP, 128), 1)
    row = lax.broadcasted_iota(jnp.int32, (GROUP, 128), 0)
    table = table_ref[...]
    skip = table[width + 2 : width + 3, :hw]
    gain = table[width + 1 : width + 2, :hw]
    bias, rate = head_ref[0:1, :], head_ref[1:2, :]

    def chunk(lap, carry):
        c = blocks - 1 - lap
        at = pl.multiple_of(c * GROUP, GROUP)
        rows = pl.ds(at, GROUP)
        causal = triangle()
        head_of = lax.broadcasted_iota(jnp.int32, (hw, 128), 0) // head_dim
        pick = (head_of == lax.broadcasted_iota(jnp.int32, (hw, 128), 1)).astype(F32)
        gate = proj_ref[rows, :hw]
        gate_sig = sigmoid(gate)
        gate_silu = gate * gate_sig
        scanned = scan_ref[rows, :]
        gated = scanned * gate_silu
        scales = scale_ref[c].T
        r, inside = scales[:, 0:1], scales[:, 1:2]
        q = mm_t(resid_all[c], out_ref[...])
        dgated = r * (gain * q) - gated * (r * r * r * inside)
        low_ref[rows, :] = (gated * gain * r).astype(BF)
        dtable_ref[width + 1 : width + 2, :hw] += jnp.sum(gated * r * q, 0, keepdims=True)
        dy = dgated * gate_silu
        dproj_ref[rows, :hw] = (dgated * scanned * (gate_sig + gate_silu * (1 - gate_sig))).astype(BF)

        mixed = mix_ref[rows, :]
        sig = sigmoid(mixed)
        conv = mixed * sig
        values = conv[:, :hw]
        b, b_rest = two_parts(conv[:, hw : hw + n])
        ct, ct_rest = two_parts(conv[:, hw + n :])
        dtable_ref[width + 2 : width + 3, :hw] += jnp.sum(dy * values, 0, keepdims=True)
        raw, steps = step_table(proj_ref[rows, 2 * hw + state2 :], bias, heads, s)
        logs = exact(causal.astype(F32), steps * rate)
        logs_t, steps_t = logs.T, steps.T
        end = logs[GROUP - 1 : GROUP, :]
        rest = jnp.exp(end - logs)
        tail = rest * steps
        ends = jnp.exp(end)
        before = entry_ref[c]
        before_low, before_rest = two_parts(before)
        later = adjoint[...]
        later_low, later_rest = two_parts(later)
        tails = spread_heads(tail, heads, head_dim)
        dy_carried = dy * spread_heads(jnp.exp(logs), heads, head_dim)
        dy_carried_low = dy_carried.astype(BF)
        carried = mm(ct, before_low)
        back = mm(b, later_low)
        dvalues = tails * back + skip * dy
        dc = mm_t(dy_carried_low, before_low) + mm_t(dy_carried_low, before_rest)
        values_tail = (values * tails).astype(BF)
        db = mm_t(values_tail, later_low) + mm_t(values_tail, later_rest)
        kept = jnp.sum(later * before, 0, keepdims=True)
        adjoint[...] = spread_heads(ends, heads, head_dim) * later + t_mm(ct, dy_carried_low)
        sums = exact(jnp.concatenate([dy_carried * carried, values * back, jnp.broadcast_to(kept, (8, hw))], 0), pick)
        from_carried, dtail, kept = sums[:GROUP], sums[GROUP : 2 * GROUP], sums[2 * GROUP : 2 * GROUP + 1]
        cross = mm_t(ct, b)
        low = values.astype(BF)
        dy_low = dy.astype(BF)
        dcross = jnp.zeros((GROUP, GROUP), F32)
        dlogs = from_carried - dtail * tail
        columns = []
        tiles = []
        for h in range(0, heads, per):
            part = low[:, h * head_dim : h * head_dim + 128]
            dy_part = dy_low[:, h * head_dim : h * head_dim + 128]
            tile = None
            for i in range(per):
                gap = logs[:, h + i : h + i + 1] - logs_t[h + i : h + i + 1, :]
                kernel = jnp.exp(jnp.where(causal, gap, -1e30))
                scaled = kernel * steps_t[h + i : h + i + 1, :]
                weights = cross * scaled
                inside_head = (lane >= i * head_dim) & (lane < (i + 1) * head_dim)
                one = t_mm(weights.astype(BF), dy_part)
                tile = one if i == 0 else jnp.where(lane >= i * head_dim, one, tile)
                dweights = mm_t(jnp.where(inside_head, dy_part, jnp.zeros_like(dy_part)), part)
                dcross = dcross + dweights * scaled
                unscaled = dweights * (cross * kernel)
                total = jnp.sum(dweights * weights, 1, keepdims=True)
                dlogs = dlogs + jnp.where(lane == h + i, total, 0.0)
                columns.append(jnp.sum(unscaled, 0, keepdims=True))
            tiles.append(tile)
        dvalues = dvalues + jnp.concatenate(tiles, 1)
        columns = jnp.concatenate(columns + [jnp.zeros((128 - heads, GROUP), F32)], 0).T
        dlogs = dlogs - columns * steps
        at_end = jnp.sum(dtail * tail, 0, keepdims=True) + ends * kept
        dlogs = dlogs + jnp.where(row == GROUP - 1, at_end, 0.0)
        da = exact(triangle(True).astype(F32), dlogs)
        dsteps = columns + dtail * rest + da * rate
        dhead_ref[1:2, :] += jnp.sum(da * steps, 0, keepdims=True)
        draw = jnp.where(lane < heads, dsteps * sigmoid(raw), 0.0)
        dhead_ref[0:1, :] += jnp.sum(draw, 0, keepdims=True)
        dproj_ref[rows, 2 * hw + state2 :] = pltpu.roll(draw, heads * s, 1).astype(BF)
        dcross_low = dcross.astype(BF)
        dc = dc + mm(dcross_low, b) + mm(dcross_low, b_rest)
        dcross_t = dcross.T.astype(BF)
        db = db + mm(dcross_t, ct) + mm(dcross_t, ct_rest)
        dmix = jnp.concatenate([dvalues, db, dc], 1) * (sig + conv * (1 - sig))
        dtable_ref[width : width + 1, :] += jnp.sum(dmix, 0, keepdims=True)
        ext = with_before(proj_ref, at, slice(hw, 2 * hw + state2), c == 0)
        dext = jnp.concatenate([dmix, after[...]], 0)
        dconv = 0.0
        for j in range(width):
            first = 8 - width + 1 + j
            dtable_ref[j : j + 1, :] += jnp.sum(dmix * ext[first : first + GROUP], 0, keepdims=True)
            dconv = dconv + table[j : j + 1] * dext[width - 1 - j : width - 1 - j + GROUP]
        after[...] = dmix[:8]
        dproj_ref[rows, hw : 2 * hw + state2] = dconv.astype(BF)
        ring.step(lap + 3)
        return carry

    lax.fori_loop(0, blocks, chunk, 0)
    model = resid_all.shape[2]
    every = resid_all[...].reshape(blocks * GROUP, model)
    for d in range(0, hw, 128):
        low_t = low_ref[:, d : d + 128].T
        grad_out_ref[d : d + 128, :] = mm(low_t, every).astype(BF)
    for k in range(blocks + 3, ne - 1):
        ring.step(k)
    wide = grad_common_ref.shape[1]
    main = dproj_ref.shape[1] - wide
    for d in range(0, model, 384):
        rows = slice(d, d + 384)
        lowered_t = lowered_ref[:, rows].T
        grad_in_ref[rows, :] = mm(lowered_t, dproj_ref[:, :main]).astype(BF)
        common = mm(lowered_t, dproj_ref[:, main:])
        grad_common_ref[rows, : wide - 128] = common[:, : wide - 128].astype(BF)
        grad_common_ref[rows, wide - 128 :] = (common[:, wide - 128 :] + router_ref[rows, :]).astype(BF)
    aux_ref[...] = jnp.zeros_like(aux_ref)
    tiles = dtable_ref.shape[1] // 128

    def put(q, tile):
        aux_ref[q % ne, q // ne] = tile

    for q in range(tiles):
        put(q, dtable_ref[:, q * 128 : (q + 1) * 128])
    put(tiles + 1, ffn_ref[:8])
    put(tiles + 2, ffn_ref[8:])
    ring.finish(sum_ref)
    ffn = sum_ref[...]
    result_ref[...] = (value_ref[...] + ffn).astype(BF)
    square = jnp.sum(jnp.sum(ffn * ffn, 1, keepdims=True), 0, keepdims=True)
    tile_row = lax.broadcasted_iota(jnp.int32, (8, 128), 0)
    tile_lane = lax.broadcasted_iota(jnp.int32, (8, 128), 1)
    heads_tile = jnp.where(tile_row == 1, dhead_ref[...] * rate, dhead_ref[...])
    heads_tile = jnp.where(tile_row == 2, stat_ref[...], heads_tile)
    put(tiles, jnp.where((tile_row == 2) & (tile_lane == 2), square, heads_tile))
    for n in range(len(experts.items)):
        experts.close(n)
    experts.drain()
    rows_in.drain()


def mix_backward(
    proj,
    table,
    head_table,
    scanned,
    mixed,
    entries,
    out_local,
    resid_low,
    scales,
    out_part,
    expert_part,
    lowered,
    router_grad,
    resid,
    ffn_grad,
    stat_terms,
    ns,
    ne,
    hw,
    state2,
    heads,
    width,
    cid,
):
    whole = proj.shape[0]
    n = state2 // 2
    rows, model = resid_low.shape
    return pl.pallas_call(
        functools.partial(mix_backward_kernel, ns, ne, hw, state2, heads, width),
        out_shape=(
            jax.ShapeDtypeStruct((rows, model), BF),
            jax.ShapeDtypeStruct(expert_part.shape[1:], F32),
            jax.ShapeDtypeStruct(proj.shape, BF),
            jax.ShapeDtypeStruct((hw, model), BF),
            jax.ShapeDtypeStruct((model, 2 * hw), BF),
            jax.ShapeDtypeStruct((model, proj.shape[1] - 2 * hw), BF),
            jax.ShapeDtypeStruct((ne, aux_slots(hw, state2, ne), 8, 128), F32),
        ),
        in_specs=[ANY, VMEM, VMEM] + [ANY] * 4 + [VMEM] * 3 + [ANY] * 2 + [VMEM] * 4,
        out_specs=(VMEM,) * 7,
        scratch_shapes=[
            pltpu.VMEM((rows, model), F32),
            pltpu.VMEM((8, hw + state2), F32),
            pltpu.VMEM((8, 128), F32),
            pltpu.VMEM((n, hw), F32),
            pltpu.VMEM((8, hw + state2), F32),
            pltpu.VMEM((whole, hw), BF),
            pltpu.VMEM((ns, rows, model), BF),
            pltpu.VMEM((ns, 8, rows), F32),
        ]
        + Loads.scratch([proj, scanned, mixed, entries, out_local, lowered])
        + RingSum.scratch(ne, 2, rows, model)
        + SeqGather.scratch(ns)
        + BlockSum.scratch(ns, [expert_part.shape]),
        compiler_params=params(cid, 53),
        name="mix_backward",
    )(
        proj,
        table,
        head_table,
        scanned,
        mixed,
        entries,
        out_local,
        resid_low,
        scales,
        out_part,
        expert_part,
        lowered,
        router_grad,
        resid,
        ffn_grad,
        stat_terms,
    )


def rms_back(value, gain, grad):
    scale = lax.rsqrt(jnp.mean(value * value, -1, keepdims=True) + EPSILON)
    inside = gain * grad
    back = scale * inside - value * scale**3 * jnp.mean(value * inside, -1, keepdims=True)
    return back, jnp.sum(value * scale * grad, 0)


def swiglu_back(a, b, grad):
    sig = jax.nn.sigmoid(a)
    return grad * b * sig * (1 + a * (1 - sig)), grad * a * sig


def on_device(
    tokens,
    routes,
    out_grad,
    norm_mix,
    in_weight,
    step_weight,
    conv_weight,
    conv_bias,
    step_bias,
    decay_log,
    skip_gain,
    norm_gate,
    out_weight,
    norm_ffn,
    router_weight,
    shared_gate,
    shared_up,
    shared_down,
    expert_gate,
    expert_up,
    expert_down,
):
    ns, ne = lax.axis_size("seq"), lax.axis_size("exp")
    s, e = lax.axis_index("seq"), lax.axis_index("exp")
    total = ns * ne
    rows, columns = in_weight.shape
    model = tokens.shape[2]
    length = tokens.shape[1]
    whole = length * ns
    width, channels = conv_weight.shape
    gains = norm_gate.shape[0]
    inner = gains * total
    hw = inner // ns
    heads = step_bias.shape[0]
    local_heads = heads // ns
    state2 = columns - 2 * inner
    experts = router_weight.shape[1]
    local_experts = expert_gate.shape[0]
    place = s * ne + e

    small = jnp.concatenate([conv_weight.reshape(-1), conv_bias, norm_gate])
    small = jnp.pad(small, (0, 16 * rows - small.shape[0])).reshape(rows, 16)
    pack = jnp.concatenate(
        [step_weight, router_weight, norm_mix[:, None], norm_ffn[:, None], small], 1
    )
    at_small = heads + experts + 2
    pack = jnp.pad(pack, ((0, 0), (0, 128 - pack.shape[1])))
    hidden_rows = shared_down.shape[0]

    def by_owner(weight):
        split = weight.reshape(rows, ns, ne, hidden_rows)
        return jnp.transpose(split, (2, 0, 1, 3)).reshape(ne, rows, ns * hidden_rows)

    shared_two = jnp.concatenate([by_owner(shared_gate), by_owner(shared_up)], -1)
    in_blocks, common_blocks, token_blocks, out_local, shared_two, local_down = gather_in(
        in_weight, pack, tokens[0], out_weight, shared_two, shared_down, ns, ne, inner, 0
    )
    out_local = out_local.reshape(hw, model)
    shared_two = shared_two.reshape(model, 2 * ns * hidden_rows)
    local_gate, local_up = shared_two[:, : ns * hidden_rows], shared_two[:, ns * hidden_rows :]
    local_down = local_down.reshape(ns * hidden_rows, model)
    grad_low = out_grad[0]
    in_local = in_blocks.reshape(model, -1)
    in_common = common_blocks.reshape(model, -1)
    full_pack = in_common[:, state2:]
    full_router = full_pack[:, heads : heads + experts]
    full_norm_mix = full_pack[:, heads + experts].astype(F32)
    full_norm_ffn = full_pack[:, heads + experts + 1].astype(F32)
    full_small = full_pack[:, at_small : at_small + 16].reshape(total, 16 * rows).astype(F32)
    full_conv = full_small[:, : (width + 1) * channels].reshape(total, width + 1, channels)
    full_conv = jnp.swapaxes(full_conv, 0, 1).reshape(width + 1, total * channels)
    at_gain = (width + 1) * channels
    full_norm_gate = full_small[:, at_gain : at_gain + gains].reshape(inner)
    local_conv = jnp.concatenate(
        [lax.dynamic_slice_in_dim(full_conv, s * hw, hw, 1), full_conv[:, inner:]], 1
    )
    local_gain = lax.dynamic_slice_in_dim(full_norm_gate, s * hw, hw)
    at_head = s * local_heads
    local_bias = lax.dynamic_slice_in_dim(step_bias, at_head, local_heads)
    local_decay = lax.dynamic_slice_in_dim(decay_log, at_head, local_heads)
    local_skip = lax.dynamic_slice_in_dim(skip_gain, at_head, local_heads)

    table = jnp.concatenate(
        [
            local_conv,
            jnp.pad(
                jnp.stack([local_gain, jnp.repeat(local_skip, hw // local_heads)]),
                ((0, 6 - width - 1), (0, state2)),
            ),
        ],
        0,
    )
    head_table = jnp.pad(
        jnp.stack([local_bias, -jnp.exp(local_decay)]), ((0, 6), (0, 128 - local_heads))
    )

    token_rows = tokens[0].astype(F32)
    projected, lowered, scanned, mixed, entries, mixed_raw, squares, grad_all = mix_forward(
        token_blocks.reshape(whole, model),
        in_local,
        in_common,
        table,
        head_table,
        out_local,
        grad_low,
        ns,
        ne,
        hw,
        state2,
        local_heads,
        width,
        heads + experts,
        1,
    )
    scale_gate = lax.rsqrt(squares[0] / inner + EPSILON)
    mixer_out = mixed_raw * scale_gate[:, None]
    resid = token_rows + mixer_out
    scale_two = lax.rsqrt(jnp.mean(resid * resid, -1, keepdims=True) + EPSILON)
    ffn_in = (resid * scale_two * full_norm_ffn).astype(BF)

    stat_terms = jnp.stack([jnp.sum(resid * resid), jnp.sum(mixer_out * mixer_out)])
    logits = matmul_plain(ffn_in, full_router)
    named = jnp.any(
        routes[0][:, :, None] == jnp.arange(experts, dtype=jnp.int32)[None, None, :], 1
    )
    top = jnp.max(jnp.where(named, logits, -jnp.inf), -1, keepdims=True)
    raised = jnp.where(named, jnp.exp(jnp.where(named, logits - top, 0.0)), 0.0)
    gates = (raised / jnp.sum(raised, -1, keepdims=True)).T

    gates_out = jnp.pad(
        gates.reshape(ne, local_experts, length), ((0, 0), (0, 8 - local_experts), (0, 0))
    )
    back_sum, gate_grads, out_part, grad_gate, grad_up, grad_down, shared_part, grad_shared_down = (
        experts_both_ways(
            ffn_in,
            gates_out,
            grad_all,
            expert_gate,
            expert_up,
            expert_down,
            shared_two,
            local_down,
            ns,
            ne,
            2,
        )
    )
    gate_grads = gate_grads[:, :local_experts].reshape(experts, length)
    picked_grad = gates * (gate_grads - jnp.sum(gates * gate_grads, 0, keepdims=True))
    logit_grad = picked_grad.T.astype(BF)
    grad_router = matmul_rows(ffn_in, logit_grad)
    ffn_in_grad = matmul_cols(logit_grad, full_router) + back_sum
    resid_norm_grad, grad_norm_ffn = rms_back(resid, full_norm_ffn, ffn_in_grad)
    resid_grad = grad_low.astype(F32) + resid_norm_grad
    resid_low = resid_grad.astype(BF)
    inside = jnp.sum(resid_low.astype(F32) * mixer_out, -1) / (scale_gate * inner)
    scales = jnp.concatenate(
        [scale_gate[None], inside[None], jnp.zeros((6, length), F32)], 0
    )

    result, grad_gate, projected_grad, grad_out, in_grad, common_grad, aux = mix_backward(
        projected,
        table,
        head_table,
        scanned,
        mixed,
        entries,
        out_local,
        resid_low,
        scales,
        out_part,
        grad_gate,
        lowered,
        jnp.pad(grad_router, ((0, 0), (heads, 128 - heads - experts))),
        resid,
        jnp.pad(grad_norm_ffn, (0, 16 * 128 - model)).reshape(16, 128),
        jnp.broadcast_to(jnp.pad(stat_terms, (0, 126))[None], (8, 128)),
        ns,
        ne,
        hw,
        state2,
        local_heads,
        width,
        4,
    )
    (
        grad_in,
        grad_pack,
        grad_out,
        tokens_grad,
        sums,
        grad_shared_gate,
        grad_shared_up,
        grad_up,
        grad_down,
        grad_shared_down,
    ) = sum_weights(
        in_grad.reshape(ns, ne, rows, -1),
        common_grad.reshape(ns, 1, ne, rows, -1),
        grad_out.reshape(ne, hw // ne, model),
        projected_grad,
        in_local,
        in_common,
        tokens[0],
        resid_grad,
        jnp.broadcast_to(full_norm_mix[None], (8, model)),
        aux,
        [
            grad_up,
            grad_down,
            grad_shared_down.reshape(ns, 1, hidden_rows, model),
            shared_part.reshape(ns, 1, ne, rows, -1),
        ],
        128,
        ns,
        ne,
        6,
    )
    grad_step = grad_pack[:, :heads]
    grad_router = grad_pack[:, heads : heads + experts]
    tiles = (hw + state2) // 128
    sums = jnp.swapaxes(sums, 1, 2).reshape(ns, -1, 8, 128)
    table_all = jnp.swapaxes(sums[:, :tiles], 1, 2).reshape(ns, 8, hw + state2)
    heads_all = sums[:, tiles]
    norm_sums = jnp.sum(sums[:, tiles + 1 : tiles + 5], 0).reshape(2, -1)[:, :model]
    grad_norm_ffn, grad_norm_mix = norm_sums[0], norm_sums[1]
    gain_all = table_all[:, width + 1, :hw]
    skip_all = jnp.sum(table_all[:, width + 2, :hw].reshape(heads, -1), -1)
    table_all = table_all[:, : width + 1]
    conv_all = jnp.concatenate(
        [
            jnp.swapaxes(table_all[:, :, :hw], 0, 1).reshape(width + 1, inner),
            jnp.sum(table_all[:, :, hw:], 0),
        ],
        1,
    )
    conv_grads = lax.dynamic_slice_in_dim(conv_all, place * channels, channels, 1)
    return (
        result[None],
        tokens_grad[None],
        lax.dynamic_slice_in_dim(grad_norm_mix, place * rows, rows),
        grad_in,
        grad_step,
        conv_grads[:width],
        conv_grads[width],
        heads_all[:, 0, :local_heads].reshape(heads),
        heads_all[:, 1, :local_heads].reshape(heads),
        skip_all,
        lax.dynamic_slice_in_dim(gain_all.reshape(inner), place * gains, gains),
        grad_out,
        lax.dynamic_slice_in_dim(grad_norm_ffn, place * rows, rows),
        grad_router,
        grad_shared_gate,
        grad_shared_up,
        grad_shared_down[0],
        grad_gate,
        grad_up,
        grad_down,
        jnp.sum(heads_all[:, 2, :3], 0) / (total * length * model),
    )


def solution(mesh):
    both = ("seq", "exp")
    return jax.shard_map(
        on_device,
        mesh=mesh,
        in_specs=(
            P("exp", "seq", None),
            P("exp", "seq", None),
            P("exp", "seq", None),
            P(both),
            P(both, None),
            P(both, None),
            P(None, both),
            P(both),
            P(),
            P(),
            P(),
            P(both),
            P(both, None),
            P(both),
            P(both, None),
            P(both, None),
            P(both, None),
            P(both, None),
            P("exp", None, None),
            P("exp", None, None),
            P("exp", None, None),
        ),
        out_specs=(
            P("exp", "seq", None),
            P("exp", "seq", None),
            P(both),
            P(both, None),
            P(both, None),
            P(None, both),
            P(both),
            P(),
            P(),
            P(),
            P(both),
            P(both, None),
            P(both),
            P(both, None),
            P(both, None),
            P(both, None),
            P(both, None),
            P("exp", "seq", None),
            P("exp", "seq", None),
            P("exp", None, "seq"),
            P(),
        ),
        check_vma=False,
    )
```
